128 devices in a mesh: seq: 16 (over z_hi, x, core), mp: 8 (over y, z_lo).
Axes of the slice: x: 4, y: 4, z: 4 (z_hi: 2, z_lo: 2; z = z_hi * 2 + z_lo), core: 2. Of those that a mesh axis runs over, the one named last changes fastest.
Arguments:
- patches: bfloat16 [9216, 6144], P('seq', 'mp'), may hold values from -6 to 6
- layer_norm_gain: float32 [6144], P('mp'), may hold values from 0.5 to 1.5
- w_qkv: bfloat16 [6144, 3, 3072], P('seq', None, 'mp'), may hold values from -0.6761612 to 0.6761612
- counts: int32 [16, 4], P('seq'), may hold values from 1 to 288, 576 in all within a row
- grad_out: bfloat16 [9216, 3072], P('seq', 'mp'), may hold values from -6 to 6
Outputs:
- heads_out: bfloat16 [9216, 3072], P('seq', 'mp')
- patch_gradient: bfloat16 [9216, 6144], P('seq', 'mp')
- gain_gradient: float32 [6144], P('mp')
- grad_qkv: float32 [6144, 3, 3072], P('seq', None, 'mp')
The draws below stay inside these ranges and needn't reach their ends.
Inputs may be any that keep to these rules, and one draw needn't show every extreme that they name: In each pack the 4 counts sum to 576, and the largest is 288.
All inputs are finite; a program needn't handle non-finite values.
Results may differ from the reference program's by a relative error of at most 0.039.
Values may be sent and summed in bfloat16 or wider, within the bound.
No kernel may reach another device: no remote copies, remote signals or barrier semaphores. Data moves between devices by JAX's collectives and lax.ppermute only.
A program may use at most 128 MiB of HBM per device.

```python
import math
import jax
import jax.numpy as jnp
import numpy as np
from jax import lax

D = 6144
HEADS = 24
HD = 128
TOK_DEV = 576
IMGS = 4
PACKS = 16
TOKENS = 9216
N_SEQ = 16
N_MP = 8


def draw_w_qkv(key, part):
    key = jax.random.fold_in(key, 11)
    first = jax.random.fold_in(key, 0)
    array_shape = (D, 3, HEADS * HD)
    drawn = jnp.clip(jax.random.normal(first, array_shape, jnp.float32), -6.0, 6.0) / math.sqrt(D)
    return drawn.astype(jnp.bfloat16)


def levels(own_key, extent, cuts, low, top_value):
    gain, own = 1.0, jax.random.fold_in(own_key, 6)
    for axis_at, parts in cuts:
        heights = jnp.exp(jax.random.uniform(jax.random.fold_in(own, axis_at), (parts,), jnp.float32, low / len(cuts), top_value / len(cuts)))
        gain = gain * jnp.repeat(heights, extent[axis_at] // parts).reshape([-1 if axis == axis_at else 1 for axis in range(len(extent))])
    return gain


def split_up(number_of, total, most, slope):
    portions = [(1 << 20) // math.isqrt(standing ** slope) + 1 for standing in range(2, number_of + 1)]
    rest, given = total - most - (number_of - 1), [1] * (number_of - 1)
    while rest > 0:
        movable = [i for i in range(number_of - 1) if given[i] < most]
        mass, remaining = sum([portions[i] for i in movable]), rest
        for i in movable:
            addition = min(most - given[i], max(1, remaining * portions[i] // mass), rest)
            given[i] = given[i] + addition
            rest = rest - addition
    return np.array([most] + given)


def ragged(stream_key, amount, total, most, skew):
    if amount == 2:
        one = jax.random.randint(stream_key, (), max(1, total - most), min(most, total - 1) + 1)
        return jnp.stack([one, total - one])
    sizes = jnp.asarray(split_up(amount, total, most, skew), jnp.int32)
    pairs = (amount - 1) // 2
    source_of, sink = sizes[1:1 + 2 * pairs:2], sizes[2:2 + 2 * pairs:2]
    slack = jnp.minimum(source_of - 1, most - sink)
    passed = jax.random.randint(jax.random.fold_in(stream_key, 1), (pairs,), 0, 1 << 20) % (slack + 1)
    sizes = sizes.at[1:1 + 2 * pairs:2].set(source_of - passed).at[2:2 + 2 * pairs:2].set(sink + passed)
    return sizes[jax.random.permutation(jax.random.fold_in(stream_key, 2), amount)]


def centred(own_key, dims, scale, most, cuts=(), kind=jnp.bfloat16):
    loudness = levels(own_key, dims, cuts, -0.22, 0.18) if cuts else 1.0
    values = jax.random.normal(own_key, dims, jnp.float32) * scale * loudness
    return jnp.minimum(jnp.maximum(values, -most), most).astype(kind)


def setup_inputs(seed: int = 0) -> dict:
    key_list = jax.random.split(jax.random.key(seed), 6)
    patches = centred(key_list[0], (TOKENS, D), 1.0, 6.0, ((0, 16), (1, 8)))
    layer_norm_gain = jnp.clip(0.5 + 1.0 * jax.random.uniform(key_list[1], (D,), jnp.float32) ** levels(key_list[1], (D,), ((0, 8),), -0.2, 0.2), 0.5, 1.5)
    w_qkv = draw_w_qkv(jax.random.fold_in(key_list[5], 71), 0)
    counts = jax.vmap(lambda own: ragged(own, IMGS, TOK_DEV, TOK_DEV // 2, 2))(jax.random.split(key_list[3], PACKS)).reshape((PACKS, IMGS)).astype(jnp.int32)
    grad_out = centred(key_list[4], (TOKENS, HEADS * HD), 1.0, 6.0, ((0, 16), (1, 8)))
    return dict(patches=patches, layer_norm_gain=layer_norm_gain, w_qkv=w_qkv, counts=counts, grad_out=grad_out)


epsilon = 1e-06
highest = lax.Precision.HIGHEST

def image_mask(lengths, row_count):
    image_ends = jnp.cumsum(lengths.astype(jnp.int32))
    position = jnp.arange(row_count, dtype=jnp.int32)
    image_ids = lax.optimization_barrier(jnp.sum((position[:, None] >= image_ends[None, :]).astype(jnp.int32), axis=1))
    return image_ids[:, None] == image_ids[None, :]

def attend(queries, key_rows, value_rows, upstream, same_image):
    scale_factor = HD ** (-0.5)
    scores = jnp.einsum('hqd,hkd->hqk', queries, key_rows, precision=highest) * scale_factor
    scores = jnp.where(same_image[None, :, :], scores, -1e+30)
    row_peak = lax.optimization_barrier(jnp.max(scores, axis=2, keepdims=True))
    exponent = jnp.exp(scores - row_peak)
    softmax_rows = exponent / lax.optimization_barrier(jnp.sum(exponent, axis=2, keepdims=True))
    attended = jnp.einsum('hqk,hkd->hqd', softmax_rows, value_rows, precision=highest)
    grad_soft = jnp.einsum('hqd,hkd->hqk', upstream, value_rows, precision=highest)
    grad_value = jnp.einsum('hqk,hqd->hkd', softmax_rows, upstream, precision=highest)
    grad_scores = softmax_rows * (grad_soft - lax.optimization_barrier(jnp.sum(grad_soft * softmax_rows, axis=2, keepdims=True)))
    grad_query = jnp.einsum('hqk,hkd->hqd', grad_scores, key_rows, precision=highest) * scale_factor
    grad_key = jnp.einsum('hqk,hqd->hkd', grad_scores, queries, precision=highest) * scale_factor
    return (attended, grad_query, grad_key, grad_value)

def reference(patches, layer_norm_gain, w_qkv, counts, grad_out):
    inputs_f = patches.astype(jnp.float32)
    row_mean = lax.optimization_barrier(jnp.mean(inputs_f, axis=1, keepdims=True))
    centered_rows = inputs_f - row_mean
    row_var = lax.optimization_barrier(jnp.mean(centered_rows * centered_rows, axis=1, keepdims=True))
    inverse_deviation = lax.rsqrt(row_var + epsilon)
    standardized_rows = centered_rows * inverse_deviation
    normalized_rows = (standardized_rows * layer_norm_gain[None, :]).astype(jnp.bfloat16)
    width = 3 * HEADS * HD
    flat_w = w_qkv.reshape(D, width)
    qkv = jnp.dot(normalized_rows, flat_w, preferred_element_type=jnp.float32)
    qkv = qkv.reshape(N_SEQ, TOK_DEV, 3, HEADS, HD)
    upstream_all = grad_out.astype(jnp.float32).reshape(N_SEQ, TOK_DEV, HEADS, HD)

    def one_pack(packed):
        pack_qkv, pack_grads, lengths = packed
        same_image = image_mask(lengths, TOK_DEV)
        qkv_parts = jnp.transpose(pack_qkv, (1, 2, 0, 3))
        upstream = jnp.transpose(pack_grads, (1, 0, 2))
        attended, grad_query, grad_key, grad_value = attend(qkv_parts[0], qkv_parts[1], qkv_parts[2], upstream, same_image)
        heads_rows = jnp.transpose(attended, (1, 0, 2)).reshape(TOK_DEV, HEADS * HD).astype(jnp.bfloat16)
        stacked = jnp.stack([grad_query, grad_key, grad_value], axis=0)
        grad_rows = jnp.transpose(stacked, (2, 0, 1, 3)).reshape(TOK_DEV, width).astype(jnp.bfloat16)
        return (heads_rows, grad_rows)
    heads_packs, dqkv_packs = lax.map(one_pack, (qkv, upstream_all, counts))
    heads_out = heads_packs.reshape(TOKENS, HEADS * HD)
    normed_packs = normalized_rows.reshape(N_SEQ, TOK_DEV, D)

    def add_pack(total, packed):
        pack_rows, pack_grads = packed
        term_rows = jnp.dot(pack_rows.T, pack_grads, preferred_element_type=jnp.float32)
        rounded = lax.optimization_barrier(term_rows.astype(jnp.bfloat16))
        return (total + rounded.astype(jnp.float32), None)
    grad_flat, _ = lax.scan(add_pack, jnp.zeros((D, width), jnp.float32), (normed_packs, dqkv_packs))
    grad_qkv = grad_flat.reshape(D, 3, HEADS * HD)
    group_cols = HEADS * HD // N_MP
    dqkv_groups = jnp.transpose(dqkv_packs.reshape(TOKENS, 3, N_MP, group_cols), (2, 0, 1, 3)).reshape(N_MP, TOKENS, 3 * group_cols)
    w_groups = jnp.transpose(w_qkv.reshape(D, 3, N_MP, group_cols), (2, 0, 1, 3)).reshape(N_MP, D, 3 * group_cols)

    def add_group(total, packed):
        group_grads, group_w = packed
        term_rows = jnp.dot(group_grads, group_w.T, preferred_element_type=jnp.float32)
        rounded = lax.optimization_barrier(term_rows.astype(jnp.bfloat16))
        return (total + rounded.astype(jnp.float32), None)
    normalized_gradient, _ = lax.scan(add_group, jnp.zeros((TOKENS, D), jnp.float32), (dqkv_groups, w_groups))
    gain_gradient = lax.optimization_barrier(jnp.sum(normalized_gradient * standardized_rows, axis=0))
    standardized_gradient = normalized_gradient * layer_norm_gain[None, :]
    first_moment = lax.optimization_barrier(jnp.mean(standardized_gradient, axis=1, keepdims=True))
    second_moment = lax.optimization_barrier(jnp.mean(standardized_gradient * standardized_rows, axis=1, keepdims=True))
    patch_gradient = ((standardized_gradient - first_moment - standardized_rows * second_moment) * inverse_deviation).astype(jnp.bfloat16)
    return (heads_out, patch_gradient, gain_gradient, grad_qkv)
```

```python
import functools

import jax
import jax.numpy as jnp
from jax import lax
from jax.experimental import pallas as pl
from jax.experimental.pallas import tpu as pltpu
from jax.sharding import PartitionSpec as P

HD = 128
NH = 3
ROWS = 576
HALF = ROWS // 2
EXT = ROWS + 16
DB = 384
D = 6144
CW = 3 * DB
EPS = 1e-06
BF = jnp.bfloat16
F32 = jnp.float32


def seq_perm(f):
    out = []
    for i in range(16):
        zh, x, c = i // 8, (i // 2) % 4, i % 2
        zh, x, c = f(zh, x, c)
        out.append((i, (zh * 4 + x % 4) * 2 + c))
    return out


def mp_perm(f):
    out = []
    for i in range(8):
        y, zl = f(i // 2, i % 2)
        out.append((i, (y % 4) * 2 + zl))
    return out


CORE = seq_perm(lambda zh, x, c: (zh, x, 1 - c))
ZHI = seq_perm(lambda zh, x, c: (1 - zh, x, c))
XP = seq_perm(lambda zh, x, c: (zh, x + 1, c))
XM = seq_perm(lambda zh, x, c: (zh, x - 1, c))
XSPLIT = seq_perm(lambda zh, x, c: (zh, x + 1 - 2 * c, c))
XA = seq_perm(lambda zh, x, c: (zh, x ^ 1, c))
XB = seq_perm(lambda zh, x, c: (zh, x ^ 3, c))
ZLO = mp_perm(lambda y, zl: (y, 1 - zl))
YP = mp_perm(lambda y, zl: (y + 1, zl))
YM = mp_perm(lambda y, zl: (y - 1, zl))
YA = mp_perm(lambda y, zl: (y ^ 1, zl))
YB = mp_perm(lambda y, zl: (y ^ 3, zl))


def sp(v, perm):
    return lax.ppermute(v, "seq", perm)


def mpp(v, perm):
    return lax.ppermute(v, "mp", perm)


def nt(a, b):
    return lax.dot_general(a, b, (((1,), (1,)), ((), ())), preferred_element_type=F32)


def tn(a, b):
    return lax.dot_general(a, b, (((0,), (0,)), ((), ())), preferred_element_type=F32)


def nn(a, b):
    return lax.dot_general(a, b, (((1,), (0,)), ((), ())), preferred_element_type=F32)


def norm_kernel(idx, *refs, parts):
    raws, (mean, rstd, gain, _, out) = refs[:parts], refs[parts:]
    g = gain[0]
    rows = ROWS // parts
    for p in range(parts):
        rs = pl.ds(p * rows, rows)
        v = (raws[p][...].astype(F32) - mean[rs, :]) * rstd[rs, :] * g
        v = v.astype(BF)
        out[0, 0, rs, :] = v[:, :DB]
        out[0, 1, rs, :] = v[:, DB:]
    hi = g.astype(BF).astype(F32)
    lo = (g - hi).astype(BF).astype(F32)
    lo2 = g - hi - lo
    row = lax.broadcasted_iota(jnp.int32, (16, 2 * DB), 0)
    tail = jnp.where(row == 0, hi, jnp.where(row == 1, lo, jnp.where(row == 2, lo2, 0.0)))
    tail = tail.astype(BF)
    out[0, 0, pl.ds(ROWS, 16), :] = tail[:, :DB]
    out[0, 1, pl.ds(ROWS, 16), :] = tail[:, DB:]


def place_normed(buf, index, raws, mean, rstd, gain):
    parts = len(raws)
    rows = ROWS // parts
    whole = lambda shape: pl.BlockSpec(shape, lambda i, s: (0,) * len(shape))
    spec = pltpu.PrefetchScalarGridSpec(
        num_scalar_prefetch=1,
        grid=(1,),
        in_specs=[whole((rows, 2 * DB))] * parts
        + [whole((ROWS, 1)), whole((ROWS, 1)), pl.BlockSpec((1, 1, 2 * DB), lambda i, s: (s[0], 0, 0)),
           pl.BlockSpec(memory_space=pl.ANY)],
        out_specs=pl.BlockSpec((1, 2, EXT, DB), lambda i, s: (s[0], 0, 0, 0)),
    )
    return pl.pallas_call(
        functools.partial(norm_kernel, parts=parts),
        grid_spec=spec,
        out_shape=jax.ShapeDtypeStruct(buf.shape, buf.dtype),
        input_output_aliases={parts + 4: 0},
        compiler_params=pltpu.CompilerParams(vmem_limit_bytes=48 << 20),
        cost_estimate=pl.CostEstimate(flops=4 * ROWS * 768, bytes_accessed=4 * ROWS * 768, transcendentals=0),
        name="normalize",
    )(index.reshape(1), *raws, mean, rstd, gain, buf)


def qkv_kernel(x, w, out):
    t = nn(x[0, 0], w[0, 0]) + nn(x[0, 1], w[0, 1])

    @pl.when(pl.program_id(0) == 0)
    def _():
        out[...] = t

    @pl.when(pl.program_id(0) > 0)
    def _():
        out[...] += t


def project(normed, w):
    return pl.pallas_call(
        qkv_kernel,
        grid=(8,),
        in_specs=[
            pl.BlockSpec((1, 2, EXT, DB), lambda m: (m, 0, 0, 0)),
            pl.BlockSpec((1, 2, DB, CW), lambda m: (m, 0, 0, 0)),
        ],
        out_specs=pl.BlockSpec((EXT, CW), lambda m: (0, 0)),
        out_shape=jax.ShapeDtypeStruct((EXT, CW), F32),
        compiler_params=pltpu.CompilerParams(vmem_limit_bytes=48 << 20),
        cost_estimate=pl.CostEstimate(flops=2 * EXT * D * CW, bytes_accessed=24 << 20, transcendentals=0),
        name="project",
    )(normed, w)


def split(v):
    hi = v.astype(BF)
    return hi, (v - hi.astype(F32)).astype(BF)


def attn_kernel(counts, q_ref, k_ref, v_ref, g_ref, out_ref, dqkv_ref, mom_ref):
    h = pl.program_id(0)
    e0 = counts[0]
    e1 = e0 + counts[1]
    e2 = e1 + counts[2]
    rid = lax.broadcasted_iota(jnp.int32, (ROWS, 1), 0)
    cid = lax.broadcasted_iota(jnp.int32, (1, ROWS), 1)
    img = lambda p: (p >= e0).astype(jnp.int32) + (p >= e1).astype(jnp.int32) + (p >= e2).astype(jnp.int32)
    same = img(rid) == img(cid)
    scale = HD ** (-0.5)
    q = q_ref[:ROWS, :] * scale
    k = k_ref[:ROWS, :]
    v = v_ref[:ROWS, :]
    qh, ql = split(q)
    kh, kl = split(k)
    vb = v.astype(BF)
    g = g_ref[...]
    s = nt(jnp.concatenate([qh, qh], 1), jnp.concatenate([kh, kl], 1)) + nt(ql, kh)
    s = jnp.where(same, s, -1e30)
    p = jnp.exp(s - jnp.max(s, axis=1, keepdims=True))
    p = p / jnp.sum(p, axis=1, keepdims=True)
    pb = p.astype(BF)
    out_ref[...] = nn(pb, vb).astype(BF)
    dp = nt(g, vb)
    dv = tn(pb, g)
    ds = p * (dp - jnp.sum(dp * p, axis=1, keepdims=True))
    dsb = ds.astype(BF)
    dq = (nn(dsb, kh) * scale).astype(BF)
    dk = tn(dsb, qh).astype(BF)
    dv = dv.astype(BF)
    dqkv_ref[0] = dq
    dqkv_ref[1] = dk
    dqkv_ref[2] = dv
    m1 = jnp.zeros((ROWS, 1), F32)
    m2 = jnp.zeros((ROWS, 1), F32)
    for d, r in ((dq, q_ref), (dk, k_ref), (dv, v_ref)):
        df = d.astype(F32)
        u = r[ROWS:ROWS + 1, :] + r[ROWS + 1:ROWS + 2, :] + r[ROWS + 2:ROWS + 3, :]
        m1 = m1 + jnp.sum(df * u, axis=1, keepdims=True)
        m2 = m2 + jnp.sum(df * r[:ROWS, :], axis=1, keepdims=True)
    lane = lax.broadcasted_iota(jnp.int32, (ROWS, 128), 1)
    mom = jnp.where(lane == 0, m1, jnp.where(lane == 1, m2, 0.0))

    @pl.when(h == 0)
    def _():
        mom_ref[...] = mom

    @pl.when(h > 0)
    def _():
        mom_ref[...] += mom


def attend(counts, qkv, grad_out):
    part = lambda j: pl.BlockSpec((EXT, HD), lambda h: (0, j * NH + h))
    return pl.pallas_call(
        attn_kernel,
        grid=(NH,),
        in_specs=[
            pl.BlockSpec(memory_space=pltpu.SMEM),
            part(0),
            part(1),
            part(2),
            pl.BlockSpec((ROWS, HD), lambda h: (0, h)),
        ],
        out_specs=[
            pl.BlockSpec((ROWS, HD), lambda h: (0, h)),
            pl.BlockSpec((3, ROWS, HD), lambda h: (0, 0, h)),
            pl.BlockSpec((ROWS, 128), lambda h: (0, 0)),
        ],
        out_shape=[
            jax.ShapeDtypeStruct((ROWS, DB), BF),
            jax.ShapeDtypeStruct((3, ROWS, DB), BF),
            jax.ShapeDtypeStruct((ROWS, 128), F32),
        ],
        compiler_params=pltpu.CompilerParams(vmem_limit_bytes=48 << 20),
        cost_estimate=pl.CostEstimate(flops=7 * 2 * NH * ROWS * ROWS * HD * 2, bytes_accessed=6 << 20,
                                      transcendentals=NH * ROWS * ROWS),
        name="attention",
    )(counts, qkv, qkv, qkv, grad_out)


def gx_kernel(idx, d_ref, w_ref, out):
    d = jnp.concatenate([d_ref[0], d_ref[1], d_ref[2]], axis=1)
    for c in range(2):
        t = nt(d, w_ref[0, c]).astype(BF)
        out[0, 0, :, pl.ds(c * DB, DB)] = t[:HALF]
        out[1, 0, :, pl.ds(c * DB, DB)] = t[HALF:]


def grad_rows(index, dqkv, w):
    n = index.shape[0]
    spec = pltpu.PrefetchScalarGridSpec(
        num_scalar_prefetch=1,
        grid=(n,),
        in_specs=[
            pl.BlockSpec((3, ROWS, DB), lambda i, s: (0, 0, 0)),
            pl.BlockSpec((1, 2, DB, CW), lambda i, s: (s[i], 0, 0, 0)),
        ],
        out_specs=pl.BlockSpec((2, 1, HALF, 2 * DB), lambda i, s: (0, i, 0, 0)),
    )
    return pl.pallas_call(
        gx_kernel,
        grid_spec=spec,
        out_shape=jax.ShapeDtypeStruct((2, n, HALF, 2 * DB), BF),
        compiler_params=pltpu.CompilerParams(vmem_limit_bytes=48 << 20),
        cost_estimate=pl.CostEstimate(flops=2 * n * ROWS * 768 * CW, bytes_accessed=n * 3 << 20, transcendentals=0),
        name="grad_rows",
    )(index, dqkv, w)


def gw_kernel(idx, n1, n2, d1, d2, out):
    da = jnp.concatenate([d1[0], d1[1], d1[2]], axis=1)
    db = jnp.concatenate([d2[0], d2[1], d2[2]], axis=1)
    t = (tn(n1[0, 0, :ROWS, :], da) + tn(n2[0, :ROWS, :], db)).astype(BF)
    out[0, 0] = t[:DB // 2]
    out[1, 0] = t[DB // 2:]


def grad_weights(index, core, normed, other, dqkv, dother):
    n = index.shape[0]
    spec = pltpu.PrefetchScalarGridSpec(
        num_scalar_prefetch=1,
        grid=(n,),
        in_specs=[
            pl.BlockSpec((1, 1, EXT, DB), lambda i, s: (s[i], s[n], 0, 0)),
            pl.BlockSpec((1, EXT, DB), lambda i, s: (s[i], 0, 0)),
            pl.BlockSpec((3, ROWS, DB), lambda i, s: (0, 0, 0)),
            pl.BlockSpec((3, ROWS, DB), lambda i, s: (0, 0, 0)),
        ],
        out_specs=pl.BlockSpec((2, 1, DB // 2, CW), lambda i, s: (0, i, 0, 0)),
    )
    return pl.pallas_call(
        gw_kernel,
        grid_spec=spec,
        out_shape=jax.ShapeDtypeStruct((2, n, DB // 2, CW), BF),
        compiler_params=pltpu.CompilerParams(vmem_limit_bytes=48 << 20),
        cost_estimate=pl.CostEstimate(flops=4 * n * ROWS * DB * CW, bytes_accessed=n * 3 << 20, transcendentals=0),
        name="grad_weights",
    )(jnp.concatenate([index, core.reshape(1)]), normed, other, dqkv, dother)


def add(a, b):
    return (a.astype(F32) + b.astype(F32)).astype(BF)


def ivec(*v):
    return jnp.stack([jnp.asarray(e, jnp.int32) for e in v])


def local(patches, gain, w_qkv, counts, grad_out):
    si, mi = lax.axis_index("seq"), lax.axis_index("mp")
    core, x, zh = si % 2, (si // 2) % 4, si // 8
    y, zl = mi // 2, mi % 2
    mw = lambda dx, dz: jnp.where(dz == 0, zh, 1 - zh) * 4 + (x + dx) % 4
    mx = lambda dy, dz: ((y + dy) % 4) * 2 + jnp.where(dz == 0, zl, 1 - zl)
    is0 = core == 0

    p0 = patches
    pz = mpp(p0, ZLO)
    p_m = mpp(p0, YP)
    p_p = mpp(p0, YM)

    w_own = w_qkv.reshape(DB, CW)
    w_oth = sp(w_own, CORE)
    ordered = lambda a, b: jnp.where(is0, jnp.stack([a, b]), jnp.stack([b, a]))
    pair = ordered(w_own, w_oth)
    wz_own = sp(w_own, ZHI)
    ra = sp(pair, XSPLIT)
    wz_oth = sp(wz_own, CORE)
    pair_z = ordered(wz_own, wz_oth)
    rb = sp(pair_z, XSPLIT)

    pf = patches.astype(F32)
    mean = jnp.mean(pf, axis=1)
    m2 = jnp.sum((pf - mean[:, None]) ** 2, axis=1)
    gains = gain.reshape(1, 768)
    count = 768.0
    for perm in (ZLO, YA, YB):
        got = mpp(jnp.concatenate([mean, m2, gains.reshape(-1)]), perm)
        o_mean, o_m2, o_g = got[:ROWS], got[ROWS:2 * ROWS], got[2 * ROWS:]
        delta = mean - o_mean
        m2 = m2 + o_m2 + delta * delta * (count / 2)
        mean = (mean + o_mean) * 0.5
        count *= 2
        gains = jnp.concatenate([gains, o_g.reshape(gains.shape)], axis=0)
    rstd = lax.rsqrt(m2 / D + EPS)
    mean, rstd = mean[:, None], rstd[:, None]
    slot_of = jnp.zeros((8,), jnp.int32)
    for k, xr in enumerate((0, 1, 2, 3, 6, 7, 4, 5)):
        slot_of = jnp.where((jnp.arange(8) ^ mi) == xr, k, slot_of)
    gain_abs = jnp.take(gains, slot_of, axis=0).reshape(8, 1, 768)

    pz_m = mpp(pz, YP)
    pz_p = mpp(pz, YM)
    f_m = mpp(jnp.stack([p_m[:HALF], pz_m[:HALF]]), YP)
    f_p = mpp(jnp.stack([p_p[HALF:], pz_p[HALF:]]), YM)

    nb = jnp.zeros((8, 2, EXT, DB), BF)
    for index, raws in (
        (mx(0, 0), [p0]),
        (mx(0, 1), [pz]),
        (mx(-1, 0), [p_m]),
        (mx(1, 0), [p_p]),
        (mx(-1, 1), [pz_m]),
        (mx(1, 1), [pz_p]),
        (mx(2, 0), [f_m[0], f_p[0]]),
        (mx(2, 1), [f_m[1], f_p[1]]),
    ):
        nb = place_normed(nb, index, raws, mean, rstd, gain_abs)

    ea = sp(ra, CORE)
    eb = sp(rb, CORE)
    half_c = lambda v: lax.dynamic_index_in_dim(v, core, 0, keepdims=False)
    rc = sp(jnp.stack([half_c(ra), half_c(rb)]), XSPLIT)
    ec = sp(rc, CORE)
    wb = jnp.zeros((8, 2, DB, CW), BF)
    dr = jnp.where(is0, -1, 1)
    put = lambda buf, v, m: lax.dynamic_update_slice(buf, v[None], (m, 0, 0, 0))
    wb = put(wb, pair, mw(0, 0))
    wb = put(wb, pair_z, mw(0, 1))
    wb = put(wb, ra, mw(dr, 0))
    wb = put(wb, ea, mw(-dr, 0))
    wb = put(wb, rb, mw(dr, 1))
    wb = put(wb, eb, mw(-dr, 1))
    wb = put(wb, ordered(rc[0], ec[0]), mw(2, 0))
    wb = put(wb, ordered(rc[1], ec[1]), mw(2, 1))

    qkv = project(nb, wb)
    n_other = sp(lax.dynamic_index_in_dim(nb, 1 - core, 1, keepdims=False), CORE)
    heads_out, dqkv, mom = attend(counts.reshape(4), qkv, grad_out)
    d_other = sp(dqkv, CORE)

    gx1 = grad_rows(ivec(mx(2, 0), mx(2, 1)), dqkv, wb)
    h_m = mpp(gx1[0], YP)
    h_p = mpp(gx1[1], YM)
    gw1 = grad_weights(ivec(mw(2, 0), mw(2, 1)), core, nb, n_other, dqkv, d_other)
    v_m = sp(gw1[0], XP)
    v_p = sp(gw1[1], XM)
    gx2 = grad_rows(ivec(mx(1, 1), mx(-1, 1)), dqkv, wb)
    gw2 = grad_weights(ivec(mw(1, 1), mw(-1, 1)), core, nb, n_other, dqkv, d_other)
    gx3 = grad_rows(ivec(mx(1, 0), mx(-1, 0)), dqkv, wb)
    gw3 = grad_weights(ivec(mw(1, 0), mw(-1, 0)), core, nb, n_other, dqkv, d_other)
    gx4 = grad_rows(ivec(mx(0, 1), mx(0, 0)), dqkv, wb)
    gw4 = grad_weights(ivec(mw(0, 1), mw(0, 0)), core, nb, n_other, dqkv, d_other)

    def ring(g, lo_in, hi_in, send, up, down):
        to_up = jnp.stack([add(g[0, 0], lo_in), g[1, 0]])
        to_down = jnp.stack([g[0, 1], add(g[1, 1], hi_in)])
        return send(to_up, up), send(to_down, down)

    ya1, ya2 = ring(gx2, h_m[1], h_p[1], mpp, YP, YM)
    xa1, xa2 = ring(gw2, v_m[1], v_p[1], sp, XP, XM)
    yb1, yb2 = ring(gx3, h_m[0], h_p[0], mpp, YP, YM)
    xb1, xb2 = ring(gw3, v_m[0], v_p[0], sp, XP, XM)
    f = lambda v: v.astype(F32)
    y_out = (f(gx4[:, 0]) + f(ya1) + f(ya2)).astype(BF)
    yz = mpp(y_out, ZLO)
    x_out = (f(gw4[:, 0]) + f(xa1) + f(xa2)).astype(BF)
    xz = sp(x_out, ZHI)

    mom = jnp.concatenate([mom[:, 0], mom[:, 1]])
    for perm in (ZLO, YA, YB):
        mom = mom + mpp(mom, perm)
    mom = mom / D

    gn = (f(gx4[:, 1]) + f(yb1) + f(yb2) + f(yz)).reshape(ROWS, 768)
    xhat = (pf - mean) * rstd
    gg = jnp.sum(gn * xhat, axis=0)
    for perm in (CORE, XA, XB, ZHI):
        gg = gg + sp(gg, perm)
    grad_p = ((gn * gain[None, :] - mom[:ROWS, None] - xhat * mom[ROWS:, None]) * rstd).astype(BF)
    gw = (f(gw4[:, 1]) + f(xb1) + f(xb2) + f(xz)).reshape(DB, 3, DB)
    return heads_out, grad_p, gg, gw


def solution(mesh):
    placed = (P("seq", "mp"), P("mp"), P("seq", None, "mp"), P("seq", None), P("seq", "mp"))
    return jax.shard_map(
        local,
        mesh=mesh,
        in_specs=placed,
        out_specs=(P("seq", "mp"), P("seq", "mp"), P("mp"), P("seq", None, "mp")),
        check_vma=False,
    )
```

```python
import functools

import jax
import jax.numpy as jnp
from jax import lax
from jax.experimental import pallas as pl
from jax.experimental.pallas import tpu as pltpu
from jax.sharding import PartitionSpec as P

HD = 128
NH = 3
ROWS = 576
HALF = ROWS // 2
EXT = ROWS + 16
DB = 384
D = 6144
CW = 3 * DB
EPS = 1e-06
BF = jnp.bfloat16
F32 = jnp.float32


def seq_perm(f):
    out = []
    for i in range(16):
        zh, x, c = i // 8, (i // 2) % 4, i % 2
        zh, x, c = f(zh, x, c)
        out.append((i, (zh * 4 + x % 4) * 2 + c))
    return out


def mp_perm(f):
    out = []
    for i in range(8):
        y, zl = f(i // 2, i % 2)
        out.append((i, (y % 4) * 2 + zl))
    return out


CORE = seq_perm(lambda zh, x, c: (zh, x, 1 - c))
ZHI = seq_perm(lambda zh, x, c: (1 - zh, x, c))
XP = seq_perm(lambda zh, x, c: (zh, x + 1, c))
XM = seq_perm(lambda zh, x, c: (zh, x - 1, c))
XSPLIT = seq_perm(lambda zh, x, c: (zh, x + 1 - 2 * c, c))
XA = seq_perm(lambda zh, x, c: (zh, x ^ 1, c))
XB = seq_perm(lambda zh, x, c: (zh, x ^ 3, c))
ZLO = mp_perm(lambda y, zl: (y, 1 - zl))
YP = mp_perm(lambda y, zl: (y + 1, zl))
YM = mp_perm(lambda y, zl: (y - 1, zl))
YA = mp_perm(lambda y, zl: (y ^ 1, zl))
YB = mp_perm(lambda y, zl: (y ^ 3, zl))


def sp(v, perm):
    return lax.ppermute(v, "seq", perm)


def mpp(v, perm):
    return lax.ppermute(v, "mp", perm)


def nt(a, b):
    return lax.dot_general(a, b, (((1,), (1,)), ((), ())), preferred_element_type=F32)


def tn(a, b):
    return lax.dot_general(a, b, (((0,), (0,)), ((), ())), preferred_element_type=F32)


def nn(a, b):
    return lax.dot_general(a, b, (((1,), (0,)), ((), ())), preferred_element_type=F32)


def stats_kernel(*refs, before, last):
    *raws, out = refs
    mean = m2 = None
    if before:
        state, *raws = raws
        mean, m2 = state[:, 0:1], state[:, 1:2]
    chunks = []
    for r in raws:
        if len(r.shape) == 2:
            chunks.append(r[:ROWS, :])
    if len(raws[0].shape) == 3:
        lo, hi = raws
        chunks += [jnp.concatenate([lo[j], hi[j, :HALF, :]], axis=0) for j in range(2)]
    n = before
    for c in chunks:
        v = c.astype(F32)
        cm = jnp.sum(v, axis=1, keepdims=True) * (1.0 / 768)
        dv = v - cm
        c2 = jnp.sum(dv * dv, axis=1, keepdims=True)
        if n == 0:
            mean, m2 = cm, c2
        else:
            delta = cm - mean
            mean = mean + delta * (1.0 / (n + 1))
            m2 = m2 + c2 + delta * delta * (768.0 * n / (n + 1))
        n += 1
    if last:
        m2 = lax.rsqrt(m2 * (1.0 / D) + EPS)
    lane = lax.broadcasted_iota(jnp.int32, (ROWS, 128), 1)
    out[...] = jnp.where(lane == 0, mean, jnp.where(lane == 1, m2, 0.0))


def stats(before, state, raws, last=False):
    args = ([state] if before else []) + list(raws)
    return pl.pallas_call(
        functools.partial(stats_kernel, before=before, last=last),
        out_shape=jax.ShapeDtypeStruct((ROWS, 128), F32),
        compiler_params=pltpu.CompilerParams(vmem_limit_bytes=48 << 20),
        cost_estimate=pl.CostEstimate(flops=0, bytes_accessed=4 << 20, transcendentals=0),
        name="row_stats",
    )(*args)


def project_kernel(idx, st, r0, r1, r2, r3, r4, r5, fm, fp, pair, ra, ea, rc, ec, pz, rb, eb,
                   acc, n_own, n_send, n_last, raw, nrm, wv, sr, sw, so):
    core = idx[16]
    copies = []
    for j, r in enumerate((r0, r1, r2, r3, r4, r5)):
        copies.append(pltpu.make_async_copy(r, raw.at[idx[j]], sr.at[j]))
    for j in range(2):
        copies.append(pltpu.make_async_copy(fm.at[j], raw.at[idx[6 + j], pl.ds(0, HALF)], sr.at[6 + j]))
        copies.append(pltpu.make_async_copy(fp.at[j], raw.at[idx[6 + j], pl.ds(HALF, EXT - HALF)], sr.at[8 + j]))
    for c in copies:
        c.start()
    wc = []
    for k, (v, flip) in enumerate(((pair, 0), (ra, 0), (ea, 1), ((rc, ec), 0), (pz, 0), (rb, 0), (eb, 1))):
        for e in range(2):
            src = v[e] if isinstance(v, tuple) else v.at[e]
            half = core if e == flip else 1 - core
            wc.append(pltpu.make_async_copy(src, wv.at[k, half], sw.at[2 * k + e]))
    for c in wc:
        c.start()
    for c in copies:
        c.wait()
    mean, rstd = st[:, 0:1], st[:, 1:2]
    out = []
    own = pl.ds(pl.multiple_of(core * DB, 128), DB)
    oth = pl.ds(pl.multiple_of((1 - core) * DB, 128), DB)

    def norm(k):
        m = idx[8 + k]
        v = raw[m]
        tail = v[ROWS:]
        t = tail.astype(F32)
        g = t[0:1] + t[1:2] + t[2:3]
        nrm[k, pl.ds(0, ROWS), :] = ((v[:ROWS].astype(F32) - mean) * rstd * g).astype(BF)
        nrm[k, pl.ds(ROWS, 16), :] = tail
        out.append(pltpu.make_async_copy(nrm.at[k, :, own], n_own.at[m], so.at[3 * k]))
        out.append(pltpu.make_async_copy(nrm.at[k, :, oth], n_send.at[m], so.at[3 * k + 1]))
        if k == 7:
            out.append(pltpu.make_async_copy(nrm.at[k], n_last, so.at[3 * k + 2]))
        for c in out[2 * k:]:
            c.start()

    norm(0)
    for k in range(7):
        wc[2 * k].wait()
        wc[2 * k + 1].wait()
        t = nn(nrm[k], wv[k].reshape(2 * DB, CW))
        if k == 0:
            acc[...] = t
        else:
            acc[...] += t
        norm(k + 1)
    for c in out:
        c.wait()


def project(index, st, raws, ws):
    hbm = pl.BlockSpec(memory_space=pl.ANY)
    vmem = pl.BlockSpec(memory_space=pltpu.VMEM)
    return pl.pallas_call(
        project_kernel,
        in_specs=[pl.BlockSpec(memory_space=pltpu.SMEM), vmem] + [hbm] * (len(raws) + len(ws)),
        out_specs=[vmem, hbm, hbm, hbm],
        out_shape=[
            jax.ShapeDtypeStruct((EXT, CW), F32),
            jax.ShapeDtypeStruct((8, EXT, DB), BF),
            jax.ShapeDtypeStruct((8, EXT, DB), BF),
            jax.ShapeDtypeStruct((EXT, 2 * DB), BF),
        ],
        scratch_shapes=[
            pltpu.VMEM((8, EXT, 2 * DB), BF),
            pltpu.VMEM((8, EXT, 2 * DB), BF),
            pltpu.VMEM((7, 2, DB, CW), BF),
            pltpu.SemaphoreType.DMA((10,)),
            pltpu.SemaphoreType.DMA((14,)),
            pltpu.SemaphoreType.DMA((24,)),
        ],
        compiler_params=pltpu.CompilerParams(vmem_limit_bytes=52 << 20),
        cost_estimate=pl.CostEstimate(flops=2 * EXT * D * CW, bytes_accessed=30 << 20, transcendentals=0),
        name="project",
    )(index, st, *raws, *ws)


def split(v):
    hi = v.astype(BF)
    return hi, (v - hi.astype(F32)).astype(BF)


def attn_kernel(counts, acc, n_last, w1, w2, g_ref, out_ref, dqkv_ref, mom_ref, qkv):
    h = pl.program_id(0)

    @pl.when(h == 0)
    def _():
        core = counts[4]
        own = pl.ds(pl.multiple_of(core * DB, 128), DB)
        oth = pl.ds(pl.multiple_of((1 - core) * DB, 128), DB)
        qkv[...] = acc[...] + nn(n_last[:, own], w1[...]) + nn(n_last[:, oth], w2[...])

    col = lambda j: pl.ds(pl.multiple_of((j * NH + h) * HD, 128), HD)
    q_ref, k_ref, v_ref = (qkv.at[:, col(j)] for j in range(3))
    e0 = counts[0]
    e1 = e0 + counts[1]
    e2 = e1 + counts[2]
    rid = lax.broadcasted_iota(jnp.int32, (ROWS, 1), 0)
    cid = lax.broadcasted_iota(jnp.int32, (1, ROWS), 1)
    img = lambda p: (p >= e0).astype(jnp.int32) + (p >= e1).astype(jnp.int32) + (p >= e2).astype(jnp.int32)
    same = img(rid) == img(cid)
    scale = HD ** (-0.5)
    q = q_ref[:ROWS, :] * scale
    k = k_ref[:ROWS, :]
    v = v_ref[:ROWS, :]
    qh, ql = split(q)
    kh, kl = split(k)
    vb = v.astype(BF)
    g = g_ref[...]
    s = nt(jnp.concatenate([qh, qh], 1), jnp.concatenate([kh, kl], 1)) + nt(ql, kh)
    s = jnp.where(same, s, -1e30)
    p = jnp.exp(s - jnp.max(s, axis=1, keepdims=True))
    p = p / jnp.sum(p, axis=1, keepdims=True)
    pb = p.astype(BF)
    out_ref[...] = nn(pb, vb).astype(BF)
    dp = nt(g, vb)
    dv = tn(pb, g)
    ds = p * (dp - jnp.sum(dp * p, axis=1, keepdims=True))
    dsb = ds.astype(BF)
    dq = (nn(dsb, kh) * scale).astype(BF)
    dk = tn(dsb, qh).astype(BF)
    dv = dv.astype(BF)
    dqkv_ref[0] = dq
    dqkv_ref[1] = dk
    dqkv_ref[2] = dv
    m1 = jnp.zeros((ROWS, 1), F32)
    m2 = jnp.zeros((ROWS, 1), F32)
    for d, r in ((dq, q_ref), (dk, k_ref), (dv, v_ref)):
        df = d.astype(F32)
        u = r[ROWS:ROWS + 1, :] + r[ROWS + 1:ROWS + 2, :] + r[ROWS + 2:ROWS + 3, :]
        m1 = m1 + jnp.sum(df * u, axis=1, keepdims=True)
        m2 = m2 + jnp.sum(df * r[:ROWS, :], axis=1, keepdims=True)
    lane = lax.broadcasted_iota(jnp.int32, (ROWS, 128), 1)
    mom = jnp.where(lane == 0, m1, jnp.where(lane == 1, m2, 0.0))

    @pl.when(h == 0)
    def _():
        mom_ref[...] = mom

    @pl.when(h > 0)
    def _():
        mom_ref[...] += mom


def attend(counts, acc, n_last, w1, w2, grad_out):
    whole = lambda shape: pl.BlockSpec(shape, lambda h: (0,) * len(shape))
    return pl.pallas_call(
        attn_kernel,
        grid=(NH,),
        in_specs=[
            pl.BlockSpec(memory_space=pltpu.SMEM),
            whole((EXT, CW)),
            whole((EXT, 2 * DB)),
            whole((DB, CW)),
            whole((DB, CW)),
            pl.BlockSpec((ROWS, HD), lambda h: (0, h)),
        ],
        out_specs=[
            pl.BlockSpec((ROWS, HD), lambda h: (0, h)),
            pl.BlockSpec((3, ROWS, HD), lambda h: (0, 0, h)),
            pl.BlockSpec((ROWS, 128), lambda h: (0, 0)),
        ],
        out_shape=[
            jax.ShapeDtypeStruct((ROWS, DB), BF),
            jax.ShapeDtypeStruct((3, ROWS, DB), BF),
            jax.ShapeDtypeStruct((ROWS, 128), F32),
        ],
        scratch_shapes=[pltpu.VMEM((EXT, CW), F32)],
        compiler_params=pltpu.CompilerParams(vmem_limit_bytes=48 << 20),
        cost_estimate=pl.CostEstimate(flops=7 * 2 * NH * ROWS * ROWS * HD * 2, bytes_accessed=6 << 20,
                                      transcendentals=NH * ROWS * ROWS),
        name="attention",
    )(counts, acc, n_last, w1, w2, grad_out)


def gx_kernel(idx, d_ref, *refs, n, nw):
    ws, (_, out, wv, sem) = refs[:nw], refs[nw:]
    core = idx[n]

    def fetch(i, act):
        for a, (v, flip) in enumerate(((ws[0], 0), (ws[1], 0), (ws[2], 1), (ws[3:5], 0),
                                       (ws[5], 0), (ws[6], 0), (ws[7], 1), (ws[8:10], 0))):
            @pl.when(idx[i] == a)
            def _():
                for e in range(2):
                    src = v[e] if isinstance(v, tuple) else v.at[e]
                    half = core if e == flip else 1 - core
                    pltpu.make_async_copy(src, wv.at[i, half], sem.at[i, e]).start()

    for i in range(n):
        fetch(i, None)
    d = jnp.concatenate([d_ref[0], d_ref[1], d_ref[2]], axis=1)
    for i in range(n):
        for e in range(2):
            pltpu.make_async_copy(ws[3], wv.at[i, e], sem.at[i, e]).wait()
        t = nt(d, wv[i].reshape(2 * DB, CW)).astype(BF)
        out[0, i] = t[:HALF]
        out[1, i] = t[HALF:]


def grad_rows(index, core, dqkv, ws, after):
    n = index.shape[0]
    hbm = pl.BlockSpec(memory_space=pl.ANY)
    vmem = pl.BlockSpec(memory_space=pltpu.VMEM)
    return pl.pallas_call(
        functools.partial(gx_kernel, n=n, nw=len(ws)),
        in_specs=[pl.BlockSpec(memory_space=pltpu.SMEM), vmem] + [hbm] * (len(ws) + 1),
        out_specs=vmem,
        out_shape=jax.ShapeDtypeStruct((2, n, HALF, 2 * DB), BF),
        scratch_shapes=[pltpu.VMEM((n, 2, DB, CW), BF), pltpu.SemaphoreType.DMA((n, 2))],
        compiler_params=pltpu.CompilerParams(vmem_limit_bytes=48 << 20),
        cost_estimate=pl.CostEstimate(flops=2 * n * ROWS * 768 * CW, bytes_accessed=n * 3 << 20, transcendentals=0),
        name="grad_rows",
    )(jnp.concatenate([index, core.reshape(1)]), dqkv, *ws, after)


def gw_kernel(idx, n1, n2, d1, d2, _, out, dcat):
    @pl.when(pl.program_id(0) == 0)
    def _():
        for j in range(3):
            dcat[pl.ds(0, ROWS), pl.ds(j * DB, DB)] = d1[j]
            dcat[pl.ds(ROWS, ROWS), pl.ds(j * DB, DB)] = d2[j]

    nc = jnp.concatenate([n1[0, :ROWS, :], n2[0, :ROWS, :]], axis=0)
    t = tn(nc, dcat[...]).astype(BF)
    out[0, 0] = t[:DB // 2]
    out[1, 0] = t[DB // 2:]


def grad_weights(index, normed, other, dqkv, dother, after):
    n = index.shape[0]
    spec = pltpu.PrefetchScalarGridSpec(
        num_scalar_prefetch=1,
        grid=(n,),
        in_specs=[
            pl.BlockSpec((1, EXT, DB), lambda i, s: (s[i], 0, 0)),
            pl.BlockSpec((1, EXT, DB), lambda i, s: (s[i], 0, 0)),
            pl.BlockSpec((3, ROWS, DB), lambda i, s: (0, 0, 0)),
            pl.BlockSpec((3, ROWS, DB), lambda i, s: (0, 0, 0)),
            pl.BlockSpec(memory_space=pl.ANY),
        ],
        out_specs=pl.BlockSpec((2, 1, DB // 2, CW), lambda i, s: (0, i, 0, 0)),
        scratch_shapes=[pltpu.VMEM((2 * ROWS, CW), BF)],
    )
    return pl.pallas_call(
        gw_kernel,
        grid_spec=spec,
        out_shape=jax.ShapeDtypeStruct((2, n, DB // 2, CW), BF),
        compiler_params=pltpu.CompilerParams(vmem_limit_bytes=48 << 20),
        cost_estimate=pl.CostEstimate(flops=4 * n * ROWS * DB * CW, bytes_accessed=n * 3 << 20, transcendentals=0),
        name="grad_weights",
    )(index, normed, other, dqkv, dother, after)


def add(a, b):
    return (a.astype(F32) + b.astype(F32)).astype(BF)


def ivec(*v):
    return jnp.stack([jnp.asarray(e, jnp.int32) for e in v])


def local(patches, gain, w_qkv, counts, grad_out):
    si, mi = lax.axis_index("seq"), lax.axis_index("mp")
    core, x, zh = si % 2, (si // 2) % 4, si // 8
    y, zl = mi // 2, mi % 2
    mw = lambda dx, dz: jnp.where(dz == 0, zh, 1 - zh) * 4 + (x + dx) % 4
    mx = lambda dy, dz: ((y + dy) % 4) * 2 + jnp.where(dz == 0, zl, 1 - zl)
    is0 = core == 0

    tie = lambda v, *after: lax.optimization_barrier((v, *after))[0]

    g_hi = gain.astype(BF)
    g_mid = (gain - g_hi.astype(F32)).astype(BF)
    g_lo = (gain - g_hi.astype(F32) - g_mid.astype(F32)).astype(BF)
    p0 = jnp.concatenate([patches, jnp.stack([g_hi, g_mid, g_lo]), jnp.zeros((13, 768), BF)])
    p_m = mpp(p0, YP)
    p_p = mpp(p0, YM)
    pz = mpp(p0, ZLO)
    pz_m = mpp(pz, YP)
    pz_p = mpp(pz, YM)
    f_m = mpp(jnp.stack([p_m[:HALF], pz_m[:HALF]]), YP)
    f_p = mpp(jnp.stack([p_p[HALF:], pz_p[HALF:]]), YM)

    w_own = w_qkv.reshape(DB, CW)
    pair = jnp.stack([w_own, sp(w_own, CORE)])
    ra = sp(pair, XSPLIT)
    wz = sp(tie(w_own, pz), ZHI)
    pair_z = jnp.stack([wz, sp(wz, CORE)])
    rc1 = sp(ra[0], XSPLIT)
    ea = sp(ra, CORE)
    rb = sp(pair_z, XSPLIT)
    ec1 = sp(rc1, CORE)
    rc2 = sp(rb[0], XSPLIT)
    eb = sp(rb, CORE)
    ec2 = sp(rc2, CORE)

    pf = patches.astype(F32)
    st = stats(0, None, [p0, pz, p_m, p_p])
    st = stats(4, st, [pz_m, pz_p])
    st = stats(6, st, [f_m, f_p], last=True)
    mean, rstd = st[:, 0:1], st[:, 1:2]

    dr = jnp.where(is0, -1, 1)
    index = ivec(mx(0, 0), mx(0, 1), mx(-1, 0), mx(1, 0), mx(-1, 1), mx(1, 1), mx(2, 0), mx(2, 1),
                 mw(0, 0), mw(dr, 0), mw(-dr, 0), mw(2, 0), mw(0, 1), mw(dr, 1), mw(-dr, 1), mw(2, 1), core)
    acc, n_own, n_send, n_last = project(
        index, st, [p0, pz, p_m, p_p, pz_m, pz_p, f_m, f_p], [pair, ra, ea, rc1, ec1, pair_z, rb, eb])
    n_other = sp(n_send, CORE)
    heads_out, dqkv, mom = attend(
        jnp.concatenate([counts.reshape(4), core.reshape(1)]), acc, n_last, rc2, ec2, grad_out)
    d_other = sp(dqkv, CORE)

    ws = [pair, ra, ea, rc1, ec1, pair_z, rb, eb, rc2, ec2]

    def source(dy, dz):
        m = mx(dy, dz)
        dx = (m % 4 - x) % 4
        near = jnp.where((dx == 1) == is0, 2, 1)
        return jnp.where(dx == 0, 0, jnp.where(dx == 2, 3, near)) + jnp.where(m // 4 == zh, 0, 4)

    rows = lambda blocks, after: grad_rows(ivec(*(source(*b) for b in blocks)), core, dqkv, ws, after)
    cols = lambda blocks, after: grad_weights(ivec(*(mw(*b) for b in blocks)), n_own, n_other, dqkv, d_other, after)
    gx1 = rows([(2, 0), (2, 1)], dqkv)
    h_m = mpp(gx1[0], YP)
    h_p = mpp(gx1[1], YM)
    gw1 = cols([(2, 0), (2, 1)], gx1)
    v_m = sp(gw1[0], XP)
    v_p = sp(gw1[1], XM)
    gx2 = rows([(1, 1), (-1, 1)], gw1)
    gw2 = cols([(1, 1), (-1, 1)], gx2)
    gx3 = rows([(1, 0), (-1, 0)], gw2)
    gw3 = cols([(1, 0), (-1, 0)], gx3)
    gx4 = rows([(0, 1), (0, 0)], gw3)
    gw4 = cols([(0, 1), (0, 0)], gx4)

    def ring(g, lo_in, hi_in, send, up, down):
        to_up = jnp.stack([add(g[0, 0], lo_in), g[1, 0]])
        to_down = jnp.stack([g[0, 1], add(g[1, 1], hi_in)])
        return send(to_up, up), send(to_down, down)

    ya1, ya2 = ring(gx2, h_m[1], h_p[1], mpp, YP, YM)
    xa1, xa2 = ring(gw2, v_m[1], v_p[1], sp, XP, XM)
    yb1, yb2 = ring(gx3, h_m[0], h_p[0], mpp, YP, YM)
    xb1, xb2 = ring(gw3, v_m[0], v_p[0], sp, XP, XM)
    f = lambda v: v.astype(F32)
    y_out = (f(gx4[:, 0]) + f(ya1) + f(ya2)).astype(BF)
    yz = mpp(y_out, ZLO)
    x_out = (f(gw4[:, 0]) + f(xa1) + f(xa2)).astype(BF)
    xz = sp(x_out, ZHI)

    mom = jnp.concatenate([mom[:, 0], mom[:, 1]])
    for perm, after in ((ZLO, h_m), (YA, ya1), (YB, yb1)):
        mom = mom + mpp(tie(mom, after), perm)
    mom = mom / D

    gn = (f(gx4[:, 1]) + f(yb1) + f(yb2) + f(yz)).reshape(ROWS, 768)
    xhat = (pf - mean) * rstd
    gg = jnp.sum(gn * xhat, axis=0)
    for perm in (CORE, XA, XB, ZHI):
        gg = gg + sp(gg, perm)
    grad_p = ((gn * gain[None, :] - mom[:ROWS, None] - xhat * mom[ROWS:, None]) * rstd).astype(BF)
    gw = (f(gw4[:, 1]) + f(xb1) + f(xb2) + f(xz)).reshape(DB, 3, DB)
    return heads_out, grad_p, gg, gw


def solution(mesh):
    placed = (P("seq", "mp"), P("mp"), P("seq", None, "mp"), P("seq", None), P("seq", "mp"))
    return jax.shard_map(
        local,
        mesh=mesh,
        in_specs=placed,
        out_specs=(P("seq", "mp"), P("seq", "mp"), P("mp"), P("seq", None, "mp")),
        check_vma=False,
    )
```

```python
import functools

import jax
import jax.numpy as jnp
from jax import lax
from jax.experimental import pallas as pl
from jax.experimental.pallas import tpu as pltpu
from jax.sharding import PartitionSpec as P

HD = 128
NH = 3
ROWS = 576
HALF = ROWS // 2
EXT = ROWS + 16
DB = 384
HB = DB // 2
D = 6144
CW = 3 * DB
EPS = 1e-06
BF = jnp.bfloat16
F32 = jnp.float32
HBM = pl.BlockSpec(memory_space=pltpu.HBM)
VMEM = pl.BlockSpec(memory_space=pltpu.VMEM)
SMEM = pl.BlockSpec(memory_space=pltpu.SMEM)


def seq_perm(f):
    out = []
    for i in range(16):
        zh, x, c = f(i // 8, (i // 2) % 4, i % 2)
        out.append((i, (zh * 4 + x % 4) * 2 + c))
    return out


def mp_perm(f):
    out = []
    for i in range(8):
        y, zl = f(i // 2, i % 2)
        out.append((i, (y % 4) * 2 + zl))
    return out


CORE = seq_perm(lambda zh, x, c: (zh, x, 1 - c))
ZHI = seq_perm(lambda zh, x, c: (1 - zh, x, c))
XP = seq_perm(lambda zh, x, c: (zh, x + 1, c))
XM = seq_perm(lambda zh, x, c: (zh, x - 1, c))
XA = seq_perm(lambda zh, x, c: (zh, x ^ 1, c))
XB = seq_perm(lambda zh, x, c: (zh, x ^ 3, c))
ZLO = mp_perm(lambda y, zl: (y, 1 - zl))
YP = mp_perm(lambda y, zl: (y + 1, zl))
YM = mp_perm(lambda y, zl: (y - 1, zl))
YA = mp_perm(lambda y, zl: (y ^ 1, zl))
YB = mp_perm(lambda y, zl: (y ^ 3, zl))


def sp(v, perm):
    return lax.ppermute(v, "seq", perm)


def mpp(v, perm):
    return lax.ppermute(v, "mp", perm)


def nt(a, b):
    return lax.dot_general(a, b, (((1,), (1,)), ((), ())), preferred_element_type=F32)


def tn(a, b):
    return lax.dot_general(a, b, (((0,), (0,)), ((), ())), preferred_element_type=F32)


def nn(a, b):
    return lax.dot_general(a, b, (((1,), (0,)), ((), ())), preferred_element_type=F32)


def sds(shape, dtype=BF):
    return jax.ShapeDtypeStruct(shape, dtype)


def params(mib=48):
    return pltpu.CompilerParams(vmem_limit_bytes=mib << 20)


def cost(flops, nbytes, exps=0):
    return pl.CostEstimate(flops=int(flops), bytes_accessed=int(nbytes), transcendentals=exps)


def move(inputs, outs, plan, deps, name):
    def kernel(*refs):
        ins, dst, sem = refs[:len(inputs)], refs[len(inputs) + len(deps):-1], refs[-1]
        copies = [
            pltpu.make_async_copy(ins[i].at[si] if si else ins[i], dst[o].at[so] if so else dst[o], sem.at[k])
            for k, (i, si, o, so) in enumerate(plan)
        ]
        for c in copies:
            c.start()
        for c in copies:
            c.wait()

    return pl.pallas_call(
        kernel,
        in_specs=[HBM] * (len(inputs) + len(deps)),
        out_specs=[HBM] * len(outs),
        out_shape=[sds(s) for s in outs],
        scratch_shapes=[pltpu.SemaphoreType.DMA((len(plan),))],
        compiler_params=params(),
        cost_estimate=cost(0, 4 << 20),
        name=name,
    )(*inputs, *deps)


def extend_kernel(p, gain, out):
    out[pl.ds(0, ROWS), :] = p[...]
    g = gain[...]
    hi = g.astype(BF).astype(F32)
    mid = (g - hi).astype(BF).astype(F32)
    row = lax.broadcasted_iota(jnp.int32, (16, 2 * DB), 0)
    tail = jnp.where(row == 0, hi, jnp.where(row == 1, mid, jnp.where(row == 2, g - hi - mid, 0.0)))
    out[pl.ds(ROWS, 16), :] = tail.astype(BF)


def extend(patches, gain):
    return pl.pallas_call(
        extend_kernel,
        out_shape=sds((EXT, 2 * DB)),
        compiler_params=params(),
        cost_estimate=cost(0, 2 << 20),
        name="extend",
    )(patches, gain.reshape(1, 2 * DB))


def stats_kernel(*refs, before, last, nraw):
    refs, out = refs[:-1], refs[-1]
    if before:
        mean, m2 = refs[0][:, 0:1], refs[0][:, 1:2]
        refs = refs[1:]
    raws = refs[:nraw]
    if len(raws[0].shape) == 3:
        lo, hi = raws
        chunks = [jnp.concatenate([lo[j], hi[j, :HALF, :]], axis=0) for j in range(2)]
    else:
        chunks = [r[:ROWS, :] for r in raws]
    n = before
    for c in chunks:
        v = c.astype(F32)
        cm = jnp.sum(v, axis=1, keepdims=True) * (1.0 / 768)
        dv = v - cm
        c2 = jnp.sum(dv * dv, axis=1, keepdims=True)
        if n == 0:
            mean, m2 = cm, c2
        else:
            delta = cm - mean
            mean = mean + delta * (1.0 / (n + 1))
            m2 = m2 + c2 + delta * delta * (768.0 * n / (n + 1))
        n += 1
    if last:
        m2 = lax.rsqrt(m2 * (1.0 / D) + EPS)
    lane = lax.broadcasted_iota(jnp.int32, (ROWS, 128), 1)
    out[...] = jnp.where(lane == 0, mean, jnp.where(lane == 1, m2, 0.0))


def stats(before, state, raws, deps=(), last=False):
    args = ([state] if before else []) + list(raws)
    return pl.pallas_call(
        functools.partial(stats_kernel, before=before, last=last, nraw=len(raws)),
        in_specs=[VMEM] * len(args) + [HBM] * len(deps),
        out_shape=sds((ROWS, 128), F32),
        compiler_params=params(),
        cost_estimate=cost(0, 4 << 20),
        name="row_stats",
    )(*args, *deps)


def w_copies(shard, buf, half, sem):
    rows = pl.ds(pl.multiple_of(half * DB, 128), DB)
    return [pltpu.make_async_copy(shard.at[j], buf.at[rows, pl.ds(j * DB, DB)], sem.at[j]) for j in range(3)]


def project_kernel(idx, st, r0, r1, r2, r3, r4, r5, fm, fp, w4, w4o, _,
                   acc, n_own, n_send, n_far, raw, nrm, wv, sr, sw, so):
    core = idx[16]
    copies = []
    for j, r in enumerate((r0, r1, r2, r3, r4, r5)):
        copies.append(pltpu.make_async_copy(r, raw.at[idx[j]], sr.at[j]))
    for j in range(2):
        copies.append(pltpu.make_async_copy(fm.at[j], raw.at[idx[6 + j], pl.ds(0, HALF)], sr.at[6 + j]))
        copies.append(pltpu.make_async_copy(fp.at[j], raw.at[idx[6 + j], pl.ds(HALF, EXT - HALF)], sr.at[8 + j]))
    for c in copies:
        c.start()
    wc = [w_copies(w4.at[k], wv.at[k], core, sw.at[k, 0]) + w_copies(w4o.at[k], wv.at[k], 1 - core, sw.at[k, 1])
          for k in range(4)]
    for k in range(4):
        for c in wc[k]:
            c.start()
    for c in copies:
        c.wait()
    mean, rstd = st[:, 0:1], st[:, 1:2]
    out = []
    own = pl.ds(pl.multiple_of(core * DB, 128), DB)
    oth = pl.ds(pl.multiple_of((1 - core) * DB, 128), DB)

    def norm(k):
        m = idx[8 + k]
        v = raw[m]
        tail = v[ROWS:]
        t = tail.astype(F32)
        g = t[0:1] + t[1:2] + t[2:3]
        nrm[k, pl.ds(0, ROWS), :] = ((v[:ROWS].astype(F32) - mean) * rstd * g).astype(BF)
        nrm[k, pl.ds(ROWS, 16), :] = tail
        mine = [pltpu.make_async_copy(nrm.at[k, :, own], n_own.at[m], so.at[k, 0]),
                pltpu.make_async_copy(nrm.at[k, :, oth], n_send.at[m], so.at[k, 1])]
        if k >= 4:
            mine.append(pltpu.make_async_copy(nrm.at[k], n_far.at[k - 4], so.at[k, 2]))
        for c in mine:
            c.start()
        out.extend(mine)

    norm(0)
    for k in range(4):
        for c in wc[k]:
            c.wait()
        t = nn(nrm[k], wv[k])
        if k == 0:
            acc[...] = t
        else:
            acc[...] += t
        norm(2 * k + 1)
        if k < 3:
            norm(2 * k + 2)
    for c in out:
        c.wait()


def project(index, st, raws, w4, w4o, after):
    return pl.pallas_call(
        project_kernel,
        in_specs=[SMEM, VMEM] + [HBM] * (len(raws) + 3),
        out_specs=[VMEM, HBM, HBM, HBM],
        out_shape=[sds((EXT, CW), F32), sds((8, EXT, DB)), sds((8, EXT, DB)), sds((4, EXT, 2 * DB))],
        scratch_shapes=[
            pltpu.VMEM((8, EXT, 2 * DB), BF),
            pltpu.VMEM((8, EXT, 2 * DB), BF),
            pltpu.VMEM((4, 2 * DB, CW), BF),
            pltpu.SemaphoreType.DMA((10,)),
            pltpu.SemaphoreType.DMA((4, 2, 3)),
            pltpu.SemaphoreType.DMA((8, 3)),
        ],
        compiler_params=params(52),
        cost_estimate=cost(EXT * D * CW, 30 << 20),
        name="project",
    )(index, st, *raws, w4, w4o, after)


def project_far_kernel(idx, acc, n_far, w3, w3o, out, nv, wv, sem):
    core = idx[0]
    nc = [pltpu.make_async_copy(n_far.at[k], nv.at[k], sem.at[k, 2, 0]) for k in range(3)]
    wc = [w_copies(w3.at[k], wv.at[k], core, sem.at[k, 0]) + w_copies(w3o.at[k], wv.at[k], 1 - core, sem.at[k, 1])
          for k in range(3)]
    for k in range(3):
        for c in [nc[k]] + wc[k]:
            c.start()
    for k in range(3):
        for c in [nc[k]] + wc[k]:
            c.wait()
        t = nn(nv[k], wv[k])
        if k == 0:
            out[...] = acc[...] + t
        else:
            out[...] += t


def project_far(core, acc, n_far, w3, w3o):
    return pl.pallas_call(
        project_far_kernel,
        in_specs=[SMEM, VMEM, HBM, HBM, HBM],
        out_specs=VMEM,
        out_shape=sds((EXT, CW), F32),
        scratch_shapes=[
            pltpu.VMEM((3, EXT, 2 * DB), BF),
            pltpu.VMEM((3, 2 * DB, CW), BF),
            pltpu.SemaphoreType.DMA((3, 3, 3)),
        ],
        compiler_params=params(),
        cost_estimate=cost(EXT * D * CW * 3 / 4, 12 << 20),
        name="project_far",
    )(core.reshape(1), acc, n_far, w3, w3o)


def split(v):
    hi = v.astype(BF)
    return hi, (v - hi.astype(F32)).astype(BF)


def attn_kernel(counts, acc, n_far, w1, w2, g_ref, _, out_ref, dqkv_ref, mom_ref, qkv):
    h = pl.program_id(0)

    @pl.when(h == 0)
    def _():
        core = counts[4]
        own = pl.ds(pl.multiple_of(core * DB, 128), DB)
        oth = pl.ds(pl.multiple_of((1 - core) * DB, 128), DB)
        for j in range(3):
            cols = pl.ds(j * DB, DB)
            qkv[:, cols] = acc[:, cols] + nn(n_far[0, :, own], w1[j]) + nn(n_far[0, :, oth], w2[j])

    col = lambda j: pl.ds(pl.multiple_of((j * NH + h) * HD, 128), HD)
    q_ref, k_ref, v_ref = (qkv.at[:, col(j)] for j in range(3))
    e0 = counts[0]
    e1 = e0 + counts[1]
    e2 = e1 + counts[2]
    rid = lax.broadcasted_iota(jnp.int32, (ROWS, 1), 0)
    cid = lax.broadcasted_iota(jnp.int32, (1, ROWS), 1)
    img = lambda p: (p >= e0).astype(jnp.int32) + (p >= e1).astype(jnp.int32) + (p >= e2).astype(jnp.int32)
    same = img(rid) == img(cid)
    scale = HD ** (-0.5)
    q = q_ref[:ROWS, :] * scale
    k = k_ref[:ROWS, :]
    v = v_ref[:ROWS, :]
    qh, ql = split(q)
    kh, kl = split(k)
    vb = v.astype(BF)
    g = g_ref[...]
    s = nt(jnp.concatenate([qh, qh], 1), jnp.concatenate([kh, kl], 1)) + nt(ql, kh)
    s = jnp.where(same, s, -1e30)
    p = jnp.exp(s - jnp.max(s, axis=1, keepdims=True))
    p = p / jnp.sum(p, axis=1, keepdims=True)
    pb = p.astype(BF)
    out_ref[...] = nn(pb, vb).astype(BF)
    dp = nt(g, vb)
    dv = tn(pb, g)
    ds = p * (dp - jnp.sum(dp * p, axis=1, keepdims=True))
    dsb = ds.astype(BF)
    dq = (nn(dsb, kh) * scale).astype(BF)
    dk = tn(dsb, qh).astype(BF)
    dv = dv.astype(BF)
    dqkv_ref[0] = dq
    dqkv_ref[1] = dk
    dqkv_ref[2] = dv
    m1 = jnp.zeros((ROWS, 1), F32)
    m2 = jnp.zeros((ROWS, 1), F32)
    for d, r in ((dq, q_ref), (dk, k_ref), (dv, v_ref)):
        df = d.astype(F32)
        u = r[ROWS:ROWS + 1, :] + r[ROWS + 1:ROWS + 2, :] + r[ROWS + 2:ROWS + 3, :]
        m1 = m1 + jnp.sum(df * u, axis=1, keepdims=True)
        m2 = m2 + jnp.sum(df * r[:ROWS, :], axis=1, keepdims=True)
    lane = lax.broadcasted_iota(jnp.int32, (ROWS, 128), 1)
    mom = jnp.where(lane == 0, m1, jnp.where(lane == 1, m2, 0.0))

    @pl.when(h == 0)
    def _():
        mom_ref[...] = mom

    @pl.when(h > 0)
    def _():
        mom_ref[...] += mom


def attend(counts, acc, n_far, w1, w2, grad_out, after):
    whole = lambda shape: pl.BlockSpec(shape, lambda h: (0,) * len(shape))
    return pl.pallas_call(
        attn_kernel,
        grid=(NH,),
        in_specs=[
            SMEM,
            whole((EXT, CW)),
            pl.BlockSpec((1, EXT, 2 * DB), lambda h: (3, 0, 0)),
            whole((3, DB, DB)),
            whole((3, DB, DB)),
            pl.BlockSpec((ROWS, HD), lambda h: (0, h)),
            HBM,
        ],
        out_specs=[
            pl.BlockSpec((ROWS, HD), lambda h: (0, h)),
            pl.BlockSpec((3, ROWS, HD), lambda h: (0, 0, h)),
            pl.BlockSpec((ROWS, 128), lambda h: (0, 0)),
        ],
        out_shape=[sds((ROWS, DB)), sds((3, ROWS, DB)), sds((ROWS, 128), F32)],
        scratch_shapes=[pltpu.VMEM((EXT, CW), F32)],
        compiler_params=params(),
        cost_estimate=cost(7 * 2 * NH * ROWS * ROWS * HD * 2, 6 << 20, NH * ROWS * ROWS),
        name="attention",
    )(counts, acc, n_far, w1, w2, grad_out, after)


def grads_kernel(idx, d1, d2, w4, w4o, w3, w3o, w1, w1o, n1, n2, *refs, ny, nx, ndeps, ysplit, xsplit):
    outs = list(refs[ndeps:-7])
    wv, nv, dcat, oy, ox, si, so = refs[-7:]
    core = idx[0]

    def start(shard, i, half, e):
        for c in w_copies(shard, wv.at[i], half, si.at[i, e]):
            c.start()

    for i in range(ny):
        a = idx[1 + i]

        @pl.when(a < 4)
        def _():
            k = jnp.minimum(a, 3)
            start(w4.at[k], i, core, 0)
            start(w4o.at[k], i, 1 - core, 1)

        @pl.when(jnp.logical_and(a >= 4, a < 7))
        def _():
            k = jnp.clip(a - 4, 0, 2)
            start(w3.at[k], i, core, 0)
            start(w3o.at[k], i, 1 - core, 1)

        @pl.when(a == 7)
        def _():
            start(w1, i, core, 0)
            start(w1o, i, 1 - core, 1)

    ncs = []
    for i in range(nx):
        m = idx[1 + ny + i]
        ncs.append([pltpu.make_async_copy(n1.at[m, pl.ds(0, ROWS)], nv.at[i, pl.ds(0, ROWS)], si.at[ny + i, 0, 0]),
                    pltpu.make_async_copy(n2.at[m, pl.ds(0, ROWS)], nv.at[i, pl.ds(ROWS, ROWS)], si.at[ny + i, 1, 0])])
        for c in ncs[-1]:
            c.start()
    for j in range(3):
        dcat[pl.ds(0, ROWS), pl.ds(j * DB, DB)] = d1[j]
        if nx:
            dcat[pl.ds(ROWS, ROWS), pl.ds(j * DB, DB)] = d2[j]
    pending = []

    def put(src, dst, sem):
        c = pltpu.make_async_copy(src, dst, sem)
        c.start()
        pending.append(c)

    for i in range(ny):
        for e in range(2):
            for c in w_copies(w1, wv.at[i], e, si.at[i, e]):
                c.wait()
        oy[i] = nt(dcat[pl.ds(0, ROWS), :], wv[i]).astype(BF)
        if i in ysplit:
            put(oy.at[i, pl.ds(0, HALF)], outs.pop(0), so.at[i, 0])
            put(oy.at[i, pl.ds(HALF, HALF)], outs.pop(0), so.at[i, 1])
        else:
            put(oy.at[i], outs.pop(0), so.at[i, 0])
    for i in range(nx):
        for c in ncs[i]:
            c.wait()
        t = tn(nv[i], dcat[...]).astype(BF)
        for j in range(3):
            ox[i, j] = t[:, j * DB:(j + 1) * DB]
        if i in xsplit:
            put(ox.at[i, :, pl.ds(0, HB)], outs.pop(0), so.at[ny + i, 0])
            put(ox.at[i, :, pl.ds(HB, HB)], outs.pop(0), so.at[ny + i, 1])
        else:
            put(ox.at[i], outs.pop(0), so.at[ny + i, 0])
    for c in pending:
        c.wait()


def grads(core, ysrc, xsrc, dqkv, d_other, ws, normed, other, deps, ysplit=(), xsplit=()):
    ny, nx = len(ysrc), len(xsrc)
    shapes = []
    for i in range(ny):
        shapes += [(HALF, 2 * DB)] * 2 if i in ysplit else [(ROWS, 2 * DB)]
    for i in range(nx):
        shapes += [(3, HB, DB)] * 2 if i in xsplit else [(3, DB, DB)]
    deps = list(deps)
    return pl.pallas_call(
        functools.partial(grads_kernel, ny=ny, nx=nx, ndeps=len(deps), ysplit=ysplit, xsplit=xsplit),
        in_specs=[SMEM, VMEM, VMEM if nx else HBM] + [HBM] * (8 + len(deps)),
        out_specs=[HBM] * len(shapes),
        out_shape=[sds(s) for s in shapes],
        scratch_shapes=[
            pltpu.VMEM((max(ny, 1), 2 * DB, CW), BF),
            pltpu.VMEM((max(nx, 1), 2 * ROWS, DB), BF),
            pltpu.VMEM((2 * ROWS, CW), BF),
            pltpu.VMEM((max(ny, 1), ROWS, 2 * DB), BF),
            pltpu.VMEM((max(nx, 1), 3, DB, DB), BF),
            pltpu.SemaphoreType.DMA((ny + nx, 2, 3)),
            pltpu.SemaphoreType.DMA((ny + nx, 2)),
        ],
        compiler_params=params(),
        cost_estimate=cost(2 * (ny + nx) * ROWS * 768 * CW, (ny + nx) * 3 << 20),
        name="grads",
    )(ivec(core, *ysrc, *xsrc), dqkv, d_other, *ws, normed, other, *deps)


def add_kernel(yu, yd, xu, xd, hm, hp, vm, vp, *refs):
    for a, b, o in zip((yu, yd, xu, xd), (hm, hp, vm, vp), refs[-4:]):
        o[...] = (a[...].astype(F32) + b[...].astype(F32)).astype(BF)


def add_halves(blocks, arrived, deps):
    whole = lambda v: pl.BlockSpec(v.shape, lambda i: (0,) * v.ndim)
    halves = [
        pl.BlockSpec((HALF, 2 * DB), lambda i: (0, 0)),
        pl.BlockSpec((HALF, 2 * DB), lambda i: (1, 0)),
        pl.BlockSpec((3, HB, DB), lambda i: (0, 0, 0)),
        pl.BlockSpec((3, HB, DB), lambda i: (0, 1, 0)),
    ]
    return pl.pallas_call(
        add_kernel,
        grid=(1,),
        in_specs=halves + [whole(v) for v in arrived] + [HBM] * len(deps),
        out_specs=halves,
        out_shape=[sds(v.shape) for v in blocks],
        input_output_aliases={0: 0, 1: 1, 2: 2, 3: 3},
        compiler_params=params(),
        cost_estimate=cost(0, 6 << 20),
        name="add_halves",
    )(*blocks, *arrived, *deps)


def ivec(*v):
    return jnp.stack([jnp.asarray(e, jnp.int32) for e in v])


def local(patches, gain, w_qkv, counts, grad_out):
    si, mi = lax.axis_index("seq"), lax.axis_index("mp")
    core, x, zh = si % 2, (si // 2) % 4, si // 8
    y, zl = mi // 2, mi % 2
    mw = lambda dx, dz: jnp.where(dz == 0, zh, 1 - zh) * 4 + (x + dx) % 4
    mx = lambda dy, dz: ((y + dy) % 4) * 2 + jnp.where(dz == 0, zl, 1 - zl)
    rows, wshape = (EXT, 2 * DB), (3, DB, DB)
    lo, hi = (slice(None), pl.ds(0, HB)), (slice(None), pl.ds(HB, HB))
    first, rest = (pl.ds(0, HALF),), (pl.ds(HALF, EXT - HALF),)

    p0 = extend(patches, gain)
    w = jnp.transpose(w_qkv, (1, 0, 2))
    p_m, p_p, pz = mpp(p0, YP), mpp(p0, YM), mpp(p0, ZLO)
    w_m, w_p = sp(w, XP), sp(w, XM)
    pz1, w1, w_lo, w_hi = move(
        [pz, w, w_m, w_p], [rows, wshape, (3, HB, DB), (3, HB, DB)],
        [(0, None, 0, None), (1, None, 1, None), (2, lo, 2, None), (3, hi, 3, None)], [p_m, p_p], "stage1")
    pz_m, pz_p = mpp(pz1, YP), mpp(pz1, YM)
    wf_m, wf_p = sp(w_lo, XP), sp(w_hi, XM)
    wz = sp(w1, ZHI)
    st = stats(0, None, [p0, pz, p_m, p_p], [pz1])
    fu, fd, wz1, w4 = move(
        [p_m, p_p, pz_m, pz_p, w1, w_m, w_p, wf_m, wf_p, wz],
        [(2, HALF, 2 * DB), (2, EXT - HALF, 2 * DB), wshape, (4,) + wshape],
        [(0, first, 0, (0,)), (2, first, 0, (1,)), (1, rest, 1, (0,)), (3, rest, 1, (1,)), (9, None, 2, None),
         (4, None, 3, (0,)), (5, None, 3, (1,)), (6, None, 3, (2,)), (7, None, 3, (3,) + lo), (8, None, 3, (3,) + hi)],
        [st], "stage2")
    f_m, f_p = mpp(fu, YP), mpp(fd, YM)
    wz_m, wz_p = sp(wz1, XP), sp(wz1, XM)
    w4o = sp(w4, CORE)
    st = stats(4, st, [pz_m, pz_p], [fu])
    wz_lo, wz_hi, w3 = move(
        [wz1, wz_m, wz_p], [(3, HB, DB), (3, HB, DB), (3,) + wshape],
        [(1, lo, 0, None), (2, hi, 1, None), (0, None, 2, (0,)), (1, None, 2, (1,)), (2, None, 2, (2,))],
        [f_m, f_p, w4o, st], "stage3")
    wzf_m, wzf_p = sp(wz_lo, XP), sp(wz_hi, XM)
    w3o = sp(w3, CORE)
    st = stats(6, st, [f_m, f_p], last=True)
    mean, rstd = st[:, 0:1], st[:, 1:2]
    index = ivec(mx(0, 0), mx(0, 1), mx(-1, 0), mx(1, 0), mx(-1, 1), mx(1, 1), mx(2, 0), mx(2, 1),
                 mw(0, 0), mw(-1, 0), mw(1, 0), mw(2, 0), mw(0, 1), mw(-1, 1), mw(1, 1), mw(2, 1), core)
    acc, n_own, n_send, n_far = project(index, st, [p0, pz, p_m, p_p, pz_m, pz_p, f_m, f_p], w4, w4o, wz_lo)
    (wl,) = move([wzf_m, wzf_p], [wshape], [(0, None, 0, lo), (1, None, 0, hi)], [w3o, acc], "stage4")
    wlo = sp(wl, CORE)
    n_other = sp(n_send, CORE)
    acc = project_far(core, acc, n_far, w3, w3o)
    heads_out, dqkv, mom = attend(
        jnp.concatenate([counts.reshape(4), core.reshape(1)]), acc, n_far, wl, wlo, grad_out, wl)

    d_other = sp(dqkv, CORE)
    mom = jnp.concatenate([mom[:, 0], mom[:, 1]])
    mom1 = mom + mpp(mom, ZLO)
    ws = [w4, w4o, w3, w3o, wl, wlo]

    def source(dy, dz):
        m = mx(dy, dz)
        dx = (m % 4 - x) % 4
        return jnp.where(dx == 3, 1, jnp.where(dx == 1, 2, jnp.where(dx == 2, 3, 0))) + jnp.where(m // 4 == zh, 0, 4)

    def blocks(yb, xb, deps, **kw):
        return grads(core, [source(*b) for b in yb], [mw(*b) for b in xb], dqkv, d_other, ws, n_own, n_other, deps, **kw)

    y2p_lo, y2p_hi = blocks([(2, 1)], [], [], ysplit=(0,))
    x2p_lo, x2p_hi = blocks([], [(2, 1)], [y2p_lo, mom1], xsplit=(0,))
    h_m, h_p = mpp(y2p_lo, YP), mpp(y2p_hi, YM)
    v_m, v_p = sp(x2p_lo, XP), sp(x2p_hi, XM)
    mom2 = mom1 + mpp(mom1, YA)
    near = blocks([(1, 1), (-1, 1)], [(1, 1), (-1, 1)], [x2p_lo])
    yu, yd, xu, xd = add_halves(near, [h_m, h_p, v_m, v_p], [mom2])
    ya1, ya2, xa1, xa2 = mpp(yu, YP), mpp(yd, YM), sp(xu, XP), sp(xd, XM)
    mom3 = mom2 + mpp(mom2, YB)
    y0p, y2_lo, y2_hi, y1u, y1d, x0p, x2_lo, x2_hi, x1u, x1d = blocks(
        [(0, 1), (2, 0), (1, 0), (-1, 0)], [(0, 1), (2, 0), (1, 0), (-1, 0)], [yu], ysplit=(1,), xsplit=(1,))
    f = lambda v: v.astype(F32)
    y_out = (f(y0p) + f(ya1) + f(ya2)).astype(BF)
    x_out = (f(x0p) + f(xa1) + f(xa2)).astype(BF)
    yz = mpp(y_out, ZLO)
    h_m, h_p = mpp(y2_lo, YP), mpp(y2_hi, YM)
    v_m, v_p = sp(x2_lo, XP), sp(x2_hi, XM)
    y0, x0 = blocks([(0, 0)], [(0, 0)], [y_out])
    yu, yd, xu, xd = add_halves([y1u, y1d, x1u, x1d], [h_m, h_p, v_m, v_p], [yz, mom3, x_out, y0])
    yb1, yb2, xb1, xb2 = mpp(yu, YP), mpp(yd, YM), sp(xu, XP), sp(xd, XM)
    xz = sp(x_out, ZHI)

    mom = mom3 / D
    gn = f(y0) + f(yb1) + f(yb2) + f(yz)
    xhat = (f(patches) - mean) * rstd
    gg = jnp.sum(gn * xhat, axis=0)
    for perm in (CORE, XA, XB, ZHI):
        gg = gg + sp(gg, perm)
    grad_p = ((gn * gain[None, :] - mom[:ROWS, None] - xhat * mom[ROWS:, None]) * rstd).astype(BF)
    gw = jnp.transpose(f(x0) + f(xb1) + f(xb2) + f(xz), (1, 0, 2))
    return heads_out, grad_p, gg, gw


def solution(mesh):
    placed = (P("seq", "mp"), P("mp"), P("seq", None, "mp"), P("seq", None), P("seq", "mp"))
    return jax.shard_map(
        local,
        mesh=mesh,
        in_specs=placed,
        out_specs=(P("seq", "mp"), P("seq", "mp"), P("mp"), P("seq", None, "mp")),
        check_vma=False,
    )
```

```python
import functools

import jax
import jax.numpy as jnp
from jax import lax
from jax.experimental import pallas as pl
from jax.experimental.pallas import tpu as pltpu
from jax.sharding import PartitionSpec as P

HD = 128
NH = 3
ROWS = 576
HALF = ROWS // 2
EXT = ROWS + 16
DB = 384
HB = DB // 2
D = 6144
CW = 3 * DB
EPS = 1e-06
BF = jnp.bfloat16
F32 = jnp.float32
HBM = pl.BlockSpec(memory_space=pltpu.HBM)
VMEM = pl.BlockSpec(memory_space=pltpu.VMEM)
SMEM = pl.BlockSpec(memory_space=pltpu.SMEM)


def seq_perm(f):
    out = []
    for i in range(16):
        zh, x, c = f(i // 8, (i // 2) % 4, i % 2)
        out.append((i, (zh * 4 + x % 4) * 2 + c))
    return out


def mp_perm(f):
    out = []
    for i in range(8):
        y, zl = f(i // 2, i % 2)
        out.append((i, (y % 4) * 2 + zl))
    return out


CORE = seq_perm(lambda zh, x, c: (zh, x, 1 - c))
ZHI = seq_perm(lambda zh, x, c: (1 - zh, x, c))
XP = seq_perm(lambda zh, x, c: (zh, x + 1, c))
XM = seq_perm(lambda zh, x, c: (zh, x - 1, c))
XA = seq_perm(lambda zh, x, c: (zh, x ^ 1, c))
XB = seq_perm(lambda zh, x, c: (zh, x ^ 3, c))
ZLO = mp_perm(lambda y, zl: (y, 1 - zl))
YP = mp_perm(lambda y, zl: (y + 1, zl))
YM = mp_perm(lambda y, zl: (y - 1, zl))
YA = mp_perm(lambda y, zl: (y ^ 1, zl))
YB = mp_perm(lambda y, zl: (y ^ 3, zl))


def sp(v, perm):
    return lax.ppermute(v, "seq", perm)


def mpp(v, perm):
    return lax.ppermute(v, "mp", perm)


def nt(a, b):
    return lax.dot_general(a, b, (((1,), (1,)), ((), ())), preferred_element_type=F32)


def tn(a, b):
    return lax.dot_general(a, b, (((0,), (0,)), ((), ())), preferred_element_type=F32)


def nn(a, b):
    return lax.dot_general(a, b, (((1,), (0,)), ((), ())), preferred_element_type=F32)


def sds(shape, dtype=BF):
    return jax.ShapeDtypeStruct(shape, dtype)


def params(mib=63):
    return pltpu.CompilerParams(vmem_limit_bytes=mib << 20)


def cost(flops, nbytes, exps=0):
    return pl.CostEstimate(flops=int(flops), bytes_accessed=int(nbytes), transcendentals=exps)


def sliced(shape, index):
    if not index:
        return shape
    out = []
    for n, i in zip(shape, index):
        if not isinstance(i, int):
            out.append(n if isinstance(i, slice) else i.size)
    return tuple(out) + tuple(shape[len(index):])


def move(inputs, outs, plan, deps, name):
    def kernel(*refs):
        ins = refs[:len(inputs)]
        dst = refs[len(inputs) + len(deps):][:len(outs)]
        *bufs, sem = refs[len(inputs) + len(deps) + len(outs):]
        get = [pltpu.make_async_copy(ins[i].at[si] if si else ins[i], bufs[k], sem.at[k, 0])
               for k, (i, si, o, so) in enumerate(plan)]
        put = [pltpu.make_async_copy(bufs[k], dst[o].at[so] if so else dst[o], sem.at[k, 1])
               for k, (i, si, o, so) in enumerate(plan)]
        for c in get:
            c.start()
        for g, p in zip(get, put):
            g.wait()
            p.start()
        for p in put:
            p.wait()

    return pl.pallas_call(
        kernel,
        in_specs=[HBM] * (len(inputs) + len(deps)),
        out_specs=[HBM] * len(outs),
        out_shape=[sds(s) for s in outs],
        scratch_shapes=[pltpu.VMEM(sliced(inputs[i].shape, si), BF) for i, si, o, so in plan]
        + [pltpu.SemaphoreType.DMA((len(plan), 2))],
        compiler_params=params(),
        cost_estimate=cost(0, 4 << 20),
        name=name,
    )(*inputs, *deps)


def extend_kernel(p, gain, out):
    out[pl.ds(0, ROWS), :] = p[...]
    g = gain[...]
    hi = g.astype(BF).astype(F32)
    mid = (g - hi).astype(BF).astype(F32)
    row = lax.broadcasted_iota(jnp.int32, (16, 2 * DB), 0)
    tail = jnp.where(row == 0, hi, jnp.where(row == 1, mid, jnp.where(row == 2, g - hi - mid, 0.0)))
    out[pl.ds(ROWS, 16), :] = tail.astype(BF)


def extend(patches, gain):
    return pl.pallas_call(
        extend_kernel,
        out_shape=sds((EXT, 2 * DB)),
        compiler_params=params(),
        cost_estimate=cost(0, 2 << 20),
        name="extend",
    )(patches, gain.reshape(1, 2 * DB))


def merge(n, mean, m2, chunk):
    v = chunk.astype(F32)
    cm = jnp.sum(v, axis=1, keepdims=True) * (1.0 / 768)
    dv = v - cm
    c2 = jnp.sum(dv * dv, axis=1, keepdims=True)
    if n == 0:
        return cm, c2
    delta = cm - mean
    return mean + delta * (1.0 / (n + 1)), m2 + c2 + delta * delta * (768.0 * n / (n + 1))


def two_lanes(a, b):
    lane = lax.broadcasted_iota(jnp.int32, (ROWS, 128), 1)
    return jnp.where(lane == 0, a, jnp.where(lane == 1, b, 0.0))


def stats_kernel(*refs, before, nraw, ndeps):
    raws, refs = refs[:nraw], refs[nraw:]
    mean = m2 = None
    if before:
        state, refs = refs[0], refs[1:]
        mean, m2 = state[:, 0:1], state[:, 1:2]
    out, buf, sem = refs[ndeps:]
    copies = [pltpu.make_async_copy(r, buf.at[j], sem.at[j]) for j, r in enumerate(raws)]
    for c in copies:
        c.start()
    for j, c in enumerate(copies):
        c.wait()
        mean, m2 = merge(before + j, mean, m2, buf[j, pl.ds(0, ROWS), :])
    out[...] = two_lanes(mean, m2)


def stats(before, state, raws, deps):
    n = len(raws)
    return pl.pallas_call(
        functools.partial(stats_kernel, before=before, nraw=n, ndeps=len(deps)),
        in_specs=[HBM] * n + [VMEM] * (before > 0) + [HBM] * len(deps),
        out_specs=VMEM,
        out_shape=sds((ROWS, 128), F32),
        scratch_shapes=[pltpu.VMEM((n, EXT, 2 * DB), BF), pltpu.SemaphoreType.DMA((n,))],
        compiler_params=params(),
        cost_estimate=cost(0, 4 << 20),
        name="row_stats",
    )(*raws, *([state] if before else []), *deps)


def norm_kernel(idx, st, r0, r1, r2, r3, r4, r5, fm, fp, _, n_own, n_oth, st_out, raw, nrm, sr, so):
    core = idx[8]
    copies = []
    for j in range(2):
        copies.append(pltpu.make_async_copy(fm.at[j], raw.at[6 + j, pl.ds(0, HALF)], sr.at[j]))
        copies.append(pltpu.make_async_copy(fp.at[j], raw.at[6 + j, pl.ds(HALF, EXT - HALF)], sr.at[2 + j]))
    for j, r in enumerate((r0, r1, r2, r3, r4, r5)):
        copies.append(pltpu.make_async_copy(r, raw.at[j], sr.at[4 + j]))
    for c in copies:
        c.start()
    for c in copies[:4]:
        c.wait()
    mean, m2 = st[:, 0:1], st[:, 1:2]
    for j in range(2):
        mean, m2 = merge(6 + j, mean, m2, raw[6 + j, pl.ds(0, ROWS), :])
    rstd = lax.rsqrt(m2 * (1.0 / D) + EPS)
    st_out[...] = two_lanes(mean, rstd)
    out = []
    own = pl.ds(pl.multiple_of(core * DB, 128), DB)
    oth = pl.ds(pl.multiple_of((1 - core) * DB, 128), DB)
    for j in (6, 7, 0, 1, 2, 3, 4, 5):
        if j < 6:
            copies[4 + j].wait()
        tail = raw[j, pl.ds(ROWS, 16), :]
        t = tail.astype(F32)
        g = t[0:1] + t[1:2] + t[2:3]
        nrm[j, pl.ds(0, ROWS), :] = ((raw[j, pl.ds(0, ROWS), :].astype(F32) - mean) * rstd * g).astype(BF)
        nrm[j, pl.ds(ROWS, 16), :] = tail
        mine = [pltpu.make_async_copy(nrm.at[j, :, own], n_own.at[idx[j]], so.at[j, 0]),
                pltpu.make_async_copy(nrm.at[j, :, oth], n_oth.at[idx[j]], so.at[j, 1])]
        for c in mine:
            c.start()
        out += mine
    for c in out:
        c.wait()


def normalize(index, st, raws, after):
    return pl.pallas_call(
        norm_kernel,
        in_specs=[SMEM, VMEM] + [HBM] * (len(raws) + 1),
        out_specs=[HBM, HBM, VMEM],
        out_shape=[sds((8, EXT, DB)), sds((8, EXT, DB)), sds((ROWS, 128), F32)],
        scratch_shapes=[
            pltpu.VMEM((8, EXT, 2 * DB), BF),
            pltpu.VMEM((8, EXT, 2 * DB), BF),
            pltpu.SemaphoreType.DMA((10,)),
            pltpu.SemaphoreType.DMA((8, 2)),
        ],
        compiler_params=params(),
        cost_estimate=cost(0, 8 << 20),
        name="normalize",
    )(index, st, *raws, after)


NW = 20


def w_sources(refs):
    out = []
    for z in range(2):
        mine, other = refs[10 * z:10 * z + 5], refs[10 * z + 5:10 * z + 10]
        for k in range(4):
            out.append(((mine[k],), (other[k],)) if k < 3 else (mine[3:5], other[3:5]))
    return out


def w_copies(parts, buf, half, sem):
    out = []
    rows = DB // len(parts)
    for h, part in enumerate(parts):
        at = pl.ds(pl.multiple_of(half * DB + h * rows, 64), rows)
        out += [pltpu.make_async_copy(part.at[j], buf.at[at, pl.ds(j * DB, DB)], sem.at[h, j]) for j in range(3)]
    return out


def split(v):
    hi = v.astype(BF)
    return hi, (v - hi.astype(F32)).astype(BF)


def attn_kernel(idx, counts, n_own, n_oth, *refs):
    w_refs, refs = refs[:NW], refs[NW:]
    g_ref, out_ref, dqkv_ref, mom_ref, qkv, nv, wv, sn, sw = refs
    h = pl.program_id(0)

    @pl.when(h == 0)
    def _():
        core = idx[8]
        own = pl.ds(pl.multiple_of(core * DB, 128), DB)
        oth = pl.ds(pl.multiple_of((1 - core) * DB, 128), DB)
        copies = []
        for k, (mine, other) in enumerate(w_sources(w_refs)):
            m = idx[k]
            copies.append([pltpu.make_async_copy(n_own.at[m], nv.at[k, :, own], sn.at[k, 0]),
                           pltpu.make_async_copy(n_oth.at[m], nv.at[k, :, oth], sn.at[k, 1])]
                          + w_copies(mine, wv.at[k], core, sw.at[k, 0])
                          + w_copies(other, wv.at[k], 1 - core, sw.at[k, 1]))
            for c in copies[-1]:
                c.start()
        for k in range(8):
            for c in copies[k]:
                c.wait()
            t = nn(nv[k], wv[k])
            if k == 0:
                qkv[...] = t
            else:
                qkv[...] += t

    col = lambda j: pl.ds(pl.multiple_of((j * NH + h) * HD, 128), HD)
    q_ref, k_ref, v_ref = (qkv.at[:, col(j)] for j in range(3))
    e0 = counts[0]
    e1 = e0 + counts[1]
    e2 = e1 + counts[2]
    rid = lax.broadcasted_iota(jnp.int32, (ROWS, 1), 0)
    cid = lax.broadcasted_iota(jnp.int32, (1, ROWS), 1)
    img = lambda p: (p >= e0).astype(jnp.int32) + (p >= e1).astype(jnp.int32) + (p >= e2).astype(jnp.int32)
    same = img(rid) == img(cid)
    scale = HD ** (-0.5)
    q = q_ref[:ROWS, :] * scale
    k = k_ref[:ROWS, :]
    v = v_ref[:ROWS, :]
    qh, ql = split(q)
    kh, kl = split(k)
    vb = v.astype(BF)
    g = g_ref[...]
    s = nt(jnp.concatenate([qh, qh], 1), jnp.concatenate([kh, kl], 1)) + nt(ql, kh)
    s = jnp.where(same, s, -1e30)
    p = jnp.exp(s - jnp.max(s, axis=1, keepdims=True))
    p = p * (1.0 / jnp.sum(p, axis=1, keepdims=True))
    pb = p.astype(BF)
    out_ref[...] = nn(pb, vb).astype(BF)
    dp = nt(g, vb)
    dv = tn(pb, g)
    ds = p * (dp - jnp.sum(dp * p, axis=1, keepdims=True))
    dsb = ds.astype(BF)
    dq = (nn(dsb, kh) * scale).astype(BF)
    dk = tn(dsb, qh).astype(BF)
    dv = dv.astype(BF)
    dqkv_ref[0] = dq
    dqkv_ref[1] = dk
    dqkv_ref[2] = dv
    m1 = jnp.zeros((ROWS, 1), F32)
    m2 = jnp.zeros((ROWS, 1), F32)
    for d, r in ((dq, q_ref), (dk, k_ref), (dv, v_ref)):
        df = d.astype(F32)
        u = r[ROWS:ROWS + 1, :] + r[ROWS + 1:ROWS + 2, :] + r[ROWS + 2:ROWS + 3, :]
        m1 = m1 + jnp.sum(df * u, axis=1, keepdims=True)
        m2 = m2 + jnp.sum(df * r[:ROWS, :], axis=1, keepdims=True)
    mom = two_lanes(m1, m2)

    @pl.when(h == 0)
    def _():
        mom_ref[...] = mom

    @pl.when(h > 0)
    def _():
        mom_ref[...] += mom


def attend(index, counts, n_own, n_oth, ws, grad_out):
    return pl.pallas_call(
        attn_kernel,
        grid=(NH,),
        in_specs=[SMEM, SMEM] + [HBM] * (2 + NW) + [pl.BlockSpec((ROWS, HD), lambda h: (0, h))],
        out_specs=[
            pl.BlockSpec((ROWS, HD), lambda h: (0, h)),
            pl.BlockSpec((3, ROWS, HD), lambda h: (0, 0, h)),
            pl.BlockSpec((ROWS, 128), lambda h: (0, 0)),
        ],
        out_shape=[sds((ROWS, DB)), sds((3, ROWS, DB)), sds((ROWS, 128), F32)],
        scratch_shapes=[
            pltpu.VMEM((EXT, CW), F32),
            pltpu.VMEM((8, EXT, 2 * DB), BF),
            pltpu.VMEM((8, 2 * DB, CW), BF),
            pltpu.SemaphoreType.DMA((8, 2)),
            pltpu.SemaphoreType.DMA((8, 2, 2, 3)),
        ],
        compiler_params=params(),
        cost_estimate=cost(2 * EXT * D * CW, 28 << 20, NH * ROWS * ROWS),
        name="attention",
    )(index, counts, n_own, n_oth, *ws, grad_out)


def grads_kernel(idx, d1, d2, *refs, ny, nx, ndeps, ysplit, xsplit):
    w_refs, (n1, n2), refs = refs[:NW], refs[NW:NW + 2], refs[NW + 2 + ndeps:]
    outs = list(refs[:-8])
    wv, nv, dcat, oy, ox, sd, si, so = refs[-8:]
    core = idx[0]
    dc = [pltpu.make_async_copy(d1.at[j], dcat.at[pl.ds(0, ROWS), pl.ds(j * DB, DB)], sd.at[0, j]) for j in range(3)]
    if nx:
        dc += [pltpu.make_async_copy(d2.at[j], dcat.at[pl.ds(ROWS, ROWS), pl.ds(j * DB, DB)], sd.at[1, j])
               for j in range(3)]
    for c in dc[:3]:
        c.start()
    sources = w_sources(w_refs)
    for i in range(ny):
        a = idx[1 + i]
        for k, (mine, other) in enumerate(sources):
            @pl.when(a == k)
            def _():
                for c in w_copies(mine, wv.at[i], core, si.at[i, 0]) + w_copies(other, wv.at[i], 1 - core, si.at[i, 1]):
                    c.start()
    for c in dc[3:]:
        c.start()
    ncs = []
    for i in range(nx):
        m = idx[1 + ny + i]
        ncs.append([pltpu.make_async_copy(n1.at[m, pl.ds(0, ROWS)], nv.at[i, pl.ds(0, ROWS)], si.at[ny + i, 0, 0, 0]),
                    pltpu.make_async_copy(n2.at[m, pl.ds(0, ROWS)], nv.at[i, pl.ds(ROWS, ROWS)], si.at[ny + i, 1, 0, 0])])
        for c in ncs[-1]:
            c.start()
    pending = []

    def put(src, dst, sem):
        c = pltpu.make_async_copy(src, dst, sem)
        c.start()
        pending.append(c)

    for c in dc[:3]:
        c.wait()
    for i in range(ny):
        a = idx[1 + i]
        halves = jnp.logical_or(a == 3, a == 7)
        for e in range(2):
            @pl.when(halves)
            def _():
                for c in w_copies(sources[3][e], wv.at[i], e, si.at[i, e]):
                    c.wait()

            @pl.when(jnp.logical_not(halves))
            def _():
                for c in w_copies(sources[0][e], wv.at[i], e, si.at[i, e]):
                    c.wait()
        oy[i] = nt(dcat[pl.ds(0, ROWS), :], wv[i]).astype(BF)
        if i in ysplit:
            put(oy.at[i, pl.ds(0, HALF)], outs.pop(0), so.at[i, 0])
            put(oy.at[i, pl.ds(HALF, HALF)], outs.pop(0), so.at[i, 1])
        else:
            put(oy.at[i], outs.pop(0), so.at[i, 0])
    for c in dc[3:]:
        c.wait()
    for i in range(nx):
        for c in ncs[i]:
            c.wait()
        t = tn(nv[i], dcat[...]).astype(BF)
        for j in range(3):
            ox[i, j] = t[:, j * DB:(j + 1) * DB]
        if i in xsplit:
            put(ox.at[i, :, pl.ds(0, HB)], outs.pop(0), so.at[ny + i, 0])
            put(ox.at[i, :, pl.ds(HB, HB)], outs.pop(0), so.at[ny + i, 1])
        else:
            put(ox.at[i], outs.pop(0), so.at[ny + i, 0])
    for c in pending:
        c.wait()


def grads(core, ysrc, xsrc, dqkv, d_other, ws, normed, other, deps, ysplit=(), xsplit=()):
    ny, nx = len(ysrc), len(xsrc)
    shapes = []
    for i in range(ny):
        shapes += [(HALF, 2 * DB)] * 2 if i in ysplit else [(ROWS, 2 * DB)]
    for i in range(nx):
        shapes += [(3, HB, DB)] * 2 if i in xsplit else [(3, DB, DB)]
    deps = list(deps)
    return pl.pallas_call(
        functools.partial(grads_kernel, ny=ny, nx=nx, ndeps=len(deps), ysplit=ysplit, xsplit=xsplit),
        in_specs=[SMEM] + [HBM] * (4 + NW + len(deps)),
        out_specs=[HBM] * len(shapes),
        out_shape=[sds(s) for s in shapes],
        scratch_shapes=[
            pltpu.VMEM((max(ny, 1), 2 * DB, CW), BF),
            pltpu.VMEM((max(nx, 1), 2 * ROWS, DB), BF),
            pltpu.VMEM((2 * ROWS, CW), BF),
            pltpu.VMEM((max(ny, 1), ROWS, 2 * DB), BF),
            pltpu.VMEM((max(nx, 1), 3, DB, DB), BF),
            pltpu.SemaphoreType.DMA((2, 3)),
            pltpu.SemaphoreType.DMA((ny + nx, 2, 2, 3)),
            pltpu.SemaphoreType.DMA((ny + nx, 2)),
        ],
        compiler_params=params(),
        cost_estimate=cost(2 * (ny + nx) * ROWS * 768 * CW, (ny + nx) * 3 << 20),
        name="grads",
    )(ivec(core, *ysrc, *xsrc), dqkv, d_other, *ws, normed, other, *deps)


def sum_kernel(ya, yb, yc, xa, xb, xc, y_out, x_out):
    y_out[...] = (ya[...].astype(F32) + yb[...].astype(F32) + yc[...].astype(F32)).astype(BF)
    x_out[...] = (xa[...].astype(F32) + xb[...].astype(F32) + xc[...].astype(F32)).astype(BF)


def sum_blocks(ys, xs):
    yspec = pl.BlockSpec((ROWS // 3, 2 * DB), lambda i: (i, 0))
    xspec = pl.BlockSpec((1, DB, DB), lambda i: (i, 0, 0))
    return pl.pallas_call(
        sum_kernel,
        grid=(3,),
        in_specs=[yspec] * 3 + [xspec] * 3,
        out_specs=[yspec, xspec],
        out_shape=[sds((ROWS, 2 * DB)), sds((3, DB, DB))],
        compiler_params=params(),
        cost_estimate=cost(0, 7 << 20),
        name="sum_blocks",
    )(*ys, *xs)


def add_kernel(yu, yd, xu, xd, hm, hp, vm, vp, *refs):
    for a, b, o in zip((yu, yd, xu, xd), (hm, hp, vm, vp), refs[-4:]):
        o[...] = (a[...].astype(F32) + b[...].astype(F32)).astype(BF)


def add_halves(blocks, arrived, deps):
    whole = lambda v: pl.BlockSpec(v.shape, lambda i: (0,) * v.ndim)
    halves = [
        pl.BlockSpec((HALF, 2 * DB), lambda i: (0, 0)),
        pl.BlockSpec((HALF, 2 * DB), lambda i: (1, 0)),
        pl.BlockSpec((3, HB, DB), lambda i: (0, 0, 0)),
        pl.BlockSpec((3, HB, DB), lambda i: (0, 1, 0)),
    ]
    return pl.pallas_call(
        add_kernel,
        grid=(1,),
        in_specs=halves + [whole(v) for v in arrived] + [HBM] * len(deps),
        out_specs=halves,
        out_shape=[sds(v.shape) for v in blocks],
        input_output_aliases={0: 0, 1: 1, 2: 2, 3: 3},
        compiler_params=params(),
        cost_estimate=cost(0, 6 << 20),
        name="add_halves",
    )(*blocks, *arrived, *deps)


def ivec(*v):
    return jnp.stack([jnp.asarray(e, jnp.int32) for e in v])


def local(patches, gain, w_qkv, counts, grad_out):
    si, mi = lax.axis_index("seq"), lax.axis_index("mp")
    core, x, zh = si % 2, (si // 2) % 4, si // 8
    y, zl = mi // 2, mi % 2
    mw = lambda dx, dz: jnp.where(dz == 0, zh, 1 - zh) * 4 + (x + dx) % 4
    mx = lambda dy, dz: ((y + dy) % 4) * 2 + jnp.where(dz == 0, zl, 1 - zl)
    rows, wshape = (EXT, 2 * DB), (3, DB, DB)
    lo, hi = (slice(None), pl.ds(0, HB)), (slice(None), pl.ds(HB, HB))
    first, rest = (pl.ds(0, HALF),), (pl.ds(HALF, EXT - HALF),)

    p0 = extend(patches, gain)
    w = jnp.transpose(w_qkv, (1, 0, 2))
    p_m, p_p, pz = mpp(p0, YP), mpp(p0, YM), mpp(p0, ZLO)
    w_m, w_p = sp(w, XP), sp(w, XM)
    pz1, w1, w_lo, w_hi = move(
        [pz, w, w_m, w_p], [rows, wshape, (3, HB, DB), (3, HB, DB)],
        [(0, None, 0, None), (1, None, 1, None), (2, lo, 2, None), (3, hi, 3, None)], [p_m, p_p], "stage1")
    pz_m, pz_p = mpp(pz1, YP), mpp(pz1, YM)
    wf_m, wf_p = sp(w_lo, XP), sp(w_hi, XM)
    wz = sp(w1, ZHI)
    st = stats(0, None, [p0, pz, p_m, p_p], [pz1])
    fu, fd, wz1, w2 = move(
        [p_m, p_p, pz_m, pz_p, wz, w1],
        [(2, HALF, 2 * DB), (2, EXT - HALF, 2 * DB), wshape, wshape],
        [(0, first, 0, (0,)), (2, first, 0, (1,)), (1, rest, 1, (0,)), (3, rest, 1, (1,)), (4, None, 2, None),
         (5, None, 3, None)],
        [st, wf_m, wf_p], "stage2")
    f_m, f_p = mpp(fu, YP), mpp(fd, YM)
    wz_m, wz_p = sp(wz1, XP), sp(wz1, XM)
    o_w, o_m, o_p, o_fm, o_fp = (sp(v, CORE) for v in (w2, w_m, w_p, wf_m, wf_p))
    st = stats(4, st, [pz_m, pz_p], [fu])
    wz_lo, wz_hi, wz2 = move(
        [wz_m, wz_p, wz1], [(3, HB, DB), (3, HB, DB), wshape],
        [(0, lo, 0, None), (1, hi, 1, None), (2, None, 2, None)],
        [f_m, f_p, o_w, o_m, o_p, o_fm, o_fp, st], "stage3")
    wzf_m, wzf_p = sp(wz_lo, XP), sp(wz_hi, XM)
    o_z, o_zm, o_zp = (sp(v, CORE) for v in (wz2, wz_m, wz_p))
    index = ivec(mx(0, 0), mx(0, 1), mx(-1, 0), mx(1, 0), mx(-1, 1), mx(1, 1), mx(2, 0), mx(2, 1), core)
    n_own, n_oth, st = normalize(index, st, [p0, pz, p_m, p_p, pz_m, pz_p, f_m, f_p], wz_lo)
    mean, rstd = st[:, 0:1], st[:, 1:2]
    o_zfm, o_zfp = sp(wzf_m, CORE), sp(wzf_p, CORE)
    n_other = sp(n_oth, CORE)
    ws = [w2, w_m, w_p, wf_m, wf_p, o_w, o_m, o_p, o_fm, o_fp,
          wz2, wz_m, wz_p, wzf_m, wzf_p, o_z, o_zm, o_zp, o_zfm, o_zfp]
    windex = ivec(mw(0, 0), mw(-1, 0), mw(1, 0), mw(2, 0), mw(0, 1), mw(-1, 1), mw(1, 1), mw(2, 1), core)
    heads_out, dqkv, mom = attend(windex, counts.reshape(4), n_own, n_oth, ws, grad_out)

    d_other = sp(dqkv, CORE)
    mom = jnp.concatenate([mom[:, 0], mom[:, 1]])
    for perm in (ZLO, YA, YB):
        mom = mom + mpp(mom, perm)

    def source(dy, dz):
        m = mx(dy, dz)
        dx = (m % 4 - x) % 4
        return jnp.where(dx == 3, 1, jnp.where(dx == 1, 2, jnp.where(dx == 2, 3, 0))) + jnp.where(m // 4 == zh, 0, 4)

    def blocks(yb, xb, deps, **kw):
        return grads(core, [source(*b) for b in yb], [mw(*b) for b in xb], dqkv, d_other, ws, n_own, n_other, deps, **kw)

    y2p_lo, y2p_hi, x2p_lo, x2p_hi = blocks([(2, 1)], [(2, 1)], [], ysplit=(0,), xsplit=(0,))
    h_m, h_p = mpp(y2p_lo, YP), mpp(y2p_hi, YM)
    v_m, v_p = sp(x2p_lo, XP), sp(x2p_hi, XM)
    near = blocks([(1, 1), (-1, 1)], [(1, 1), (-1, 1)], [x2p_lo])
    yu, yd, xu, xd = add_halves(near, [h_m, h_p, v_m, v_p], [])
    ya1, ya2, xa1, xa2 = mpp(yu, YP), mpp(yd, YM), sp(xu, XP), sp(xd, XM)
    y0p, y2_lo, y2_hi, y1u, y1d, x0p, x2_lo, x2_hi, x1u, x1d = blocks(
        [(0, 1), (2, 0), (1, 0), (-1, 0)], [(0, 1), (2, 0), (1, 0), (-1, 0)], [yu], ysplit=(1,), xsplit=(1,))
    y_out, x_out = sum_blocks([y0p, ya1, ya2], [x0p, xa1, xa2])
    yz = mpp(y_out, ZLO)
    h_m, h_p = mpp(y2_lo, YP), mpp(y2_hi, YM)
    v_m, v_p = sp(x2_lo, XP), sp(x2_hi, XM)
    y0, x0 = blocks([(0, 0)], [(0, 0)], [y_out])
    yu, yd, xu, xd = add_halves([y1u, y1d, x1u, x1d], [h_m, h_p, v_m, v_p], [yz, x_out, y0])
    yb1, yb2, xb1, xb2 = mpp(yu, YP), mpp(yd, YM), sp(xu, XP), sp(xd, XM)
    xz = sp(x_out, ZHI)

    f = lambda v: v.astype(F32)
    mom = mom / D
    gn = f(y0) + f(yb1) + f(yb2) + f(yz)
    xhat = (f(patches) - mean) * rstd
    gg = jnp.sum(gn * xhat, axis=0)
    for perm in (CORE, XA, XB, ZHI):
        gg = gg + sp(gg, perm)
    grad_p = ((gn * gain[None, :] - mom[:ROWS, None] - xhat * mom[ROWS:, None]) * rstd).astype(BF)
    gw = jnp.transpose(f(x0) + f(xb1) + f(xb2) + f(xz), (1, 0, 2))
    return heads_out, grad_p, gg, gw


def solution(mesh):
    placed = (P("seq", "mp"), P("mp"), P("seq", None, "mp"), P("seq", None), P("seq", "mp"))
    return jax.shard_map(
        local,
        mesh=mesh,
        in_specs=placed,
        out_specs=(P("seq", "mp"), P("seq", "mp"), P("mp"), P("seq", None, "mp")),
        check_vma=False,
    )
```

```python
import functools

import jax
import jax.numpy as jnp
from jax import lax
from jax.experimental import pallas as pl
from jax.experimental.pallas import tpu as pltpu
from jax.sharding import PartitionSpec as P

HD = 128
NH = 3
ROWS = 576
HALF = ROWS // 2
EXT = ROWS + 16
DB = 384
HB = DB // 2
D = 6144
CW = 3 * DB
EPS = 1e-06
BF = jnp.bfloat16
F32 = jnp.float32
HBM = pl.BlockSpec(memory_space=pltpu.HBM)
VMEM = pl.BlockSpec(memory_space=pltpu.VMEM)
SMEM = pl.BlockSpec(memory_space=pltpu.SMEM)


def seq_perm(f):
    out = []
    for i in range(16):
        zh, x, c = f(i // 8, (i // 2) % 4, i % 2)
        out.append((i, (zh * 4 + x % 4) * 2 + c))
    return out


def mp_perm(f):
    out = []
    for i in range(8):
        y, zl = f(i // 2, i % 2)
        out.append((i, (y % 4) * 2 + zl))
    return out


CORE = seq_perm(lambda zh, x, c: (zh, x, 1 - c))
ZHI = seq_perm(lambda zh, x, c: (1 - zh, x, c))
XP = seq_perm(lambda zh, x, c: (zh, x + 1, c))
XM = seq_perm(lambda zh, x, c: (zh, x - 1, c))
X2 = seq_perm(lambda zh, x, c: (zh, x + 2, c))
ZLO = mp_perm(lambda y, zl: (y, 1 - zl))
YP = mp_perm(lambda y, zl: (y + 1, zl))
YM = mp_perm(lambda y, zl: (y - 1, zl))
YA = mp_perm(lambda y, zl: (y ^ 1, zl))
YB = mp_perm(lambda y, zl: (y ^ 3, zl))


def sp(v, perm):
    return lax.ppermute(v, "seq", perm)


def mpp(v, perm):
    return lax.ppermute(v, "mp", perm)


def nt(a, b):
    return lax.dot_general(a, b, (((1,), (1,)), ((), ())), preferred_element_type=F32)


def tn(a, b):
    return lax.dot_general(a, b, (((0,), (0,)), ((), ())), preferred_element_type=F32)


def nn(a, b):
    return lax.dot_general(a, b, (((1,), (0,)), ((), ())), preferred_element_type=F32)


def sds(shape, dtype=BF):
    return jax.ShapeDtypeStruct(shape, dtype)


def params(mib=63):
    return pltpu.CompilerParams(vmem_limit_bytes=mib << 20)


def cost(flops, nbytes, exps=0):
    return pl.CostEstimate(flops=int(flops), bytes_accessed=int(nbytes), transcendentals=exps)


def sliced(shape, index):
    if not index:
        return shape
    out = []
    for n, i in zip(shape, index):
        if not isinstance(i, int):
            out.append(n if isinstance(i, slice) else i.size)
    return tuple(out) + tuple(shape[len(index):])


def move(inputs, outs, plan, deps, name):
    def kernel(*refs):
        ins = refs[:len(inputs)]
        dst = refs[len(inputs) + len(deps):][:len(outs)]
        *bufs, sem = refs[len(inputs) + len(deps) + len(outs):]
        get = [pltpu.make_async_copy(ins[i].at[si] if si else ins[i], bufs[k], sem.at[k, 0])
               for k, (i, si, o, so) in enumerate(plan)]
        put = [pltpu.make_async_copy(bufs[k], dst[o].at[so] if so else dst[o], sem.at[k, 1])
               for k, (i, si, o, so) in enumerate(plan)]
        for c in get:
            c.start()
        for g, p in zip(get, put):
            g.wait()
            p.start()
        for p in put:
            p.wait()

    return pl.pallas_call(
        kernel,
        in_specs=[HBM] * (len(inputs) + len(deps)),
        out_specs=[HBM] * len(outs),
        out_shape=[sds(s) for s in outs],
        scratch_shapes=[pltpu.VMEM(sliced(inputs[i].shape, si), BF) for i, si, o, so in plan]
        + [pltpu.SemaphoreType.DMA((len(plan), 2))],
        compiler_params=params(),
        cost_estimate=cost(0, 4 << 20),
        name=name,
    )(*inputs, *deps)


def hold(value, deps):
    def kernel(*refs):
        pass

    return pl.pallas_call(
        kernel,
        in_specs=[HBM] * (1 + len(deps)),
        out_specs=HBM,
        out_shape=sds(value.shape, value.dtype),
        input_output_aliases={0: 0},
        compiler_params=params(),
        cost_estimate=cost(0, 1 << 10),
        name="hold",
    )(value, *deps)


def extend_kernel(p, gain, out):
    out[pl.ds(0, ROWS), :] = p[...]
    g = gain[...]
    hi = g.astype(BF).astype(F32)
    mid = (g - hi).astype(BF).astype(F32)
    row = lax.broadcasted_iota(jnp.int32, (16, 2 * DB), 0)
    tail = jnp.where(row == 0, hi, jnp.where(row == 1, mid, jnp.where(row == 2, g - hi - mid, 0.0)))
    out[pl.ds(ROWS, 16), :] = tail.astype(BF)


def extend(patches, gain):
    return pl.pallas_call(
        extend_kernel,
        out_shape=sds((EXT, 2 * DB)),
        compiler_params=params(),
        cost_estimate=cost(0, 2 << 20),
        name="extend",
    )(patches, gain.reshape(1, 2 * DB))


def merge(n, mean, m2, chunk):
    v = chunk.astype(F32)
    cm = jnp.sum(v, axis=1, keepdims=True) * (1.0 / 768)
    dv = v - cm
    c2 = jnp.sum(dv * dv, axis=1, keepdims=True)
    if n == 0:
        return cm, c2
    delta = cm - mean
    return mean + delta * (1.0 / (n + 1)), m2 + c2 + delta * delta * (768.0 * n / (n + 1))


def two_lanes(a, b):
    lane = lax.broadcasted_iota(jnp.int32, (ROWS, 128), 1)
    return jnp.where(lane == 0, a, jnp.where(lane == 1, b, 0.0))


def stats_kernel(*refs, nraw, ndeps):
    raws = refs[:nraw]
    out, buf, sem = refs[nraw + ndeps:]
    copies = [pltpu.make_async_copy(r, buf.at[j], sem.at[j]) for j, r in enumerate(raws)]
    for c in copies:
        c.start()
    mean = m2 = None
    for j, c in enumerate(copies):
        c.wait()
        mean, m2 = merge(j, mean, m2, buf[j, pl.ds(0, ROWS), :])
    out[...] = two_lanes(mean, m2)


def stats(raws, deps):
    n = len(raws)
    return pl.pallas_call(
        functools.partial(stats_kernel, nraw=n, ndeps=len(deps)),
        in_specs=[HBM] * (n + len(deps)),
        out_specs=VMEM,
        out_shape=sds((ROWS, 128), F32),
        scratch_shapes=[pltpu.VMEM((n, EXT, 2 * DB), BF), pltpu.SemaphoreType.DMA((n,))],
        compiler_params=params(),
        cost_estimate=cost(0, 4 << 20),
        name="row_stats",
    )(*raws, *deps)


def norm_kernel(idx, st, r0, r1, r2, r3, r4, r5, fm, fp, _, n_own, n_oth, st_out, raw, nrm, sr, so):
    core = idx[8]
    copies = []
    for j in range(2):
        copies.append(pltpu.make_async_copy(fm.at[j], raw.at[6 + j, pl.ds(0, HALF)], sr.at[j]))
        copies.append(pltpu.make_async_copy(fp.at[j], raw.at[6 + j, pl.ds(HALF, EXT - HALF)], sr.at[2 + j]))
    for j, r in enumerate((r0, r1, r2, r3, r4, r5)):
        copies.append(pltpu.make_async_copy(r, raw.at[j], sr.at[4 + j]))
    for c in copies:
        c.start()
    for c in copies[:4]:
        c.wait()
    mean, m2 = st[:, 0:1], st[:, 1:2]
    for j in range(2):
        mean, m2 = merge(6 + j, mean, m2, raw[6 + j, pl.ds(0, ROWS), :])
    rstd = lax.rsqrt(m2 * (1.0 / D) + EPS)
    st_out[...] = two_lanes(mean, rstd)
    out = []
    own = pl.ds(pl.multiple_of(core * DB, 128), DB)
    oth = pl.ds(pl.multiple_of((1 - core) * DB, 128), DB)
    for j in (6, 7, 0, 1, 2, 3, 4, 5):
        if j < 6:
            copies[4 + j].wait()
        tail = raw[j, pl.ds(ROWS, 16), :]
        t = tail.astype(F32)
        g = t[0:1] + t[1:2] + t[2:3]
        nrm[j, pl.ds(0, ROWS), :] = ((raw[j, pl.ds(0, ROWS), :].astype(F32) - mean) * rstd * g).astype(BF)
        nrm[j, pl.ds(ROWS, 16), :] = tail
        mine = [pltpu.make_async_copy(nrm.at[j, :, own], n_own.at[idx[j]], so.at[j, 0]),
                pltpu.make_async_copy(nrm.at[j, :, oth], n_oth.at[idx[j]], so.at[j, 1])]
        for c in mine:
            c.start()
        out += mine
    for c in out:
        c.wait()


def normalize(index, st, raws, after):
    return pl.pallas_call(
        norm_kernel,
        in_specs=[SMEM, VMEM] + [HBM] * (len(raws) + 1),
        out_specs=[HBM, HBM, VMEM],
        out_shape=[sds((8, EXT, DB)), sds((8, EXT, DB)), sds((ROWS, 128), F32)],
        scratch_shapes=[
            pltpu.VMEM((8, EXT, 2 * DB), BF),
            pltpu.VMEM((8, EXT, 2 * DB), BF),
            pltpu.SemaphoreType.DMA((10,)),
            pltpu.SemaphoreType.DMA((8, 2)),
        ],
        compiler_params=params(),
        cost_estimate=cost(0, 8 << 20),
        name="normalize",
    )(index, st, *raws, after)


NW = 20


def w_sources(refs):
    out = []
    for z in range(2):
        mine, other = refs[10 * z:10 * z + 5], refs[10 * z + 5:10 * z + 10]
        for k in range(4):
            out.append(((mine[k],), (other[k],)) if k < 3 else (mine[3:5], other[3:5]))
    return out


def w_copies(parts, buf, half, sem):
    out = []
    rows = DB // len(parts)
    for h, part in enumerate(parts):
        at = pl.ds(pl.multiple_of(half * DB + h * rows, 64), rows)
        out += [pltpu.make_async_copy(part.at[j], buf.at[at, pl.ds(j * DB, DB)], sem.at[h, j]) for j in range(3)]
    return out


def split(v):
    hi = v.astype(BF)
    return hi, (v - hi.astype(F32)).astype(BF)


def attn_kernel(idx, counts, n_own, n_oth, *refs):
    w_refs, refs = refs[:NW], refs[NW:]
    g_ref, out_ref, dqkv_ref, mom_ref, qkv, nv, wv, sn, sw = refs
    h = pl.program_id(0)

    @pl.when(h == 0)
    def _():
        core = idx[8]
        own = pl.ds(pl.multiple_of(core * DB, 128), DB)
        oth = pl.ds(pl.multiple_of((1 - core) * DB, 128), DB)
        copies = []
        for k, (mine, other) in enumerate(w_sources(w_refs)):
            m = idx[k]
            copies.append([pltpu.make_async_copy(n_own.at[m], nv.at[k, :, own], sn.at[k, 0]),
                           pltpu.make_async_copy(n_oth.at[m], nv.at[k, :, oth], sn.at[k, 1])]
                          + w_copies(mine, wv.at[k], core, sw.at[k, 0])
                          + w_copies(other, wv.at[k], 1 - core, sw.at[k, 1]))
            for c in copies[-1]:
                c.start()
        for k in range(8):
            for c in copies[k]:
                c.wait()
            t = nn(nv[k], wv[k])
            if k == 0:
                qkv[...] = t
            else:
                qkv[...] += t

    col = lambda j: pl.ds(pl.multiple_of((j * NH + h) * HD, 128), HD)
    q_ref, k_ref, v_ref = (qkv.at[:, col(j)] for j in range(3))
    e0 = counts[0]
    e1 = e0 + counts[1]
    e2 = e1 + counts[2]
    rid = lax.broadcasted_iota(jnp.int32, (ROWS, 1), 0)
    cid = lax.broadcasted_iota(jnp.int32, (1, ROWS), 1)
    img = lambda p: (p >= e0).astype(jnp.int32) + (p >= e1).astype(jnp.int32) + (p >= e2).astype(jnp.int32)
    same = img(rid) == img(cid)
    scale = HD ** (-0.5)
    q = q_ref[:ROWS, :] * scale
    k = k_ref[:ROWS, :]
    v = v_ref[:ROWS, :]
    qh, ql = split(q)
    kh, kl = split(k)
    vb = v.astype(BF)
    g = g_ref[...]
    s = nt(jnp.concatenate([qh, qh], 1), jnp.concatenate([kh, kl], 1)) + nt(ql, kh)
    s = jnp.where(same, s, -1e30)
    p = jnp.exp(s - jnp.max(s, axis=1, keepdims=True))
    p = p * (1.0 / jnp.sum(p, axis=1, keepdims=True))
    pb = p.astype(BF)
    out_ref[...] = nn(pb, vb).astype(BF)
    dp = nt(g, vb)
    dv = tn(pb, g)
    ds = p * (dp - jnp.sum(dp * p, axis=1, keepdims=True))
    dsb = ds.astype(BF)
    dq = (nn(dsb, kh) * scale).astype(BF)
    dk = tn(dsb, qh).astype(BF)
    dv = dv.astype(BF)
    dqkv_ref[0] = dq
    dqkv_ref[1] = dk
    dqkv_ref[2] = dv
    m1 = jnp.zeros((ROWS, 1), F32)
    m2 = jnp.zeros((ROWS, 1), F32)
    for d, r in ((dq, q_ref), (dk, k_ref), (dv, v_ref)):
        df = d.astype(F32)
        u = r[ROWS:ROWS + 1, :] + r[ROWS + 1:ROWS + 2, :] + r[ROWS + 2:ROWS + 3, :]
        m1 = m1 + jnp.sum(df * u, axis=1, keepdims=True)
        m2 = m2 + jnp.sum(df * r[:ROWS, :], axis=1, keepdims=True)
    mom = two_lanes(m1, m2)

    @pl.when(h == 0)
    def _():
        mom_ref[...] = mom

    @pl.when(h > 0)
    def _():
        mom_ref[...] += mom


def attend(index, counts, n_own, n_oth, ws, grad_out):
    return pl.pallas_call(
        attn_kernel,
        grid=(NH,),
        in_specs=[SMEM, SMEM] + [HBM] * (2 + NW) + [pl.BlockSpec((ROWS, HD), lambda h: (0, h))],
        out_specs=[
            pl.BlockSpec((ROWS, HD), lambda h: (0, h)),
            pl.BlockSpec((3, ROWS, HD), lambda h: (0, 0, h)),
            pl.BlockSpec((ROWS, 128), lambda h: (0, 0)),
        ],
        out_shape=[sds((ROWS, DB)), sds((3, ROWS, DB)), sds((ROWS, 128), F32)],
        scratch_shapes=[
            pltpu.VMEM((EXT, CW), F32),
            pltpu.VMEM((8, EXT, 2 * DB), BF),
            pltpu.VMEM((8, 2 * DB, CW), BF),
            pltpu.SemaphoreType.DMA((8, 2)),
            pltpu.SemaphoreType.DMA((8, 2, 2, 3)),
        ],
        compiler_params=params(),
        cost_estimate=cost(2 * EXT * D * CW, 28 << 20, NH * ROWS * ROWS),
        name="attention",
    )(index, counts, n_own, n_oth, *ws, grad_out)


def grads_kernel(idx, d1, d2, *refs, ny, nx, ndeps, ysplit, xsplit):
    w_refs, (n1, n2), refs = refs[:NW], refs[NW:NW + 2], refs[NW + 2 + ndeps:]
    outs = list(refs[:-8])
    wv, nv, dcat, oy, ox, sd, si, so = refs[-8:]
    core = idx[0]
    dc = [pltpu.make_async_copy(d1.at[j], dcat.at[pl.ds(0, ROWS), pl.ds(j * DB, DB)], sd.at[0, j]) for j in range(3)]
    if nx:
        dc += [pltpu.make_async_copy(d2.at[j], dcat.at[pl.ds(ROWS, ROWS), pl.ds(j * DB, DB)], sd.at[1, j])
               for j in range(3)]
    for c in dc[:3]:
        c.start()
    sources = w_sources(w_refs)
    for i in range(ny):
        a = idx[1 + i]
        for k, (mine, other) in enumerate(sources):
            @pl.when(a == k)
            def _():
                for c in w_copies(mine, wv.at[i], core, si.at[i, 0]) + w_copies(other, wv.at[i], 1 - core, si.at[i, 1]):
                    c.start()
    for c in dc[3:]:
        c.start()
    ncs = []
    for i in range(nx):
        m = idx[1 + ny + i]
        ncs.append([pltpu.make_async_copy(n1.at[m, pl.ds(0, ROWS)], nv.at[i, pl.ds(0, ROWS)], si.at[ny + i, 0, 0, 0]),
                    pltpu.make_async_copy(n2.at[m, pl.ds(0, ROWS)], nv.at[i, pl.ds(ROWS, ROWS)], si.at[ny + i, 1, 0, 0])])
        for c in ncs[-1]:
            c.start()
    pending = []

    def put(src, dst, sem):
        c = pltpu.make_async_copy(src, dst, sem)
        c.start()
        pending.append(c)

    for c in dc[:3]:
        c.wait()
    for i in range(ny):
        a = idx[1 + i]
        halves = jnp.logical_or(a == 3, a == 7)
        for e in range(2):
            @pl.when(halves)
            def _():
                for c in w_copies(sources[3][e], wv.at[i], e, si.at[i, e]):
                    c.wait()

            @pl.when(jnp.logical_not(halves))
            def _():
                for c in w_copies(sources[0][e], wv.at[i], e, si.at[i, e]):
                    c.wait()
        oy[i] = nt(dcat[pl.ds(0, ROWS), :], wv[i]).astype(BF)
        if i in ysplit:
            put(oy.at[i, pl.ds(0, HALF)], outs.pop(0), so.at[i, 0])
            put(oy.at[i, pl.ds(HALF, HALF)], outs.pop(0), so.at[i, 1])
        else:
            put(oy.at[i], outs.pop(0), so.at[i, 0])
    for c in dc[3:]:
        c.wait()
    for i in range(nx):
        for c in ncs[i]:
            c.wait()
        t = tn(nv[i], dcat[...]).astype(BF)
        for j in range(3):
            ox[i, j] = t[:, j * DB:(j + 1) * DB]
        if i in xsplit:
            put(ox.at[i, :, pl.ds(0, HB)], outs.pop(0), so.at[ny + i, 0])
            put(ox.at[i, :, pl.ds(HB, HB)], outs.pop(0), so.at[ny + i, 1])
        else:
            put(ox.at[i], outs.pop(0), so.at[ny + i, 0])
    for c in pending:
        c.wait()


def grads(core, ysrc, xsrc, dqkv, d_other, ws, normed, other, deps, ysplit=(), xsplit=()):
    ny, nx = len(ysrc), len(xsrc)
    shapes = []
    for i in range(ny):
        shapes += [(HALF, 2 * DB)] * 2 if i in ysplit else [(ROWS, 2 * DB)]
    for i in range(nx):
        shapes += [(3, HB, DB)] * 2 if i in xsplit else [(3, DB, DB)]
    deps = list(deps)
    return pl.pallas_call(
        functools.partial(grads_kernel, ny=ny, nx=nx, ndeps=len(deps), ysplit=ysplit, xsplit=xsplit),
        in_specs=[SMEM] + [HBM] * (4 + NW + len(deps)),
        out_specs=[HBM] * len(shapes),
        out_shape=[sds(s) for s in shapes],
        scratch_shapes=[
            pltpu.VMEM((max(ny, 1), 2 * DB, CW), BF),
            pltpu.VMEM((max(nx, 1), 2 * ROWS, DB), BF),
            pltpu.VMEM((2 * ROWS, CW), BF),
            pltpu.VMEM((max(ny, 1), ROWS, 2 * DB), BF),
            pltpu.VMEM((max(nx, 1), 3, DB, DB), BF),
            pltpu.SemaphoreType.DMA((2, 3)),
            pltpu.SemaphoreType.DMA((ny + nx, 2, 2, 3)),
            pltpu.SemaphoreType.DMA((ny + nx, 2)),
        ],
        compiler_params=params(),
        cost_estimate=cost(2 * (ny + nx) * ROWS * 768 * CW, (ny + nx) * 3 << 20),
        name="grads",
    )(ivec(core, *ysrc, *xsrc), dqkv, d_other, *ws, normed, other, *deps)


def sum_kernel(a, b, c, *refs):
    refs[-1][...] = (a[...].astype(F32) + b[...].astype(F32) + c[...].astype(F32)).astype(BF)


def sum_blocks(vs, deps):
    shape = vs[0].shape
    spec = (pl.BlockSpec((ROWS // 3, 2 * DB), lambda i: (i, 0)) if len(shape) == 2
            else pl.BlockSpec((1, DB, DB), lambda i: (i, 0, 0)))
    return pl.pallas_call(
        sum_kernel,
        grid=(3,),
        in_specs=[spec] * 3 + [HBM] * len(deps),
        out_specs=spec,
        out_shape=sds(shape),
        compiler_params=params(),
        cost_estimate=cost(0, 4 << 20),
        name="sum_blocks",
    )(*vs, *deps)


def add_kernel(yu, yd, xu, xd, hm, hp, vm, vp, *refs):
    for a, b, o in zip((yu, yd, xu, xd), (hm, hp, vm, vp), refs[-4:]):
        o[...] = (a[...].astype(F32) + b[...].astype(F32)).astype(BF)


def add_halves(blocks, arrived, deps):
    whole = lambda v: pl.BlockSpec(v.shape, lambda i: (0,) * v.ndim)
    halves = [
        pl.BlockSpec((HALF, 2 * DB), lambda i: (0, 0)),
        pl.BlockSpec((HALF, 2 * DB), lambda i: (1, 0)),
        pl.BlockSpec((3, HB, DB), lambda i: (0, 0, 0)),
        pl.BlockSpec((3, HB, DB), lambda i: (0, 1, 0)),
    ]
    return pl.pallas_call(
        add_kernel,
        grid=(1,),
        in_specs=halves + [whole(v) for v in arrived] + [HBM] * len(deps),
        out_specs=halves,
        out_shape=[sds(v.shape) for v in blocks],
        input_output_aliases={0: 0, 1: 1, 2: 2, 3: 3},
        compiler_params=params(),
        cost_estimate=cost(0, 6 << 20),
        name="add_halves",
    )(*blocks, *arrived, *deps)


def ivec(*v):
    return jnp.stack([jnp.asarray(e, jnp.int32) for e in v])


def local(patches, gain, w_qkv, counts, grad_out):
    si, mi = lax.axis_index("seq"), lax.axis_index("mp")
    core, x, zh = si % 2, (si // 2) % 4, si // 8
    y, zl = mi // 2, mi % 2
    mw = lambda dx, dz: jnp.where(dz == 0, zh, 1 - zh) * 4 + (x + dx) % 4
    mx = lambda dy, dz: ((y + dy) % 4) * 2 + jnp.where(dz == 0, zl, 1 - zl)
    rows, wshape = (EXT, 2 * DB), (3, DB, DB)
    lo, hi = (slice(None), pl.ds(0, HB)), (slice(None), pl.ds(HB, HB))
    first, rest = (pl.ds(0, HALF),), (pl.ds(HALF, EXT - HALF),)

    p0 = extend(patches, gain)
    w = jnp.transpose(w_qkv, (1, 0, 2))
    p_m, p_p, pz = mpp(p0, YP), mpp(p0, YM), mpp(p0, ZLO)
    w_m, w_p = sp(w, XP), sp(w, XM)
    pz1, w1, w_lo, w_hi = move(
        [pz, w, w_m, w_p], [rows, wshape, (3, HB, DB), (3, HB, DB)],
        [(0, None, 0, None), (1, None, 1, None), (2, lo, 2, None), (3, hi, 3, None)], [p_m, p_p], "stage1")
    pz_m, pz_p = mpp(pz1, YP), mpp(pz1, YM)
    wf_m, wf_p = sp(w_lo, XP), sp(w_hi, XM)
    wz = sp(w1, ZHI)
    fu, fd, wz1, w2 = move(
        [p_m, p_p, pz_m, pz_p, wz, w1],
        [(2, HALF, 2 * DB), (2, EXT - HALF, 2 * DB), wshape, wshape],
        [(0, first, 0, (0,)), (2, first, 0, (1,)), (1, rest, 1, (0,)), (3, rest, 1, (1,)), (4, None, 2, None),
         (5, None, 3, None)],
        [wf_m, wf_p], "stage2")
    f_m, f_p = mpp(fu, YP), mpp(fd, YM)
    wz_m, wz_p = sp(wz1, XP), sp(wz1, XM)
    o_w, o_m, o_p, o_fm, o_fp = (sp(v, CORE) for v in (w2, w_m, w_p, wf_m, wf_p))
    st = stats([p0, pz, p_m, p_p, pz_m, pz_p], [fu])
    wz_lo, wz_hi, wz2 = move(
        [wz_m, wz_p, wz1], [(3, HB, DB), (3, HB, DB), wshape],
        [(0, lo, 0, None), (1, hi, 1, None), (2, None, 2, None)],
        [f_m, f_p, o_w, o_m, o_p, o_fm, o_fp, st], "stage3")
    wzf_m, wzf_p = sp(wz_lo, XP), sp(wz_hi, XM)
    o_z, o_zm, o_zp = (sp(v, CORE) for v in (wz2, wz_m, wz_p))
    index = ivec(mx(0, 0), mx(0, 1), mx(-1, 0), mx(1, 0), mx(-1, 1), mx(1, 1), mx(2, 0), mx(2, 1), core)
    n_own, n_oth, st = normalize(index, st, [p0, pz, p_m, p_p, pz_m, pz_p, f_m, f_p], wz_lo)
    mean, rstd = st[:, 0:1], st[:, 1:2]
    n_oth = hold(n_oth, [wzf_m, wzf_p, o_z])
    wzf_p = hold(wzf_p, [n_oth])
    o_zfm, o_zfp = sp(wzf_m, CORE), sp(wzf_p, CORE)
    n_other = sp(n_oth, CORE)
    ws = [w2, w_m, w_p, wf_m, wf_p, o_w, o_m, o_p, o_fm, o_fp,
          wz2, wz_m, wz_p, wzf_m, wzf_p, o_z, o_zm, o_zp, o_zfm, o_zfp]
    windex = ivec(mw(0, 0), mw(-1, 0), mw(1, 0), mw(2, 0), mw(0, 1), mw(-1, 1), mw(1, 1), mw(2, 1), core)
    heads_out, dqkv, mom = attend(windex, counts.reshape(4), n_own, n_oth, ws, grad_out)

    d_other = sp(dqkv, CORE)
    mom = jnp.concatenate([mom[:, 0], mom[:, 1]])
    mom1 = mom + mpp(mom, ZLO)
    mom2 = mom1 + mpp(mom1, YA)
    mom3 = mom2 + mpp(mom2, YB)

    def source(dy, dz):
        m = mx(dy, dz)
        dx = (m % 4 - x) % 4
        return jnp.where(dx == 3, 1, jnp.where(dx == 1, 2, jnp.where(dx == 2, 3, 0))) + jnp.where(m // 4 == zh, 0, 4)

    def blocks(yb, xb, deps, **kw):
        return grads(core, [source(*b) for b in yb], [mw(*b) for b in xb], dqkv, d_other, ws, n_own, n_other, deps, **kw)

    y2p_lo, y2p_hi, x2p_lo, x2p_hi = blocks([(2, 1)], [(2, 1)], [mom1], ysplit=(0,), xsplit=(0,))
    h_m, h_p = mpp(y2p_lo, YP), mpp(y2p_hi, YM)
    v_m, v_p = sp(x2p_lo, XP), sp(x2p_hi, XM)
    near = blocks([(1, 1), (-1, 1)], [(1, 1), (-1, 1)], [x2p_lo])
    yu, yd, xu, xd = add_halves(near, [h_m, h_p, v_m, v_p], [mom2])
    ya1, ya2, xa1, xa2 = mpp(yu, YP), mpp(yd, YM), sp(xu, XP), sp(xd, XM)
    y0p, y2_lo, y2_hi, y1u, y1d, x0p, x2_lo, x2_hi = blocks(
        [(0, 1), (2, 0), (1, 0), (-1, 0)], [(0, 1), (2, 0)], [yu], ysplit=(1,), xsplit=(1,))
    y_out = sum_blocks([y0p, ya1, ya2], [mom3, xa1, xa2])
    yz = mpp(y_out, ZLO)
    h_m, h_p = mpp(y2_lo, YP), mpp(y2_hi, YM)
    v_m, v_p = sp(x2_lo, XP), sp(x2_hi, XM)
    y0, x1u, x1d, x0 = blocks([(0, 0)], [(1, 0), (-1, 0), (0, 0)], [y_out])
    x_out = sum_blocks([x0p, xa1, xa2], [x0])
    yu, yd, xu, xd = add_halves([y1u, y1d, x1u, x1d], [h_m, h_p, v_m, v_p], [yz, x_out, y0])
    yb1, yb2, xb1, xb2 = mpp(yu, YP), mpp(yd, YM), sp(xu, XP), sp(xd, XM)
    xz = sp(x_out, ZHI)

    f = lambda v: v.astype(F32)
    mom = mom3 / D
    gn = f(y0) + f(yb1) + f(yb2) + f(yz)
    xhat = (f(patches) - mean) * rstd
    gg = jnp.sum(gn * xhat, axis=0)
    for perm in (CORE, ZHI):
        gg = gg + sp(gg, perm)
    gg = (gg + sp(gg, X2)) + (sp(gg, XP) + sp(gg, XM))
    grad_p = ((gn * gain[None, :] - mom[:ROWS, None] - xhat * mom[ROWS:, None]) * rstd).astype(BF)
    gw = jnp.transpose(f(x0) + f(xb1) + f(xb2) + f(xz), (1, 0, 2))
    return heads_out, grad_p, gg, gw


def solution(mesh):
    placed = (P("seq", "mp"), P("mp"), P("seq", None, "mp"), P("seq", None), P("seq", "mp"))
    return jax.shard_map(
        local,
        mesh=mesh,
        in_specs=placed,
        out_specs=(P("seq", "mp"), P("seq", "mp"), P("mp"), P("seq", None, "mp")),
        check_vma=False,
    )
```

```python
import functools

import jax
import jax.numpy as jnp
from jax import lax
from jax.experimental import pallas as pl
from jax.experimental.pallas import tpu as pltpu
from jax.sharding import PartitionSpec as P

HD = 128
NH = 3
ROWS = 576
HALF = ROWS // 2
EXT = ROWS + 16
DB = 384
HB = DB // 2
D = 6144
CW = 3 * DB
EPS = 1e-06
BF = jnp.bfloat16
F32 = jnp.float32
HBM = pl.BlockSpec(memory_space=pltpu.HBM)
VMEM = pl.BlockSpec(memory_space=pltpu.VMEM)
SMEM = pl.BlockSpec(memory_space=pltpu.SMEM)


def seq_perm(f):
    out = []
    for i in range(16):
        zh, x, c = f(i // 8, (i // 2) % 4, i % 2)
        out.append((i, (zh * 4 + x % 4) * 2 + c))
    return out


def mp_perm(f):
    out = []
    for i in range(8):
        y, zl = f(i // 2, i % 2)
        out.append((i, (y % 4) * 2 + zl))
    return out


CORE = seq_perm(lambda zh, x, c: (zh, x, 1 - c))
ZHI = seq_perm(lambda zh, x, c: (1 - zh, x, c))
XP = seq_perm(lambda zh, x, c: (zh, x + 1, c))
XM = seq_perm(lambda zh, x, c: (zh, x - 1, c))
X2 = seq_perm(lambda zh, x, c: (zh, x + 2, c))
ZLO = mp_perm(lambda y, zl: (y, 1 - zl))
YP = mp_perm(lambda y, zl: (y + 1, zl))
YM = mp_perm(lambda y, zl: (y - 1, zl))
YA = mp_perm(lambda y, zl: (y ^ 1, zl))
YB = mp_perm(lambda y, zl: (y ^ 3, zl))


def sp(v, perm):
    return lax.ppermute(v, "seq", perm)


def mpp(v, perm):
    return lax.ppermute(v, "mp", perm)


def nt(a, b):
    return lax.dot_general(a, b, (((1,), (1,)), ((), ())), preferred_element_type=F32)


def tn(a, b):
    return lax.dot_general(a, b, (((0,), (0,)), ((), ())), preferred_element_type=F32)


def nn(a, b):
    return lax.dot_general(a, b, (((1,), (0,)), ((), ())), preferred_element_type=F32)


def sds(shape, dtype=BF):
    return jax.ShapeDtypeStruct(shape, dtype)


def params(mib=63):
    return pltpu.CompilerParams(vmem_limit_bytes=mib << 20)


def cost(flops, nbytes, exps=0):
    return pl.CostEstimate(flops=int(flops), bytes_accessed=int(nbytes), transcendentals=exps)


def sliced(shape, index):
    if not index:
        return shape
    out = []
    for n, i in zip(shape, index):
        if not isinstance(i, int):
            out.append(n if isinstance(i, slice) else i.size)
    return tuple(out) + tuple(shape[len(index):])


def move(inputs, outs, plan, deps, name):
    def kernel(*refs):
        ins = refs[:len(inputs)]
        dst = refs[len(inputs) + len(deps):][:len(outs)]
        *bufs, sem = refs[len(inputs) + len(deps) + len(outs):]
        get = [pltpu.make_async_copy(ins[i].at[si] if si else ins[i], bufs[k], sem.at[k, 0])
               for k, (i, si, o, so) in enumerate(plan)]
        put = [pltpu.make_async_copy(bufs[k], dst[o].at[so] if so else dst[o], sem.at[k, 1])
               for k, (i, si, o, so) in enumerate(plan)]
        for c in get:
            c.start()
        for g, p in zip(get, put):
            g.wait()
            p.start()
        for p in put:
            p.wait()

    return pl.pallas_call(
        kernel,
        in_specs=[HBM] * (len(inputs) + len(deps)),
        out_specs=[HBM] * len(outs),
        out_shape=[sds(s) for s in outs],
        scratch_shapes=[pltpu.VMEM(sliced(inputs[i].shape, si), BF) for i, si, o, so in plan]
        + [pltpu.SemaphoreType.DMA((len(plan), 2))],
        compiler_params=params(),
        cost_estimate=cost(0, 4 << 20),
        name=name,
    )(*inputs, *deps)


def hold(values, deps):
    def kernel(*refs):
        pass

    n = len(values)
    return pl.pallas_call(
        kernel,
        in_specs=[HBM] * (n + len(deps)),
        out_specs=[HBM] * n,
        out_shape=[sds(v.shape, v.dtype) for v in values],
        input_output_aliases={k: k for k in range(n)},
        compiler_params=params(),
        cost_estimate=cost(0, 1 << 10),
        name="hold",
    )(*values, *deps)


def extend_kernel(p, gain, out):
    out[pl.ds(0, ROWS), :] = p[...]
    g = gain[...]
    hi = g.astype(BF).astype(F32)
    mid = (g - hi).astype(BF).astype(F32)
    row = lax.broadcasted_iota(jnp.int32, (16, 2 * DB), 0)
    tail = jnp.where(row == 0, hi, jnp.where(row == 1, mid, jnp.where(row == 2, g - hi - mid, 0.0)))
    out[pl.ds(ROWS, 16), :] = tail.astype(BF)


def extend(patches, gain):
    return pl.pallas_call(
        extend_kernel,
        out_shape=sds((EXT, 2 * DB)),
        compiler_params=params(),
        cost_estimate=cost(0, 2 << 20),
        name="extend",
    )(patches, gain.reshape(1, 2 * DB))


def merge(n, mean, m2, chunk):
    v = chunk.astype(F32)
    cm = jnp.sum(v, axis=1, keepdims=True) * (1.0 / 768)
    dv = v - cm
    c2 = jnp.sum(dv * dv, axis=1, keepdims=True)
    if n == 0:
        return cm, c2
    delta = cm - mean
    return mean + delta * (1.0 / (n + 1)), m2 + c2 + delta * delta * (768.0 * n / (n + 1))


def two_lanes(a, b):
    lane = lax.broadcasted_iota(jnp.int32, (ROWS, 128), 1)
    return jnp.where(lane == 0, a, jnp.where(lane == 1, b, 0.0))


def stats_kernel(*refs, nraw, ndeps):
    raws = refs[:nraw]
    out, buf, sem = refs[nraw + ndeps:]
    copies = [pltpu.make_async_copy(r, buf.at[j], sem.at[j]) for j, r in enumerate(raws)]
    for c in copies:
        c.start()
    mean = m2 = None
    for j, c in enumerate(copies):
        c.wait()
        mean, m2 = merge(j, mean, m2, buf[j, pl.ds(0, ROWS), :])
    out[...] = two_lanes(mean, m2)


def stats(raws, deps):
    n = len(raws)
    return pl.pallas_call(
        functools.partial(stats_kernel, nraw=n, ndeps=len(deps)),
        in_specs=[HBM] * (n + len(deps)),
        out_specs=VMEM,
        out_shape=sds((ROWS, 128), F32),
        scratch_shapes=[pltpu.VMEM((n, EXT, 2 * DB), BF), pltpu.SemaphoreType.DMA((n,))],
        compiler_params=params(),
        cost_estimate=cost(0, 4 << 20),
        name="row_stats",
    )(*raws, *deps)


def norm_kernel(idx, st, r0, r1, r2, r3, r4, r5, fm, fp, _, n_own, n_oth, st_out, raw, nrm, sr, so):
    core = idx[8]
    copies = []
    for j in range(2):
        copies.append(pltpu.make_async_copy(fm.at[j], raw.at[6 + j, pl.ds(0, HALF)], sr.at[j]))
        copies.append(pltpu.make_async_copy(fp.at[j], raw.at[6 + j, pl.ds(HALF, EXT - HALF)], sr.at[2 + j]))
    for j, r in enumerate((r0, r1, r2, r3, r4, r5)):
        copies.append(pltpu.make_async_copy(r, raw.at[j], sr.at[4 + j]))
    for c in copies:
        c.start()
    for c in copies[:4]:
        c.wait()
    mean, m2 = st[:, 0:1], st[:, 1:2]
    for j in range(2):
        mean, m2 = merge(6 + j, mean, m2, raw[6 + j, pl.ds(0, ROWS), :])
    rstd = lax.rsqrt(m2 * (1.0 / D) + EPS)
    st_out[...] = two_lanes(mean, rstd)
    out = []
    own = pl.ds(pl.multiple_of(core * DB, 128), DB)
    oth = pl.ds(pl.multiple_of((1 - core) * DB, 128), DB)
    for j in (6, 7, 0, 1, 2, 3, 4, 5):
        if j < 6:
            copies[4 + j].wait()
        tail = raw[j, pl.ds(ROWS, 16), :]
        t = tail.astype(F32)
        g = t[0:1] + t[1:2] + t[2:3]
        nrm[j, pl.ds(0, ROWS), :] = ((raw[j, pl.ds(0, ROWS), :].astype(F32) - mean) * rstd * g).astype(BF)
        nrm[j, pl.ds(ROWS, 16), :] = tail
        mine = [pltpu.make_async_copy(nrm.at[j, :, own], n_own.at[idx[j]], so.at[j, 0]),
                pltpu.make_async_copy(nrm.at[j, :, oth], n_oth.at[idx[j]], so.at[j, 1])]
        for c in mine:
            c.start()
        out += mine
    for c in out:
        c.wait()


def normalize(index, st, raws, after):
    return pl.pallas_call(
        norm_kernel,
        in_specs=[SMEM, VMEM] + [HBM] * (len(raws) + 1),
        out_specs=[HBM, HBM, VMEM],
        out_shape=[sds((8, EXT, DB)), sds((8, EXT, DB)), sds((ROWS, 128), F32)],
        scratch_shapes=[
            pltpu.VMEM((8, EXT, 2 * DB), BF),
            pltpu.VMEM((8, EXT, 2 * DB), BF),
            pltpu.SemaphoreType.DMA((10,)),
            pltpu.SemaphoreType.DMA((8, 2)),
        ],
        compiler_params=params(),
        cost_estimate=cost(0, 8 << 20),
        name="normalize",
    )(index, st, *raws, after)


NW = 16


def w_sources(refs):
    own, packed, pair, other = refs[:5], refs[5], refs[6:11], refs[11:16]
    out = [((own[k],) if k < 3 else own[3:5], (packed.at[k],)) for k in range(4)]
    return out + [((pair[k],), (other[k],)) if k < 3 else (pair[3:5], other[3:5]) for k in range(4)]


def w_copies(parts, buf, half, sem):
    out = []
    rows = DB // len(parts)
    for h, part in enumerate(parts):
        at = pl.ds(pl.multiple_of(half * DB + h * rows, 64), rows)
        out += [pltpu.make_async_copy(part.at[j], buf.at[at, pl.ds(j * DB, DB)], sem.at[h, j]) for j in range(3)]
    return out


def split(v):
    hi = v.astype(BF)
    return hi, (v - hi.astype(F32)).astype(BF)


def attn_kernel(idx, counts, n_own, n_oth, *refs):
    w_refs, refs = refs[:NW], refs[NW:]
    g_ref, out_ref, dqkv_ref, mom_ref, qkv, nv, wv, sn, sw = refs
    h = pl.program_id(0)

    @pl.when(h == 0)
    def _():
        core = idx[8]
        own = pl.ds(pl.multiple_of(core * DB, 128), DB)
        oth = pl.ds(pl.multiple_of((1 - core) * DB, 128), DB)
        copies = []
        for k, (mine, other) in enumerate(w_sources(w_refs)):
            m = idx[k]
            copies.append([pltpu.make_async_copy(n_own.at[m], nv.at[k, :, own], sn.at[k, 0]),
                           pltpu.make_async_copy(n_oth.at[m], nv.at[k, :, oth], sn.at[k, 1])]
                          + w_copies(mine, wv.at[k], core, sw.at[k, 0])
                          + w_copies(other, wv.at[k], 1 - core, sw.at[k, 1]))
            for c in copies[-1]:
                c.start()
        for k in range(8):
            for c in copies[k]:
                c.wait()
            t = nn(nv[k], wv[k])
            if k == 0:
                qkv[...] = t
            else:
                qkv[...] += t

    col = lambda j: pl.ds(pl.multiple_of((j * NH + h) * HD, 128), HD)
    q_ref, k_ref, v_ref = (qkv.at[:, col(j)] for j in range(3))
    e0 = counts[0]
    e1 = e0 + counts[1]
    e2 = e1 + counts[2]
    rid = lax.broadcasted_iota(jnp.int32, (ROWS, 1), 0)
    cid = lax.broadcasted_iota(jnp.int32, (1, ROWS), 1)
    img = lambda p: (p >= e0).astype(jnp.int32) + (p >= e1).astype(jnp.int32) + (p >= e2).astype(jnp.int32)
    same = img(rid) == img(cid)
    scale = HD ** (-0.5)
    q = q_ref[:ROWS, :] * scale
    k = k_ref[:ROWS, :]
    v = v_ref[:ROWS, :]
    qh, ql = split(q)
    kh, kl = split(k)
    vb = v.astype(BF)
    g = g_ref[...]
    s = nt(jnp.concatenate([qh, qh], 1), jnp.concatenate([kh, kl], 1)) + nt(ql, kh)
    s = jnp.where(same, s, -1e30)
    p = jnp.exp(s - jnp.max(s, axis=1, keepdims=True))
    p = p * (1.0 / jnp.sum(p, axis=1, keepdims=True))
    pb = p.astype(BF)
    out_ref[...] = nn(pb, vb).astype(BF)
    dp = nt(g, vb)
    dv = tn(pb, g)
    ds = p * (dp - jnp.sum(dp * p, axis=1, keepdims=True))
    dsb = ds.astype(BF)
    dq = (nn(dsb, kh) * scale).astype(BF)
    dk = tn(dsb, qh).astype(BF)
    dv = dv.astype(BF)
    dqkv_ref[0] = dq
    dqkv_ref[1] = dk
    dqkv_ref[2] = dv
    m1 = jnp.zeros((ROWS, 1), F32)
    m2 = jnp.zeros((ROWS, 1), F32)
    for d, r in ((dq, q_ref), (dk, k_ref), (dv, v_ref)):
        df = d.astype(F32)
        u = r[ROWS:ROWS + 1, :] + r[ROWS + 1:ROWS + 2, :] + r[ROWS + 2:ROWS + 3, :]
        m1 = m1 + jnp.sum(df * u, axis=1, keepdims=True)
        m2 = m2 + jnp.sum(df * r[:ROWS, :], axis=1, keepdims=True)
    mom = two_lanes(m1, m2)

    @pl.when(h == 0)
    def _():
        mom_ref[...] = mom

    @pl.when(h > 0)
    def _():
        mom_ref[...] += mom


def attend(index, counts, n_own, n_oth, ws, grad_out):
    return pl.pallas_call(
        attn_kernel,
        grid=(NH,),
        in_specs=[SMEM, SMEM] + [HBM] * (2 + NW) + [pl.BlockSpec((ROWS, HD), lambda h: (0, h))],
        out_specs=[
            pl.BlockSpec((ROWS, HD), lambda h: (0, h)),
            pl.BlockSpec((3, ROWS, HD), lambda h: (0, 0, h)),
            pl.BlockSpec((ROWS, 128), lambda h: (0, 0)),
        ],
        out_shape=[sds((ROWS, DB)), sds((3, ROWS, DB)), sds((ROWS, 128), F32)],
        scratch_shapes=[
            pltpu.VMEM((EXT, CW), F32),
            pltpu.VMEM((8, EXT, 2 * DB), BF),
            pltpu.VMEM((8, 2 * DB, CW), BF),
            pltpu.SemaphoreType.DMA((8, 2)),
            pltpu.SemaphoreType.DMA((8, 2, 2, 3)),
        ],
        compiler_params=params(),
        cost_estimate=cost(2 * EXT * D * CW, 28 << 20, NH * ROWS * ROWS),
        name="attention",
    )(index, counts, n_own, n_oth, *ws, grad_out)


def grads_kernel(idx, d1, d2, *refs, ny, nx, ndeps, ysplit, xsplit):
    w_refs, (n1, n2), refs = refs[:NW], refs[NW:NW + 2], refs[NW + 2 + ndeps:]
    outs = list(refs[:-8])
    wv, nv, dcat, oy, ox, sd, si, so = refs[-8:]
    core = idx[0]
    dc = [pltpu.make_async_copy(d1.at[j], dcat.at[pl.ds(0, ROWS), pl.ds(j * DB, DB)], sd.at[0, j]) for j in range(3)]
    if nx:
        dc += [pltpu.make_async_copy(d2.at[j], dcat.at[pl.ds(ROWS, ROWS), pl.ds(j * DB, DB)], sd.at[1, j])
               for j in range(3)]
    for c in dc[:3]:
        c.start()
    sources = w_sources(w_refs)
    for i in range(ny):
        a = idx[1 + i]
        for k, (mine, other) in enumerate(sources):
            @pl.when(a == k)
            def _():
                for c in w_copies(mine, wv.at[i], core, si.at[i, 0]) + w_copies(other, wv.at[i], 1 - core, si.at[i, 1]):
                    c.start()
    for c in dc[3:]:
        c.start()
    ncs = []
    for i in range(nx):
        m = idx[1 + ny + i]
        ncs.append([pltpu.make_async_copy(n1.at[m, pl.ds(0, ROWS)], nv.at[i, pl.ds(0, ROWS)], si.at[ny + i, 0, 0, 0]),
                    pltpu.make_async_copy(n2.at[m, pl.ds(0, ROWS)], nv.at[i, pl.ds(ROWS, ROWS)], si.at[ny + i, 1, 0, 0])])
        for c in ncs[-1]:
            c.start()
    pending = []

    def put(src, dst, sem):
        c = pltpu.make_async_copy(src, dst, sem)
        c.start()
        pending.append(c)

    for c in dc[:3]:
        c.wait()
    for i in range(ny):
        a = idx[1 + i]
        for e in range(2):
            halves = jnp.logical_or(a == 7, a == 3) if e == 0 else a == 7

            @pl.when(halves)
            def _():
                for c in w_copies(sources[7][e], wv.at[i], e, si.at[i, e]):
                    c.wait()

            @pl.when(jnp.logical_not(halves))
            def _():
                for c in w_copies(sources[0][e], wv.at[i], e, si.at[i, e]):
                    c.wait()
        oy[i] = nt(dcat[pl.ds(0, ROWS), :], wv[i]).astype(BF)
        if i in ysplit:
            put(oy.at[i, pl.ds(0, HALF)], outs.pop(0), so.at[i, 0])
            put(oy.at[i, pl.ds(HALF, HALF)], outs.pop(0), so.at[i, 1])
        else:
            put(oy.at[i], outs.pop(0), so.at[i, 0])
    for c in dc[3:]:
        c.wait()
    for i in range(nx):
        for c in ncs[i]:
            c.wait()
        t = tn(nv[i], dcat[...]).astype(BF)
        for j in range(3):
            ox[i, j] = t[:, j * DB:(j + 1) * DB]
        if i in xsplit:
            put(ox.at[i, :, pl.ds(0, HB)], outs.pop(0), so.at[ny + i, 0])
            put(ox.at[i, :, pl.ds(HB, HB)], outs.pop(0), so.at[ny + i, 1])
        else:
            put(ox.at[i], outs.pop(0), so.at[ny + i, 0])
    for c in pending:
        c.wait()


def grads(core, ysrc, xsrc, dqkv, d_other, ws, normed, other, deps, ysplit=(), xsplit=()):
    ny, nx = len(ysrc), len(xsrc)
    shapes = []
    for i in range(ny):
        shapes += [(HALF, 2 * DB)] * 2 if i in ysplit else [(ROWS, 2 * DB)]
    for i in range(nx):
        shapes += [(3, HB, DB)] * 2 if i in xsplit else [(3, DB, DB)]
    deps = list(deps)
    return pl.pallas_call(
        functools.partial(grads_kernel, ny=ny, nx=nx, ndeps=len(deps), ysplit=ysplit, xsplit=xsplit),
        in_specs=[SMEM] + [HBM] * (4 + NW + len(deps)),
        out_specs=[HBM] * len(shapes),
        out_shape=[sds(s) for s in shapes],
        scratch_shapes=[
            pltpu.VMEM((max(ny, 1), 2 * DB, CW), BF),
            pltpu.VMEM((max(nx, 1), 2 * ROWS, DB), BF),
            pltpu.VMEM((2 * ROWS, CW), BF),
            pltpu.VMEM((max(ny, 1), ROWS, 2 * DB), BF),
            pltpu.VMEM((max(nx, 1), 3, DB, DB), BF),
            pltpu.SemaphoreType.DMA((2, 3)),
            pltpu.SemaphoreType.DMA((ny + nx, 2, 2, 3)),
            pltpu.SemaphoreType.DMA((ny + nx, 2)),
        ],
        compiler_params=params(),
        cost_estimate=cost(2 * (ny + nx) * ROWS * 768 * CW, (ny + nx) * 3 << 20),
        name="grads",
    )(ivec(core, *ysrc, *xsrc), dqkv, d_other, *ws, normed, other, *deps)


def sum_kernel(a, b, c, *refs):
    refs[-1][...] = (a[...].astype(F32) + b[...].astype(F32) + c[...].astype(F32)).astype(BF)


def sum_blocks(vs, deps):
    shape = vs[0].shape
    spec = (pl.BlockSpec((ROWS // 3, 2 * DB), lambda i: (i, 0)) if len(shape) == 2
            else pl.BlockSpec((1, DB, DB), lambda i: (i, 0, 0)))
    return pl.pallas_call(
        sum_kernel,
        grid=(3,),
        in_specs=[spec] * 3 + [HBM] * len(deps),
        out_specs=spec,
        out_shape=sds(shape),
        compiler_params=params(),
        cost_estimate=cost(0, 4 << 20),
        name="sum_blocks",
    )(*vs, *deps)


def add_kernel(a1, a2, b1, b2, *refs):
    for a, b, o in zip((a1, a2), (b1, b2), refs[-2:]):
        o[...] = (a[...].astype(F32) + b[...].astype(F32)).astype(BF)


def add_halves(blocks, arrived, deps):
    shape = arrived[0].shape
    whole = pl.BlockSpec(shape, lambda i: (0,) * len(shape))
    if len(shape) == 2:
        halves = [pl.BlockSpec(shape, lambda i: (0, 0)), pl.BlockSpec(shape, lambda i: (1, 0))]
    else:
        halves = [pl.BlockSpec(shape, lambda i: (0, 0, 0)), pl.BlockSpec(shape, lambda i: (0, 1, 0))]
    return pl.pallas_call(
        add_kernel,
        grid=(1,),
        in_specs=halves + [whole] * 2 + [HBM] * len(deps),
        out_specs=halves,
        out_shape=[sds(v.shape) for v in blocks],
        input_output_aliases={0: 0, 1: 1},
        compiler_params=params(),
        cost_estimate=cost(0, 3 << 20),
        name="add_halves",
    )(*blocks, *arrived, *deps)


def accumulate(a, b, deps):
    def kernel(a_ref, b_ref, *refs):
        refs[-1][...] = a_ref[...] + b_ref[...]

    return pl.pallas_call(
        kernel,
        in_specs=[VMEM, VMEM] + [HBM] * len(deps),
        out_specs=VMEM,
        out_shape=sds(a.shape, F32),
        compiler_params=params(),
        cost_estimate=cost(0, 1 << 12),
        name="accumulate",
    )(a, b, *deps)


def ivec(*v):
    return jnp.stack([jnp.asarray(e, jnp.int32) for e in v])


def local(patches, gain, w_qkv, counts, grad_out):
    si, mi = lax.axis_index("seq"), lax.axis_index("mp")
    core, x, zh = si % 2, (si // 2) % 4, si // 8
    y, zl = mi // 2, mi % 2
    mw = lambda dx, dz: jnp.where(dz == 0, zh, 1 - zh) * 4 + (x + dx) % 4
    mx = lambda dy, dz: ((y + dy) % 4) * 2 + jnp.where(dz == 0, zl, 1 - zl)
    rows, wshape = (EXT, 2 * DB), (3, DB, DB)
    lo, hi = (slice(None), pl.ds(0, HB)), (slice(None), pl.ds(HB, HB))
    first, rest = (pl.ds(0, HALF),), (pl.ds(HALF, EXT - HALF),)

    p0 = extend(patches, gain)
    w = jnp.transpose(w_qkv, (1, 0, 2))
    p_m, p_p, pz = mpp(p0, YP), mpp(p0, YM), mpp(p0, ZLO)
    w_m, w_p = sp(w, XP), sp(w, XM)
    pz1, w1 = move([pz, w], [rows, wshape], [(0, None, 0, None), (1, None, 1, None)], [p_m, p_p], "gate_y1")
    pz_m, pz_p = mpp(pz1, YP), mpp(pz1, YM)
    wz = sp(w1, ZHI)
    w_lo, w_hi = move([w_m, w_p], [(3, HB, DB)] * 2, [(0, lo, 0, None), (1, hi, 1, None)], [pz1], "gate_x1")
    wf_m, wf_p = sp(w_lo, XP), sp(w_hi, XM)
    fu, fd = move(
        [p_m, p_p, pz_m, pz_p], [(2, HALF, 2 * DB), (2, EXT - HALF, 2 * DB)],
        [(0, first, 0, (0,)), (2, first, 0, (1,)), (1, rest, 1, (0,)), (3, rest, 1, (1,))], [w_lo], "gate_y2")
    f_m, f_p = mpp(fu, YP), mpp(fd, YM)
    wz1, w2 = move([wz, w1], [wshape, wshape], [(0, None, 0, None), (1, None, 1, None)], [wf_m, wf_p, fu], "gate_x2")
    wz_m, wz_p = sp(wz1, XP), sp(wz1, XM)
    (w4,) = move(
        [w2, w_m, w_p, wf_m, wf_p], [(4,) + wshape],
        [(0, None, 0, (0,)), (1, None, 0, (1,)), (2, None, 0, (2,)), (3, None, 0, (3,) + lo), (4, None, 0, (3,) + hi)],
        [wz1], "pack")
    o_w = sp(w4, CORE)
    st = stats([p0, pz, p_m, p_p, pz_m, pz_p], [wz1])
    wz_lo, wz_hi, wz2 = move(
        [wz_m, wz_p, wz1], [(3, HB, DB), (3, HB, DB), wshape],
        [(0, lo, 0, None), (1, hi, 1, None), (2, None, 2, None)],
        [f_m, f_p, o_w, st], "gate_x3")
    wzf_m, wzf_p = sp(wz_lo, XP), sp(wz_hi, XM)
    o_z, o_zm, o_zp = (sp(v, CORE) for v in (wz2, wz_m, wz_p))
    index = ivec(mx(0, 0), mx(0, 1), mx(-1, 0), mx(1, 0), mx(-1, 1), mx(1, 1), mx(2, 0), mx(2, 1), core)
    n_own, n_oth, st = normalize(index, st, [p0, pz, p_m, p_p, pz_m, pz_p, f_m, f_p], wz_lo)
    mean, rstd = st[:, 0:1], st[:, 1:2]
    wzf_m, wzf_p, n_oth = hold([wzf_m, wzf_p, n_oth], [o_z])
    o_zfm, o_zfp = sp(wzf_m, CORE), sp(wzf_p, CORE)
    (n_oth,) = hold([n_oth], [o_zfm, o_zfp, o_zm, o_zp])
    n_other = sp(n_oth, CORE)
    ws = [w2, w_m, w_p, wf_m, wf_p, o_w,
          wz2, wz_m, wz_p, wzf_m, wzf_p, o_z, o_zm, o_zp, o_zfm, o_zfp]
    windex = ivec(mw(0, 0), mw(-1, 0), mw(1, 0), mw(2, 0), mw(0, 1), mw(-1, 1), mw(1, 1), mw(2, 1), core)
    heads_out, dqkv, mom = attend(windex, counts.reshape(4), n_own, n_oth, ws, grad_out)

    d_other = sp(dqkv, CORE)
    mom = jnp.concatenate([mom[:, 0], mom[:, 1]]).reshape(9, 128)

    def source(dy, dz):
        m = mx(dy, dz)
        dx = (m % 4 - x) % 4
        return jnp.where(dx == 3, 1, jnp.where(dx == 1, 2, jnp.where(dx == 2, 3, 0))) + jnp.where(m // 4 == zh, 0, 4)

    def blocks(yb, xb, deps, **kw):
        return grads(core, [source(*b) for b in yb], [mw(*b) for b in xb], dqkv, d_other, ws, n_own, n_other, deps, **kw)

    y2p_lo, y2p_hi = blocks([(2, 1)], [], [], ysplit=(0,))
    h_m, h_p = mpp(y2p_lo, YP), mpp(y2p_hi, YM)
    x2p_lo, x2p_hi = blocks([], [(2, 1)], [y2p_lo], xsplit=(0,))
    v_m, v_p = sp(x2p_lo, XP), sp(x2p_hi, XM)
    mom1 = accumulate(mom, mpp(mom, ZLO), [x2p_lo])
    yu, yd = blocks([(1, 1), (-1, 1)], [], [x2p_lo])
    yu, yd = add_halves([yu, yd], [h_m, h_p], [])
    ya1, ya2 = mpp(yu, YP), mpp(yd, YM)
    xu, xd = blocks([], [(1, 1), (-1, 1)], [yu])
    xu, xd = add_halves([xu, xd], [v_m, v_p], [])
    xa1, xa2 = sp(xu, XP), sp(xd, XM)
    y0p, y2_lo, y2_hi, y1u, y1d = blocks([(0, 1), (2, 0), (1, 0), (-1, 0)], [], [xu], ysplit=(1,))
    mom2 = accumulate(mom1, mpp(mom1, YA), [y0p])
    y_out = sum_blocks([y0p, ya1, ya2], [mom2])
    yz = mpp(y_out, ZLO)
    h_m, h_p = mpp(y2_lo, YP), mpp(y2_hi, YM)
    x0p, x2_lo, x2_hi, x1u, x1d = blocks([], [(0, 1), (2, 0), (1, 0), (-1, 0)], [y_out], xsplit=(1,))
    x_out = sum_blocks([x0p, xa1, xa2], [])
    v_m, v_p = sp(x2_lo, XP), sp(x2_hi, XM)
    y0, x0 = blocks([(0, 0)], [(0, 0)], [x_out])
    mom3 = accumulate(mom2, mpp(mom2, YB), [y0])
    yu, yd = add_halves([y1u, y1d], [h_m, h_p], [y0, mom3])
    yb1, yb2 = mpp(yu, YP), mpp(yd, YM)
    xu, xd = add_halves([x1u, x1d], [v_m, v_p], [yu, yz])
    xb1, xb2 = sp(xu, XP), sp(xd, XM)
    xz = sp(x_out, ZHI)

    f = lambda v: v.astype(F32)
    mom = mom3.reshape(2 * ROWS) / D
    gn = f(y0) + f(yb1) + f(yb2) + f(yz)
    xhat = (f(patches) - mean) * rstd
    gg = jnp.sum(gn * xhat, axis=0)
    for perm in (CORE, ZHI):
        gg = gg + sp(gg, perm)
    gg = (gg + sp(gg, X2)) + (sp(gg, XP) + sp(gg, XM))
    grad_p = ((gn * gain[None, :] - mom[:ROWS, None] - xhat * mom[ROWS:, None]) * rstd).astype(BF)
    gw = jnp.transpose(f(x0) + f(xb1) + f(xb2) + f(xz), (1, 0, 2))
    return heads_out, grad_p, gg, gw


def solution(mesh):
    placed = (P("seq", "mp"), P("mp"), P("seq", None, "mp"), P("seq", None), P("seq", "mp"))
    return jax.shard_map(
        local,
        mesh=mesh,
        in_specs=placed,
        out_specs=(P("seq", "mp"), P("seq", "mp"), P("mp"), P("seq", None, "mp")),
        check_vma=False,
    )
```

```python
import functools

import jax
import jax.numpy as jnp
from jax import lax
from jax.experimental import pallas as pl
from jax.experimental.pallas import tpu as pltpu
from jax.sharding import PartitionSpec as P

HD = 128
NH = 3
ROWS = 576
HALF = ROWS // 2
EXT = ROWS + 16
DB = 384
HB = DB // 2
D = 6144
CW = 3 * DB
EPS = 1e-06
BF = jnp.bfloat16
F32 = jnp.float32
HBM = pl.BlockSpec(memory_space=pltpu.HBM)
VMEM = pl.BlockSpec(memory_space=pltpu.VMEM)
SMEM = pl.BlockSpec(memory_space=pltpu.SMEM)


def seq_perm(f):
    out = []
    for i in range(16):
        zh, x, c = f(i // 8, (i // 2) % 4, i % 2)
        out.append((i, (zh * 4 + x % 4) * 2 + c))
    return out


def mp_perm(f):
    out = []
    for i in range(8):
        y, zl = f(i // 2, i % 2)
        out.append((i, (y % 4) * 2 + zl))
    return out


CORE = seq_perm(lambda zh, x, c: (zh, x, 1 - c))
ZHI = seq_perm(lambda zh, x, c: (1 - zh, x, c))
XP = seq_perm(lambda zh, x, c: (zh, x + 1, c))
XM = seq_perm(lambda zh, x, c: (zh, x - 1, c))
X2 = seq_perm(lambda zh, x, c: (zh, x + 2, c))
ZLO = mp_perm(lambda y, zl: (y, 1 - zl))
YP = mp_perm(lambda y, zl: (y + 1, zl))
YM = mp_perm(lambda y, zl: (y - 1, zl))
YA = mp_perm(lambda y, zl: (y ^ 1, zl))
YB = mp_perm(lambda y, zl: (y ^ 3, zl))


def sp(v, perm):
    return lax.ppermute(v, "seq", perm)


def mpp(v, perm):
    return lax.ppermute(v, "mp", perm)


def nt(a, b):
    return lax.dot_general(a, b, (((1,), (1,)), ((), ())), preferred_element_type=F32)


def tn(a, b):
    return lax.dot_general(a, b, (((0,), (0,)), ((), ())), preferred_element_type=F32)


def nn(a, b):
    return lax.dot_general(a, b, (((1,), (0,)), ((), ())), preferred_element_type=F32)


def sds(shape, dtype=BF):
    return jax.ShapeDtypeStruct(shape, dtype)


def params(mib=63):
    return pltpu.CompilerParams(vmem_limit_bytes=mib << 20)


def cost(flops, nbytes, exps=0):
    return pl.CostEstimate(flops=int(flops), bytes_accessed=int(nbytes), transcendentals=exps)


def sliced(shape, index):
    if not index:
        return shape
    out = []
    for n, i in zip(shape, index):
        if not isinstance(i, int):
            out.append(n if isinstance(i, slice) else i.size)
    return tuple(out) + tuple(shape[len(index):])


def move(inputs, outs, plan, deps, name):
    def kernel(*refs):
        ins = refs[:len(inputs)]
        dst = refs[len(inputs) + len(deps):][:len(outs)]
        *bufs, sem = refs[len(inputs) + len(deps) + len(outs):]
        get = [pltpu.make_async_copy(ins[i].at[si] if si else ins[i], bufs[k], sem.at[k, 0])
               for k, (i, si, o, so) in enumerate(plan)]
        put = [pltpu.make_async_copy(bufs[k], dst[o].at[so] if so else dst[o], sem.at[k, 1])
               for k, (i, si, o, so) in enumerate(plan)]
        for c in get:
            c.start()
        for g, p in zip(get, put):
            g.wait()
            p.start()
        for p in put:
            p.wait()

    return pl.pallas_call(
        kernel,
        in_specs=[HBM] * (len(inputs) + len(deps)),
        out_specs=[HBM] * len(outs),
        out_shape=[sds(s) for s in outs],
        scratch_shapes=[pltpu.VMEM(sliced(inputs[i].shape, si), BF) for i, si, o, so in plan]
        + [pltpu.SemaphoreType.DMA((len(plan), 2))],
        compiler_params=params(),
        cost_estimate=cost(0, 4 << 20),
        name=name,
    )(*inputs, *deps)


def hold(values, deps):
    def kernel(*refs):
        pass

    n = len(values)
    return pl.pallas_call(
        kernel,
        in_specs=[HBM] * (n + len(deps)),
        out_specs=[HBM] * n,
        out_shape=[sds(v.shape, v.dtype) for v in values],
        input_output_aliases={k: k for k in range(n)},
        compiler_params=params(),
        cost_estimate=cost(0, 1 << 10),
        name="hold",
    )(*values, *deps)


def extend_kernel(p, gain, out):
    out[pl.ds(0, ROWS), :] = p[...]
    g = gain[...]
    hi = g.astype(BF).astype(F32)
    mid = (g - hi).astype(BF).astype(F32)
    row = lax.broadcasted_iota(jnp.int32, (16, 2 * DB), 0)
    tail = jnp.where(row == 0, hi, jnp.where(row == 1, mid, jnp.where(row == 2, g - hi - mid, 0.0)))
    out[pl.ds(ROWS, 16), :] = tail.astype(BF)


def extend(patches, gain):
    return pl.pallas_call(
        extend_kernel,
        out_shape=sds((EXT, 2 * DB)),
        compiler_params=params(),
        cost_estimate=cost(0, 2 << 20),
        name="extend",
    )(patches, gain.reshape(1, 2 * DB))


def merge(n, mean, m2, chunk):
    v = chunk.astype(F32)
    cm = jnp.sum(v, axis=1, keepdims=True) * (1.0 / 768)
    dv = v - cm
    c2 = jnp.sum(dv * dv, axis=1, keepdims=True)
    if n == 0:
        return cm, c2
    delta = cm - mean
    return mean + delta * (1.0 / (n + 1)), m2 + c2 + delta * delta * (768.0 * n / (n + 1))


def two_lanes(a, b):
    lane = lax.broadcasted_iota(jnp.int32, (ROWS, 128), 1)
    return jnp.where(lane == 0, a, jnp.where(lane == 1, b, 0.0))


def stats_kernel(*refs, nraw, ndeps):
    raws = refs[:nraw]
    out, buf, sem = refs[nraw + ndeps:]
    copies = [pltpu.make_async_copy(r, buf.at[j], sem.at[j]) for j, r in enumerate(raws)]
    for c in copies:
        c.start()
    mean = m2 = None
    for j, c in enumerate(copies):
        c.wait()
        mean, m2 = merge(j, mean, m2, buf[j, pl.ds(0, ROWS), :])
    out[...] = two_lanes(mean, m2)


def stats(raws, deps):
    n = len(raws)
    return pl.pallas_call(
        functools.partial(stats_kernel, nraw=n, ndeps=len(deps)),
        in_specs=[HBM] * (n + len(deps)),
        out_specs=VMEM,
        out_shape=sds((ROWS, 128), F32),
        scratch_shapes=[pltpu.VMEM((n, EXT, 2 * DB), BF), pltpu.SemaphoreType.DMA((n,))],
        compiler_params=params(),
        cost_estimate=cost(0, 4 << 20),
        name="row_stats",
    )(*raws, *deps)


def norm_kernel(idx, st, r0, r1, r2, r3, r4, r5, fm, fp, _, n_own, n_oth, st_out, raw, nrm, sr, so):
    core = idx[8]
    copies = []
    for j in range(2):
        copies.append(pltpu.make_async_copy(fm.at[j], raw.at[6 + j, pl.ds(0, HALF)], sr.at[j]))
        copies.append(pltpu.make_async_copy(fp.at[j], raw.at[6 + j, pl.ds(HALF, EXT - HALF)], sr.at[2 + j]))
    for j, r in enumerate((r0, r1, r2, r3, r4, r5)):
        copies.append(pltpu.make_async_copy(r, raw.at[j], sr.at[4 + j]))
    for c in copies:
        c.start()
    for c in copies[:4]:
        c.wait()
    mean, m2 = st[:, 0:1], st[:, 1:2]
    for j in range(2):
        mean, m2 = merge(6 + j, mean, m2, raw[6 + j, pl.ds(0, ROWS), :])
    rstd = lax.rsqrt(m2 * (1.0 / D) + EPS)
    st_out[...] = two_lanes(mean, rstd)
    out = []
    own = pl.ds(pl.multiple_of(core * DB, 128), DB)
    oth = pl.ds(pl.multiple_of((1 - core) * DB, 128), DB)
    for j in (6, 7, 0, 1, 2, 3, 4, 5):
        if j < 6:
            copies[4 + j].wait()
        tail = raw[j, pl.ds(ROWS, 16), :]
        t = tail.astype(F32)
        g = t[0:1] + t[1:2] + t[2:3]
        nrm[j, pl.ds(0, ROWS), :] = ((raw[j, pl.ds(0, ROWS), :].astype(F32) - mean) * rstd * g).astype(BF)
        nrm[j, pl.ds(ROWS, 16), :] = tail
        mine = [pltpu.make_async_copy(nrm.at[j, :, own], n_own.at[idx[j]], so.at[j, 0]),
                pltpu.make_async_copy(nrm.at[j, :, oth], n_oth.at[idx[j]], so.at[j, 1])]
        for c in mine:
            c.start()
        out += mine
    for c in out:
        c.wait()


def normalize(index, st, raws, after):
    return pl.pallas_call(
        norm_kernel,
        in_specs=[SMEM, VMEM] + [HBM] * (len(raws) + 1),
        out_specs=[HBM, HBM, VMEM],
        out_shape=[sds((8, EXT, DB)), sds((8, EXT, DB)), sds((ROWS, 128), F32)],
        scratch_shapes=[
            pltpu.VMEM((8, EXT, 2 * DB), BF),
            pltpu.VMEM((8, EXT, 2 * DB), BF),
            pltpu.SemaphoreType.DMA((10,)),
            pltpu.SemaphoreType.DMA((8, 2)),
        ],
        compiler_params=params(),
        cost_estimate=cost(0, 8 << 20),
        name="normalize",
    )(index, st, *raws, after)


NW = 16


def w_sources(refs):
    own, packed, pair, other = refs[:5], refs[5], refs[6:11], refs[11:16]
    out = [((own[k],) if k < 3 else own[3:5], (packed.at[k],)) for k in range(4)]
    return out + [((pair[k],), (other[k],)) if k < 3 else (pair[3:5], other[3:5]) for k in range(4)]


def w_copies(parts, buf, half, sem):
    out = []
    rows = DB // len(parts)
    for h, part in enumerate(parts):
        at = pl.ds(pl.multiple_of(half * DB + h * rows, 64), rows)
        out += [pltpu.make_async_copy(part.at[j], buf.at[at, pl.ds(j * DB, DB)], sem.at[h, j]) for j in range(3)]
    return out


def split(v):
    hi = v.astype(BF)
    return hi, (v - hi.astype(F32)).astype(BF)


def attn_kernel(idx, counts, n_own, n_oth, *refs):
    w_refs, refs = refs[:NW], refs[NW:]
    g_ref, out_ref, dqkv_ref, mom_ref, qkv, nv, wv, sn, sw = refs
    h = pl.program_id(0)

    @pl.when(h == 0)
    def _():
        core = idx[8]
        own = pl.ds(pl.multiple_of(core * DB, 128), DB)
        oth = pl.ds(pl.multiple_of((1 - core) * DB, 128), DB)
        copies = []
        for k, (mine, other) in enumerate(w_sources(w_refs)):
            m = idx[k]
            copies.append([pltpu.make_async_copy(n_own.at[m], nv.at[k, :, own], sn.at[k, 0]),
                           pltpu.make_async_copy(n_oth.at[m], nv.at[k, :, oth], sn.at[k, 1])]
                          + w_copies(mine, wv.at[k], core, sw.at[k, 0])
                          + w_copies(other, wv.at[k], 1 - core, sw.at[k, 1]))
            for c in copies[-1]:
                c.start()
        for k in range(8):
            for c in copies[k]:
                c.wait()
            t = nn(nv[k], wv[k])
            if k == 0:
                qkv[...] = t
            else:
                qkv[...] += t

    col = lambda j: pl.ds(pl.multiple_of((j * NH + h) * HD, 128), HD)
    q_ref, k_ref, v_ref = (qkv.at[:, col(j)] for j in range(3))
    e0 = counts[0]
    e1 = e0 + counts[1]
    e2 = e1 + counts[2]
    rid = lax.broadcasted_iota(jnp.int32, (ROWS, 1), 0)
    cid = lax.broadcasted_iota(jnp.int32, (1, ROWS), 1)
    img = lambda p: (p >= e0).astype(jnp.int32) + (p >= e1).astype(jnp.int32) + (p >= e2).astype(jnp.int32)
    same = img(rid) == img(cid)
    scale = HD ** (-0.5)
    q = q_ref[:ROWS, :] * scale
    k = k_ref[:ROWS, :]
    v = v_ref[:ROWS, :]
    qh, ql = split(q)
    kh, kl = split(k)
    vb = v.astype(BF)
    g = g_ref[...]
    s = nt(jnp.concatenate([qh, qh], 1), jnp.concatenate([kh, kl], 1)) + nt(ql, kh)
    s = jnp.where(same, s, -1e30)
    p = jnp.exp(s - jnp.max(s, axis=1, keepdims=True))
    p = p * (1.0 / jnp.sum(p, axis=1, keepdims=True))
    pb = p.astype(BF)
    out_ref[...] = nn(pb, vb).astype(BF)
    dp = nt(g, vb)
    dv = tn(pb, g)
    ds = p * (dp - jnp.sum(dp * p, axis=1, keepdims=True))
    dsb = ds.astype(BF)
    dq = (nn(dsb, kh) * scale).astype(BF)
    dk = tn(dsb, qh).astype(BF)
    dv = dv.astype(BF)
    dqkv_ref[0] = dq
    dqkv_ref[1] = dk
    dqkv_ref[2] = dv
    m1 = jnp.zeros((ROWS, 1), F32)
    m2 = jnp.zeros((ROWS, 1), F32)
    for d, r in ((dq, q_ref), (dk, k_ref), (dv, v_ref)):
        df = d.astype(F32)
        u = r[ROWS:ROWS + 1, :] + r[ROWS + 1:ROWS + 2, :] + r[ROWS + 2:ROWS + 3, :]
        m1 = m1 + jnp.sum(df * u, axis=1, keepdims=True)
        m2 = m2 + jnp.sum(df * r[:ROWS, :], axis=1, keepdims=True)
    mom = two_lanes(m1, m2)

    @pl.when(h == 0)
    def _():
        mom_ref[...] = mom

    @pl.when(h > 0)
    def _():
        mom_ref[...] += mom


def attend(index, counts, n_own, n_oth, ws, grad_out):
    return pl.pallas_call(
        attn_kernel,
        grid=(NH,),
        in_specs=[SMEM, SMEM] + [HBM] * (2 + NW) + [pl.BlockSpec((ROWS, HD), lambda h: (0, h))],
        out_specs=[
            pl.BlockSpec((ROWS, HD), lambda h: (0, h)),
            pl.BlockSpec((3, ROWS, HD), lambda h: (0, 0, h)),
            pl.BlockSpec((ROWS, 128), lambda h: (0, 0)),
        ],
        out_shape=[sds((ROWS, DB)), sds((3, ROWS, DB)), sds((ROWS, 128), F32)],
        scratch_shapes=[
            pltpu.VMEM((EXT, CW), F32),
            pltpu.VMEM((8, EXT, 2 * DB), BF),
            pltpu.VMEM((8, 2 * DB, CW), BF),
            pltpu.SemaphoreType.DMA((8, 2)),
            pltpu.SemaphoreType.DMA((8, 2, 2, 3)),
        ],
        compiler_params=params(),
        cost_estimate=cost(2 * EXT * D * CW, 28 << 20, NH * ROWS * ROWS),
        name="attention",
    )(index, counts, n_own, n_oth, *ws, grad_out)


def grads_kernel(idx, d1, d2, *refs, ny, nx, ndeps, ysplit, xsplit):
    w_refs, (n1, n2), refs = refs[:NW], refs[NW:NW + 2], refs[NW + 2 + ndeps:]
    outs = list(refs[:-8])
    wv, nv, dcat, oy, ox, sd, si, so = refs[-8:]
    core = idx[0]
    dc = [pltpu.make_async_copy(d1.at[j], dcat.at[pl.ds(0, ROWS), pl.ds(j * DB, DB)], sd.at[0, j]) for j in range(3)]
    if nx:
        dc += [pltpu.make_async_copy(d2.at[j], dcat.at[pl.ds(ROWS, ROWS), pl.ds(j * DB, DB)], sd.at[1, j])
               for j in range(3)]
    for c in dc[:3]:
        c.start()
    sources = w_sources(w_refs)
    for i in range(ny):
        a = idx[1 + i]
        for k, (mine, other) in enumerate(sources):
            @pl.when(a == k)
            def _():
                for c in w_copies(mine, wv.at[i], core, si.at[i, 0]) + w_copies(other, wv.at[i], 1 - core, si.at[i, 1]):
                    c.start()
    for c in dc[3:]:
        c.start()
    ncs = []
    for i in range(nx):
        m = idx[1 + ny + i]
        ncs.append([pltpu.make_async_copy(n1.at[m, pl.ds(0, ROWS)], nv.at[i, pl.ds(0, ROWS)], si.at[ny + i, 0, 0, 0]),
                    pltpu.make_async_copy(n2.at[m, pl.ds(0, ROWS)], nv.at[i, pl.ds(ROWS, ROWS)], si.at[ny + i, 1, 0, 0])])
        for c in ncs[-1]:
            c.start()
    pending = []

    def put(src, dst, sem):
        c = pltpu.make_async_copy(src, dst, sem)
        c.start()
        pending.append(c)

    for c in dc[:3]:
        c.wait()
    for i in range(ny):
        a = idx[1 + i]
        for e in range(2):
            halves = jnp.logical_or(a == 7, a == 3) if e == 0 else a == 7

            @pl.when(halves)
            def _():
                for c in w_copies(sources[7][e], wv.at[i], e, si.at[i, e]):
                    c.wait()

            @pl.when(jnp.logical_not(halves))
            def _():
                for c in w_copies(sources[0][e], wv.at[i], e, si.at[i, e]):
                    c.wait()
        oy[i] = nt(dcat[pl.ds(0, ROWS), :], wv[i]).astype(BF)
        if i in ysplit:
            put(oy.at[i, pl.ds(0, HALF)], outs.pop(0), so.at[i, 0])
            put(oy.at[i, pl.ds(HALF, HALF)], outs.pop(0), so.at[i, 1])
        else:
            put(oy.at[i], outs.pop(0), so.at[i, 0])
    for c in dc[3:]:
        c.wait()
    for i in range(nx):
        for c in ncs[i]:
            c.wait()
        t = tn(nv[i], dcat[...]).astype(BF)
        for j in range(3):
            ox[i, j] = t[:, j * DB:(j + 1) * DB]
        if i in xsplit:
            put(ox.at[i, :, pl.ds(0, HB)], outs.pop(0), so.at[ny + i, 0])
            put(ox.at[i, :, pl.ds(HB, HB)], outs.pop(0), so.at[ny + i, 1])
        else:
            put(ox.at[i], outs.pop(0), so.at[ny + i, 0])
    for c in pending:
        c.wait()


def grads(core, ysrc, xsrc, dqkv, d_other, ws, normed, other, deps, ysplit=(), xsplit=()):
    ny, nx = len(ysrc), len(xsrc)
    shapes = []
    for i in range(ny):
        shapes += [(HALF, 2 * DB)] * 2 if i in ysplit else [(ROWS, 2 * DB)]
    for i in range(nx):
        shapes += [(3, HB, DB)] * 2 if i in xsplit else [(3, DB, DB)]
    deps = list(deps)
    return pl.pallas_call(
        functools.partial(grads_kernel, ny=ny, nx=nx, ndeps=len(deps), ysplit=ysplit, xsplit=xsplit),
        in_specs=[SMEM] + [HBM] * (4 + NW + len(deps)),
        out_specs=[HBM] * len(shapes),
        out_shape=[sds(s) for s in shapes],
        scratch_shapes=[
            pltpu.VMEM((max(ny, 1), 2 * DB, CW), BF),
            pltpu.VMEM((max(nx, 1), 2 * ROWS, DB), BF),
            pltpu.VMEM((2 * ROWS, CW), BF),
            pltpu.VMEM((max(ny, 1), ROWS, 2 * DB), BF),
            pltpu.VMEM((max(nx, 1), 3, DB, DB), BF),
            pltpu.SemaphoreType.DMA((2, 3)),
            pltpu.SemaphoreType.DMA((ny + nx, 2, 2, 3)),
            pltpu.SemaphoreType.DMA((ny + nx, 2)),
        ],
        compiler_params=params(),
        cost_estimate=cost(2 * (ny + nx) * ROWS * 768 * CW, (ny + nx) * 3 << 20),
        name="grads",
    )(ivec(core, *ysrc, *xsrc), dqkv, d_other, *ws, normed, other, *deps)


def sum_kernel(a, b, c, *refs):
    refs[-1][...] = (a[...].astype(F32) + b[...].astype(F32) + c[...].astype(F32)).astype(BF)


def sum_blocks(vs, deps):
    shape = vs[0].shape
    spec = (pl.BlockSpec((ROWS // 3, 2 * DB), lambda i: (i, 0)) if len(shape) == 2
            else pl.BlockSpec((1, DB, DB), lambda i: (i, 0, 0)))
    return pl.pallas_call(
        sum_kernel,
        grid=(3,),
        in_specs=[spec] * 3 + [HBM] * len(deps),
        out_specs=spec,
        out_shape=sds(shape),
        compiler_params=params(),
        cost_estimate=cost(0, 4 << 20),
        name="sum_blocks",
    )(*vs, *deps)


def add_kernel(yu, yd, xu, xd, hm, hp, vm, vp, *refs):
    for a, b, o in zip((yu, yd, xu, xd), (hm, hp, vm, vp), refs[-4:]):
        o[...] = (a[...].astype(F32) + b[...].astype(F32)).astype(BF)


def add_halves(blocks, arrived, deps):
    whole = lambda v: pl.BlockSpec(v.shape, lambda i: (0,) * v.ndim)
    halves = [
        pl.BlockSpec((HALF, 2 * DB), lambda i: (0, 0)),
        pl.BlockSpec((HALF, 2 * DB), lambda i: (1, 0)),
        pl.BlockSpec((3, HB, DB), lambda i: (0, 0, 0)),
        pl.BlockSpec((3, HB, DB), lambda i: (0, 1, 0)),
    ]
    return pl.pallas_call(
        add_kernel,
        grid=(1,),
        in_specs=halves + [whole(v) for v in arrived] + [HBM] * len(deps),
        out_specs=halves,
        out_shape=[sds(v.shape) for v in blocks],
        input_output_aliases={0: 0, 1: 1, 2: 2, 3: 3},
        compiler_params=params(),
        cost_estimate=cost(0, 6 << 20),
        name="add_halves",
    )(*blocks, *arrived, *deps)


def accumulate(a, b, deps):
    def kernel(a_ref, b_ref, *refs):
        refs[-1][...] = a_ref[...] + b_ref[...]

    return pl.pallas_call(
        kernel,
        in_specs=[VMEM, VMEM] + [HBM] * len(deps),
        out_specs=VMEM,
        out_shape=sds(a.shape, F32),
        compiler_params=params(),
        cost_estimate=cost(0, 1 << 12),
        name="accumulate",
    )(a, b, *deps)


def ivec(*v):
    return jnp.stack([jnp.asarray(e, jnp.int32) for e in v])


def local(patches, gain, w_qkv, counts, grad_out):
    si, mi = lax.axis_index("seq"), lax.axis_index("mp")
    core, x, zh = si % 2, (si // 2) % 4, si // 8
    y, zl = mi // 2, mi % 2
    mw = lambda dx, dz: jnp.where(dz == 0, zh, 1 - zh) * 4 + (x + dx) % 4
    mx = lambda dy, dz: ((y + dy) % 4) * 2 + jnp.where(dz == 0, zl, 1 - zl)
    rows, wshape = (EXT, 2 * DB), (3, DB, DB)
    lo, hi = (slice(None), pl.ds(0, HB)), (slice(None), pl.ds(HB, HB))
    first, rest = (pl.ds(0, HALF),), (pl.ds(HALF, EXT - HALF),)

    p0 = extend(patches, gain)
    w = jnp.transpose(w_qkv, (1, 0, 2))
    p_m, p_p, pz = mpp(p0, YP), mpp(p0, YM), mpp(p0, ZLO)
    w_m, w_p = sp(w, XP), sp(w, XM)
    pz1, w1 = move([pz, w], [rows, wshape], [(0, None, 0, None), (1, None, 1, None)], [p_m, p_p], "gate_y1")
    pz_m, pz_p = mpp(pz1, YP), mpp(pz1, YM)
    wz = sp(w1, ZHI)
    w_lo, w_hi = move([w_m, w_p], [(3, HB, DB)] * 2, [(0, lo, 0, None), (1, hi, 1, None)], [pz1], "gate_x1")
    wf_m, wf_p = sp(w_lo, XP), sp(w_hi, XM)
    fu, fd = move(
        [p_m, p_p, pz_m, pz_p], [(2, HALF, 2 * DB), (2, EXT - HALF, 2 * DB)],
        [(0, first, 0, (0,)), (2, first, 0, (1,)), (1, rest, 1, (0,)), (3, rest, 1, (1,))], [w_lo], "gate_y2")
    f_m, f_p = mpp(fu, YP), mpp(fd, YM)
    wz1, w2 = move([wz, w1], [wshape, wshape], [(0, None, 0, None), (1, None, 1, None)], [wf_m, wf_p, fu], "gate_x2")
    wz_m, wz_p = sp(wz1, XP), sp(wz1, XM)
    (w4,) = move(
        [w2, w_m, w_p, wf_m, wf_p], [(4,) + wshape],
        [(0, None, 0, (0,)), (1, None, 0, (1,)), (2, None, 0, (2,)), (3, None, 0, (3,) + lo), (4, None, 0, (3,) + hi)],
        [wz1], "pack")
    o_w = sp(w4, CORE)
    st = stats([p0, pz, p_m, p_p, pz_m, pz_p], [wz1])
    wz_lo, wz_hi, wz2 = move(
        [wz_m, wz_p, wz1], [(3, HB, DB), (3, HB, DB), wshape],
        [(0, lo, 0, None), (1, hi, 1, None), (2, None, 2, None)],
        [f_m, f_p, o_w, st], "gate_x3")
    wzf_m, wzf_p = sp(wz_lo, XP), sp(wz_hi, XM)
    o_z, o_zm, o_zp = (sp(v, CORE) for v in (wz2, wz_m, wz_p))
    index = ivec(mx(0, 0), mx(0, 1), mx(-1, 0), mx(1, 0), mx(-1, 1), mx(1, 1), mx(2, 0), mx(2, 1), core)
    n_own, n_oth, st = normalize(index, st, [p0, pz, p_m, p_p, pz_m, pz_p, f_m, f_p], wz_lo)
    mean, rstd = st[:, 0:1], st[:, 1:2]
    wzf_m, wzf_p, n_oth = hold([wzf_m, wzf_p, n_oth], [o_z])
    o_zfm, o_zfp = sp(wzf_m, CORE), sp(wzf_p, CORE)
    (n_oth,) = hold([n_oth], [o_zfm, o_zfp, o_zm, o_zp])
    n_other = sp(n_oth, CORE)
    ws = [w2, w_m, w_p, wf_m, wf_p, o_w,
          wz2, wz_m, wz_p, wzf_m, wzf_p, o_z, o_zm, o_zp, o_zfm, o_zfp]
    windex = ivec(mw(0, 0), mw(-1, 0), mw(1, 0), mw(2, 0), mw(0, 1), mw(-1, 1), mw(1, 1), mw(2, 1), core)
    heads_out, dqkv, mom = attend(windex, counts.reshape(4), n_own, n_oth, ws, grad_out)

    d_other = sp(dqkv, CORE)
    mom = jnp.concatenate([mom[:, 0], mom[:, 1]]).reshape(9, 128)

    def source(dy, dz):
        m = mx(dy, dz)
        dx = (m % 4 - x) % 4
        return jnp.where(dx == 3, 1, jnp.where(dx == 1, 2, jnp.where(dx == 2, 3, 0))) + jnp.where(m // 4 == zh, 0, 4)

    def blocks(yb, xb, deps, **kw):
        return grads(core, [source(*b) for b in yb], [mw(*b) for b in xb], dqkv, d_other, ws, n_own, n_other, deps, **kw)

    y2p_lo, y2p_hi, x2p_lo, x2p_hi = blocks([(2, 1)], [(2, 1)], [], ysplit=(0,), xsplit=(0,))
    h_m, h_p = mpp(y2p_lo, YP), mpp(y2p_hi, YM)
    v_m, v_p = sp(x2p_lo, XP), sp(x2p_hi, XM)
    mom1 = accumulate(mom, mpp(mom, ZLO), [y2p_lo])
    near = blocks([(1, 1), (-1, 1)], [(1, 1), (-1, 1)], [x2p_lo])
    mom2 = accumulate(mom1, mpp(mom1, YA), [near[0]])
    yu, yd, xu, xd = add_halves(near, [h_m, h_p, v_m, v_p], [])
    ya1, ya2, xa1, xa2 = mpp(yu, YP), mpp(yd, YM), sp(xu, XP), sp(xd, XM)
    y0p, y2_lo, y2_hi, y1u, y1d, x0p, x2_lo, x2_hi = blocks(
        [(0, 1), (2, 0), (1, 0), (-1, 0)], [(0, 1), (2, 0)], [yu], ysplit=(1,), xsplit=(1,))
    mom3 = accumulate(mom2, mpp(mom2, YB), [y0p])
    y_out = sum_blocks([y0p, ya1, ya2], [xa1, xa2])
    yz = mpp(y_out, ZLO)
    h_m, h_p = mpp(y2_lo, YP), mpp(y2_hi, YM)
    v_m, v_p = sp(x2_lo, XP), sp(x2_hi, XM)
    x1u, x1d = blocks([], [(1, 0), (-1, 0)], [y_out])
    x_out = sum_blocks([x0p, xa1, xa2], [x1u])
    yu, yd, xu, xd = add_halves([y1u, y1d, x1u, x1d], [h_m, h_p, v_m, v_p], [yz, x_out, mom3])
    yb1, yb2, xb1, xb2 = mpp(yu, YP), mpp(yd, YM), sp(xu, XP), sp(xd, XM)
    xz = sp(x_out, ZHI)
    y0, x0 = blocks([(0, 0)], [(0, 0)], [yu])

    f = lambda v: v.astype(F32)
    mom = mom3.reshape(2 * ROWS) / D
    gn = f(y0) + f(yb1) + f(yb2) + f(yz)
    xhat = (f(patches) - mean) * rstd
    gg = jnp.sum(gn * xhat, axis=0)
    for perm in (CORE, ZHI):
        gg = gg + sp(gg, perm)
    gg = (gg + sp(gg, X2)) + (sp(gg, XP) + sp(gg, XM))
    grad_p = ((gn * gain[None, :] - mom[:ROWS, None] - xhat * mom[ROWS:, None]) * rstd).astype(BF)
    gw = jnp.transpose(f(x0) + f(xb1) + f(xb2) + f(xz), (1, 0, 2))
    return heads_out, grad_p, gg, gw


def solution(mesh):
    placed = (P("seq", "mp"), P("mp"), P("seq", None, "mp"), P("seq", None), P("seq", "mp"))
    return jax.shard_map(
        local,
        mesh=mesh,
        in_specs=placed,
        out_specs=(P("seq", "mp"), P("seq", "mp"), P("mp"), P("seq", None, "mp")),
        check_vma=False,
    )
```

```python
import functools

import jax
import jax.numpy as jnp
from jax import lax
from jax.experimental import pallas as pl
from jax.experimental.pallas import tpu as pltpu
from jax.sharding import PartitionSpec as P

HD = 128
NH = 3
ROWS = 576
HALF = ROWS // 2
EXT = ROWS + 16
DB = 384
HB = DB // 2
D = 6144
CW = 3 * DB
EPS = 1e-06
BF = jnp.bfloat16
F32 = jnp.float32
HBM = pl.BlockSpec(memory_space=pltpu.HBM)
VMEM = pl.BlockSpec(memory_space=pltpu.VMEM)
SMEM = pl.BlockSpec(memory_space=pltpu.SMEM)


def seq_perm(f):
    out = []
    for i in range(16):
        zh, x, c = f(i // 8, (i // 2) % 4, i % 2)
        out.append((i, (zh * 4 + x % 4) * 2 + c))
    return out


def mp_perm(f):
    out = []
    for i in range(8):
        y, zl = f(i // 2, i % 2)
        out.append((i, (y % 4) * 2 + zl))
    return out


CORE = seq_perm(lambda zh, x, c: (zh, x, 1 - c))
ZHI = seq_perm(lambda zh, x, c: (1 - zh, x, c))
XP = seq_perm(lambda zh, x, c: (zh, x + 1, c))
XM = seq_perm(lambda zh, x, c: (zh, x - 1, c))
ZCORE = seq_perm(lambda zh, x, c: (1 - zh, x, 1 - c))
X2 = seq_perm(lambda zh, x, c: (zh, x + 2, c))
ZLO = mp_perm(lambda y, zl: (y, 1 - zl))
YP = mp_perm(lambda y, zl: (y + 1, zl))
YM = mp_perm(lambda y, zl: (y - 1, zl))
Y2 = mp_perm(lambda y, zl: (y + 2, zl))
YA = mp_perm(lambda y, zl: (y ^ 1, zl))
YB = mp_perm(lambda y, zl: (y ^ 3, zl))


def sp(v, perm):
    return lax.ppermute(v, "seq", perm)


def mpp(v, perm):
    return lax.ppermute(v, "mp", perm)


def nt(a, b):
    return lax.dot_general(a, b, (((1,), (1,)), ((), ())), preferred_element_type=F32)


def tn(a, b):
    return lax.dot_general(a, b, (((0,), (0,)), ((), ())), preferred_element_type=F32)


def nn(a, b):
    return lax.dot_general(a, b, (((1,), (0,)), ((), ())), preferred_element_type=F32)


def sds(shape, dtype=BF):
    return jax.ShapeDtypeStruct(shape, dtype)


def params(mib=63):
    return pltpu.CompilerParams(vmem_limit_bytes=mib << 20)


def cost(flops, nbytes, exps=0):
    return pl.CostEstimate(flops=int(flops), bytes_accessed=int(nbytes), transcendentals=exps)


def sliced(shape, index):
    if not index:
        return shape
    out = []
    for n, i in zip(shape, index):
        if not isinstance(i, int):
            out.append(n if isinstance(i, slice) else i.size)
    return tuple(out) + tuple(shape[len(index):])


def move(inputs, outs, plan, deps, name):
    def kernel(*refs):
        ins = refs[:len(inputs)]
        dst = refs[len(inputs) + len(deps):][:len(outs)]
        *bufs, sem = refs[len(inputs) + len(deps) + len(outs):]
        get = [pltpu.make_async_copy(ins[i].at[si] if si else ins[i], bufs[k], sem.at[k, 0])
               for k, (i, si, o, so) in enumerate(plan)]
        put = [pltpu.make_async_copy(bufs[k], dst[o].at[so] if so else dst[o], sem.at[k, 1])
               for k, (i, si, o, so) in enumerate(plan)]
        for c in get:
            c.start()
        for g, p in zip(get, put):
            g.wait()
            p.start()
        for p in put:
            p.wait()

    return pl.pallas_call(
        kernel,
        in_specs=[HBM] * (len(inputs) + len(deps)),
        out_specs=[HBM] * len(outs),
        out_shape=[sds(s) for s in outs],
        scratch_shapes=[pltpu.VMEM(sliced(inputs[i].shape, si), BF) for i, si, o, so in plan]
        + [pltpu.SemaphoreType.DMA((len(plan), 2))],
        compiler_params=params(),
        cost_estimate=cost(0, 4 << 20),
        name=name,
    )(*inputs, *deps)


def hold(values, deps):
    def kernel(*refs):
        pass

    n = len(values)
    return pl.pallas_call(
        kernel,
        in_specs=[HBM] * (n + len(deps)),
        out_specs=[HBM] * n,
        out_shape=[sds(v.shape, v.dtype) for v in values],
        input_output_aliases={k: k for k in range(n)},
        compiler_params=params(),
        cost_estimate=cost(0, 1 << 10),
        name="hold",
    )(*values, *deps)


def extend_kernel(p, gain, out):
    out[pl.ds(0, ROWS), :] = p[...]
    g = gain[...]
    hi = g.astype(BF).astype(F32)
    mid = (g - hi).astype(BF).astype(F32)
    row = lax.broadcasted_iota(jnp.int32, (16, 2 * DB), 0)
    tail = jnp.where(row == 0, hi, jnp.where(row == 1, mid, jnp.where(row == 2, g - hi - mid, 0.0)))
    out[pl.ds(ROWS, 16), :] = tail.astype(BF)


def extend(patches, gain):
    return pl.pallas_call(
        extend_kernel,
        out_shape=sds((EXT, 2 * DB)),
        compiler_params=params(),
        cost_estimate=cost(0, 2 << 20),
        name="extend",
    )(patches, gain.reshape(1, 2 * DB))


def merge(n, mean, m2, chunk):
    v = chunk.astype(F32)
    cm = jnp.sum(v, axis=1, keepdims=True) * (1.0 / 768)
    dv = v - cm
    c2 = jnp.sum(dv * dv, axis=1, keepdims=True)
    if n == 0:
        return cm, c2
    delta = cm - mean
    return mean + delta * (1.0 / (n + 1)), m2 + c2 + delta * delta * (768.0 * n / (n + 1))


def two_lanes(a, b):
    lane = lax.broadcasted_iota(jnp.int32, (ROWS, 128), 1)
    return jnp.where(lane == 0, a, jnp.where(lane == 1, b, 0.0))


def stats_kernel(*refs, nraw, ndeps):
    raws = refs[:nraw]
    out, buf, sem = refs[nraw + ndeps:]
    copies = [pltpu.make_async_copy(r, buf.at[j], sem.at[j]) for j, r in enumerate(raws)]
    for c in copies:
        c.start()
    mean = m2 = None
    for j, c in enumerate(copies):
        c.wait()
        mean, m2 = merge(j, mean, m2, buf[j, pl.ds(0, ROWS), :])
    out[...] = two_lanes(mean, m2)


def stats(raws, deps):
    n = len(raws)
    return pl.pallas_call(
        functools.partial(stats_kernel, nraw=n, ndeps=len(deps)),
        in_specs=[HBM] * (n + len(deps)),
        out_specs=VMEM,
        out_shape=sds((ROWS, 128), F32),
        scratch_shapes=[pltpu.VMEM((n, EXT, 2 * DB), BF), pltpu.SemaphoreType.DMA((n,))],
        compiler_params=params(),
        cost_estimate=cost(0, 4 << 20),
        name="row_stats",
    )(*raws, *deps)


def norm_kernel(idx, st, r0, r1, r2, r3, r4, r5, fm, fp, _, n_own, n_oth, st_out, raw, nrm, sr, so):
    core = idx[8]
    copies = []
    for j in range(2):
        copies.append(pltpu.make_async_copy(fm.at[j], raw.at[6 + j, pl.ds(0, HALF)], sr.at[j]))
        copies.append(pltpu.make_async_copy(fp.at[j], raw.at[6 + j, pl.ds(HALF, EXT - HALF)], sr.at[2 + j]))
    for j, r in enumerate((r0, r1, r2, r3, r4, r5)):
        copies.append(pltpu.make_async_copy(r, raw.at[j], sr.at[4 + j]))
    for c in copies:
        c.start()
    for c in copies[:4]:
        c.wait()
    mean, m2 = st[:, 0:1], st[:, 1:2]
    for j in range(2):
        mean, m2 = merge(6 + j, mean, m2, raw[6 + j, pl.ds(0, ROWS), :])
    rstd = lax.rsqrt(m2 * (1.0 / D) + EPS)
    st_out[...] = two_lanes(mean, rstd)
    out = []
    own = pl.ds(pl.multiple_of(core * DB, 128), DB)
    oth = pl.ds(pl.multiple_of((1 - core) * DB, 128), DB)
    for j in (6, 7, 0, 1, 2, 3, 4, 5):
        if j < 6:
            copies[4 + j].wait()
        tail = raw[j, pl.ds(ROWS, 16), :]
        t = tail.astype(F32)
        g = t[0:1] + t[1:2] + t[2:3]
        nrm[j, pl.ds(0, ROWS), :] = ((raw[j, pl.ds(0, ROWS), :].astype(F32) - mean) * rstd * g).astype(BF)
        nrm[j, pl.ds(ROWS, 16), :] = tail
        mine = [pltpu.make_async_copy(nrm.at[j, :, own], n_own.at[idx[j]], so.at[j, 0]),
                pltpu.make_async_copy(nrm.at[j, :, oth], n_oth.at[idx[j]], so.at[j, 1])]
        for c in mine:
            c.start()
        out += mine
    for c in out:
        c.wait()


def normalize(index, st, raws, after):
    return pl.pallas_call(
        norm_kernel,
        in_specs=[SMEM, VMEM] + [HBM] * (len(raws) + 1),
        out_specs=[HBM, HBM, VMEM],
        out_shape=[sds((8, EXT, DB)), sds((8, EXT, DB)), sds((ROWS, 128), F32)],
        scratch_shapes=[
            pltpu.VMEM((8, EXT, 2 * DB), BF),
            pltpu.VMEM((8, EXT, 2 * DB), BF),
            pltpu.SemaphoreType.DMA((10,)),
            pltpu.SemaphoreType.DMA((8, 2)),
        ],
        compiler_params=params(),
        cost_estimate=cost(0, 8 << 20),
        name="normalize",
    )(index, st, *raws, after)


NW = 18


def w_sources(refs):
    own, packed, far, pair, other = refs[:5], refs[5], refs[6:8], refs[8:13], refs[13:18]
    out = [((own[k],), (packed.at[k],)) if k < 3 else (own[3:5], far) for k in range(4)]
    return out + [((pair[k],), (other[k],)) if k < 3 else (pair[3:5], other[3:5]) for k in range(4)]


def w_copies(parts, buf, half, sem):
    out = []
    rows = DB // len(parts)
    for h, part in enumerate(parts):
        at = pl.ds(pl.multiple_of(half * DB + h * rows, 64), rows)
        out += [pltpu.make_async_copy(part.at[j], buf.at[at, pl.ds(j * DB, DB)], sem.at[h, j]) for j in range(3)]
    return out


def split(v):
    hi = v.astype(BF)
    return hi, (v - hi.astype(F32)).astype(BF)


def attn_kernel(idx, counts, n_own, n_oth, *refs):
    w_refs, refs = refs[:NW], refs[NW:]
    g_ref, out_ref, dqkv_ref, mom_ref, qkv, nv, wv, sn, sw = refs
    h = pl.program_id(0)

    @pl.when(h == 0)
    def _():
        core = idx[8]
        own = pl.ds(pl.multiple_of(core * DB, 128), DB)
        oth = pl.ds(pl.multiple_of((1 - core) * DB, 128), DB)
        copies = []
        for k, (mine, other) in enumerate(w_sources(w_refs)):
            m = idx[k]
            copies.append([pltpu.make_async_copy(n_own.at[m], nv.at[k, :, own], sn.at[k, 0]),
                           pltpu.make_async_copy(n_oth.at[m], nv.at[k, :, oth], sn.at[k, 1])]
                          + w_copies(mine, wv.at[k], core, sw.at[k, 0])
                          + w_copies(other, wv.at[k], 1 - core, sw.at[k, 1]))
            for c in copies[-1]:
                c.start()
        for k in range(8):
            for c in copies[k]:
                c.wait()
            t = nn(nv[k], wv[k])
            if k == 0:
                qkv[...] = t
            else:
                qkv[...] += t

    col = lambda j: pl.ds(pl.multiple_of((j * NH + h) * HD, 128), HD)
    q_ref, k_ref, v_ref = (qkv.at[:, col(j)] for j in range(3))
    e0 = counts[0]
    e1 = e0 + counts[1]
    e2 = e1 + counts[2]
    rid = lax.broadcasted_iota(jnp.int32, (ROWS, 1), 0)
    cid = lax.broadcasted_iota(jnp.int32, (1, ROWS), 1)
    img = lambda p: (p >= e0).astype(jnp.int32) + (p >= e1).astype(jnp.int32) + (p >= e2).astype(jnp.int32)
    same = img(rid) == img(cid)
    scale = HD ** (-0.5)
    q = q_ref[:ROWS, :] * scale
    k = k_ref[:ROWS, :]
    v = v_ref[:ROWS, :]
    qh, ql = split(q)
    kh, kl = split(k)
    vb = v.astype(BF)
    g = g_ref[...]
    s = nt(jnp.concatenate([qh, qh], 1), jnp.concatenate([kh, kl], 1)) + nt(ql, kh)
    s = jnp.where(same, s, -1e30)
    p = jnp.exp(s - jnp.max(s, axis=1, keepdims=True))
    p = p * (1.0 / jnp.sum(p, axis=1, keepdims=True))
    pb = p.astype(BF)
    out_ref[...] = nn(pb, vb).astype(BF)
    dp = nt(g, vb)
    dv = tn(pb, g)
    ds = p * (dp - jnp.sum(dp * p, axis=1, keepdims=True))
    dsb = ds.astype(BF)
    dq = (nn(dsb, kh) * scale).astype(BF)
    dk = tn(dsb, qh).astype(BF)
    dv = dv.astype(BF)
    dqkv_ref[0] = dq
    dqkv_ref[1] = dk
    dqkv_ref[2] = dv
    m1 = jnp.zeros((ROWS, 1), F32)
    m2 = jnp.zeros((ROWS, 1), F32)
    for d, r in ((dq, q_ref), (dk, k_ref), (dv, v_ref)):
        df = d.astype(F32)
        u = r[ROWS:ROWS + 1, :] + r[ROWS + 1:ROWS + 2, :] + r[ROWS + 2:ROWS + 3, :]
        m1 = m1 + jnp.sum(df * u, axis=1, keepdims=True)
        m2 = m2 + jnp.sum(df * r[:ROWS, :], axis=1, keepdims=True)
    mom = two_lanes(m1, m2)

    @pl.when(h == 0)
    def _():
        mom_ref[...] = mom

    @pl.when(h > 0)
    def _():
        mom_ref[...] += mom


def attend(index, counts, n_own, n_oth, ws, grad_out):
    return pl.pallas_call(
        attn_kernel,
        grid=(NH,),
        in_specs=[SMEM, SMEM] + [HBM] * (2 + NW) + [pl.BlockSpec((ROWS, HD), lambda h: (0, h))],
        out_specs=[
            pl.BlockSpec((ROWS, HD), lambda h: (0, h)),
            pl.BlockSpec((3, ROWS, HD), lambda h: (0, 0, h)),
            pl.BlockSpec((ROWS, 128), lambda h: (0, 0)),
        ],
        out_shape=[sds((ROWS, DB)), sds((3, ROWS, DB)), sds((ROWS, 128), F32)],
        scratch_shapes=[
            pltpu.VMEM((EXT, CW), F32),
            pltpu.VMEM((8, EXT, 2 * DB), BF),
            pltpu.VMEM((8, 2 * DB, CW), BF),
            pltpu.SemaphoreType.DMA((8, 2)),
            pltpu.SemaphoreType.DMA((8, 2, 2, 3)),
        ],
        compiler_params=params(),
        cost_estimate=cost(2 * EXT * D * CW, 28 << 20, NH * ROWS * ROWS),
        name="attention",
    )(index, counts, n_own, n_oth, *ws, grad_out)


def grads_kernel(idx, d1, d2, *refs, ny, nx, ndeps, ysplit, xsplit):
    w_refs, (n1, n2), refs = refs[:NW], refs[NW:NW + 2], refs[NW + 2 + ndeps:]
    outs = list(refs[:-8])
    wv, nv, dcat, oy, ox, sd, si, so = refs[-8:]
    core = idx[0]
    dc = [pltpu.make_async_copy(d1.at[j], dcat.at[pl.ds(0, ROWS), pl.ds(j * DB, DB)], sd.at[0, j]) for j in range(3)]
    if nx:
        dc += [pltpu.make_async_copy(d2.at[j], dcat.at[pl.ds(ROWS, ROWS), pl.ds(j * DB, DB)], sd.at[1, j])
               for j in range(3)]
    for c in dc[:3]:
        c.start()
    sources = w_sources(w_refs)
    for i in range(ny):
        a = idx[1 + i]
        for k, (mine, other) in enumerate(sources):
            @pl.when(a == k)
            def _():
                for c in w_copies(mine, wv.at[i], core, si.at[i, 0]) + w_copies(other, wv.at[i], 1 - core, si.at[i, 1]):
                    c.start()
    for c in dc[3:]:
        c.start()
    ncs = []
    for i in range(nx):
        m = idx[1 + ny + i]
        ncs.append([pltpu.make_async_copy(n1.at[m, pl.ds(0, ROWS)], nv.at[i, pl.ds(0, ROWS)], si.at[ny + i, 0, 0, 0]),
                    pltpu.make_async_copy(n2.at[m, pl.ds(0, ROWS)], nv.at[i, pl.ds(ROWS, ROWS)], si.at[ny + i, 1, 0, 0])])
        for c in ncs[-1]:
            c.start()
    pending = []

    def put(src, dst, sem):
        c = pltpu.make_async_copy(src, dst, sem)
        c.start()
        pending.append(c)

    for c in dc[:3]:
        c.wait()
    for i in range(ny):
        a = idx[1 + i]
        for e in range(2):
            halves = jnp.logical_or(a == 7, a == 3)

            @pl.when(halves)
            def _():
                for c in w_copies(sources[7][e], wv.at[i], e, si.at[i, e]):
                    c.wait()

            @pl.when(jnp.logical_not(halves))
            def _():
                for c in w_copies(sources[0][e], wv.at[i], e, si.at[i, e]):
                    c.wait()
        oy[i] = nt(dcat[pl.ds(0, ROWS), :], wv[i]).astype(BF)
        if i in ysplit:
            put(oy.at[i, pl.ds(0, HALF)], outs.pop(0), so.at[i, 0])
            put(oy.at[i, pl.ds(HALF, HALF)], outs.pop(0), so.at[i, 1])
        else:
            put(oy.at[i], outs.pop(0), so.at[i, 0])
    for c in dc[3:]:
        c.wait()
    for i in range(nx):
        for c in ncs[i]:
            c.wait()
        t = tn(nv[i], dcat[...]).astype(BF)
        for j in range(3):
            ox[i, j] = t[:, j * DB:(j + 1) * DB]
        if i in xsplit:
            put(ox.at[i, :, pl.ds(0, HB)], outs.pop(0), so.at[ny + i, 0])
            put(ox.at[i, :, pl.ds(HB, HB)], outs.pop(0), so.at[ny + i, 1])
        else:
            put(ox.at[i], outs.pop(0), so.at[ny + i, 0])
    for c in pending:
        c.wait()


def grads(core, ysrc, xsrc, dqkv, d_other, ws, normed, other, deps, ysplit=(), xsplit=()):
    ny, nx = len(ysrc), len(xsrc)
    shapes = []
    for i in range(ny):
        shapes += [(HALF, 2 * DB)] * 2 if i in ysplit else [(ROWS, 2 * DB)]
    for i in range(nx):
        shapes += [(3, HB, DB)] * 2 if i in xsplit else [(3, DB, DB)]
    deps = list(deps)
    return pl.pallas_call(
        functools.partial(grads_kernel, ny=ny, nx=nx, ndeps=len(deps), ysplit=ysplit, xsplit=xsplit),
        in_specs=[SMEM] + [HBM] * (4 + NW + len(deps)),
        out_specs=[HBM] * len(shapes),
        out_shape=[sds(s) for s in shapes],
        scratch_shapes=[
            pltpu.VMEM((max(ny, 1), 2 * DB, CW), BF),
            pltpu.VMEM((max(nx, 1), 2 * ROWS, DB), BF),
            pltpu.VMEM((2 * ROWS, CW), BF),
            pltpu.VMEM((max(ny, 1), ROWS, 2 * DB), BF),
            pltpu.VMEM((max(nx, 1), 3, DB, DB), BF),
            pltpu.SemaphoreType.DMA((2, 3)),
            pltpu.SemaphoreType.DMA((ny + nx, 2, 2, 3)),
            pltpu.SemaphoreType.DMA((ny + nx, 2)),
        ],
        compiler_params=params(),
        cost_estimate=cost(0, 1 << 12),
        name="grads",
    )(ivec(core, *ysrc, *xsrc), dqkv, d_other, *ws, normed, other, *deps)


def sum_kernel(*refs, n):
    total = refs[0][...].astype(F32)
    for r in refs[1:n]:
        total = total + r[...].astype(F32)
    refs[-1][...] = total.astype(BF)


def sum_blocks(vs, deps):
    n, shape = len(vs), vs[0].shape
    spec = (pl.BlockSpec((ROWS // 3, 2 * DB), lambda i: (i, 0)) if len(shape) == 2
            else pl.BlockSpec((1, DB, DB), lambda i: (i, 0, 0)))
    return pl.pallas_call(
        functools.partial(sum_kernel, n=n),
        grid=(3,),
        in_specs=[spec] * n + [HBM] * len(deps),
        out_specs=spec,
        out_shape=sds(shape),
        compiler_params=params(),
        cost_estimate=cost(0, 1 << 12),
        name="sum_blocks",
    )(*vs, *deps)


def add_kernel(a1, a2, b1, b2, *refs):
    for a, b, o in zip((a1, a2), (b1, b2), refs[-2:]):
        o[...] = (a[...].astype(F32) + b[...].astype(F32)).astype(BF)


def add_halves(blocks, arrived, deps):
    shape = arrived[0].shape
    whole = pl.BlockSpec(shape, lambda i: (0,) * len(shape))
    if len(shape) == 2:
        halves = [pl.BlockSpec(shape, lambda i: (0, 0)), pl.BlockSpec(shape, lambda i: (1, 0))]
    else:
        halves = [pl.BlockSpec(shape, lambda i: (0, 0, 0)), pl.BlockSpec(shape, lambda i: (0, 1, 0))]
    return pl.pallas_call(
        add_kernel,
        grid=(1,),
        in_specs=halves + [whole] * 2 + [HBM] * len(deps),
        out_specs=halves,
        out_shape=[sds(v.shape) for v in blocks],
        input_output_aliases={0: 0, 1: 1},
        compiler_params=params(),
        cost_estimate=cost(0, 1 << 12),
        name="add_halves",
    )(*blocks, *arrived, *deps)


def accumulate(a, b, deps):
    def kernel(a_ref, b_ref, *refs):
        refs[-1][...] = a_ref[...] + b_ref[...]

    return pl.pallas_call(
        kernel,
        in_specs=[VMEM, VMEM] + [HBM] * len(deps),
        out_specs=VMEM,
        out_shape=sds(a.shape, F32),
        compiler_params=params(),
        cost_estimate=cost(0, 1 << 12),
        name="accumulate",
    )(a, b, *deps)


def ivec(*v):
    return jnp.stack([jnp.asarray(e, jnp.int32) for e in v])


def local(patches, gain, w_qkv, counts, grad_out):
    si, mi = lax.axis_index("seq"), lax.axis_index("mp")
    core, x, zh = si % 2, (si // 2) % 4, si // 8
    y, zl = mi // 2, mi % 2
    mw = lambda dx, dz: jnp.where(dz == 0, zh, 1 - zh) * 4 + (x + dx) % 4
    mx = lambda dy, dz: ((y + dy) % 4) * 2 + jnp.where(dz == 0, zl, 1 - zl)
    rows, wshape = (EXT, 2 * DB), (3, DB, DB)
    lo, hi = (slice(None), pl.ds(0, HB)), (slice(None), pl.ds(HB, HB))
    first, rest = (pl.ds(0, HALF),), (pl.ds(HALF, EXT - HALF),)

    p0 = extend(patches, gain)
    w = jnp.transpose(w_qkv, (1, 0, 2))
    p_m, p_p, pz = mpp(p0, YP), mpp(p0, YM), mpp(p0, ZLO)
    w_m, w_p = sp(w, XP), sp(w, XM)
    pz1, w1 = move([pz, w], [rows, wshape], [(0, None, 0, None), (1, None, 1, None)], [p_m, p_p], "gate_y1")
    pz_m, pz_p = mpp(pz1, YP), mpp(pz1, YM)
    wz = sp(w1, ZHI)
    w_lo, w_hi = move([w_m, w_p], [(3, HB, DB)] * 2, [(0, lo, 0, None), (1, hi, 1, None)], [pz1], "gate_x1")
    wf_m, wf_p = sp(w_lo, XP), sp(w_hi, XM)
    (w3,) = move([w1, w_m, w_p], [(3,) + wshape], [(k, None, 0, (k,)) for k in range(3)], [w_lo], "pack")
    fu, fd = move(
        [p_m, p_p, pz_m, pz_p], [(2, HALF, 2 * DB), (2, EXT - HALF, 2 * DB)],
        [(0, first, 0, (0,)), (2, first, 0, (1,)), (1, rest, 1, (0,)), (3, rest, 1, (1,))], [w_lo, w3], "gate_y2")
    f_m, f_p = mpp(fu, YP), mpp(fd, YM)
    (wz1,) = move([wz], [wshape], [(0, None, 0, None)], [wf_m, wf_p, fu], "gate_x2")
    wz_m, wz_p = sp(wz1, XP), sp(wz1, XM)
    (w3,) = hold([w3], [wz1])
    o_w = sp(w3, CORE)
    st = stats([p0, pz, p_m, p_p, pz_m, pz_p], [wz1])
    wz_lo, wz_hi, wz2 = move(
        [wz_m, wz_p, wz1], [(3, HB, DB), (3, HB, DB), wshape],
        [(0, lo, 0, None), (1, hi, 1, None), (2, None, 2, None)],
        [f_m, f_p, o_w, st], "gate_x3")
    wzf_m, wzf_p = sp(wz_lo, XP), sp(wz_hi, XM)
    wf_m, wf_p = hold([wf_m, wf_p], [wz_lo])
    o_fm, o_fp = sp(wf_m, CORE), sp(wf_p, CORE)
    o_z, o_zm, o_zp = (sp(v, CORE) for v in (wz2, wz_m, wz_p))
    index = ivec(mx(0, 0), mx(0, 1), mx(-1, 0), mx(1, 0), mx(-1, 1), mx(1, 1), mx(2, 0), mx(2, 1), core)
    n_own, n_oth, st = normalize(index, st, [p0, pz, p_m, p_p, pz_m, pz_p, f_m, f_p], wz_lo)
    mean, rstd = st[:, 0:1], st[:, 1:2]
    wzf_m, wzf_p, n_oth = hold([wzf_m, wzf_p, n_oth], [o_z])
    o_zfm, o_zfp = sp(wzf_m, CORE), sp(wzf_p, CORE)
    (n_oth,) = hold([n_oth], [o_zfm, o_zfp, o_zm, o_zp, o_fm, o_fp])
    n_other = sp(n_oth, CORE)
    ws = [w1, w_m, w_p, wf_m, wf_p, o_w, o_fm, o_fp,
          wz2, wz_m, wz_p, wzf_m, wzf_p, o_z, o_zm, o_zp, o_zfm, o_zfp]
    windex = ivec(mw(0, 0), mw(-1, 0), mw(1, 0), mw(2, 0), mw(0, 1), mw(-1, 1), mw(1, 1), mw(2, 1), core)
    heads_out, dqkv, mom = attend(windex, counts.reshape(4), n_own, n_oth, ws, grad_out)

    d_other = sp(dqkv, CORE)
    mom = jnp.concatenate([mom[:, 0], mom[:, 1]]).reshape(9, 128)

    def source(dy, dz):
        m = mx(dy, dz)
        dx = (m % 4 - x) % 4
        return jnp.where(dx == 3, 1, jnp.where(dx == 1, 2, jnp.where(dx == 2, 3, 0))) + jnp.where(m // 4 == zh, 0, 4)

    def blocks(yb, xb, deps, **kw):
        return grads(core, [source(*b) for b in yb], [mw(*b) for b in xb], dqkv, d_other, ws, n_own, n_other, deps, **kw)

    mom1 = accumulate(mom, mpp(mom, ZLO), [])
    mom2 = accumulate(mom1, mpp(mom1, YA), [])
    yu, yd, y2 = blocks([(1, 1), (-1, 1), (2, 1)], [], [mom2])
    ya = [mpp(yu, YP), mpp(yd, YM), mpp(y2, Y2)]
    mom3 = accumulate(mom2, mpp(mom2, YB), [yu])
    xu, xd = blocks([], [(1, 1), (-1, 1)], [mom3])
    xa = [sp(xu, XP), sp(xd, XM)]
    y2_lo, y2_hi, y1u, y1d, y0p, x2 = blocks([(2, 0), (1, 0), (-1, 0), (0, 1)], [(2, 1)], [xu], ysplit=(0,))
    xa.append(sp(x2, X2))
    x2_lo, x2_hi, x1u, x1d, x0p = blocks([], [(2, 0), (1, 0), (-1, 0), (0, 1)], [y0p], xsplit=(0,))
    y_out = sum_blocks([y0p, *ya], [x0p])
    yz = mpp(y_out, ZLO)
    h_m, h_p = mpp(y2_lo, YP), mpp(y2_hi, YM)
    x_out = sum_blocks([x0p, *xa], [y_out])
    v_m, v_p = sp(x2_lo, XP), sp(x2_hi, XM)
    yu, yd = add_halves([y1u, y1d], [h_m, h_p], [x_out])
    yb1, yb2 = mpp(yu, YP), mpp(yd, YM)
    y0, x0 = blocks([(0, 0)], [(0, 0)], [yu, yz])
    xu, xd = add_halves([x1u, x1d], [v_m, v_p], [y0])
    xb1, xb2 = sp(xu, XP), sp(xd, XM)
    (x_out,) = hold([x_out], [yz, xu])
    xz = sp(x_out, ZHI)
    f = lambda v: v.astype(F32)
    mom = mom3.reshape(2 * ROWS) / D
    gn = f(y0) + f(yb1) + f(yb2) + f(yz)
    xhat = (f(patches) - mean) * rstd
    gg = jnp.sum(gn * xhat, axis=0)
    gg = (gg + sp(gg, CORE)) + (sp(gg, ZHI) + sp(gg, ZCORE))
    gg = (gg + sp(gg, X2)) + (sp(gg, XP) + sp(gg, XM))
    grad_p = ((gn * gain[None, :] - mom[:ROWS, None] - xhat * mom[ROWS:, None]) * rstd).astype(BF)
    gw = jnp.transpose(f(x0) + f(xb1) + f(xb2) + f(xz), (1, 0, 2))
    return heads_out, grad_p, gg, gw


def solution(mesh):
    placed = (P("seq", "mp"), P("mp"), P("seq", None, "mp"), P("seq", None), P("seq", "mp"))
    return jax.shard_map(
        local,
        mesh=mesh,
        in_specs=placed,
        out_specs=(P("seq", "mp"), P("seq", "mp"), P("mp"), P("seq", None, "mp")),
        check_vma=False,
    )
```

```python
import functools

import jax
import jax.numpy as jnp
from jax import lax
from jax.experimental import pallas as pl
from jax.experimental.pallas import tpu as pltpu
from jax.sharding import PartitionSpec as P

HD = 128
NH = 3
ROWS = 576
HALF = ROWS // 2
EXT = ROWS + 16
DB = 384
HB = DB // 2
D = 6144
CW = 3 * DB
EPS = 1e-06
BF = jnp.bfloat16
F32 = jnp.float32
HBM = pl.BlockSpec(memory_space=pltpu.HBM)
VMEM = pl.BlockSpec(memory_space=pltpu.VMEM)
SMEM = pl.BlockSpec(memory_space=pltpu.SMEM)


def seq_perm(f):
    out = []
    for i in range(16):
        zh, x, c = f(i // 8, (i // 2) % 4, i % 2)
        out.append((i, (zh * 4 + x % 4) * 2 + c))
    return out


def mp_perm(f):
    out = []
    for i in range(8):
        y, zl = f(i // 2, i % 2)
        out.append((i, (y % 4) * 2 + zl))
    return out


CORE = seq_perm(lambda zh, x, c: (zh, x, 1 - c))
ZHI = seq_perm(lambda zh, x, c: (1 - zh, x, c))
XP = seq_perm(lambda zh, x, c: (zh, x + 1, c))
XM = seq_perm(lambda zh, x, c: (zh, x - 1, c))
X2 = seq_perm(lambda zh, x, c: (zh, x + 2, c))
ZLO = mp_perm(lambda y, zl: (y, 1 - zl))
YP = mp_perm(lambda y, zl: (y + 1, zl))
YM = mp_perm(lambda y, zl: (y - 1, zl))
Y2 = mp_perm(lambda y, zl: (y + 2, zl))


def sp(v, perm):
    return lax.ppermute(v, "seq", perm)


def mpp(v, perm):
    return lax.ppermute(v, "mp", perm)


def nt(a, b):
    return lax.dot_general(a, b, (((1,), (1,)), ((), ())), preferred_element_type=F32)


def tn(a, b):
    return lax.dot_general(a, b, (((0,), (0,)), ((), ())), preferred_element_type=F32)


def nn(a, b):
    return lax.dot_general(a, b, (((1,), (0,)), ((), ())), preferred_element_type=F32)


def sds(shape, dtype=BF):
    return jax.ShapeDtypeStruct(shape, dtype)


def params(mib=63):
    return pltpu.CompilerParams(vmem_limit_bytes=mib << 20)


def cost(flops, nbytes, exps=0):
    return pl.CostEstimate(flops=int(flops), bytes_accessed=int(nbytes), transcendentals=exps)


def sliced(shape, index):
    if not index:
        return shape
    out = []
    for n, i in zip(shape, index):
        if not isinstance(i, int):
            out.append(n if isinstance(i, slice) else i.size)
    return tuple(out) + tuple(shape[len(index):])


def move(inputs, outs, plan, deps, name):
    def kernel(*refs):
        ins = refs[:len(inputs)]
        dst = refs[len(inputs) + len(deps):][:len(outs)]
        *bufs, sem = refs[len(inputs) + len(deps) + len(outs):]
        get = [pltpu.make_async_copy(ins[i].at[si] if si else ins[i], bufs[k], sem.at[k, 0])
               for k, (i, si, o, so) in enumerate(plan)]
        put = [pltpu.make_async_copy(bufs[k], dst[o].at[so] if so else dst[o], sem.at[k, 1])
               for k, (i, si, o, so) in enumerate(plan)]
        for c in get:
            c.start()
        for g, p in zip(get, put):
            g.wait()
            p.start()
        for p in put:
            p.wait()

    return pl.pallas_call(
        kernel,
        in_specs=[HBM] * (len(inputs) + len(deps)),
        out_specs=[HBM] * len(outs),
        out_shape=[sds(s) for s in outs],
        scratch_shapes=[pltpu.VMEM(sliced(inputs[i].shape, si), BF) for i, si, o, so in plan]
        + [pltpu.SemaphoreType.DMA((len(plan), 2))],
        compiler_params=params(),
        cost_estimate=cost(0, 4 << 20),
        name=name,
    )(*inputs, *deps)


def hold(values, deps):
    def kernel(*refs):
        pass

    n = len(values)
    return pl.pallas_call(
        kernel,
        in_specs=[HBM] * (n + len(deps)),
        out_specs=[HBM] * n,
        out_shape=[sds(v.shape, v.dtype) for v in values],
        input_output_aliases={k: k for k in range(n)},
        compiler_params=params(),
        cost_estimate=cost(0, 1 << 10),
        name="hold",
    )(*values, *deps)


def extend_kernel(p, gain, out):
    out[pl.ds(0, ROWS), :] = p[...]
    g = gain[...]
    hi = g.astype(BF).astype(F32)
    mid = (g - hi).astype(BF).astype(F32)
    row = lax.broadcasted_iota(jnp.int32, (16, 2 * DB), 0)
    tail = jnp.where(row == 0, hi, jnp.where(row == 1, mid, jnp.where(row == 2, g - hi - mid, 0.0)))
    out[pl.ds(ROWS, 16), :] = tail.astype(BF)


def extend(patches, gain):
    return pl.pallas_call(
        extend_kernel,
        out_shape=sds((EXT, 2 * DB)),
        compiler_params=params(),
        cost_estimate=cost(0, 2 << 20),
        name="extend",
    )(patches, gain.reshape(1, 2 * DB))


def merge(n, mean, m2, chunk):
    v = chunk.astype(F32)
    cm = jnp.sum(v, axis=1, keepdims=True) * (1.0 / 768)
    dv = v - cm
    c2 = jnp.sum(dv * dv, axis=1, keepdims=True)
    if n == 0:
        return cm, c2
    delta = cm - mean
    return mean + delta * (1.0 / (n + 1)), m2 + c2 + delta * delta * (768.0 * n / (n + 1))


def two_lanes(a, b):
    lane = lax.broadcasted_iota(jnp.int32, (ROWS, 128), 1)
    return jnp.where(lane == 0, a, jnp.where(lane == 1, b, 0.0))


def stats_kernel(*refs, nraw, ndeps):
    raws = refs[:nraw]
    out, buf, sem = refs[nraw + ndeps:]
    copies = [pltpu.make_async_copy(r, buf.at[j], sem.at[j]) for j, r in enumerate(raws)]
    for c in copies:
        c.start()
    mean = m2 = None
    for j, c in enumerate(copies):
        c.wait()
        mean, m2 = merge(j, mean, m2, buf[j, pl.ds(0, ROWS), :])
    out[...] = two_lanes(mean, m2)


def stats(raws, deps):
    n = len(raws)
    return pl.pallas_call(
        functools.partial(stats_kernel, nraw=n, ndeps=len(deps)),
        in_specs=[HBM] * (n + len(deps)),
        out_specs=VMEM,
        out_shape=sds((ROWS, 128), F32),
        scratch_shapes=[pltpu.VMEM((n, EXT, 2 * DB), BF), pltpu.SemaphoreType.DMA((n,))],
        compiler_params=params(),
        cost_estimate=cost(0, 4 << 20),
        name="row_stats",
    )(*raws, *deps)


def norm_kernel(idx, st, r0, r1, r2, r3, r4, r5, fm, fp, _, n_own, n_oth, st_out, raw, nrm, sr, so):
    core = idx[8]
    copies = []
    for j in range(2):
        copies.append(pltpu.make_async_copy(fm.at[j], raw.at[6 + j, pl.ds(0, HALF)], sr.at[j]))
        copies.append(pltpu.make_async_copy(fp.at[j], raw.at[6 + j, pl.ds(HALF, EXT - HALF)], sr.at[2 + j]))
    for j, r in enumerate((r0, r1, r2, r3, r4, r5)):
        copies.append(pltpu.make_async_copy(r, raw.at[j], sr.at[4 + j]))
    for c in copies:
        c.start()
    for c in copies[:4]:
        c.wait()
    mean, m2 = st[:, 0:1], st[:, 1:2]
    for j in range(2):
        mean, m2 = merge(6 + j, mean, m2, raw[6 + j, pl.ds(0, ROWS), :])
    rstd = lax.rsqrt(m2 * (1.0 / D) + EPS)
    st_out[...] = two_lanes(mean, rstd)
    out = []
    own = pl.ds(pl.multiple_of(core * DB, 128), DB)
    oth = pl.ds(pl.multiple_of((1 - core) * DB, 128), DB)
    for j in (6, 7, 0, 1, 2, 3, 4, 5):
        if j < 6:
            copies[4 + j].wait()
        tail = raw[j, pl.ds(ROWS, 16), :]
        t = tail.astype(F32)
        g = t[0:1] + t[1:2] + t[2:3]
        nrm[j, pl.ds(0, ROWS), :] = ((raw[j, pl.ds(0, ROWS), :].astype(F32) - mean) * rstd * g).astype(BF)
        nrm[j, pl.ds(ROWS, 16), :] = tail
        mine = [pltpu.make_async_copy(nrm.at[j, :, own], n_own.at[idx[j]], so.at[j, 0]),
                pltpu.make_async_copy(nrm.at[j, :, oth], n_oth.at[idx[j]], so.at[j, 1])]
        for c in mine:
            c.start()
        out += mine
    for c in out:
        c.wait()


def normalize(index, st, raws, after):
    return pl.pallas_call(
        norm_kernel,
        in_specs=[SMEM, VMEM] + [HBM] * (len(raws) + 1),
        out_specs=[HBM, HBM, VMEM],
        out_shape=[sds((8, EXT, DB)), sds((8, EXT, DB)), sds((ROWS, 128), F32)],
        scratch_shapes=[
            pltpu.VMEM((8, EXT, 2 * DB), BF),
            pltpu.VMEM((8, EXT, 2 * DB), BF),
            pltpu.SemaphoreType.DMA((10,)),
            pltpu.SemaphoreType.DMA((8, 2)),
        ],
        compiler_params=params(),
        cost_estimate=cost(0, 8 << 20),
        name="normalize",
    )(index, st, *raws, after)


NW = 18


def w_sources(refs):
    own, packed, far, pair, other = refs[:5], refs[5], refs[6:8], refs[8:13], refs[13:18]
    out = [((own[k],), (packed.at[k],)) if k < 3 else (own[3:5], far) for k in range(4)]
    return out + [((pair[k],), (other[k],)) if k < 3 else (pair[3:5], other[3:5]) for k in range(4)]


def w_copies(parts, buf, half, sem):
    out = []
    rows = DB // len(parts)
    for h, part in enumerate(parts):
        at = pl.ds(pl.multiple_of(half * DB + h * rows, 64), rows)
        out += [pltpu.make_async_copy(part.at[j], buf.at[at, pl.ds(j * DB, DB)], sem.at[h, j]) for j in range(3)]
    return out


def to_rows(m1, m2):
    row = lax.broadcasted_iota(jnp.int32, (16, m1.shape[1]), 0)
    out = jnp.zeros((16, m1.shape[1]), F32)
    for k, m in enumerate((m1, m2)):
        hi = m.astype(BF).astype(F32)
        mid = (m - hi).astype(BF).astype(F32)
        for j, part in enumerate((hi, mid, m - hi - mid)):
            out = jnp.where(row == 3 * k + j, part, out)
    return out.astype(BF)


def split(v):
    hi = v.astype(BF)
    return hi, (v - hi.astype(F32)).astype(BF)


def attn_kernel(idx, counts, n_own, n_oth, *refs):
    w_refs, refs = refs[:NW], refs[NW:]
    g_ref, out_ref, dqkv_ref, mom_ref, qkv, nv, wv, mom_s, sn, sw = refs
    h = pl.program_id(0)

    @pl.when(h == 0)
    def _():
        core = idx[8]
        copies = []
        for k, (mine, other) in enumerate(w_sources(w_refs)):
            m = idx[k]
            at = (k % 2) * 2 * DB
            lanes = lambda c: pl.ds(pl.multiple_of(at + c * DB, 128), DB)
            copies.append([pltpu.make_async_copy(n_own.at[m], nv.at[k // 2, :, lanes(core)], sn.at[k, 0]),
                           pltpu.make_async_copy(n_oth.at[m], nv.at[k // 2, :, lanes(1 - core)], sn.at[k, 1])]
                          + w_copies(mine, wv.at[k // 2, pl.ds(at, 2 * DB)], core, sw.at[k, 0])
                          + w_copies(other, wv.at[k // 2, pl.ds(at, 2 * DB)], 1 - core, sw.at[k, 1]))
            for c in copies[-1]:
                c.start()
        mom_s[...] = jnp.zeros_like(mom_s)
        for k in range(4):
            for c in copies[2 * k] + copies[2 * k + 1]:
                c.wait()
            t = nn(nv[k], wv[k])
            if k == 0:
                qkv[...] = t
            else:
                qkv[...] += t

    col = lambda j: pl.ds(pl.multiple_of((j * NH + h) * HD, 128), HD)
    q_ref, k_ref, v_ref = (qkv.at[:, col(j)] for j in range(3))
    e0 = counts[0]
    e1 = e0 + counts[1]
    e2 = e1 + counts[2]
    rid = lax.broadcasted_iota(jnp.int32, (ROWS, 1), 0)
    cid = lax.broadcasted_iota(jnp.int32, (1, ROWS), 1)
    img = lambda p: (p >= e0).astype(jnp.int32) + (p >= e1).astype(jnp.int32) + (p >= e2).astype(jnp.int32)
    same = img(rid) == img(cid)
    scale = HD ** (-0.5)
    q = q_ref[:ROWS, :] * scale
    k = k_ref[:ROWS, :]
    v = v_ref[:ROWS, :]
    qh, ql = split(q)
    kh, kl = split(k)
    vb = v.astype(BF)
    g = g_ref[...]
    s = nt(jnp.concatenate([qh, qh, ql], 1), jnp.concatenate([kh, kl, kh], 1))
    s = jnp.where(same, s, -1e30)
    p = jnp.exp(s - jnp.max(s, axis=1, keepdims=True))
    p = p * (1.0 / jnp.sum(p, axis=1, keepdims=True))
    pb = p.astype(BF)
    out_ref[...] = nn(pb, vb).astype(BF)
    dp = nt(g, vb)
    dv = tn(pb, g)
    ds = p * (dp - jnp.sum(dp * p, axis=1, keepdims=True))
    dsb = ds.astype(BF)
    dq = (nn(dsb, kh) * scale).astype(BF)
    dk = tn(dsb, qh).astype(BF)
    dv = dv.astype(BF)
    dqkv_ref[0] = dq
    dqkv_ref[1] = dk
    dqkv_ref[2] = dv
    m1 = jnp.zeros((ROWS, 1), F32)
    m2 = jnp.zeros((ROWS, 1), F32)
    for d, r in ((dq, q_ref), (dk, k_ref), (dv, v_ref)):
        df = d.astype(F32)
        u = r[ROWS:ROWS + 1, :] + r[ROWS + 1:ROWS + 2, :] + r[ROWS + 2:ROWS + 3, :]
        m1 = m1 + jnp.sum(df * u, axis=1, keepdims=True)
        m2 = m2 + jnp.sum(df * r[:ROWS, :], axis=1, keepdims=True)
    mom_s[pl.ds(0, ROWS), :] += two_lanes(m1, m2)

    @pl.when(h == NH - 1)
    def _():
        t = jnp.transpose(mom_s[...])
        mom_ref[...] = jnp.zeros_like(mom_ref)
        mom_ref[:, pl.ds(0, 640)] = to_rows(t[0:1, :], t[1:2, :])


def attend(index, counts, n_own, n_oth, ws, grad_out):
    return pl.pallas_call(
        attn_kernel,
        grid=(NH,),
        in_specs=[SMEM, SMEM] + [HBM] * (2 + NW) + [pl.BlockSpec((ROWS, HD), lambda h: (0, h))],
        out_specs=[
            pl.BlockSpec((ROWS, HD), lambda h: (0, h)),
            pl.BlockSpec((3, ROWS, HD), lambda h: (0, 0, h)),
            pl.BlockSpec((16, 2 * DB), lambda h: (0, 0)),
        ],
        out_shape=[sds((ROWS, DB)), sds((3, ROWS, DB)), sds((16, 2 * DB))],
        scratch_shapes=[
            pltpu.VMEM((EXT, CW), F32),
            pltpu.VMEM((4, EXT, 4 * DB), BF),
            pltpu.VMEM((4, 4 * DB, CW), BF),
            pltpu.VMEM((640, 128), F32),
            pltpu.SemaphoreType.DMA((8, 2)),
            pltpu.SemaphoreType.DMA((8, 2, 2, 3)),
        ],
        compiler_params=params(),
        cost_estimate=cost(2 * EXT * D * CW, 28 << 20, NH * ROWS * ROWS),
        name="attention",
    )(index, counts, n_own, n_oth, *ws, grad_out)


def grads_kernel(idx, d1, d2, *refs, ny, nx, ndeps, ysplit, xsplit, tail):
    w_refs, (n1, n2), extra, refs = refs[:NW], refs[NW:NW + 2], refs[NW + 1 + ndeps], refs[NW + 2 + ndeps:]
    outs = list(refs[:-8])
    wv, nv, dcat, oy, ox, sd, si, so = refs[-8:]
    core = idx[0]
    dc = [pltpu.make_async_copy(d1.at[j], dcat.at[pl.ds(0, ROWS), pl.ds(j * DB, DB)], sd.at[0, j]) for j in range(3)]
    if nx:
        dc += [pltpu.make_async_copy(d2.at[j], dcat.at[pl.ds(ROWS, ROWS), pl.ds(j * DB, DB)], sd.at[1, j])
               for j in range(3)]
    for c in dc[:3]:
        c.start()
    sources = w_sources(w_refs)
    for i in range(ny):
        a = idx[1 + i]
        for k, (mine, other) in enumerate(sources):
            @pl.when(a == k)
            def _():
                for c in w_copies(mine, wv.at[i], core, si.at[i, 0]) + w_copies(other, wv.at[i], 1 - core, si.at[i, 1]):
                    c.start()
    for c in dc[3:]:
        c.start()
    ncs = []
    for i in range(nx):
        m = idx[1 + ny + i]
        ncs.append([pltpu.make_async_copy(n1.at[m, pl.ds(0, ROWS)], nv.at[i, pl.ds(0, ROWS)], si.at[ny + i, 0, 0, 0]),
                    pltpu.make_async_copy(n2.at[m, pl.ds(0, ROWS)], nv.at[i, pl.ds(ROWS, ROWS)], si.at[ny + i, 1, 0, 0])])
        for c in ncs[-1]:
            c.start()
    ends = []
    if tail:
        ends = [pltpu.make_async_copy(extra, oy.at[i, pl.ds(ROWS, 16)], so.at[i, 1]) for i in range(ny)]
        for c in ends:
            c.start()
    pending = []

    def put(src, dst, sem):
        c = pltpu.make_async_copy(src, dst, sem)
        c.start()
        pending.append(c)

    for c in dc[:3]:
        c.wait()
    for i in range(ny):
        a = idx[1 + i]
        for e in range(2):
            halves = jnp.logical_or(a == 7, a == 3)

            @pl.when(halves)
            def _():
                for c in w_copies(sources[7][e], wv.at[i], e, si.at[i, e]):
                    c.wait()

            @pl.when(jnp.logical_not(halves))
            def _():
                for c in w_copies(sources[0][e], wv.at[i], e, si.at[i, e]):
                    c.wait()
        oy[i, pl.ds(0, ROWS), :] = nt(dcat[pl.ds(0, ROWS), :], wv[i]).astype(BF)
        if tail:
            ends[i].wait()
        if i in ysplit:
            put(oy.at[i, pl.ds(0, HALF)], outs.pop(0), so.at[i, 0])
            put(oy.at[i, pl.ds(HALF, HALF)], outs.pop(0), so.at[i, 1])
        else:
            put(oy.at[i], outs.pop(0), so.at[i, 0])
    for c in dc[3:]:
        c.wait()
    for i in range(nx):
        for c in ncs[i]:
            c.wait()
        t = tn(nv[i], dcat[...]).astype(BF)
        for j in range(3):
            ox[i, j] = t[:, j * DB:(j + 1) * DB]
        if i in xsplit:
            put(ox.at[i, :, pl.ds(0, HB)], outs.pop(0), so.at[ny + i, 0])
            put(ox.at[i, :, pl.ds(HB, HB)], outs.pop(0), so.at[ny + i, 1])
        else:
            put(ox.at[i], outs.pop(0), so.at[ny + i, 0])
    for c in pending:
        c.wait()


def grads(core, ysrc, xsrc, dqkv, d_other, ws, normed, other, deps, ysplit=(), xsplit=(), tail=False):
    ny, nx = len(ysrc), len(xsrc)
    shapes, yrows = [], EXT if tail else ROWS
    for i in range(ny):
        shapes += [(HALF, 2 * DB)] * 2 if i in ysplit else [(yrows, 2 * DB)]
    for i in range(nx):
        shapes += [(3, HB, DB)] * 2 if i in xsplit else [(3, DB, DB)]
    deps = list(deps)
    return pl.pallas_call(
        functools.partial(grads_kernel, ny=ny, nx=nx, ndeps=len(deps), ysplit=ysplit, xsplit=xsplit,
                          tail=tail),
        in_specs=[SMEM] + [HBM] * (4 + NW + len(deps)),
        out_specs=[HBM] * len(shapes),
        out_shape=[sds(s) for s in shapes],
        scratch_shapes=[
            pltpu.VMEM((max(ny, 1), 2 * DB, CW), BF),
            pltpu.VMEM((max(nx, 1), 2 * ROWS, DB), BF),
            pltpu.VMEM((2 * ROWS, CW), BF),
            pltpu.VMEM((max(ny, 1), yrows, 2 * DB), BF),
            pltpu.VMEM((max(nx, 1), 3, DB, DB), BF),
            pltpu.SemaphoreType.DMA((2, 3)),
            pltpu.SemaphoreType.DMA((ny + nx, 2, 2, 3)),
            pltpu.SemaphoreType.DMA((ny + nx, 2)),
        ],
        compiler_params=params(),
        cost_estimate=cost(0, 1 << 12),
        name="grads",
    )(ivec(core, *ysrc, *xsrc), dqkv, d_other, *ws, normed, other, *deps)


def sum_rows_kernel(mine, own, *refs):
    out = refs[-1]
    total = mine[...].astype(F32)
    rows = own[...].astype(F32)
    for r in refs[:3]:
        total = total + r[pl.ds(0, ROWS), :].astype(F32)
        rows = rows + r[pl.ds(ROWS, 16), :].astype(F32)
    out[pl.ds(0, ROWS), :] = total.astype(BF)
    m1 = rows[0:1] + rows[1:2] + rows[2:3]
    m2 = rows[3:4] + rows[4:5] + rows[5:6]
    out[pl.ds(ROWS, 16), :] = to_rows(m1, m2)


def sum_rows(mine, own, arrived, deps):
    whole = lambda v: pl.BlockSpec(v.shape, lambda i: (0,) * v.ndim)
    return pl.pallas_call(
        sum_rows_kernel,
        grid=(1,),
        in_specs=[whole(v) for v in (mine, own, *arrived)] + [HBM] * len(deps),
        out_specs=whole(arrived[0]),
        out_shape=sds(arrived[0].shape),
        compiler_params=params(),
        cost_estimate=cost(0, 1 << 12),
        name="sum_rows",
    )(mine, own, *arrived, *deps)


def sum_kernel(*refs, n):
    total = refs[0][...].astype(F32)
    for r in refs[1:n]:
        total = total + r[...].astype(F32)
    refs[-1][...] = total.astype(BF)


def sum_blocks(vs, deps):
    n = len(vs)
    spec = pl.BlockSpec((1, DB, DB), lambda i: (i, 0, 0))
    return pl.pallas_call(
        functools.partial(sum_kernel, n=n),
        grid=(3,),
        in_specs=[spec] * n + [HBM] * len(deps),
        out_specs=spec,
        out_shape=sds(vs[0].shape),
        compiler_params=params(),
        cost_estimate=cost(0, 1 << 12),
        name="sum_blocks",
    )(*vs, *deps)


def add_kernel(a1, a2, b1, b2, *refs):
    for a, b, o in zip((a1, a2), (b1, b2), refs[-2:]):
        o[...] = (a[...].astype(F32) + b[...].astype(F32)).astype(BF)


def add_halves(blocks, arrived, deps):
    shape = arrived[0].shape
    whole = pl.BlockSpec(shape, lambda i: (0,) * len(shape))
    if len(shape) == 2:
        halves = [pl.BlockSpec(shape, lambda i: (0, 0)), pl.BlockSpec(shape, lambda i: (1, 0))]
    else:
        halves = [pl.BlockSpec(shape, lambda i: (0, 0, 0)), pl.BlockSpec(shape, lambda i: (0, 1, 0))]
    return pl.pallas_call(
        add_kernel,
        grid=(1,),
        in_specs=halves + [whole] * 2 + [HBM] * len(deps),
        out_specs=halves,
        out_shape=[sds(v.shape) for v in blocks],
        input_output_aliases={0: 0, 1: 1},
        compiler_params=params(),
        cost_estimate=cost(0, 1 << 12),
        name="add_halves",
    )(*blocks, *arrived, *deps)


def ivec(*v):
    return jnp.stack([jnp.asarray(e, jnp.int32) for e in v])


def local(patches, gain, w_qkv, counts, grad_out):
    si, mi = lax.axis_index("seq"), lax.axis_index("mp")
    core, x, zh = si % 2, (si // 2) % 4, si // 8
    y, zl = mi // 2, mi % 2
    mw = lambda dx, dz: jnp.where(dz == 0, zh, 1 - zh) * 4 + (x + dx) % 4
    mx = lambda dy, dz: ((y + dy) % 4) * 2 + jnp.where(dz == 0, zl, 1 - zl)
    rows, wshape = (EXT, 2 * DB), (3, DB, DB)
    lo, hi = (slice(None), pl.ds(0, HB)), (slice(None), pl.ds(HB, HB))
    first, rest = (pl.ds(0, HALF),), (pl.ds(HALF, EXT - HALF),)

    p0 = extend(patches, gain)
    w = jnp.transpose(w_qkv, (1, 0, 2))
    p_m, p_p, pz = mpp(p0, YP), mpp(p0, YM), mpp(p0, ZLO)
    w_m, w_p = sp(w, XP), sp(w, XM)
    pz1, w1 = move([pz, w], [rows, wshape], [(0, None, 0, None), (1, None, 1, None)], [p_m, p_p], "gate_y1")
    pz_m, pz_p = mpp(pz1, YP), mpp(pz1, YM)
    wz = sp(w1, ZHI)
    w_lo, w_hi = move([w_m, w_p], [(3, HB, DB)] * 2, [(0, lo, 0, None), (1, hi, 1, None)], [pz1], "gate_x1")
    wf_m, wf_p = sp(w_lo, XP), sp(w_hi, XM)
    (w3,) = move([w1, w_m, w_p], [(3,) + wshape], [(k, None, 0, (k,)) for k in range(3)], [w_lo], "pack")
    fu, fd = move(
        [p_m, p_p, pz_m, pz_p], [(2, HALF, 2 * DB), (2, EXT - HALF, 2 * DB)],
        [(0, first, 0, (0,)), (2, first, 0, (1,)), (1, rest, 1, (0,)), (3, rest, 1, (1,))], [w_lo, w3], "gate_y2")
    f_m, f_p = mpp(fu, YP), mpp(fd, YM)
    (wz1,) = move([wz], [wshape], [(0, None, 0, None)], [wf_m, wf_p, fu], "gate_x2")
    wz_m, wz_p = sp(wz1, XP), sp(wz1, XM)
    (w3,) = hold([w3], [wz1])
    o_w = sp(w3, CORE)
    st = stats([p0, pz, p_m, p_p, pz_m, pz_p], [wz1])
    wz_lo, wz_hi, wz2 = move(
        [wz_m, wz_p, wz1], [(3, HB, DB), (3, HB, DB), wshape],
        [(0, lo, 0, None), (1, hi, 1, None), (2, None, 2, None)],
        [f_m, f_p, o_w, st], "gate_x3")
    wzf_m, wzf_p = sp(wz_lo, XP), sp(wz_hi, XM)
    wf_m, wf_p = hold([wf_m, wf_p], [wz_lo])
    o_fm, o_fp = sp(wf_m, CORE), sp(wf_p, CORE)
    o_z, o_zm, o_zp = (sp(v, CORE) for v in (wz2, wz_m, wz_p))
    index = ivec(mx(0, 0), mx(0, 1), mx(-1, 0), mx(1, 0), mx(-1, 1), mx(1, 1), mx(2, 0), mx(2, 1), core)
    n_own, n_oth, st = normalize(index, st, [p0, pz, p_m, p_p, pz_m, pz_p, f_m, f_p], wz_lo)
    mean, rstd = st[:, 0:1], st[:, 1:2]
    wzf_m, wzf_p, n_oth = hold([wzf_m, wzf_p, n_oth], [o_z])
    o_zfm, o_zfp = sp(wzf_m, CORE), sp(wzf_p, CORE)
    (n_oth,) = hold([n_oth], [o_zfm, o_zfp, o_zm, o_zp, o_fm, o_fp])
    n_other = sp(n_oth, CORE)
    ws = [w1, w_m, w_p, wf_m, wf_p, o_w, o_fm, o_fp,
          wz2, wz_m, wz_p, wzf_m, wzf_p, o_z, o_zm, o_zp, o_zfm, o_zfp]
    windex = ivec(mw(0, 0), mw(-1, 0), mw(1, 0), mw(2, 0), mw(0, 1), mw(-1, 1), mw(1, 1), mw(2, 1), core)
    heads_out, dqkv, mom = attend(windex, counts.reshape(4), n_own, n_oth, ws, grad_out)

    d_other = sp(dqkv, CORE)

    def source(dy, dz):
        m = mx(dy, dz)
        dx = (m % 4 - x) % 4
        return jnp.where(dx == 3, 1, jnp.where(dx == 1, 2, jnp.where(dx == 2, 3, 0))) + jnp.where(m // 4 == zh, 0, 4)

    def blocks(yb, xb, deps, **kw):
        return grads(core, [source(*b) for b in yb], [mw(*b) for b in xb], dqkv, d_other if xb else dqkv, ws, n_own,
                     n_other if xb else n_own, deps, **kw)

    yu, yd, y2 = blocks([(1, 1), (-1, 1), (2, 1)], [], [mom], tail=True)
    ya = [mpp(yu, YP), mpp(yd, YM), mpp(y2, Y2)]
    xu, xd = blocks([], [(1, 1), (-1, 1)], [yu])
    xa = [sp(xu, XP), sp(xd, XM)]
    y2_lo, y2_hi, y1u, y1d, y0p, x2 = blocks([(2, 0), (1, 0), (-1, 0), (0, 1)], [(2, 1)], [xu], ysplit=(0,))
    xa.append(sp(x2, X2))
    x2_lo, x2_hi, x1u, x1d, x0p = blocks([], [(2, 0), (1, 0), (-1, 0), (0, 1)], [y0p], xsplit=(0,))
    y_out = sum_rows(y0p, mom, ya, [x0p])
    yz = mpp(y_out, ZLO)
    h_m, h_p = mpp(y2_lo, YP), mpp(y2_hi, YM)
    x_out = sum_blocks([x0p, *xa], [y_out])
    v_m, v_p = sp(x2_lo, XP), sp(x2_hi, XM)
    yu, yd = add_halves([y1u, y1d], [h_m, h_p], [x_out])
    yb1, yb2 = mpp(yu, YP), mpp(yd, YM)
    y0, x0 = blocks([(0, 0)], [(0, 0)], [yu, yz])
    xu, xd = add_halves([x1u, x1d], [v_m, v_p], [y0])
    xb1, xb2 = sp(xu, XP), sp(xd, XM)
    (x_out,) = hold([x_out], [yz])
    xz = sp(x_out, ZHI)
    f = lambda v: v.astype(F32)
    mom = jnp.sum((f(y_out[ROWS:ROWS + 6]) + f(yz[ROWS:ROWS + 6])).reshape(2, 3, 2 * DB), axis=1)[:, :ROWS] / D
    gn = f(y0) + f(yb1) + f(yb2) + f(yz[:ROWS])
    xhat = (f(patches) - mean) * rstd
    gg = jnp.sum(gn * xhat, axis=0)
    for perm in (CORE, ZHI):
        gg = gg + sp(gg, perm)
    gg = (gg + sp(gg, X2)) + (sp(gg, XP) + sp(gg, XM))
    grad_p = ((gn * gain[None, :] - mom[0][:, None] - xhat * mom[1][:, None]) * rstd).astype(BF)
    gw = jnp.transpose(f(x0) + f(xb1) + f(xb2) + f(xz), (1, 0, 2))
    return heads_out, grad_p, gg, gw


def solution(mesh):
    placed = (P("seq", "mp"), P("mp"), P("seq", None, "mp"), P("seq", None), P("seq", "mp"))
    return jax.shard_map(
        local,
        mesh=mesh,
        in_specs=placed,
        out_specs=(P("seq", "mp"), P("seq", "mp"), P("mp"), P("seq", None, "mp")),
        check_vma=False,
    )
```

```python
import functools

import jax
import jax.numpy as jnp
from jax import lax
from jax.experimental import pallas as pl
from jax.experimental.pallas import tpu as pltpu
from jax.sharding import PartitionSpec as P

HD = 128
NH = 3
ROWS = 576
HALF = ROWS // 2
EXT = ROWS + 16
DB = 384
HB = DB // 2
D = 6144
CW = 3 * DB
EPS = 1e-06
BF = jnp.bfloat16
F32 = jnp.float32
HBM = pl.BlockSpec(memory_space=pltpu.HBM)
VMEM = pl.BlockSpec(memory_space=pltpu.VMEM)
SMEM = pl.BlockSpec(memory_space=pltpu.SMEM)


def seq_perm(f):
    out = []
    for i in range(16):
        zh, x, c = f(i // 8, (i // 2) % 4, i % 2)
        out.append((i, (zh * 4 + x % 4) * 2 + c))
    return out


def mp_perm(f):
    out = []
    for i in range(8):
        y, zl = f(i // 2, i % 2)
        out.append((i, (y % 4) * 2 + zl))
    return out


CORE = seq_perm(lambda zh, x, c: (zh, x, 1 - c))
ZHI = seq_perm(lambda zh, x, c: (1 - zh, x, c))
XP = seq_perm(lambda zh, x, c: (zh, x + 1, c))
XM = seq_perm(lambda zh, x, c: (zh, x - 1, c))
X2 = seq_perm(lambda zh, x, c: (zh, x + 2, c))
ZLO = mp_perm(lambda y, zl: (y, 1 - zl))
YP = mp_perm(lambda y, zl: (y + 1, zl))
YM = mp_perm(lambda y, zl: (y - 1, zl))
Y2 = mp_perm(lambda y, zl: (y + 2, zl))


def sp(v, perm):
    return lax.ppermute(v, "seq", perm)


def mpp(v, perm):
    return lax.ppermute(v, "mp", perm)


def nt(a, b):
    return lax.dot_general(a, b, (((1,), (1,)), ((), ())), preferred_element_type=F32)


def tn(a, b):
    return lax.dot_general(a, b, (((0,), (0,)), ((), ())), preferred_element_type=F32)


def nn(a, b):
    return lax.dot_general(a, b, (((1,), (0,)), ((), ())), preferred_element_type=F32)


def sds(shape, dtype=BF):
    return jax.ShapeDtypeStruct(shape, dtype)


def params(mib=63):
    return pltpu.CompilerParams(vmem_limit_bytes=mib << 20)


def cost(flops, nbytes, exps=0):
    return pl.CostEstimate(flops=int(flops), bytes_accessed=int(nbytes), transcendentals=exps)


def sliced(shape, index):
    if not index:
        return shape
    out = []
    for n, i in zip(shape, index):
        if not isinstance(i, int):
            out.append(n if isinstance(i, slice) else i.size)
    return tuple(out) + tuple(shape[len(index):])


def move(inputs, outs, plan, deps, name):
    def kernel(*refs):
        ins = refs[:len(inputs)]
        dst = refs[len(inputs) + len(deps):][:len(outs)]
        *bufs, sem = refs[len(inputs) + len(deps) + len(outs):]
        get = [pltpu.make_async_copy(ins[i].at[si] if si else ins[i], bufs[k], sem.at[k, 0])
               for k, (i, si, o, so) in enumerate(plan)]
        put = [pltpu.make_async_copy(bufs[k], dst[o].at[so] if so else dst[o], sem.at[k, 1])
               for k, (i, si, o, so) in enumerate(plan)]
        for c in get:
            c.start()
        for g, p in zip(get, put):
            g.wait()
            p.start()
        for p in put:
            p.wait()

    return pl.pallas_call(
        kernel,
        in_specs=[HBM] * (len(inputs) + len(deps)),
        out_specs=[HBM] * len(outs),
        out_shape=[sds(s) for s in outs],
        scratch_shapes=[pltpu.VMEM(sliced(inputs[i].shape, si), BF) for i, si, o, so in plan]
        + [pltpu.SemaphoreType.DMA((len(plan), 2))],
        compiler_params=params(),
        cost_estimate=cost(0, 4 << 20),
        name=name,
    )(*inputs, *deps)


def hold(values, deps):
    def kernel(*refs):
        pass

    n = len(values)
    return pl.pallas_call(
        kernel,
        in_specs=[HBM] * (n + len(deps)),
        out_specs=[HBM] * n,
        out_shape=[sds(v.shape, v.dtype) for v in values],
        input_output_aliases={k: k for k in range(n)},
        compiler_params=params(),
        cost_estimate=cost(0, 1 << 10),
        name="hold",
    )(*values, *deps)


def extend_kernel(p, gain, out):
    out[pl.ds(0, ROWS), :] = p[...]
    g = gain[...]
    hi = g.astype(BF).astype(F32)
    mid = (g - hi).astype(BF).astype(F32)
    row = lax.broadcasted_iota(jnp.int32, (16, 2 * DB), 0)
    tail = jnp.where(row == 0, hi, jnp.where(row == 1, mid, jnp.where(row == 2, g - hi - mid, 0.0)))
    out[pl.ds(ROWS, 16), :] = tail.astype(BF)


def extend(patches, gain):
    return pl.pallas_call(
        extend_kernel,
        out_shape=sds((EXT, 2 * DB)),
        compiler_params=params(),
        cost_estimate=cost(0, 2 << 20),
        name="extend",
    )(patches, gain.reshape(1, 2 * DB))


def merge(n, mean, m2, chunk):
    v = chunk.astype(F32)
    cm = jnp.sum(v, axis=1, keepdims=True) * (1.0 / 768)
    dv = v - cm
    c2 = jnp.sum(dv * dv, axis=1, keepdims=True)
    if n == 0:
        return cm, c2
    delta = cm - mean
    return mean + delta * (1.0 / (n + 1)), m2 + c2 + delta * delta * (768.0 * n / (n + 1))


def two_lanes(a, b):
    lane = lax.broadcasted_iota(jnp.int32, (ROWS, 128), 1)
    return jnp.where(lane == 0, a, jnp.where(lane == 1, b, 0.0))


def stats_kernel(*refs, nraw, ndeps):
    raws = refs[:nraw]
    out, buf, sem = refs[nraw + ndeps:]
    copies = [pltpu.make_async_copy(r, buf.at[j], sem.at[j]) for j, r in enumerate(raws)]
    for c in copies:
        c.start()
    mean = m2 = None
    for j, c in enumerate(copies):
        c.wait()
        mean, m2 = merge(j, mean, m2, buf[j, pl.ds(0, ROWS), :])
    out[...] = two_lanes(mean, m2)


def stats(raws, deps):
    n = len(raws)
    return pl.pallas_call(
        functools.partial(stats_kernel, nraw=n, ndeps=len(deps)),
        in_specs=[HBM] * (n + len(deps)),
        out_specs=VMEM,
        out_shape=sds((ROWS, 128), F32),
        scratch_shapes=[pltpu.VMEM((n, EXT, 2 * DB), BF), pltpu.SemaphoreType.DMA((n,))],
        compiler_params=params(),
        cost_estimate=cost(0, 4 << 20),
        name="row_stats",
    )(*raws, *deps)


def norm_kernel(idx, st, r0, r1, r2, r3, r4, r5, fm, fp, _, n_own, n_oth, st_out, raw, nrm, sr, so):
    core = idx[8]
    copies = []
    for j in range(2):
        copies.append(pltpu.make_async_copy(fm.at[j], raw.at[6 + j, pl.ds(0, HALF)], sr.at[j]))
        copies.append(pltpu.make_async_copy(fp.at[j], raw.at[6 + j, pl.ds(HALF, EXT - HALF)], sr.at[2 + j]))
    for j, r in enumerate((r0, r1, r2, r3, r4, r5)):
        copies.append(pltpu.make_async_copy(r, raw.at[j], sr.at[4 + j]))
    for c in copies:
        c.start()
    for c in copies[:4]:
        c.wait()
    mean, m2 = st[:, 0:1], st[:, 1:2]
    for j in range(2):
        mean, m2 = merge(6 + j, mean, m2, raw[6 + j, pl.ds(0, ROWS), :])
    rstd = lax.rsqrt(m2 * (1.0 / D) + EPS)
    st_out[...] = two_lanes(mean, rstd)
    out = []
    own = pl.ds(pl.multiple_of(core * DB, 128), DB)
    oth = pl.ds(pl.multiple_of((1 - core) * DB, 128), DB)
    for j in (6, 7, 0, 1, 2, 3, 4, 5):
        if j < 6:
            copies[4 + j].wait()
        tail = raw[j, pl.ds(ROWS, 16), :]
        t = tail.astype(F32)
        g = t[0:1] + t[1:2] + t[2:3]
        nrm[j, pl.ds(0, ROWS), :] = ((raw[j, pl.ds(0, ROWS), :].astype(F32) - mean) * rstd * g).astype(BF)
        nrm[j, pl.ds(ROWS, 16), :] = tail
        mine = [pltpu.make_async_copy(nrm.at[j, :, own], n_own.at[idx[j]], so.at[j, 0]),
                pltpu.make_async_copy(nrm.at[j, :, oth], n_oth.at[idx[j]], so.at[j, 1])]
        for c in mine:
            c.start()
        out += mine
    for c in out:
        c.wait()


def normalize(index, st, raws, after):
    return pl.pallas_call(
        norm_kernel,
        in_specs=[SMEM, VMEM] + [HBM] * (len(raws) + 1),
        out_specs=[HBM, HBM, VMEM],
        out_shape=[sds((8, EXT, DB)), sds((8, EXT, DB)), sds((ROWS, 128), F32)],
        scratch_shapes=[
            pltpu.VMEM((8, EXT, 2 * DB), BF),
            pltpu.VMEM((8, EXT, 2 * DB), BF),
            pltpu.SemaphoreType.DMA((10,)),
            pltpu.SemaphoreType.DMA((8, 2)),
        ],
        compiler_params=params(),
        cost_estimate=cost(0, 8 << 20),
        name="normalize",
    )(index, st, *raws, after)


NW = 18


def w_sources(refs):
    own, packed, far, pair, other = refs[:5], refs[5], refs[6:8], refs[8:13], refs[13:18]
    out = [((own[k],), (packed.at[k],)) if k < 3 else (own[3:5], far) for k in range(4)]
    return out + [((pair[k],), (other[k],)) if k < 3 else (pair[3:5], other[3:5]) for k in range(4)]


def w_copies(parts, buf, half, sem):
    out = []
    rows = DB // len(parts)
    for h, part in enumerate(parts):
        at = pl.ds(pl.multiple_of(half * DB + h * rows, 64), rows)
        out += [pltpu.make_async_copy(part.at[j], buf.at[at, pl.ds(j * DB, DB)], sem.at[h, j]) for j in range(3)]
    return out


def to_rows(m1, m2):
    row = lax.broadcasted_iota(jnp.int32, (16, m1.shape[1]), 0)
    out = jnp.zeros((16, m1.shape[1]), F32)
    for k, m in enumerate((m1, m2)):
        hi = m.astype(BF).astype(F32)
        mid = (m - hi).astype(BF).astype(F32)
        for j, part in enumerate((hi, mid, m - hi - mid)):
            out = jnp.where(row == 3 * k + j, part, out)
    return out.astype(BF)


def split(v):
    hi = v.astype(BF)
    return hi, (v - hi.astype(F32)).astype(BF)


def attn_kernel(idx, counts, n_own, n_oth, *refs):
    w_refs, refs = refs[:NW], refs[NW:]
    g_ref, out_ref, dqkv_ref, mom_ref, qkv, nv, wv, mom_s, sn, sw = refs
    h = pl.program_id(0)

    @pl.when(h == 0)
    def _():
        core = idx[8]
        copies = []
        for k, (mine, other) in enumerate(w_sources(w_refs)):
            m = idx[k]
            at = (k % 2) * 2 * DB
            lanes = lambda c: pl.ds(pl.multiple_of(at + c * DB, 128), DB)
            copies.append([pltpu.make_async_copy(n_own.at[m], nv.at[k // 2, :, lanes(core)], sn.at[k, 0]),
                           pltpu.make_async_copy(n_oth.at[m], nv.at[k // 2, :, lanes(1 - core)], sn.at[k, 1])]
                          + w_copies(mine, wv.at[k // 2, pl.ds(at, 2 * DB)], core, sw.at[k, 0])
                          + w_copies(other, wv.at[k // 2, pl.ds(at, 2 * DB)], 1 - core, sw.at[k, 1]))
            for c in copies[-1]:
                c.start()
        mom_s[...] = jnp.zeros_like(mom_s)
        for k in range(4):
            for c in copies[2 * k] + copies[2 * k + 1]:
                c.wait()
            t = nn(nv[k], wv[k])
            if k == 0:
                qkv[...] = t
            else:
                qkv[...] += t

    col = lambda j: pl.ds(pl.multiple_of((j * NH + h) * HD, 128), HD)
    q_ref, k_ref, v_ref = (qkv.at[:, col(j)] for j in range(3))
    e0 = counts[0]
    e1 = e0 + counts[1]
    e2 = e1 + counts[2]
    rid = lax.broadcasted_iota(jnp.int32, (ROWS, 1), 0)
    cid = lax.broadcasted_iota(jnp.int32, (1, ROWS), 1)
    img = lambda p: (p >= e0).astype(jnp.int32) + (p >= e1).astype(jnp.int32) + (p >= e2).astype(jnp.int32)
    same = img(rid) == img(cid)
    scale = HD ** (-0.5)
    q = q_ref[:ROWS, :] * scale
    k = k_ref[:ROWS, :]
    v = v_ref[:ROWS, :]
    qh, ql = split(q)
    kh, kl = split(k)
    vb = v.astype(BF)
    g = g_ref[...]
    s = nt(jnp.concatenate([qh, qh, ql], 1), jnp.concatenate([kh, kl, kh], 1))
    s = jnp.where(same, s, -1e30)
    p = jnp.exp(s - jnp.max(s, axis=1, keepdims=True))
    p = p * (1.0 / jnp.sum(p, axis=1, keepdims=True))
    pb = p.astype(BF)
    out_ref[...] = nn(pb, vb).astype(BF)
    dp = nt(g, vb)
    dv = tn(pb, g)
    ds = p * (dp - jnp.sum(dp * p, axis=1, keepdims=True))
    dsb = ds.astype(BF)
    dq = (nn(dsb, kh) * scale).astype(BF)
    dk = tn(dsb, qh).astype(BF)
    dv = dv.astype(BF)
    dqkv_ref[0] = dq
    dqkv_ref[1] = dk
    dqkv_ref[2] = dv
    m1 = jnp.zeros((ROWS, 1), F32)
    m2 = jnp.zeros((ROWS, 1), F32)
    for d, r in ((dq, q_ref), (dk, k_ref), (dv, v_ref)):
        df = d.astype(F32)
        u = r[ROWS:ROWS + 1, :] + r[ROWS + 1:ROWS + 2, :] + r[ROWS + 2:ROWS + 3, :]
        m1 = m1 + jnp.sum(df * u, axis=1, keepdims=True)
        m2 = m2 + jnp.sum(df * r[:ROWS, :], axis=1, keepdims=True)
    mom_s[pl.ds(0, ROWS), :] += two_lanes(m1, m2)

    @pl.when(h == NH - 1)
    def _():
        t = jnp.transpose(mom_s[...])
        mom_ref[...] = jnp.zeros_like(mom_ref)
        mom_ref[:, pl.ds(0, 640)] = to_rows(t[0:1, :], t[1:2, :])


def attend(index, counts, n_own, n_oth, ws, grad_out):
    return pl.pallas_call(
        attn_kernel,
        grid=(NH,),
        in_specs=[SMEM, SMEM] + [HBM] * (2 + NW) + [pl.BlockSpec((ROWS, HD), lambda h: (0, h))],
        out_specs=[
            pl.BlockSpec((ROWS, HD), lambda h: (0, h)),
            pl.BlockSpec((3, ROWS, HD), lambda h: (0, 0, h)),
            pl.BlockSpec((16, 2 * DB), lambda h: (0, 0)),
        ],
        out_shape=[sds((ROWS, DB)), sds((3, ROWS, DB)), sds((16, 2 * DB))],
        scratch_shapes=[
            pltpu.VMEM((EXT, CW), F32),
            pltpu.VMEM((4, EXT, 4 * DB), BF),
            pltpu.VMEM((4, 4 * DB, CW), BF),
            pltpu.VMEM((640, 128), F32),
            pltpu.SemaphoreType.DMA((8, 2)),
            pltpu.SemaphoreType.DMA((8, 2, 2, 3)),
        ],
        compiler_params=params(),
        cost_estimate=cost(2 * EXT * D * CW, 28 << 20, NH * ROWS * ROWS),
        name="attention",
    )(index, counts, n_own, n_oth, *ws, grad_out)


def grads_kernel(idx, d1, d2, *refs, ny, nx, ndeps, ysplit, xsplit, tail):
    w_refs, (n1, n2), extra, refs = refs[:NW], refs[NW:NW + 2], refs[NW + 1 + ndeps], refs[NW + 2 + ndeps:]
    outs = list(refs[:-8])
    wv, nv, dcat, oy, ox, sd, si, so = refs[-8:]
    core = idx[0]
    dc = [pltpu.make_async_copy(d1.at[j], dcat.at[pl.ds(0, ROWS), pl.ds(j * DB, DB)], sd.at[0, j]) for j in range(3)]
    if nx:
        dc += [pltpu.make_async_copy(d2.at[j], dcat.at[pl.ds(ROWS, ROWS), pl.ds(j * DB, DB)], sd.at[1, j])
               for j in range(3)]
    for c in dc[:3]:
        c.start()
    sources = w_sources(w_refs)
    for i in range(ny):
        a = idx[1 + i]
        for k, (mine, other) in enumerate(sources):
            @pl.when(a == k)
            def _():
                for c in w_copies(mine, wv.at[i], core, si.at[i, 0]) + w_copies(other, wv.at[i], 1 - core, si.at[i, 1]):
                    c.start()
    for c in dc[3:]:
        c.start()
    ncs = []
    for i in range(nx):
        m = idx[1 + ny + i]
        ncs.append([pltpu.make_async_copy(n1.at[m, pl.ds(0, ROWS)], nv.at[i, pl.ds(0, ROWS)], si.at[ny + i, 0, 0, 0]),
                    pltpu.make_async_copy(n2.at[m, pl.ds(0, ROWS)], nv.at[i, pl.ds(ROWS, ROWS)], si.at[ny + i, 1, 0, 0])])
        for c in ncs[-1]:
            c.start()
    ends = []
    if tail:
        ends = [pltpu.make_async_copy(extra, oy.at[i, pl.ds(ROWS, 16)], so.at[i, 1]) for i in range(ny)]
        for c in ends:
            c.start()
    pending = []

    def put(src, dst, sem):
        c = pltpu.make_async_copy(src, dst, sem)
        c.start()
        pending.append(c)

    for c in dc[:3]:
        c.wait()
    for i in range(ny):
        a = idx[1 + i]
        for e in range(2):
            halves = jnp.logical_or(a == 7, a == 3)

            @pl.when(halves)
            def _():
                for c in w_copies(sources[7][e], wv.at[i], e, si.at[i, e]):
                    c.wait()

            @pl.when(jnp.logical_not(halves))
            def _():
                for c in w_copies(sources[0][e], wv.at[i], e, si.at[i, e]):
                    c.wait()
        oy[i, pl.ds(0, ROWS), :] = nt(dcat[pl.ds(0, ROWS), :], wv[i]).astype(BF)
        if tail:
            ends[i].wait()
        if i in ysplit:
            put(oy.at[i, pl.ds(0, HALF)], outs.pop(0), so.at[i, 0])
            put(oy.at[i, pl.ds(HALF, HALF)], outs.pop(0), so.at[i, 1])
        else:
            put(oy.at[i], outs.pop(0), so.at[i, 0])
    for c in dc[3:]:
        c.wait()
    for i in range(nx):
        for c in ncs[i]:
            c.wait()
        t = tn(nv[i], dcat[...]).astype(BF)
        for j in range(3):
            ox[i, j] = t[:, j * DB:(j + 1) * DB]
        if i in xsplit:
            put(ox.at[i, :, pl.ds(0, HB)], outs.pop(0), so.at[ny + i, 0])
            put(ox.at[i, :, pl.ds(HB, HB)], outs.pop(0), so.at[ny + i, 1])
        else:
            put(ox.at[i], outs.pop(0), so.at[ny + i, 0])
    for c in pending:
        c.wait()


def grads(core, ysrc, xsrc, dqkv, d_other, ws, normed, other, deps, ysplit=(), xsplit=(), tail=False):
    ny, nx = len(ysrc), len(xsrc)
    shapes, yrows = [], EXT if tail else ROWS
    for i in range(ny):
        shapes += [(HALF, 2 * DB)] * 2 if i in ysplit else [(yrows, 2 * DB)]
    for i in range(nx):
        shapes += [(3, HB, DB)] * 2 if i in xsplit else [(3, DB, DB)]
    deps = list(deps)
    return pl.pallas_call(
        functools.partial(grads_kernel, ny=ny, nx=nx, ndeps=len(deps), ysplit=ysplit, xsplit=xsplit,
                          tail=tail),
        in_specs=[SMEM] + [HBM] * (4 + NW + len(deps)),
        out_specs=[HBM] * len(shapes),
        out_shape=[sds(s) for s in shapes],
        scratch_shapes=[
            pltpu.VMEM((max(ny, 1), 2 * DB, CW), BF),
            pltpu.VMEM((max(nx, 1), 2 * ROWS, DB), BF),
            pltpu.VMEM((2 * ROWS, CW), BF),
            pltpu.VMEM((max(ny, 1), yrows, 2 * DB), BF),
            pltpu.VMEM((max(nx, 1), 3, DB, DB), BF),
            pltpu.SemaphoreType.DMA((2, 3)),
            pltpu.SemaphoreType.DMA((ny + nx, 2, 2, 3)),
            pltpu.SemaphoreType.DMA((ny + nx, 2)),
        ],
        compiler_params=params(),
        cost_estimate=cost(0, 1 << 12),
        name="grads",
    )(ivec(core, *ysrc, *xsrc), dqkv, d_other, *ws, normed, other, *deps)


def sum_rows_kernel(mine, own, *refs):
    out = refs[-1]
    total = mine[...].astype(F32)
    rows = own[...].astype(F32)
    for r in refs[:3]:
        total = total + r[pl.ds(0, ROWS), :].astype(F32)
        rows = rows + r[pl.ds(ROWS, 16), :].astype(F32)
    out[pl.ds(0, ROWS), :] = total.astype(BF)
    m1 = rows[0:1] + rows[1:2] + rows[2:3]
    m2 = rows[3:4] + rows[4:5] + rows[5:6]
    out[pl.ds(ROWS, 16), :] = to_rows(m1, m2)


def sum_rows(mine, own, arrived, deps):
    whole = lambda v: pl.BlockSpec(v.shape, lambda i: (0,) * v.ndim)
    return pl.pallas_call(
        sum_rows_kernel,
        grid=(1,),
        in_specs=[whole(v) for v in (mine, own, *arrived)] + [HBM] * len(deps),
        out_specs=whole(arrived[0]),
        out_shape=sds(arrived[0].shape),
        compiler_params=params(),
        cost_estimate=cost(0, 1 << 12),
        name="sum_rows",
    )(mine, own, *arrived, *deps)


def sum_kernel(*refs, n):
    total = refs[0][...].astype(F32)
    for r in refs[1:n]:
        total = total + r[...].astype(F32)
    refs[-1][...] = total.astype(BF)


def sum_blocks(vs, deps):
    n = len(vs)
    spec = pl.BlockSpec((1, DB, DB), lambda i: (i, 0, 0))
    return pl.pallas_call(
        functools.partial(sum_kernel, n=n),
        grid=(3,),
        in_specs=[spec] * n + [HBM] * len(deps),
        out_specs=spec,
        out_shape=sds(vs[0].shape),
        compiler_params=params(),
        cost_estimate=cost(0, 1 << 12),
        name="sum_blocks",
    )(*vs, *deps)


def ivec(*v):
    return jnp.stack([jnp.asarray(e, jnp.int32) for e in v])


def local(patches, gain, w_qkv, counts, grad_out):
    si, mi = lax.axis_index("seq"), lax.axis_index("mp")
    core, x, zh = si % 2, (si // 2) % 4, si // 8
    y, zl = mi // 2, mi % 2
    mw = lambda dx, dz: jnp.where(dz == 0, zh, 1 - zh) * 4 + (x + dx) % 4
    mx = lambda dy, dz: ((y + dy) % 4) * 2 + jnp.where(dz == 0, zl, 1 - zl)
    rows, wshape = (EXT, 2 * DB), (3, DB, DB)
    lo, hi = (slice(None), pl.ds(0, HB)), (slice(None), pl.ds(HB, HB))
    first, rest = (pl.ds(0, HALF),), (pl.ds(HALF, EXT - HALF),)

    p0 = extend(patches, gain)
    w = jnp.transpose(w_qkv, (1, 0, 2))
    p_m, p_p, pz = mpp(p0, YP), mpp(p0, YM), mpp(p0, ZLO)
    w_m, w_p = sp(w, XP), sp(w, XM)
    pz1, w1 = move([pz, w], [rows, wshape], [(0, None, 0, None), (1, None, 1, None)], [p_m, p_p], "gate_y1")
    pz_m, pz_p = mpp(pz1, YP), mpp(pz1, YM)
    wz = sp(w1, ZHI)
    w_lo, w_hi = move([w_m, w_p], [(3, HB, DB)] * 2, [(0, lo, 0, None), (1, hi, 1, None)], [pz1], "gate_x1")
    wf_m, wf_p = sp(w_lo, XP), sp(w_hi, XM)
    (w3,) = move([w1, w_m, w_p], [(3,) + wshape], [(k, None, 0, (k,)) for k in range(3)], [w_lo], "pack")
    fu, fd = move(
        [p_m, p_p, pz_m, pz_p], [(2, HALF, 2 * DB), (2, EXT - HALF, 2 * DB)],
        [(0, first, 0, (0,)), (2, first, 0, (1,)), (1, rest, 1, (0,)), (3, rest, 1, (1,))], [w_lo, w3], "gate_y2")
    f_m, f_p = mpp(fu, YP), mpp(fd, YM)
    (wz1,) = move([wz], [wshape], [(0, None, 0, None)], [wf_m, wf_p, fu], "gate_x2")
    wz_m, wz_p = sp(wz1, XP), sp(wz1, XM)
    (w3,) = hold([w3], [wz1])
    o_w = sp(w3, CORE)
    st = stats([p0, pz, p_m, p_p, pz_m, pz_p], [wz1])
    wz_lo, wz_hi, wz2 = move(
        [wz_m, wz_p, wz1], [(3, HB, DB), (3, HB, DB), wshape],
        [(0, lo, 0, None), (1, hi, 1, None), (2, None, 2, None)],
        [f_m, f_p, o_w, st], "gate_x3")
    wzf_m, wzf_p = sp(wz_lo, XP), sp(wz_hi, XM)
    wf_m, wf_p = hold([wf_m, wf_p], [wz_lo])
    o_fm, o_fp = sp(wf_m, CORE), sp(wf_p, CORE)
    o_z, o_zm, o_zp = (sp(v, CORE) for v in (wz2, wz_m, wz_p))
    index = ivec(mx(0, 0), mx(0, 1), mx(-1, 0), mx(1, 0), mx(-1, 1), mx(1, 1), mx(2, 0), mx(2, 1), core)
    n_own, n_oth, st = normalize(index, st, [p0, pz, p_m, p_p, pz_m, pz_p, f_m, f_p], wz_lo)
    mean, rstd = st[:, 0:1], st[:, 1:2]
    wzf_m, wzf_p, n_oth = hold([wzf_m, wzf_p, n_oth], [o_z])
    o_zfm, o_zfp = sp(wzf_m, CORE), sp(wzf_p, CORE)
    (n_oth,) = hold([n_oth], [o_zfm, o_zfp, o_zm, o_zp, o_fm, o_fp])
    n_other = sp(n_oth, CORE)
    ws = [w1, w_m, w_p, wf_m, wf_p, o_w, o_fm, o_fp,
          wz2, wz_m, wz_p, wzf_m, wzf_p, o_z, o_zm, o_zp, o_zfm, o_zfp]
    windex = ivec(mw(0, 0), mw(-1, 0), mw(1, 0), mw(2, 0), mw(0, 1), mw(-1, 1), mw(1, 1), mw(2, 1), core)
    heads_out, dqkv, mom = attend(windex, counts.reshape(4), n_own, n_oth, ws, grad_out)

    d_other = sp(dqkv, CORE)

    def source(dy, dz):
        m = mx(dy, dz)
        dx = (m % 4 - x) % 4
        return jnp.where(dx == 3, 1, jnp.where(dx == 1, 2, jnp.where(dx == 2, 3, 0))) + jnp.where(m // 4 == zh, 0, 4)

    def blocks(yb, xb, deps, **kw):
        return grads(core, [source(*b) for b in yb], [mw(*b) for b in xb], dqkv, d_other if xb else dqkv, ws, n_own,
                     n_other if xb else n_own, deps, **kw)

    yu, yd, y2 = blocks([(1, 1), (-1, 1), (2, 1)], [], [mom], tail=True)
    ya = [mpp(yu, YP), mpp(yd, YM), mpp(y2, Y2)]
    xu, xd = blocks([], [(1, 1), (-1, 1)], [yu])
    xa = [sp(xu, XP), sp(xd, XM)]
    y2o, y1u, y1d, y0p, x2 = blocks([(2, 0), (1, 0), (-1, 0), (0, 1)], [(2, 1)], [xu])
    xa.append(sp(x2, X2))
    x2o, x1u, x1d, x0p = blocks([], [(2, 0), (1, 0), (-1, 0), (0, 1)], [y0p])
    y_out = sum_rows(y0p, mom, ya, [x0p])
    yz = mpp(y_out, ZLO)
    yb1, yb2 = mpp(y1u, YP), mpp(y1d, YM)
    x_out = sum_blocks([x0p, *xa], [y_out])
    xb1, xb2 = sp(x1u, XP), sp(x1d, XM)
    (y2o,) = hold([y2o], [yz, yb1, yb2, x_out])
    (x_out,) = hold([x_out], [y2o])
    yb3, xz = mpp(y2o, Y2), sp(x_out, ZHI)
    y0, x0 = blocks([(0, 0)], [(0, 0)], [x_out])
    (x2o,) = hold([x2o], [xb1, xb2, y0])
    xb3 = sp(x2o, X2)

    f = lambda v: v.astype(F32)
    mom = jnp.sum((f(y_out[ROWS:ROWS + 6]) + f(yz[ROWS:ROWS + 6])).reshape(2, 3, 2 * DB), axis=1)[:, :ROWS] / D
    gn = f(y0) + f(yb1) + f(yb2) + f(yb3) + f(yz[:ROWS])
    xhat = (f(patches) - mean) * rstd
    gg = jnp.sum(gn * xhat, axis=0)
    for perm in (CORE, ZHI):
        gg = gg + sp(gg, perm)
    gg = (gg + sp(gg, X2)) + (sp(gg, XP) + sp(gg, XM))
    grad_p = ((gn * gain[None, :] - mom[0][:, None] - xhat * mom[1][:, None]) * rstd).astype(BF)
    gw = jnp.transpose(f(x0) + f(xb1) + f(xb2) + f(xb3) + f(xz), (1, 0, 2))
    return heads_out, grad_p, gg, gw


def solution(mesh):
    placed = (P("seq", "mp"), P("mp"), P("seq", None, "mp"), P("seq", None), P("seq", "mp"))
    return jax.shard_map(
        local,
        mesh=mesh,
        in_specs=placed,
        out_specs=(P("seq", "mp"), P("seq", "mp"), P("mp"), P("seq", None, "mp")),
        check_vma=False,
    )
```

```python
import functools

import jax
import jax.numpy as jnp
from jax import lax
from jax.experimental import pallas as pl
from jax.experimental.pallas import tpu as pltpu
from jax.sharding import PartitionSpec as P

HD = 128
NH = 3
ROWS = 576
HALF = ROWS // 2
EXT = ROWS + 16
DB = 384
HB = DB // 2
D = 6144
CW = 3 * DB
EPS = 1e-06
BF = jnp.bfloat16
F32 = jnp.float32
HBM = pl.BlockSpec(memory_space=pltpu.HBM)
VMEM = pl.BlockSpec(memory_space=pltpu.VMEM)
SMEM = pl.BlockSpec(memory_space=pltpu.SMEM)


def seq_perm(f):
    out = []
    for i in range(16):
        zh, x, c = f(i // 8, (i // 2) % 4, i % 2)
        out.append((i, (zh * 4 + x % 4) * 2 + c))
    return out


def mp_perm(f):
    out = []
    for i in range(8):
        y, zl = f(i // 2, i % 2)
        out.append((i, (y % 4) * 2 + zl))
    return out


CORE = seq_perm(lambda zh, x, c: (zh, x, 1 - c))
ZHI = seq_perm(lambda zh, x, c: (1 - zh, x, c))
XP = seq_perm(lambda zh, x, c: (zh, x + 1, c))
XM = seq_perm(lambda zh, x, c: (zh, x - 1, c))
X2 = seq_perm(lambda zh, x, c: (zh, x + 2, c))
ZLO = mp_perm(lambda y, zl: (y, 1 - zl))
YP = mp_perm(lambda y, zl: (y + 1, zl))
YM = mp_perm(lambda y, zl: (y - 1, zl))
Y2 = mp_perm(lambda y, zl: (y + 2, zl))


def sp(v, perm):
    return lax.ppermute(v, "seq", perm)


def mpp(v, perm):
    return lax.ppermute(v, "mp", perm)


def nt(a, b):
    return lax.dot_general(a, b, (((1,), (1,)), ((), ())), preferred_element_type=F32)


def tn(a, b):
    return lax.dot_general(a, b, (((0,), (0,)), ((), ())), preferred_element_type=F32)


def nn(a, b):
    return lax.dot_general(a, b, (((1,), (0,)), ((), ())), preferred_element_type=F32)


def sds(shape, dtype=BF):
    return jax.ShapeDtypeStruct(shape, dtype)


def params(mib=63):
    return pltpu.CompilerParams(vmem_limit_bytes=mib << 20)


def cost(flops, nbytes, exps=0):
    return pl.CostEstimate(flops=int(flops), bytes_accessed=int(nbytes), transcendentals=exps)


def sliced(shape, index):
    if not index:
        return shape
    out = []
    for n, i in zip(shape, index):
        if not isinstance(i, int):
            out.append(n if isinstance(i, slice) else i.size)
    return tuple(out) + tuple(shape[len(index):])


def move(inputs, outs, plan, deps, name):
    def kernel(*refs):
        ins = refs[:len(inputs)]
        dst = refs[len(inputs) + len(deps):][:len(outs)]
        *bufs, sem = refs[len(inputs) + len(deps) + len(outs):]
        get = [pltpu.make_async_copy(ins[i].at[si] if si else ins[i], bufs[k], sem.at[k, 0])
               for k, (i, si, o, so) in enumerate(plan)]
        put = [pltpu.make_async_copy(bufs[k], dst[o].at[so] if so else dst[o], sem.at[k, 1])
               for k, (i, si, o, so) in enumerate(plan)]
        for c in get:
            c.start()
        for g, p in zip(get, put):
            g.wait()
            p.start()
        for p in put:
            p.wait()

    return pl.pallas_call(
        kernel,
        in_specs=[HBM] * (len(inputs) + len(deps)),
        out_specs=[HBM] * len(outs),
        out_shape=[sds(s) for s in outs],
        scratch_shapes=[pltpu.VMEM(sliced(inputs[i].shape, si), BF) for i, si, o, so in plan]
        + [pltpu.SemaphoreType.DMA((len(plan), 2))],
        compiler_params=params(),
        cost_estimate=cost(0, 4 << 20),
        name=name,
    )(*inputs, *deps)


def hold(values, deps):
    def kernel(*refs):
        pass

    n = len(values)
    return pl.pallas_call(
        kernel,
        in_specs=[HBM] * (n + len(deps)),
        out_specs=[HBM] * n,
        out_shape=[sds(v.shape, v.dtype) for v in values],
        input_output_aliases={k: k for k in range(n)},
        compiler_params=params(),
        cost_estimate=cost(0, 1 << 10),
        name="hold",
    )(*values, *deps)


def extend_kernel(p, gain, out):
    out[pl.ds(0, ROWS), :] = p[...]
    g = gain[...]
    hi = g.astype(BF).astype(F32)
    mid = (g - hi).astype(BF).astype(F32)
    row = lax.broadcasted_iota(jnp.int32, (16, 2 * DB), 0)
    tail = jnp.where(row == 0, hi, jnp.where(row == 1, mid, jnp.where(row == 2, g - hi - mid, 0.0)))
    out[pl.ds(ROWS, 16), :] = tail.astype(BF)


def extend(patches, gain):
    return pl.pallas_call(
        extend_kernel,
        out_shape=sds((EXT, 2 * DB)),
        compiler_params=params(),
        cost_estimate=cost(0, 2 << 20),
        name="extend",
    )(patches, gain.reshape(1, 2 * DB))


def merge(n, mean, m2, chunk):
    v = chunk.astype(F32)
    cm = jnp.sum(v, axis=1, keepdims=True) * (1.0 / 768)
    dv = v - cm
    c2 = jnp.sum(dv * dv, axis=1, keepdims=True)
    if n == 0:
        return cm, c2
    delta = cm - mean
    return mean + delta * (1.0 / (n + 1)), m2 + c2 + delta * delta * (768.0 * n / (n + 1))


def two_lanes(a, b):
    lane = lax.broadcasted_iota(jnp.int32, (ROWS, 128), 1)
    return jnp.where(lane == 0, a, jnp.where(lane == 1, b, 0.0))


def stats_kernel(*refs, nraw, ndeps):
    raws = refs[:nraw]
    out, buf, sem = refs[nraw + ndeps:]
    copies = [pltpu.make_async_copy(r, buf.at[j], sem.at[j]) for j, r in enumerate(raws)]
    for c in copies:
        c.start()
    mean = m2 = None
    for j, c in enumerate(copies):
        c.wait()
        mean, m2 = merge(j, mean, m2, buf[j, pl.ds(0, ROWS), :])
    out[...] = two_lanes(mean, m2)


def stats(raws, deps):
    n = len(raws)
    return pl.pallas_call(
        functools.partial(stats_kernel, nraw=n, ndeps=len(deps)),
        in_specs=[HBM] * (n + len(deps)),
        out_specs=VMEM,
        out_shape=sds((ROWS, 128), F32),
        scratch_shapes=[pltpu.VMEM((n, EXT, 2 * DB), BF), pltpu.SemaphoreType.DMA((n,))],
        compiler_params=params(),
        cost_estimate=cost(0, 4 << 20),
        name="row_stats",
    )(*raws, *deps)


def norm_kernel(idx, st, r0, r1, r2, r3, r4, r5, fm, fp, _, n_own, n_oth, st_out, raw, nrm, sr, so):
    core = idx[8]
    copies = []
    for j in range(2):
        copies.append(pltpu.make_async_copy(fm.at[j], raw.at[6 + j, pl.ds(0, HALF)], sr.at[j]))
        copies.append(pltpu.make_async_copy(fp.at[j], raw.at[6 + j, pl.ds(HALF, EXT - HALF)], sr.at[2 + j]))
    for j, r in enumerate((r0, r1, r2, r3, r4, r5)):
        copies.append(pltpu.make_async_copy(r, raw.at[j], sr.at[4 + j]))
    for c in copies:
        c.start()
    for c in copies[:4]:
        c.wait()
    mean, m2 = st[:, 0:1], st[:, 1:2]
    for j in range(2):
        mean, m2 = merge(6 + j, mean, m2, raw[6 + j, pl.ds(0, ROWS), :])
    rstd = lax.rsqrt(m2 * (1.0 / D) + EPS)
    st_out[...] = two_lanes(mean, rstd)
    out = []
    own = pl.ds(pl.multiple_of(core * DB, 128), DB)
    oth = pl.ds(pl.multiple_of((1 - core) * DB, 128), DB)
    for j in (6, 7, 0, 1, 2, 3, 4, 5):
        if j < 6:
            copies[4 + j].wait()
        tail = raw[j, pl.ds(ROWS, 16), :]
        t = tail.astype(F32)
        g = t[0:1] + t[1:2] + t[2:3]
        nrm[j, pl.ds(0, ROWS), :] = ((raw[j, pl.ds(0, ROWS), :].astype(F32) - mean) * rstd * g).astype(BF)
        nrm[j, pl.ds(ROWS, 16), :] = tail
        mine = [pltpu.make_async_copy(nrm.at[j, :, own], n_own.at[idx[j]], so.at[j, 0]),
                pltpu.make_async_copy(nrm.at[j, :, oth], n_oth.at[idx[j]], so.at[j, 1])]
        for c in mine:
            c.start()
        out += mine
    for c in out:
        c.wait()


def normalize(index, st, raws, after):
    return pl.pallas_call(
        norm_kernel,
        in_specs=[SMEM, VMEM] + [HBM] * (len(raws) + 1),
        out_specs=[HBM, HBM, VMEM],
        out_shape=[sds((8, EXT, DB)), sds((8, EXT, DB)), sds((ROWS, 128), F32)],
        scratch_shapes=[
            pltpu.VMEM((8, EXT, 2 * DB), BF),
            pltpu.VMEM((8, EXT, 2 * DB), BF),
            pltpu.SemaphoreType.DMA((10,)),
            pltpu.SemaphoreType.DMA((8, 2)),
        ],
        compiler_params=params(),
        cost_estimate=cost(0, 8 << 20),
        name="normalize",
    )(index, st, *raws, after)


NW = 18


def w_sources(refs):
    own, packed, far, pair, other = refs[:5], refs[5], refs[6:8], refs[8:13], refs[13:18]
    out = [((own[k],), (packed.at[k],)) if k < 3 else (own[3:5], far) for k in range(4)]
    return out + [((pair[k],), (other[k],)) if k < 3 else (pair[3:5], other[3:5]) for k in range(4)]


def w_copies(parts, buf, half, sem):
    out = []
    rows = DB // len(parts)
    for h, part in enumerate(parts):
        at = pl.ds(pl.multiple_of(half * DB + h * rows, 64), rows)
        out += [pltpu.make_async_copy(part.at[j], buf.at[at, pl.ds(j * DB, DB)], sem.at[h, j]) for j in range(3)]
    return out


def to_rows(m1, m2):
    row = lax.broadcasted_iota(jnp.int32, (16, m1.shape[1]), 0)
    out = jnp.zeros((16, m1.shape[1]), F32)
    for k, m in enumerate((m1, m2)):
        hi = m.astype(BF).astype(F32)
        mid = (m - hi).astype(BF).astype(F32)
        for j, part in enumerate((hi, mid, m - hi - mid)):
            out = jnp.where(row == 3 * k + j, part, out)
    return out.astype(BF)


def split(v):
    hi = v.astype(BF)
    return hi, (v - hi.astype(F32)).astype(BF)


def attn_kernel(idx, counts, n_own, n_oth, *refs):
    w_refs, refs = refs[:NW], refs[NW:]
    g_ref, out_ref, dqkv_ref, mom_ref, qkv, nv, wv, mom_s, sn, sw = refs
    h = pl.program_id(0)

    @pl.when(h == 0)
    def _():
        core = idx[8]
        copies = []
        for k, (mine, other) in enumerate(w_sources(w_refs)):
            m = idx[k]
            at = (k % 2) * 2 * DB
            lanes = lambda c: pl.ds(pl.multiple_of(at + c * DB, 128), DB)
            copies.append([pltpu.make_async_copy(n_own.at[m], nv.at[k // 2, :, lanes(core)], sn.at[k, 0]),
                           pltpu.make_async_copy(n_oth.at[m], nv.at[k // 2, :, lanes(1 - core)], sn.at[k, 1])]
                          + w_copies(mine, wv.at[k // 2, pl.ds(at, 2 * DB)], core, sw.at[k, 0])
                          + w_copies(other, wv.at[k // 2, pl.ds(at, 2 * DB)], 1 - core, sw.at[k, 1]))
            for c in copies[-1]:
                c.start()
        mom_s[...] = jnp.zeros_like(mom_s)
        for k in range(4):
            for c in copies[2 * k] + copies[2 * k + 1]:
                c.wait()
            t = nn(nv[k], wv[k])
            if k == 0:
                qkv[...] = t
            else:
                qkv[...] += t

    col = lambda j: pl.ds(pl.multiple_of((j * NH + h) * HD, 128), HD)
    q_ref, k_ref, v_ref = (qkv.at[:, col(j)] for j in range(3))
    e0 = counts[0]
    e1 = e0 + counts[1]
    e2 = e1 + counts[2]
    rid = lax.broadcasted_iota(jnp.int32, (ROWS, 1), 0)
    cid = lax.broadcasted_iota(jnp.int32, (1, ROWS), 1)
    img = lambda p: (p >= e0).astype(jnp.int32) + (p >= e1).astype(jnp.int32) + (p >= e2).astype(jnp.int32)
    same = img(rid) == img(cid)
    scale = HD ** (-0.5)
    q = q_ref[:ROWS, :] * scale
    k = k_ref[:ROWS, :]
    v = v_ref[:ROWS, :]
    qh, ql = split(q)
    kh, kl = split(k)
    vb = v.astype(BF)
    g = g_ref[...]
    s = nt(jnp.concatenate([qh, qh, ql], 1), jnp.concatenate([kh, kl, kh], 1))
    s = jnp.where(same, s, -1e30)
    p = jnp.exp(s - jnp.max(s, axis=1, keepdims=True))
    p = p * (1.0 / jnp.sum(p, axis=1, keepdims=True))
    pb = p.astype(BF)
    out_ref[...] = nn(pb, vb).astype(BF)
    dp = nt(g, vb)
    dv = tn(pb, g)
    ds = p * (dp - jnp.sum(dp * p, axis=1, keepdims=True))
    dsb = ds.astype(BF)
    dq = (nn(dsb, kh) * scale).astype(BF)
    dk = tn(dsb, qh).astype(BF)
    dv = dv.astype(BF)
    dqkv_ref[0] = dq
    dqkv_ref[1] = dk
    dqkv_ref[2] = dv
    m1 = jnp.zeros((ROWS, 1), F32)
    m2 = jnp.zeros((ROWS, 1), F32)
    for d, r in ((dq, q_ref), (dk, k_ref), (dv, v_ref)):
        df = d.astype(F32)
        u = r[ROWS:ROWS + 1, :] + r[ROWS + 1:ROWS + 2, :] + r[ROWS + 2:ROWS + 3, :]
        m1 = m1 + jnp.sum(df * u, axis=1, keepdims=True)
        m2 = m2 + jnp.sum(df * r[:ROWS, :], axis=1, keepdims=True)
    mom_s[pl.ds(0, ROWS), :] += two_lanes(m1, m2)

    @pl.when(h == NH - 1)
    def _():
        t = jnp.transpose(mom_s[...])
        mom_ref[...] = jnp.zeros_like(mom_ref)
        mom_ref[:, pl.ds(0, 640)] = to_rows(t[0:1, :], t[1:2, :])


def attend(index, counts, n_own, n_oth, ws, grad_out):
    return pl.pallas_call(
        attn_kernel,
        grid=(NH,),
        in_specs=[SMEM, SMEM] + [HBM] * (2 + NW) + [pl.BlockSpec((ROWS, HD), lambda h: (0, h))],
        out_specs=[
            pl.BlockSpec((ROWS, HD), lambda h: (0, h)),
            pl.BlockSpec((3, ROWS, HD), lambda h: (0, 0, h)),
            pl.BlockSpec((16, 2 * DB), lambda h: (0, 0)),
        ],
        out_shape=[sds((ROWS, DB)), sds((3, ROWS, DB)), sds((16, 2 * DB))],
        scratch_shapes=[
            pltpu.VMEM((EXT, CW), F32),
            pltpu.VMEM((4, EXT, 4 * DB), BF),
            pltpu.VMEM((4, 4 * DB, CW), BF),
            pltpu.VMEM((640, 128), F32),
            pltpu.SemaphoreType.DMA((8, 2)),
            pltpu.SemaphoreType.DMA((8, 2, 2, 3)),
        ],
        compiler_params=params(),
        cost_estimate=cost(2 * EXT * D * CW, 28 << 20, NH * ROWS * ROWS),
        name="attention",
    )(index, counts, n_own, n_oth, *ws, grad_out)


def grads_kernel(idx, d1, d2, *refs, ny, nx, ndeps, ysplit, xsplit, tail):
    w_refs, (n1, n2), extra, refs = refs[:NW], refs[NW:NW + 2], refs[NW + 1 + ndeps], refs[NW + 2 + ndeps:]
    outs = list(refs[:-8])
    wv, nv, dcat, oy, ox, sd, si, so = refs[-8:]
    core = idx[0]
    dc = [pltpu.make_async_copy(d1.at[j], dcat.at[pl.ds(0, ROWS), pl.ds(j * DB, DB)], sd.at[0, j]) for j in range(3)]
    if nx:
        dc += [pltpu.make_async_copy(d2.at[j], dcat.at[pl.ds(ROWS, ROWS), pl.ds(j * DB, DB)], sd.at[1, j])
               for j in range(3)]
    for c in dc[:3]:
        c.start()
    sources = w_sources(w_refs)
    for i in range(ny):
        a = idx[1 + i]
        for k, (mine, other) in enumerate(sources):
            @pl.when(a == k)
            def _():
                for c in w_copies(mine, wv.at[i], core, si.at[i, 0]) + w_copies(other, wv.at[i], 1 - core, si.at[i, 1]):
                    c.start()
    for c in dc[3:]:
        c.start()
    ncs = []
    for i in range(nx):
        m = idx[1 + ny + i]
        ncs.append([pltpu.make_async_copy(n1.at[m, pl.ds(0, ROWS)], nv.at[i, pl.ds(0, ROWS)], si.at[ny + i, 0, 0, 0]),
                    pltpu.make_async_copy(n2.at[m, pl.ds(0, ROWS)], nv.at[i, pl.ds(ROWS, ROWS)], si.at[ny + i, 1, 0, 0])])
        for c in ncs[-1]:
            c.start()
    ends = []
    if tail:
        ends = [pltpu.make_async_copy(extra, oy.at[i, pl.ds(ROWS, 16)], so.at[i, 1]) for i in range(ny)]
        for c in ends:
            c.start()
    pending = []

    def put(src, dst, sem):
        c = pltpu.make_async_copy(src, dst, sem)
        c.start()
        pending.append(c)

    for c in dc[:3]:
        c.wait()
    for i in range(ny):
        a = idx[1 + i]
        for e in range(2):
            halves = jnp.logical_or(a == 7, a == 3)

            @pl.when(halves)
            def _():
                for c in w_copies(sources[7][e], wv.at[i], e, si.at[i, e]):
                    c.wait()

            @pl.when(jnp.logical_not(halves))
            def _():
                for c in w_copies(sources[0][e], wv.at[i], e, si.at[i, e]):
                    c.wait()
        oy[i, pl.ds(0, ROWS), :] = nt(dcat[pl.ds(0, ROWS), :], wv[i]).astype(BF)
        if tail:
            ends[i].wait()
        if i in ysplit:
            put(oy.at[i, pl.ds(0, HALF)], outs.pop(0), so.at[i, 0])
            put(oy.at[i, pl.ds(HALF, HALF)], outs.pop(0), so.at[i, 1])
        else:
            put(oy.at[i], outs.pop(0), so.at[i, 0])
    for c in dc[3:]:
        c.wait()
    for i in range(nx):
        for c in ncs[i]:
            c.wait()
        t = tn(nv[i], dcat[...]).astype(BF)
        for j in range(3):
            ox[i, j] = t[:, j * DB:(j + 1) * DB]
        if i in xsplit:
            put(ox.at[i, :, pl.ds(0, HB)], outs.pop(0), so.at[ny + i, 0])
            put(ox.at[i, :, pl.ds(HB, HB)], outs.pop(0), so.at[ny + i, 1])
        else:
            put(ox.at[i], outs.pop(0), so.at[ny + i, 0])
    for c in pending:
        c.wait()


def grads(core, ysrc, xsrc, dqkv, d_other, ws, normed, other, deps, ysplit=(), xsplit=(), tail=False):
    ny, nx = len(ysrc), len(xsrc)
    shapes, yrows = [], EXT if tail else ROWS
    for i in range(ny):
        shapes += [(HALF, 2 * DB)] * 2 if i in ysplit else [(yrows, 2 * DB)]
    for i in range(nx):
        shapes += [(3, HB, DB)] * 2 if i in xsplit else [(3, DB, DB)]
    deps = list(deps)
    return pl.pallas_call(
        functools.partial(grads_kernel, ny=ny, nx=nx, ndeps=len(deps), ysplit=ysplit, xsplit=xsplit,
                          tail=tail),
        in_specs=[SMEM] + [HBM] * (4 + NW + len(deps)),
        out_specs=[HBM] * len(shapes),
        out_shape=[sds(s) for s in shapes],
        scratch_shapes=[
            pltpu.VMEM((max(ny, 1), 2 * DB, CW), BF),
            pltpu.VMEM((max(nx, 1), 2 * ROWS, DB), BF),
            pltpu.VMEM((2 * ROWS, CW), BF),
            pltpu.VMEM((max(ny, 1), yrows, 2 * DB), BF),
            pltpu.VMEM((max(nx, 1), 3, DB, DB), BF),
            pltpu.SemaphoreType.DMA((2, 3)),
            pltpu.SemaphoreType.DMA((ny + nx, 2, 2, 3)),
            pltpu.SemaphoreType.DMA((ny + nx, 2)),
        ],
        compiler_params=params(),
        cost_estimate=cost(0, 1 << 12),
        name="grads",
    )(ivec(core, *ysrc, *xsrc), dqkv, d_other, *ws, normed, other, *deps)


def sum_rows_kernel(mine, own, *refs):
    out = refs[-1]
    total = mine[...].astype(F32)
    rows = own[...].astype(F32)
    for r in refs[:3]:
        total = total + r[pl.ds(0, ROWS), :].astype(F32)
        rows = rows + r[pl.ds(ROWS, 16), :].astype(F32)
    out[pl.ds(0, ROWS), :] = total.astype(BF)
    m1 = rows[0:1] + rows[1:2] + rows[2:3]
    m2 = rows[3:4] + rows[4:5] + rows[5:6]
    out[pl.ds(ROWS, 16), :] = to_rows(m1, m2)


def sum_rows(mine, own, arrived, deps):
    whole = lambda v: pl.BlockSpec(v.shape, lambda i: (0,) * v.ndim)
    return pl.pallas_call(
        sum_rows_kernel,
        grid=(1,),
        in_specs=[whole(v) for v in (mine, own, *arrived)] + [HBM] * len(deps),
        out_specs=whole(arrived[0]),
        out_shape=sds(arrived[0].shape),
        compiler_params=params(),
        cost_estimate=cost(0, 1 << 12),
        name="sum_rows",
    )(mine, own, *arrived, *deps)


def sum_kernel(*refs, n):
    total = refs[0][...].astype(F32)
    for r in refs[1:n]:
        total = total + r[...].astype(F32)
    refs[-1][...] = total.astype(BF)


def sum_blocks(vs, deps):
    n = len(vs)
    spec = pl.BlockSpec((1, DB, DB), lambda i: (i, 0, 0))
    return pl.pallas_call(
        functools.partial(sum_kernel, n=n),
        grid=(3,),
        in_specs=[spec] * n + [HBM] * len(deps),
        out_specs=spec,
        out_shape=sds(vs[0].shape),
        compiler_params=params(),
        cost_estimate=cost(0, 1 << 12),
        name="sum_blocks",
    )(*vs, *deps)


def ivec(*v):
    return jnp.stack([jnp.asarray(e, jnp.int32) for e in v])


def local(patches, gain, w_qkv, counts, grad_out):
    si, mi = lax.axis_index("seq"), lax.axis_index("mp")
    core, x, zh = si % 2, (si // 2) % 4, si // 8
    y, zl = mi // 2, mi % 2
    mw = lambda dx, dz: jnp.where(dz == 0, zh, 1 - zh) * 4 + (x + dx) % 4
    mx = lambda dy, dz: ((y + dy) % 4) * 2 + jnp.where(dz == 0, zl, 1 - zl)
    rows, wshape = (EXT, 2 * DB), (3, DB, DB)
    lo, hi = (slice(None), pl.ds(0, HB)), (slice(None), pl.ds(HB, HB))
    first, rest = (pl.ds(0, HALF),), (pl.ds(HALF, EXT - HALF),)

    p0 = extend(patches, gain)
    w = jnp.transpose(w_qkv, (1, 0, 2))
    p_m, p_p, pz = mpp(p0, YP), mpp(p0, YM), mpp(p0, ZLO)
    w_m, w_p = sp(w, XP), sp(w, XM)
    pz1, w1 = move([pz, w], [rows, wshape], [(0, None, 0, None), (1, None, 1, None)], [p_m, p_p], "gate_y1")
    pz_m, pz_p = mpp(pz1, YP), mpp(pz1, YM)
    wz = sp(w1, ZHI)
    w_lo, w_hi = move([w_m, w_p], [(3, HB, DB)] * 2, [(0, lo, 0, None), (1, hi, 1, None)], [pz1], "gate_x1")
    wf_m, wf_p = sp(w_lo, XP), sp(w_hi, XM)
    (w3,) = move([w1, w_m, w_p], [(3,) + wshape], [(k, None, 0, (k,)) for k in range(3)], [w_lo], "pack")
    fu, fd = move(
        [p_m, p_p, pz_m, pz_p], [(2, HALF, 2 * DB), (2, EXT - HALF, 2 * DB)],
        [(0, first, 0, (0,)), (2, first, 0, (1,)), (1, rest, 1, (0,)), (3, rest, 1, (1,))], [w_lo, w3], "gate_y2")
    f_m, f_p = mpp(fu, YP), mpp(fd, YM)
    (wz1,) = move([wz], [wshape], [(0, None, 0, None)], [wf_m, wf_p, fu], "gate_x2")
    wz_m, wz_p = sp(wz1, XP), sp(wz1, XM)
    (w3,) = hold([w3], [wz1])
    o_w = sp(w3, CORE)
    st = stats([p0, pz, p_m, p_p, pz_m, pz_p], [wz1])
    wz_lo, wz_hi, wz2 = move(
        [wz_m, wz_p, wz1], [(3, HB, DB), (3, HB, DB), wshape],
        [(0, lo, 0, None), (1, hi, 1, None), (2, None, 2, None)],
        [f_m, f_p, o_w, st], "gate_x3")
    wzf_m, wzf_p = sp(wz_lo, XP), sp(wz_hi, XM)
    wf_m, wf_p = hold([wf_m, wf_p], [wz_lo])
    o_fm, o_fp = sp(wf_m, CORE), sp(wf_p, CORE)
    o_z, o_zm, o_zp = (sp(v, CORE) for v in (wz2, wz_m, wz_p))
    index = ivec(mx(0, 0), mx(0, 1), mx(-1, 0), mx(1, 0), mx(-1, 1), mx(1, 1), mx(2, 0), mx(2, 1), core)
    n_own, n_oth, st = normalize(index, st, [p0, pz, p_m, p_p, pz_m, pz_p, f_m, f_p], wz_lo)
    mean, rstd = st[:, 0:1], st[:, 1:2]
    wzf_m, wzf_p, n_oth = hold([wzf_m, wzf_p, n_oth], [o_z])
    o_zfm, o_zfp = sp(wzf_m, CORE), sp(wzf_p, CORE)
    (n_oth,) = hold([n_oth], [o_zfm, o_zfp, o_zm, o_zp, o_fm, o_fp])
    n_other = sp(n_oth, CORE)
    ws = [w1, w_m, w_p, wf_m, wf_p, o_w, o_fm, o_fp,
          wz2, wz_m, wz_p, wzf_m, wzf_p, o_z, o_zm, o_zp, o_zfm, o_zfp]
    windex = ivec(mw(0, 0), mw(-1, 0), mw(1, 0), mw(2, 0), mw(0, 1), mw(-1, 1), mw(1, 1), mw(2, 1), core)
    heads_out, dqkv, mom = attend(windex, counts.reshape(4), n_own, n_oth, ws, grad_out)

    d_other = sp(dqkv, CORE)

    def source(dy, dz):
        m = mx(dy, dz)
        dx = (m % 4 - x) % 4
        return jnp.where(dx == 3, 1, jnp.where(dx == 1, 2, jnp.where(dx == 2, 3, 0))) + jnp.where(m // 4 == zh, 0, 4)

    def blocks(yb, xb, deps, **kw):
        return grads(core, [source(*b) for b in yb], [mw(*b) for b in xb], dqkv, d_other if xb else dqkv, ws, n_own,
                     n_other if xb else n_own, deps, **kw)

    yu, yd = blocks([(1, 1), (-1, 1)], [], [mom], tail=True)
    ya = [mpp(yu, YP), mpp(yd, YM)]
    xu, xd = blocks([], [(1, 1), (-1, 1)], [yu])
    xa = [sp(xu, XP), sp(xd, XM)]
    y2, x2 = blocks([(2, 1)], [(2, 1)], [xu, mom], tail=True)
    ya.append(mpp(y2, Y2))
    xa.append(sp(x2, X2))
    y0p, y1u, y1d = blocks([(0, 1), (1, 0), (-1, 0)], [], [y2])
    x0p, x1u, x1d = blocks([], [(0, 1), (1, 0), (-1, 0)], [y0p])
    y_out = sum_rows(y0p, mom, ya, [x0p])
    yz = mpp(y_out, ZLO)
    yb1, yb2 = mpp(y1u, YP), mpp(y1d, YM)
    x_out = sum_blocks([x0p, *xa], [y_out])
    xb1, xb2 = sp(x1u, XP), sp(x1d, XM)
    y2o, y0, x2o, x0 = blocks([(2, 0), (0, 0)], [(2, 0), (0, 0)], [x_out])
    (y2o,) = hold([y2o], [yz, yb1, yb2])
    (x_out,) = hold([x_out], [y2o])
    yb3, xz = mpp(y2o, Y2), sp(x_out, ZHI)
    (x2o,) = hold([x2o], [xb1, xb2, x_out])
    xb3 = sp(x2o, X2)

    f = lambda v: v.astype(F32)
    mom = jnp.sum((f(y_out[ROWS:ROWS + 6]) + f(yz[ROWS:ROWS + 6])).reshape(2, 3, 2 * DB), axis=1)[:, :ROWS] / D
    gn = f(y0) + f(yb1) + f(yb2) + f(yb3) + f(yz[:ROWS])
    xhat = (f(patches) - mean) * rstd
    gg = jnp.sum(gn * xhat, axis=0)
    for perm in (CORE, ZHI):
        gg = gg + sp(gg, perm)
    gg = (gg + sp(gg, X2)) + (sp(gg, XP) + sp(gg, XM))
    grad_p = ((gn * gain[None, :] - mom[0][:, None] - xhat * mom[1][:, None]) * rstd).astype(BF)
    gw = jnp.transpose(f(x0) + f(xb1) + f(xb2) + f(xb3) + f(xz), (1, 0, 2))
    return heads_out, grad_p, gg, gw


def solution(mesh):
    placed = (P("seq", "mp"), P("mp"), P("seq", None, "mp"), P("seq", None), P("seq", "mp"))
    return jax.shard_map(
        local,
        mesh=mesh,
        in_specs=placed,
        out_specs=(P("seq", "mp"), P("seq", "mp"), P("mp"), P("seq", None, "mp")),
        check_vma=False,
    )
```

```python
import functools

import jax
import jax.numpy as jnp
from jax import lax
from jax.experimental import pallas as pl
from jax.experimental.pallas import tpu as pltpu
from jax.sharding import PartitionSpec as P

HD = 128
NH = 3
ROWS = 576
HALF = ROWS // 2
EXT = ROWS + 16
DB = 384
HB = DB // 2
D = 6144
CW = 3 * DB
EPS = 1e-06
BF = jnp.bfloat16
F32 = jnp.float32
HBM = pl.BlockSpec(memory_space=pltpu.HBM)
VMEM = pl.BlockSpec(memory_space=pltpu.VMEM)
SMEM = pl.BlockSpec(memory_space=pltpu.SMEM)


def seq_perm(f):
    out = []
    for i in range(16):
        zh, x, c = f(i // 8, (i // 2) % 4, i % 2)
        out.append((i, (zh * 4 + x % 4) * 2 + c))
    return out


def mp_perm(f):
    out = []
    for i in range(8):
        y, zl = f(i // 2, i % 2)
        out.append((i, (y % 4) * 2 + zl))
    return out


CORE = seq_perm(lambda zh, x, c: (zh, x, 1 - c))
ZHI = seq_perm(lambda zh, x, c: (1 - zh, x, c))
XP = seq_perm(lambda zh, x, c: (zh, x + 1, c))
XM = seq_perm(lambda zh, x, c: (zh, x - 1, c))
X2 = seq_perm(lambda zh, x, c: (zh, x + 2, c))
ZLO = mp_perm(lambda y, zl: (y, 1 - zl))
YP = mp_perm(lambda y, zl: (y + 1, zl))
YM = mp_perm(lambda y, zl: (y - 1, zl))
Y2 = mp_perm(lambda y, zl: (y + 2, zl))


def sp(v, perm):
    return lax.ppermute(v, "seq", perm)


def mpp(v, perm):
    return lax.ppermute(v, "mp", perm)


def nt(a, b):
    return lax.dot_general(a, b, (((1,), (1,)), ((), ())), preferred_element_type=F32)


def tn(a, b):
    return lax.dot_general(a, b, (((0,), (0,)), ((), ())), preferred_element_type=F32)


def nn(a, b):
    return lax.dot_general(a, b, (((1,), (0,)), ((), ())), preferred_element_type=F32)


def sds(shape, dtype=BF):
    return jax.ShapeDtypeStruct(shape, dtype)


def params(mib=63):
    return pltpu.CompilerParams(vmem_limit_bytes=mib << 20)


def cost(flops, nbytes, exps=0):
    return pl.CostEstimate(flops=int(flops), bytes_accessed=int(nbytes), transcendentals=exps)


def sliced(shape, index):
    if not index:
        return shape
    out = []
    for n, i in zip(shape, index):
        if not isinstance(i, int):
            out.append(n if isinstance(i, slice) else i.size)
    return tuple(out) + tuple(shape[len(index):])


def move(inputs, outs, plan, deps, name):
    def kernel(*refs):
        ins = refs[:len(inputs)]
        dst = refs[len(inputs) + len(deps):][:len(outs)]
        *bufs, sem = refs[len(inputs) + len(deps) + len(outs):]
        get = [pltpu.make_async_copy(ins[i].at[si] if si else ins[i], bufs[k], sem.at[k, 0])
               for k, (i, si, o, so) in enumerate(plan)]
        put = [pltpu.make_async_copy(bufs[k], dst[o].at[so] if so else dst[o], sem.at[k, 1])
               for k, (i, si, o, so) in enumerate(plan)]
        for c in get:
            c.start()
        for g, p in zip(get, put):
            g.wait()
            p.start()
        for p in put:
            p.wait()

    return pl.pallas_call(
        kernel,
        in_specs=[HBM] * (len(inputs) + len(deps)),
        out_specs=[HBM] * len(outs),
        out_shape=[sds(s) for s in outs],
        scratch_shapes=[pltpu.VMEM(sliced(inputs[i].shape, si), BF) for i, si, o, so in plan]
        + [pltpu.SemaphoreType.DMA((len(plan), 2))],
        compiler_params=params(),
        cost_estimate=cost(0, 4 << 20),
        name=name,
    )(*inputs, *deps)


def hold(values, deps):
    def kernel(*refs):
        pass

    n = len(values)
    return pl.pallas_call(
        kernel,
        in_specs=[HBM] * (n + len(deps)),
        out_specs=[HBM] * n,
        out_shape=[sds(v.shape, v.dtype) for v in values],
        input_output_aliases={k: k for k in range(n)},
        compiler_params=params(),
        cost_estimate=cost(0, 1 << 10),
        name="hold",
    )(*values, *deps)


def extend_kernel(p, gain, out):
    out[pl.ds(0, ROWS), :] = p[...]
    g = gain[...]
    hi = g.astype(BF).astype(F32)
    mid = (g - hi).astype(BF).astype(F32)
    row = lax.broadcasted_iota(jnp.int32, (16, 2 * DB), 0)
    tail = jnp.where(row == 0, hi, jnp.where(row == 1, mid, jnp.where(row == 2, g - hi - mid, 0.0)))
    out[pl.ds(ROWS, 16), :] = tail.astype(BF)


def extend(patches, gain):
    return pl.pallas_call(
        extend_kernel,
        out_shape=sds((EXT, 2 * DB)),
        compiler_params=params(),
        cost_estimate=cost(0, 2 << 20),
        name="extend",
    )(patches, gain.reshape(1, 2 * DB))


def merge(n, mean, m2, chunk):
    v = chunk.astype(F32)
    cm = jnp.sum(v, axis=1, keepdims=True) * (1.0 / 768)
    dv = v - cm
    c2 = jnp.sum(dv * dv, axis=1, keepdims=True)
    if n == 0:
        return cm, c2
    delta = cm - mean
    return mean + delta * (1.0 / (n + 1)), m2 + c2 + delta * delta * (768.0 * n / (n + 1))


def two_lanes(a, b):
    lane = lax.broadcasted_iota(jnp.int32, (ROWS, 128), 1)
    return jnp.where(lane == 0, a, jnp.where(lane == 1, b, 0.0))


def stats_kernel(*refs, nraw, ndeps):
    raws = refs[:nraw]
    out, buf, sem = refs[nraw + ndeps:]
    copies = [pltpu.make_async_copy(r, buf.at[j], sem.at[j]) for j, r in enumerate(raws)]
    for c in copies:
        c.start()
    mean = m2 = None
    for j, c in enumerate(copies):
        c.wait()
        mean, m2 = merge(j, mean, m2, buf[j, pl.ds(0, ROWS), :])
    out[...] = two_lanes(mean, m2)


def stats(raws, deps):
    n = len(raws)
    return pl.pallas_call(
        functools.partial(stats_kernel, nraw=n, ndeps=len(deps)),
        in_specs=[HBM] * (n + len(deps)),
        out_specs=VMEM,
        out_shape=sds((ROWS, 128), F32),
        scratch_shapes=[pltpu.VMEM((n, EXT, 2 * DB), BF), pltpu.SemaphoreType.DMA((n,))],
        compiler_params=params(),
        cost_estimate=cost(0, 4 << 20),
        name="row_stats",
    )(*raws, *deps)


def norm_kernel(idx, st, r0, r1, r2, r3, r4, r5, fm, fp, _, n_own, n_oth, st_out, raw, nrm, sr, so):
    core = idx[8]
    copies = []
    for j in range(2):
        copies.append(pltpu.make_async_copy(fm.at[j], raw.at[6 + j, pl.ds(0, HALF)], sr.at[j]))
        copies.append(pltpu.make_async_copy(fp.at[j], raw.at[6 + j, pl.ds(HALF, EXT - HALF)], sr.at[2 + j]))
    for j, r in enumerate((r0, r1, r2, r3, r4, r5)):
        copies.append(pltpu.make_async_copy(r, raw.at[j], sr.at[4 + j]))
    for c in copies:
        c.start()
    for c in copies[:4]:
        c.wait()
    mean, m2 = st[:, 0:1], st[:, 1:2]
    for j in range(2):
        mean, m2 = merge(6 + j, mean, m2, raw[6 + j, pl.ds(0, ROWS), :])
    rstd = lax.rsqrt(m2 * (1.0 / D) + EPS)
    st_out[...] = two_lanes(mean, rstd)
    out = []
    own = pl.ds(pl.multiple_of(core * DB, 128), DB)
    oth = pl.ds(pl.multiple_of((1 - core) * DB, 128), DB)
    for j in (6, 7, 0, 1, 2, 3, 4, 5):
        if j < 6:
            copies[4 + j].wait()
        tail = raw[j, pl.ds(ROWS, 16), :]
        t = tail.astype(F32)
        g = t[0:1] + t[1:2] + t[2:3]
        nrm[j, pl.ds(0, ROWS), :] = ((raw[j, pl.ds(0, ROWS), :].astype(F32) - mean) * rstd * g).astype(BF)
        nrm[j, pl.ds(ROWS, 16), :] = tail
        mine = [pltpu.make_async_copy(nrm.at[j, :, own], n_own.at[idx[j]], so.at[j, 0]),
                pltpu.make_async_copy(nrm.at[j, :, oth], n_oth.at[idx[j]], so.at[j, 1])]
        for c in mine:
            c.start()
        out += mine
    for c in out:
        c.wait()


def normalize(index, st, raws, after):
    return pl.pallas_call(
        norm_kernel,
        in_specs=[SMEM, VMEM] + [HBM] * (len(raws) + 1),
        out_specs=[HBM, HBM, VMEM],
        out_shape=[sds((8, EXT, DB)), sds((8, EXT, DB)), sds((ROWS, 128), F32)],
        scratch_shapes=[
            pltpu.VMEM((8, EXT, 2 * DB), BF),
            pltpu.VMEM((8, EXT, 2 * DB), BF),
            pltpu.SemaphoreType.DMA((10,)),
            pltpu.SemaphoreType.DMA((8, 2)),
        ],
        compiler_params=params(),
        cost_estimate=cost(0, 8 << 20),
        name="normalize",
    )(index, st, *raws, after)


NW = 18


def w_sources(refs):
    own, packed, far, pair, other = refs[:5], refs[5], refs[6:8], refs[8:13], refs[13:18]
    out = [((own[k],), (packed.at[k],)) if k < 3 else (own[3:5], far) for k in range(4)]
    return out + [((pair[k],), (other[k],)) if k < 3 else (pair[3:5], other[3:5]) for k in range(4)]


def w_copies(parts, buf, half, sem):
    out = []
    rows = DB // len(parts)
    for h, part in enumerate(parts):
        at = pl.ds(pl.multiple_of(half * DB + h * rows, 64), rows)
        out += [pltpu.make_async_copy(part.at[j], buf.at[at, pl.ds(j * DB, DB)], sem.at[h, j]) for j in range(3)]
    return out


def to_rows(m1, m2):
    row = lax.broadcasted_iota(jnp.int32, (16, m1.shape[1]), 0)
    out = jnp.zeros((16, m1.shape[1]), F32)
    for k, m in enumerate((m1, m2)):
        hi = m.astype(BF).astype(F32)
        mid = (m - hi).astype(BF).astype(F32)
        for j, part in enumerate((hi, mid, m - hi - mid)):
            out = jnp.where(row == 3 * k + j, part, out)
    return out.astype(BF)


def split(v):
    hi = v.astype(BF)
    return hi, (v - hi.astype(F32)).astype(BF)


def attn_kernel(idx, counts, n_own, n_oth, *refs):
    w_refs, refs = refs[:NW], refs[NW:]
    g_ref, out_ref, dqkv_ref, mom_ref, qkv, nv, wv, mom_s, sn, sw = refs
    h = pl.program_id(0)

    @pl.when(h == 0)
    def _():
        core = idx[8]
        copies = []
        for k, (mine, other) in enumerate(w_sources(w_refs)):
            m = idx[k]
            at = (k % 2) * 2 * DB
            lanes = lambda c: pl.ds(pl.multiple_of(at + c * DB, 128), DB)
            copies.append([pltpu.make_async_copy(n_own.at[m], nv.at[k // 2, :, lanes(core)], sn.at[k, 0]),
                           pltpu.make_async_copy(n_oth.at[m], nv.at[k // 2, :, lanes(1 - core)], sn.at[k, 1])]
                          + w_copies(mine, wv.at[k // 2, pl.ds(at, 2 * DB)], core, sw.at[k, 0])
                          + w_copies(other, wv.at[k // 2, pl.ds(at, 2 * DB)], 1 - core, sw.at[k, 1]))
            for c in copies[-1]:
                c.start()
        mom_s[...] = jnp.zeros_like(mom_s)
        for k in range(4):
            for c in copies[2 * k] + copies[2 * k + 1]:
                c.wait()
            t = nn(nv[k], wv[k])
            if k == 0:
                qkv[...] = t
            else:
                qkv[...] += t

    col = lambda j: pl.ds(pl.multiple_of((j * NH + h) * HD, 128), HD)
    q_ref, k_ref, v_ref = (qkv.at[:, col(j)] for j in range(3))
    e0 = counts[0]
    e1 = e0 + counts[1]
    e2 = e1 + counts[2]
    rid = lax.broadcasted_iota(jnp.int32, (ROWS, 1), 0)
    cid = lax.broadcasted_iota(jnp.int32, (1, ROWS), 1)
    img = lambda p: (p >= e0).astype(jnp.int32) + (p >= e1).astype(jnp.int32) + (p >= e2).astype(jnp.int32)
    same = img(rid) == img(cid)
    scale = HD ** (-0.5)
    q = q_ref[:ROWS, :] * scale
    k = k_ref[:ROWS, :]
    v = v_ref[:ROWS, :]
    qh, ql = split(q)
    kh, kl = split(k)
    vb = v.astype(BF)
    g = g_ref[...]
    s = nt(jnp.concatenate([qh, qh, ql], 1), jnp.concatenate([kh, kl, kh], 1))
    s = jnp.where(same, s, -1e30)
    p = jnp.exp(s - jnp.max(s, axis=1, keepdims=True))
    p = p * (1.0 / jnp.sum(p, axis=1, keepdims=True))
    pb = p.astype(BF)
    out_ref[...] = nn(pb, vb).astype(BF)
    dp = nt(g, vb)
    dv = tn(pb, g)
    ds = p * (dp - jnp.sum(dp * p, axis=1, keepdims=True))
    dsb = ds.astype(BF)
    dq = (nn(dsb, kh) * scale).astype(BF)
    dk = tn(dsb, qh).astype(BF)
    dv = dv.astype(BF)
    dqkv_ref[0] = dq
    dqkv_ref[1] = dk
    dqkv_ref[2] = dv
    m1 = jnp.zeros((ROWS, 1), F32)
    m2 = jnp.zeros((ROWS, 1), F32)
    for d, r in ((dq, q_ref), (dk, k_ref), (dv, v_ref)):
        df = d.astype(F32)
        u = r[ROWS:ROWS + 1, :] + r[ROWS + 1:ROWS + 2, :] + r[ROWS + 2:ROWS + 3, :]
        m1 = m1 + jnp.sum(df * u, axis=1, keepdims=True)
        m2 = m2 + jnp.sum(df * r[:ROWS, :], axis=1, keepdims=True)
    mom_s[pl.ds(0, ROWS), :] += two_lanes(m1, m2)

    @pl.when(h == NH - 1)
    def _():
        t = jnp.transpose(mom_s[...])
        mom_ref[...] = jnp.zeros_like(mom_ref)
        mom_ref[:, pl.ds(0, 640)] = to_rows(t[0:1, :], t[1:2, :])


def attend(index, counts, n_own, n_oth, ws, grad_out):
    return pl.pallas_call(
        attn_kernel,
        grid=(NH,),
        in_specs=[SMEM, SMEM] + [HBM] * (2 + NW) + [pl.BlockSpec((ROWS, HD), lambda h: (0, h))],
        out_specs=[
            pl.BlockSpec((ROWS, HD), lambda h: (0, h)),
            pl.BlockSpec((3, ROWS, HD), lambda h: (0, 0, h)),
            pl.BlockSpec((16, 2 * DB), lambda h: (0, 0)),
        ],
        out_shape=[sds((ROWS, DB)), sds((3, ROWS, DB)), sds((16, 2 * DB))],
        scratch_shapes=[
            pltpu.VMEM((EXT, CW), F32),
            pltpu.VMEM((4, EXT, 4 * DB), BF),
            pltpu.VMEM((4, 4 * DB, CW), BF),
            pltpu.VMEM((640, 128), F32),
            pltpu.SemaphoreType.DMA((8, 2)),
            pltpu.SemaphoreType.DMA((8, 2, 2, 3)),
        ],
        compiler_params=params(),
        cost_estimate=cost(2 * EXT * D * CW, 28 << 20, NH * ROWS * ROWS),
        name="attention",
    )(index, counts, n_own, n_oth, *ws, grad_out)


def grads_kernel(idx, d1, d2, *refs, ny, nx, ndeps, ysplit, xsplit, tail):
    w_refs, (n1, n2), extra, refs = refs[:NW], refs[NW:NW + 2], refs[NW + 1 + ndeps], refs[NW + 2 + ndeps:]
    outs = list(refs[:-8])
    wv, nv, dcat, oy, ox, sd, si, so = refs[-8:]
    core = idx[0]
    dc = [pltpu.make_async_copy(d1.at[j], dcat.at[pl.ds(0, ROWS), pl.ds(j * DB, DB)], sd.at[0, j]) for j in range(3)]
    if nx:
        dc += [pltpu.make_async_copy(d2.at[j], dcat.at[pl.ds(ROWS, ROWS), pl.ds(j * DB, DB)], sd.at[1, j])
               for j in range(3)]
    for c in dc[:3]:
        c.start()
    sources = w_sources(w_refs)
    for i in range(ny):
        a = idx[1 + i]
        for k, (mine, other) in enumerate(sources):
            @pl.when(a == k)
            def _():
                for c in w_copies(mine, wv.at[i], core, si.at[i, 0]) + w_copies(other, wv.at[i], 1 - core, si.at[i, 1]):
                    c.start()
    for c in dc[3:]:
        c.start()
    ncs = []
    for i in range(nx):
        m = idx[1 + ny + i]
        ncs.append([pltpu.make_async_copy(n1.at[m, pl.ds(0, ROWS)], nv.at[i, pl.ds(0, ROWS)], si.at[ny + i, 0, 0, 0]),
                    pltpu.make_async_copy(n2.at[m, pl.ds(0, ROWS)], nv.at[i, pl.ds(ROWS, ROWS)], si.at[ny + i, 1, 0, 0])])
        for c in ncs[-1]:
            c.start()
    ends = []
    if tail:
        ends = [pltpu.make_async_copy(extra, oy.at[i, pl.ds(ROWS, 16)], so.at[i, 1]) for i in range(ny)]
        for c in ends:
            c.start()
    pending = []

    def put(src, dst, sem):
        c = pltpu.make_async_copy(src, dst, sem)
        c.start()
        pending.append(c)

    for c in dc[:3]:
        c.wait()
    for i in range(ny):
        a = idx[1 + i]
        for e in range(2):
            halves = jnp.logical_or(a == 7, a == 3)

            @pl.when(halves)
            def _():
                for c in w_copies(sources[7][e], wv.at[i], e, si.at[i, e]):
                    c.wait()

            @pl.when(jnp.logical_not(halves))
            def _():
                for c in w_copies(sources[0][e], wv.at[i], e, si.at[i, e]):
                    c.wait()
        oy[i, pl.ds(0, ROWS), :] = nt(dcat[pl.ds(0, ROWS), :], wv[i]).astype(BF)
        if tail:
            ends[i].wait()
        if i in ysplit:
            put(oy.at[i, pl.ds(0, HALF)], outs.pop(0), so.at[i, 0])
            put(oy.at[i, pl.ds(HALF, HALF)], outs.pop(0), so.at[i, 1])
        else:
            put(oy.at[i], outs.pop(0), so.at[i, 0])
    for c in dc[3:]:
        c.wait()
    for i in range(nx):
        for c in ncs[i]:
            c.wait()
        t = tn(nv[i], dcat[...]).astype(BF)
        for j in range(3):
            ox[i, j] = t[:, j * DB:(j + 1) * DB]
        if i in xsplit:
            put(ox.at[i, :, pl.ds(0, HB)], outs.pop(0), so.at[ny + i, 0])
            put(ox.at[i, :, pl.ds(HB, HB)], outs.pop(0), so.at[ny + i, 1])
        else:
            put(ox.at[i], outs.pop(0), so.at[ny + i, 0])
    for c in pending:
        c.wait()


def grads(core, ysrc, xsrc, dqkv, d_other, ws, normed, other, deps, ysplit=(), xsplit=(), tail=False):
    ny, nx = len(ysrc), len(xsrc)
    shapes, yrows = [], EXT if tail else ROWS
    for i in range(ny):
        shapes += [(HALF, 2 * DB)] * 2 if i in ysplit else [(yrows, 2 * DB)]
    for i in range(nx):
        shapes += [(3, HB, DB)] * 2 if i in xsplit else [(3, DB, DB)]
    deps = list(deps)
    return pl.pallas_call(
        functools.partial(grads_kernel, ny=ny, nx=nx, ndeps=len(deps), ysplit=ysplit, xsplit=xsplit,
                          tail=tail),
        in_specs=[SMEM] + [HBM] * (4 + NW + len(deps)),
        out_specs=[HBM] * len(shapes),
        out_shape=[sds(s) for s in shapes],
        scratch_shapes=[
            pltpu.VMEM((max(ny, 1), 2 * DB, CW), BF),
            pltpu.VMEM((max(nx, 1), 2 * ROWS, DB), BF),
            pltpu.VMEM((2 * ROWS, CW), BF),
            pltpu.VMEM((max(ny, 1), yrows, 2 * DB), BF),
            pltpu.VMEM((max(nx, 1), 3, DB, DB), BF),
            pltpu.SemaphoreType.DMA((2, 3)),
            pltpu.SemaphoreType.DMA((ny + nx, 2, 2, 3)),
            pltpu.SemaphoreType.DMA((ny + nx, 2)),
        ],
        compiler_params=params(),
        cost_estimate=cost(0, 1 << 12),
        name="grads",
    )(ivec(core, *ysrc, *xsrc), dqkv, d_other, *ws, normed, other, *deps)


def sum_rows_kernel(mine, own, *refs):
    out = refs[-1]
    total = mine[...].astype(F32)
    rows = own[...].astype(F32)
    for r in refs[:3]:
        total = total + r[pl.ds(0, ROWS), :].astype(F32)
        rows = rows + r[pl.ds(ROWS, 16), :].astype(F32)
    out[pl.ds(0, ROWS), :] = total.astype(BF)
    m1 = rows[0:1] + rows[1:2] + rows[2:3]
    m2 = rows[3:4] + rows[4:5] + rows[5:6]
    out[pl.ds(ROWS, 16), :] = to_rows(m1, m2)


def sum_rows(mine, own, arrived, deps):
    whole = lambda v: pl.BlockSpec(v.shape, lambda i: (0,) * v.ndim)
    return pl.pallas_call(
        sum_rows_kernel,
        grid=(1,),
        in_specs=[whole(v) for v in (mine, own, *arrived)] + [HBM] * len(deps),
        out_specs=whole(arrived[0]),
        out_shape=sds(arrived[0].shape),
        compiler_params=params(),
        cost_estimate=cost(0, 1 << 12),
        name="sum_rows",
    )(mine, own, *arrived, *deps)


def sum_kernel(*refs, n):
    total = refs[0][...].astype(F32)
    for r in refs[1:n]:
        total = total + r[...].astype(F32)
    refs[-1][...] = total.astype(BF)


def sum_blocks(vs, deps):
    n = len(vs)
    spec = pl.BlockSpec((1, DB, DB), lambda i: (i, 0, 0))
    return pl.pallas_call(
        functools.partial(sum_kernel, n=n),
        grid=(3,),
        in_specs=[spec] * n + [HBM] * len(deps),
        out_specs=spec,
        out_shape=sds(vs[0].shape),
        compiler_params=params(),
        cost_estimate=cost(0, 1 << 12),
        name="sum_blocks",
    )(*vs, *deps)


def ivec(*v):
    return jnp.stack([jnp.asarray(e, jnp.int32) for e in v])


def local(patches, gain, w_qkv, counts, grad_out):
    si, mi = lax.axis_index("seq"), lax.axis_index("mp")
    core, x, zh = si % 2, (si // 2) % 4, si // 8
    y, zl = mi // 2, mi % 2
    mw = lambda dx, dz: jnp.where(dz == 0, zh, 1 - zh) * 4 + (x + dx) % 4
    mx = lambda dy, dz: ((y + dy) % 4) * 2 + jnp.where(dz == 0, zl, 1 - zl)
    rows, wshape = (EXT, 2 * DB), (3, DB, DB)
    lo, hi = (slice(None), pl.ds(0, HB)), (slice(None), pl.ds(HB, HB))
    first, rest = (pl.ds(0, HALF),), (pl.ds(HALF, EXT - HALF),)

    p0 = extend(patches, gain)
    w = jnp.transpose(w_qkv, (1, 0, 2))
    p_m, p_p, pz = mpp(p0, YP), mpp(p0, YM), mpp(p0, ZLO)
    w_m, w_p = sp(w, XP), sp(w, XM)
    pz1, w1 = move([pz, w], [rows, wshape], [(0, None, 0, None), (1, None, 1, None)], [p_m, p_p], "gate_y1")
    pz_m, pz_p = mpp(pz1, YP), mpp(pz1, YM)
    wz = sp(w1, ZHI)
    w_lo, w_hi = move([w_m, w_p], [(3, HB, DB)] * 2, [(0, lo, 0, None), (1, hi, 1, None)], [pz1], "gate_x1")
    wf_m, wf_p = sp(w_lo, XP), sp(w_hi, XM)
    (w3,) = move([w1, w_m, w_p], [(3,) + wshape], [(k, None, 0, (k,)) for k in range(3)], [w_lo], "pack")
    fu, fd = move(
        [p_m, p_p, pz_m, pz_p], [(2, HALF, 2 * DB), (2, EXT - HALF, 2 * DB)],
        [(0, first, 0, (0,)), (2, first, 0, (1,)), (1, rest, 1, (0,)), (3, rest, 1, (1,))], [w_lo, w3], "gate_y2")
    f_m, f_p = mpp(fu, YP), mpp(fd, YM)
    (wz1,) = move([wz], [wshape], [(0, None, 0, None)], [wf_m, wf_p, fu], "gate_x2")
    wz_m, wz_p = sp(wz1, XP), sp(wz1, XM)
    (w3,) = hold([w3], [wz1])
    o_w = sp(w3, CORE)
    st = stats([p0, pz, p_m, p_p, pz_m, pz_p], [wz1])
    wz_lo, wz_hi, wz2 = move(
        [wz_m, wz_p, wz1], [(3, HB, DB), (3, HB, DB), wshape],
        [(0, lo, 0, None), (1, hi, 1, None), (2, None, 2, None)],
        [f_m, f_p, o_w, st], "gate_x3")
    wzf_m, wzf_p = sp(wz_lo, XP), sp(wz_hi, XM)
    wf_m, wf_p = hold([wf_m, wf_p], [wz_lo])
    o_fm, o_fp = sp(wf_m, CORE), sp(wf_p, CORE)
    o_z, o_zm, o_zp = (sp(v, CORE) for v in (wz2, wz_m, wz_p))
    index = ivec(mx(0, 0), mx(0, 1), mx(-1, 0), mx(1, 0), mx(-1, 1), mx(1, 1), mx(2, 0), mx(2, 1), core)
    n_own, n_oth, st = normalize(index, st, [p0, pz, p_m, p_p, pz_m, pz_p, f_m, f_p], wz_lo)
    mean, rstd = st[:, 0:1], st[:, 1:2]
    wzf_m, wzf_p, n_oth = hold([wzf_m, wzf_p, n_oth], [o_z])
    o_zfm, o_zfp = sp(wzf_m, CORE), sp(wzf_p, CORE)
    (n_oth,) = hold([n_oth], [o_zfm, o_zfp, o_zm, o_zp, o_fm, o_fp])
    n_other = sp(n_oth, CORE)
    ws = [w1, w_m, w_p, wf_m, wf_p, o_w, o_fm, o_fp,
          wz2, wz_m, wz_p, wzf_m, wzf_p, o_z, o_zm, o_zp, o_zfm, o_zfp]
    windex = ivec(mw(0, 0), mw(-1, 0), mw(1, 0), mw(2, 0), mw(0, 1), mw(-1, 1), mw(1, 1), mw(2, 1), core)
    heads_out, dqkv, mom = attend(windex, counts.reshape(4), n_own, n_oth, ws, grad_out)

    d_other = sp(dqkv, CORE)

    def source(dy, dz):
        m = mx(dy, dz)
        dx = (m % 4 - x) % 4
        return jnp.where(dx == 3, 1, jnp.where(dx == 1, 2, jnp.where(dx == 2, 3, 0))) + jnp.where(m // 4 == zh, 0, 4)

    def blocks(yb, xb, deps, **kw):
        return grads(core, [source(*b) for b in yb], [mw(*b) for b in xb], dqkv, d_other if xb else dqkv, ws, n_own,
                     n_other if xb else n_own, deps, **kw)

    yu, yd, y2 = blocks([(1, 1), (-1, 1), (2, 1)], [], [mom], tail=True)
    ya = [mpp(yu, YP), mpp(yd, YM), mpp(y2, Y2)]
    xu, xd = blocks([], [(1, 1), (-1, 1)], [yu])
    xa = [sp(xu, XP), sp(xd, XM)]
    y2o, y1u, y1d, y0p = blocks([(2, 0), (1, 0), (-1, 0), (0, 1)], [], [xu])
    x2, x1u, x1d, x0p = blocks([], [(2, 1), (1, 0), (-1, 0), (0, 1)], [y0p])
    xa.append(sp(x2, X2))
    y_out = sum_rows(y0p, mom, ya, [x0p])
    yz = mpp(y_out, ZLO)
    yb1, yb2 = mpp(y1u, YP), mpp(y1d, YM)
    x_out = sum_blocks([x0p, *xa], [y_out])
    xb1, xb2 = sp(x1u, XP), sp(x1d, XM)
    (y2o,) = hold([y2o], [yz, yb1, yb2, x_out])
    (x_out,) = hold([x_out], [y2o])
    yb3, xz = mpp(y2o, Y2), sp(x_out, ZHI)
    y0, x0, x2o = blocks([(0, 0)], [(0, 0), (2, 0)], [x_out])
    (x2o,) = hold([x2o], [xb1, xb2, y0])
    xb3 = sp(x2o, X2)

    f = lambda v: v.astype(F32)
    mom = jnp.sum((f(y_out[ROWS:ROWS + 6]) + f(yz[ROWS:ROWS + 6])).reshape(2, 3, 2 * DB), axis=1)[:, :ROWS] / D
    gn = f(y0) + f(yb1) + f(yb2) + f(yb3) + f(yz[:ROWS])
    xhat = (f(patches) - mean) * rstd
    gg = jnp.sum(gn * xhat, axis=0)
    for perm in (CORE, ZHI):
        gg = gg + sp(gg, perm)
    gg = (gg + sp(gg, X2)) + (sp(gg, XP) + sp(gg, XM))
    grad_p = ((gn * gain[None, :] - mom[0][:, None] - xhat * mom[1][:, None]) * rstd).astype(BF)
    gw = jnp.transpose(f(x0) + f(xb1) + f(xb2) + f(xb3) + f(xz), (1, 0, 2))
    return heads_out, grad_p, gg, gw


def solution(mesh):
    placed = (P("seq", "mp"), P("mp"), P("seq", None, "mp"), P("seq", None), P("seq", "mp"))
    return jax.shard_map(
        local,
        mesh=mesh,
        in_specs=placed,
        out_specs=(P("seq", "mp"), P("seq", "mp"), P("mp"), P("seq", None, "mp")),
        check_vma=False,
    )
```

```python
import functools

import jax
import jax.numpy as jnp
from jax import lax
from jax.experimental import pallas as pl
from jax.experimental.pallas import tpu as pltpu
from jax.sharding import PartitionSpec as P

HD = 128
NH = 3
ROWS = 576
HALF = ROWS // 2
EXT = ROWS + 16
DB = 384
HB = DB // 2
D = 6144
CW = 3 * DB
EPS = 1e-06
BF = jnp.bfloat16
F32 = jnp.float32
HBM = pl.BlockSpec(memory_space=pltpu.HBM)
VMEM = pl.BlockSpec(memory_space=pltpu.VMEM)
SMEM = pl.BlockSpec(memory_space=pltpu.SMEM)


def seq_perm(f):
    out = []
    for i in range(16):
        zh, x, c = f(i // 8, (i // 2) % 4, i % 2)
        out.append((i, (zh * 4 + x % 4) * 2 + c))
    return out


def mp_perm(f):
    out = []
    for i in range(8):
        y, zl = f(i // 2, i % 2)
        out.append((i, (y % 4) * 2 + zl))
    return out


CORE = seq_perm(lambda zh, x, c: (zh, x, 1 - c))
ZHI = seq_perm(lambda zh, x, c: (1 - zh, x, c))
XP = seq_perm(lambda zh, x, c: (zh, x + 1, c))
XM = seq_perm(lambda zh, x, c: (zh, x - 1, c))
X2 = seq_perm(lambda zh, x, c: (zh, x + 2, c))
ZLO = mp_perm(lambda y, zl: (y, 1 - zl))
YP = mp_perm(lambda y, zl: (y + 1, zl))
YM = mp_perm(lambda y, zl: (y - 1, zl))
Y2 = mp_perm(lambda y, zl: (y + 2, zl))


def sp(v, perm):
    return lax.ppermute(v, "seq", perm)


def mpp(v, perm):
    return lax.ppermute(v, "mp", perm)


def nt(a, b):
    return lax.dot_general(a, b, (((1,), (1,)), ((), ())), preferred_element_type=F32)


def tn(a, b):
    return lax.dot_general(a, b, (((0,), (0,)), ((), ())), preferred_element_type=F32)


def nn(a, b):
    return lax.dot_general(a, b, (((1,), (0,)), ((), ())), preferred_element_type=F32)


def sds(shape, dtype=BF):
    return jax.ShapeDtypeStruct(shape, dtype)


def params(mib=63):
    return pltpu.CompilerParams(vmem_limit_bytes=mib << 20)


def cost(flops, nbytes, exps=0):
    return pl.CostEstimate(flops=int(flops), bytes_accessed=int(nbytes), transcendentals=exps)


def sliced(shape, index):
    if not index:
        return shape
    out = []
    for n, i in zip(shape, index):
        if not isinstance(i, int):
            out.append(n if isinstance(i, slice) else i.size)
    return tuple(out) + tuple(shape[len(index):])


def move(inputs, outs, plan, deps, name):
    def kernel(*refs):
        ins = refs[:len(inputs)]
        dst = refs[len(inputs) + len(deps):][:len(outs)]
        *bufs, sem = refs[len(inputs) + len(deps) + len(outs):]
        get = [pltpu.make_async_copy(ins[i].at[si] if si else ins[i], bufs[k], sem.at[k, 0])
               for k, (i, si, o, so) in enumerate(plan)]
        put = [pltpu.make_async_copy(bufs[k], dst[o].at[so] if so else dst[o], sem.at[k, 1])
               for k, (i, si, o, so) in enumerate(plan)]
        for c in get:
            c.start()
        for g, p in zip(get, put):
            g.wait()
            p.start()
        for p in put:
            p.wait()

    return pl.pallas_call(
        kernel,
        in_specs=[HBM] * (len(inputs) + len(deps)),
        out_specs=[HBM] * len(outs),
        out_shape=[sds(s) for s in outs],
        scratch_shapes=[pltpu.VMEM(sliced(inputs[i].shape, si), BF) for i, si, o, so in plan]
        + [pltpu.SemaphoreType.DMA((len(plan), 2))],
        compiler_params=params(),
        cost_estimate=cost(0, 4 << 20),
        name=name,
    )(*inputs, *deps)


def hold(values, deps):
    def kernel(*refs):
        pass

    n = len(values)
    return pl.pallas_call(
        kernel,
        in_specs=[HBM] * (n + len(deps)),
        out_specs=[HBM] * n,
        out_shape=[sds(v.shape, v.dtype) for v in values],
        input_output_aliases={k: k for k in range(n)},
        compiler_params=params(),
        cost_estimate=cost(0, 1 << 10),
        name="hold",
    )(*values, *deps)


def extend_kernel(p, gain, out):
    out[pl.ds(0, ROWS), :] = p[...]
    g = gain[...]
    hi = g.astype(BF).astype(F32)
    mid = (g - hi).astype(BF).astype(F32)
    row = lax.broadcasted_iota(jnp.int32, (16, 2 * DB), 0)
    tail = jnp.where(row == 0, hi, jnp.where(row == 1, mid, jnp.where(row == 2, g - hi - mid, 0.0)))
    out[pl.ds(ROWS, 16), :] = tail.astype(BF)


def extend(patches, gain):
    return pl.pallas_call(
        extend_kernel,
        out_shape=sds((EXT, 2 * DB)),
        compiler_params=params(),
        cost_estimate=cost(0, 2 << 20),
        name="extend",
    )(patches, gain.reshape(1, 2 * DB))


def merge(n, mean, m2, chunk):
    v = chunk.astype(F32)
    cm = jnp.sum(v, axis=1, keepdims=True) * (1.0 / 768)
    dv = v - cm
    c2 = jnp.sum(dv * dv, axis=1, keepdims=True)
    if n == 0:
        return cm, c2
    delta = cm - mean
    return mean + delta * (1.0 / (n + 1)), m2 + c2 + delta * delta * (768.0 * n / (n + 1))


def two_lanes(a, b):
    lane = lax.broadcasted_iota(jnp.int32, (ROWS, 128), 1)
    return jnp.where(lane == 0, a, jnp.where(lane == 1, b, 0.0))


def stats_kernel(*refs, nraw, ndeps):
    raws = refs[:nraw]
    out, buf, sem = refs[nraw + ndeps:]
    copies = [pltpu.make_async_copy(r, buf.at[j], sem.at[j]) for j, r in enumerate(raws)]
    for c in copies:
        c.start()
    mean = m2 = None
    for j, c in enumerate(copies):
        c.wait()
        mean, m2 = merge(j, mean, m2, buf[j, pl.ds(0, ROWS), :])
    out[...] = two_lanes(mean, m2)


def stats(raws, deps):
    n = len(raws)
    return pl.pallas_call(
        functools.partial(stats_kernel, nraw=n, ndeps=len(deps)),
        in_specs=[HBM] * (n + len(deps)),
        out_specs=VMEM,
        out_shape=sds((ROWS, 128), F32),
        scratch_shapes=[pltpu.VMEM((n, EXT, 2 * DB), BF), pltpu.SemaphoreType.DMA((n,))],
        compiler_params=params(),
        cost_estimate=cost(0, 4 << 20),
        name="row_stats",
    )(*raws, *deps)


def norm_kernel(idx, st, r0, r1, r2, r3, r4, r5, fm, fp, _, n_own, n_oth, st_out, raw, nrm, sr, so):
    core = idx[8]
    copies = []
    for j in range(2):
        copies.append(pltpu.make_async_copy(fm.at[j], raw.at[6 + j, pl.ds(0, HALF)], sr.at[j]))
        copies.append(pltpu.make_async_copy(fp.at[j], raw.at[6 + j, pl.ds(HALF, EXT - HALF)], sr.at[2 + j]))
    for j, r in enumerate((r0, r1, r2, r3, r4, r5)):
        copies.append(pltpu.make_async_copy(r, raw.at[j], sr.at[4 + j]))
    for c in copies:
        c.start()
    for c in copies[:4]:
        c.wait()
    mean, m2 = st[:, 0:1], st[:, 1:2]
    for j in range(2):
        mean, m2 = merge(6 + j, mean, m2, raw[6 + j, pl.ds(0, ROWS), :])
    rstd = lax.rsqrt(m2 * (1.0 / D) + EPS)
    st_out[...] = two_lanes(mean, rstd)
    out = []
    own = pl.ds(pl.multiple_of(core * DB, 128), DB)
    oth = pl.ds(pl.multiple_of((1 - core) * DB, 128), DB)
    for j in (6, 7, 0, 1, 2, 3, 4, 5):
        if j < 6:
            copies[4 + j].wait()
        tail = raw[j, pl.ds(ROWS, 16), :]
        t = tail.astype(F32)
        g = t[0:1] + t[1:2] + t[2:3]
        nrm[j, pl.ds(0, ROWS), :] = ((raw[j, pl.ds(0, ROWS), :].astype(F32) - mean) * rstd * g).astype(BF)
        nrm[j, pl.ds(ROWS, 16), :] = tail
        mine = [pltpu.make_async_copy(nrm.at[j, :, own], n_own.at[idx[j]], so.at[j, 0]),
                pltpu.make_async_copy(nrm.at[j, :, oth], n_oth.at[idx[j]], so.at[j, 1])]
        for c in mine:
            c.start()
        out += mine
    for c in out:
        c.wait()


def normalize(index, st, raws, after):
    return pl.pallas_call(
        norm_kernel,
        in_specs=[SMEM, VMEM] + [HBM] * (len(raws) + 1),
        out_specs=[HBM, HBM, VMEM],
        out_shape=[sds((8, EXT, DB)), sds((8, EXT, DB)), sds((ROWS, 128), F32)],
        scratch_shapes=[
            pltpu.VMEM((8, EXT, 2 * DB), BF),
            pltpu.VMEM((8, EXT, 2 * DB), BF),
            pltpu.SemaphoreType.DMA((10,)),
            pltpu.SemaphoreType.DMA((8, 2)),
        ],
        compiler_params=params(),
        cost_estimate=cost(0, 8 << 20),
        name="normalize",
    )(index, st, *raws, after)


NW = 18


def w_sources(refs):
    own, packed, far, pair, other = refs[:5], refs[5], refs[6:8], refs[8:13], refs[13:18]
    out = [((own[k],), (packed.at[k],)) if k < 3 else (own[3:5], far) for k in range(4)]
    return out + [((pair[k],), (other[k],)) if k < 3 else (pair[3:5], other[3:5]) for k in range(4)]


def w_copies(parts, buf, half, sem):
    out = []
    rows = DB // len(parts)
    for h, part in enumerate(parts):
        at = pl.ds(pl.multiple_of(half * DB + h * rows, 64), rows)
        out += [pltpu.make_async_copy(part.at[j], buf.at[at, pl.ds(j * DB, DB)], sem.at[h, j]) for j in range(3)]
    return out


def to_rows(m1, m2):
    row = lax.broadcasted_iota(jnp.int32, (16, m1.shape[1]), 0)
    out = jnp.zeros((16, m1.shape[1]), F32)
    for k, m in enumerate((m1, m2)):
        hi = m.astype(BF).astype(F32)
        mid = (m - hi).astype(BF).astype(F32)
        for j, part in enumerate((hi, mid, m - hi - mid)):
            out = jnp.where(row == 3 * k + j, part, out)
    return out.astype(BF)


def split(v):
    hi = v.astype(BF)
    return hi, (v - hi.astype(F32)).astype(BF)


def attn_kernel(idx, counts, n_own, n_oth, *refs):
    w_refs, refs = refs[:NW], refs[NW:]
    g_ref, out_ref, dqkv_ref, mom_ref, qkv, nv, wv, mom_s, sn, sw = refs
    h = pl.program_id(0)

    @pl.when(h == 0)
    def _():
        core = idx[17]
        copies = []
        for k, (mine, other) in enumerate(w_sources(w_refs)):
            m = idx[9 + k]
            at = (k % 2) * 2 * DB
            lanes = lambda c: pl.ds(pl.multiple_of(at + c * DB, 128), DB)
            copies.append([pltpu.make_async_copy(n_own.at[m], nv.at[k // 2, :, lanes(core)], sn.at[k, 0]),
                           pltpu.make_async_copy(n_oth.at[m], nv.at[k // 2, :, lanes(1 - core)], sn.at[k, 1])]
                          + w_copies(mine, wv.at[k // 2, pl.ds(at, 2 * DB)], core, sw.at[k, 0])
                          + w_copies(other, wv.at[k // 2, pl.ds(at, 2 * DB)], 1 - core, sw.at[k, 1]))
            for c in copies[-1]:
                c.start()
        mom_s[...] = jnp.zeros_like(mom_s)
        for k in range(4):
            for c in copies[2 * k] + copies[2 * k + 1]:
                c.wait()
            t = nn(nv[k], wv[k])
            if k == 0:
                qkv[...] = t
            else:
                qkv[...] += t

    col = lambda j: pl.ds(pl.multiple_of((j * NH + h) * HD, 128), HD)
    q_ref, k_ref, v_ref = (qkv.at[:, col(j)] for j in range(3))
    e0 = counts[0]
    e1 = e0 + counts[1]
    e2 = e1 + counts[2]
    rid = lax.broadcasted_iota(jnp.int32, (ROWS, 1), 0)
    cid = lax.broadcasted_iota(jnp.int32, (1, ROWS), 1)
    img = lambda p: (p >= e0).astype(jnp.int32) + (p >= e1).astype(jnp.int32) + (p >= e2).astype(jnp.int32)
    same = img(rid) == img(cid)
    scale = HD ** (-0.5)
    q = q_ref[:ROWS, :] * scale
    k = k_ref[:ROWS, :]
    v = v_ref[:ROWS, :]
    qh, ql = split(q)
    kh, kl = split(k)
    vb = v.astype(BF)
    g = g_ref[...]
    s = nt(jnp.concatenate([qh, qh, ql], 1), jnp.concatenate([kh, kl, kh], 1))
    s = jnp.where(same, s, -1e30)
    p = jnp.exp(s - jnp.max(s, axis=1, keepdims=True))
    p = p * (1.0 / jnp.sum(p, axis=1, keepdims=True))
    pb = p.astype(BF)
    out_ref[...] = nn(pb, vb).astype(BF)
    dp = nt(g, vb)
    dv = tn(pb, g)
    ds = p * (dp - jnp.sum(dp * p, axis=1, keepdims=True))
    dsb = ds.astype(BF)
    dq = (nn(dsb, kh) * scale).astype(BF)
    dk = tn(dsb, qh).astype(BF)
    dv = dv.astype(BF)
    dqkv_ref[0] = dq
    dqkv_ref[1] = dk
    dqkv_ref[2] = dv
    m1 = jnp.zeros((ROWS, 1), F32)
    m2 = jnp.zeros((ROWS, 1), F32)
    for d, r in ((dq, q_ref), (dk, k_ref), (dv, v_ref)):
        df = d.astype(F32)
        u = r[ROWS:ROWS + 1, :] + r[ROWS + 1:ROWS + 2, :] + r[ROWS + 2:ROWS + 3, :]
        m1 = m1 + jnp.sum(df * u, axis=1, keepdims=True)
        m2 = m2 + jnp.sum(df * r[:ROWS, :], axis=1, keepdims=True)
    mom_s[pl.ds(0, ROWS), :] += two_lanes(m1, m2)

    @pl.when(h == NH - 1)
    def _():
        t = jnp.transpose(mom_s[...])
        mom_ref[...] = jnp.zeros_like(mom_ref)
        mom_ref[:, pl.ds(0, 640)] = to_rows(t[0:1, :], t[1:2, :])


def attend(index, counts, n_own, n_oth, ws, grad_out):
    return pl.pallas_call(
        attn_kernel,
        grid=(NH,),
        in_specs=[SMEM, SMEM] + [HBM] * (2 + NW) + [pl.BlockSpec((ROWS, HD), lambda h: (0, h))],
        out_specs=[
            pl.BlockSpec((ROWS, HD), lambda h: (0, h)),
            pl.BlockSpec((3, ROWS, HD), lambda h: (0, 0, h)),
            pl.BlockSpec((16, 2 * DB), lambda h: (0, 0)),
        ],
        out_shape=[sds((ROWS, DB)), sds((3, ROWS, DB)), sds((16, 2 * DB))],
        scratch_shapes=[
            pltpu.VMEM((EXT, CW), F32),
            pltpu.VMEM((4, EXT, 4 * DB), BF),
            pltpu.VMEM((4, 4 * DB, CW), BF),
            pltpu.VMEM((640, 128), F32),
            pltpu.SemaphoreType.DMA((8, 2)),
            pltpu.SemaphoreType.DMA((8, 2, 2, 3)),
        ],
        compiler_params=params(),
        cost_estimate=cost(2 * EXT * D * CW, 28 << 20, NH * ROWS * ROWS),
        name="attention",
    )(index, counts, n_own, n_oth, *ws, grad_out)


def grads_kernel(idx, d1, d2, *refs, base, ny, nx, ndeps, ysplit, xsplit, tail):
    w_refs, (n1, n2), extra, refs = refs[:NW], refs[NW:NW + 2], refs[NW + 1 + ndeps], refs[NW + 2 + ndeps:]
    outs = list(refs[:-8])
    wv, nv, dcat, oy, ox, sd, si, so = refs[-8:]
    core = idx[base]
    dc = [pltpu.make_async_copy(d1.at[j], dcat.at[pl.ds(0, ROWS), pl.ds(j * DB, DB)], sd.at[0, j]) for j in range(3)]
    if nx:
        dc += [pltpu.make_async_copy(d2.at[j], dcat.at[pl.ds(ROWS, ROWS), pl.ds(j * DB, DB)], sd.at[1, j])
               for j in range(3)]
    for c in dc[:3]:
        c.start()
    sources = w_sources(w_refs)
    for i in range(ny):
        a = idx[base + 1 + i]
        for k, (mine, other) in enumerate(sources):
            @pl.when(a == k)
            def _():
                for c in w_copies(mine, wv.at[i], core, si.at[i, 0]) + w_copies(other, wv.at[i], 1 - core, si.at[i, 1]):
                    c.start()
    for c in dc[3:]:
        c.start()
    ncs = []
    for i in range(nx):
        m = idx[base + 1 + ny + i]
        ncs.append([pltpu.make_async_copy(n1.at[m, pl.ds(0, ROWS)], nv.at[i, pl.ds(0, ROWS)], si.at[ny + i, 0, 0, 0]),
                    pltpu.make_async_copy(n2.at[m, pl.ds(0, ROWS)], nv.at[i, pl.ds(ROWS, ROWS)], si.at[ny + i, 1, 0, 0])])
        for c in ncs[-1]:
            c.start()
    ends = []
    if tail:
        ends = [pltpu.make_async_copy(extra, oy.at[i, pl.ds(ROWS, 16)], so.at[i, 1]) for i in range(ny)]
        for c in ends:
            c.start()
    pending = []

    def put(src, dst, sem):
        c = pltpu.make_async_copy(src, dst, sem)
        c.start()
        pending.append(c)

    for c in dc[:3]:
        c.wait()
    for i in range(ny):
        a = idx[base + 1 + i]
        for e in range(2):
            halves = jnp.logical_or(a == 7, a == 3)

            @pl.when(halves)
            def _():
                for c in w_copies(sources[7][e], wv.at[i], e, si.at[i, e]):
                    c.wait()

            @pl.when(jnp.logical_not(halves))
            def _():
                for c in w_copies(sources[0][e], wv.at[i], e, si.at[i, e]):
                    c.wait()
        oy[i, pl.ds(0, ROWS), :] = nt(dcat[pl.ds(0, ROWS), :], wv[i]).astype(BF)
        if tail:
            ends[i].wait()
        if i in ysplit:
            put(oy.at[i, pl.ds(0, HALF)], outs.pop(0), so.at[i, 0])
            put(oy.at[i, pl.ds(HALF, HALF)], outs.pop(0), so.at[i, 1])
        else:
            put(oy.at[i], outs.pop(0), so.at[i, 0])
    for c in dc[3:]:
        c.wait()
    for i in range(nx):
        for c in ncs[i]:
            c.wait()
        t = tn(nv[i], dcat[...]).astype(BF)
        for j in range(3):
            ox[i, j] = t[:, j * DB:(j + 1) * DB]
        if i in xsplit:
            put(ox.at[i, :, pl.ds(0, HB)], outs.pop(0), so.at[ny + i, 0])
            put(ox.at[i, :, pl.ds(HB, HB)], outs.pop(0), so.at[ny + i, 1])
        else:
            put(ox.at[i], outs.pop(0), so.at[ny + i, 0])
    for c in pending:
        c.wait()


def grads(table, base, ny, nx, dqkv, d_other, ws, normed, other, deps, ysplit=(), xsplit=(), tail=False):
    shapes, yrows = [], EXT if tail else ROWS
    for i in range(ny):
        shapes += [(HALF, 2 * DB)] * 2 if i in ysplit else [(yrows, 2 * DB)]
    for i in range(nx):
        shapes += [(3, HB, DB)] * 2 if i in xsplit else [(3, DB, DB)]
    deps = list(deps)
    return pl.pallas_call(
        functools.partial(grads_kernel, base=base, ny=ny, nx=nx, ndeps=len(deps), ysplit=ysplit, xsplit=xsplit,
                          tail=tail),
        in_specs=[SMEM] + [HBM] * (4 + NW + len(deps)),
        out_specs=[HBM] * len(shapes),
        out_shape=[sds(s) for s in shapes],
        scratch_shapes=[
            pltpu.VMEM((max(ny, 1), 2 * DB, CW), BF),
            pltpu.VMEM((max(nx, 1), 2 * ROWS, DB), BF),
            pltpu.VMEM((2 * ROWS, CW), BF),
            pltpu.VMEM((max(ny, 1), yrows, 2 * DB), BF),
            pltpu.VMEM((max(nx, 1), 3, DB, DB), BF),
            pltpu.SemaphoreType.DMA((2, 3)),
            pltpu.SemaphoreType.DMA((ny + nx, 2, 2, 3)),
            pltpu.SemaphoreType.DMA((ny + nx, 2)),
        ],
        compiler_params=params(),
        cost_estimate=cost(0, 1 << 12),
        name="grads",
    )(table, dqkv, d_other, *ws, normed, other, *deps)


def sum_rows_kernel(mine, own, *refs):
    out = refs[-1]
    total = mine[...].astype(F32)
    rows = own[...].astype(F32)
    for r in refs[:3]:
        total = total + r[pl.ds(0, ROWS), :].astype(F32)
        rows = rows + r[pl.ds(ROWS, 16), :].astype(F32)
    out[pl.ds(0, ROWS), :] = total.astype(BF)
    m1 = rows[0:1] + rows[1:2] + rows[2:3]
    m2 = rows[3:4] + rows[4:5] + rows[5:6]
    out[pl.ds(ROWS, 16), :] = to_rows(m1, m2)


def sum_rows(mine, own, arrived, deps):
    whole = lambda v: pl.BlockSpec(v.shape, lambda i: (0,) * v.ndim)
    return pl.pallas_call(
        sum_rows_kernel,
        grid=(1,),
        in_specs=[whole(v) for v in (mine, own, *arrived)] + [HBM] * len(deps),
        out_specs=whole(arrived[0]),
        out_shape=sds(arrived[0].shape),
        compiler_params=params(),
        cost_estimate=cost(0, 1 << 12),
        name="sum_rows",
    )(mine, own, *arrived, *deps)


def sum_kernel(*refs, n):
    total = refs[0][...].astype(F32)
    for r in refs[1:n]:
        total = total + r[...].astype(F32)
    refs[-1][...] = total.astype(BF)


def sum_blocks(vs, deps):
    n = len(vs)
    spec = pl.BlockSpec((1, DB, DB), lambda i: (i, 0, 0))
    return pl.pallas_call(
        functools.partial(sum_kernel, n=n),
        grid=(3,),
        in_specs=[spec] * n + [HBM] * len(deps),
        out_specs=spec,
        out_shape=sds(vs[0].shape),
        compiler_params=params(),
        cost_estimate=cost(0, 1 << 12),
        name="sum_blocks",
    )(*vs, *deps)


def ivec(*v):
    return jnp.stack([jnp.asarray(e, jnp.int32) for e in v])


def local(patches, gain, w_qkv, counts, grad_out):
    si, mi = lax.axis_index("seq"), lax.axis_index("mp")
    core, x, zh = si % 2, (si // 2) % 4, si // 8
    y, zl = mi // 2, mi % 2
    mw = lambda dx, dz: jnp.where(dz == 0, zh, 1 - zh) * 4 + (x + dx) % 4
    mx = lambda dy, dz: ((y + dy) % 4) * 2 + jnp.where(dz == 0, zl, 1 - zl)
    rows, wshape = (EXT, 2 * DB), (3, DB, DB)
    lo, hi = (slice(None), pl.ds(0, HB)), (slice(None), pl.ds(HB, HB))
    first, rest = (pl.ds(0, HALF),), (pl.ds(HALF, EXT - HALF),)

    p0 = extend(patches, gain)
    w = jnp.transpose(w_qkv, (1, 0, 2))
    p_m, p_p, pz = mpp(p0, YP), mpp(p0, YM), mpp(p0, ZLO)
    w_m, w_p = sp(w, XP), sp(w, XM)
    pz1, w1 = move([pz, w], [rows, wshape], [(0, None, 0, None), (1, None, 1, None)], [p_m, p_p], "gate_y1")
    pz_m, pz_p = mpp(pz1, YP), mpp(pz1, YM)
    wz = sp(w1, ZHI)
    w_lo, w_hi = move([w_m, w_p], [(3, HB, DB)] * 2, [(0, lo, 0, None), (1, hi, 1, None)], [pz1], "gate_x1")
    wf_m, wf_p = sp(w_lo, XP), sp(w_hi, XM)
    (w3,) = move([w1, w_m, w_p], [(3,) + wshape], [(k, None, 0, (k,)) for k in range(3)], [w_lo], "pack")
    fu, fd = move(
        [p_m, p_p, pz_m, pz_p], [(2, HALF, 2 * DB), (2, EXT - HALF, 2 * DB)],
        [(0, first, 0, (0,)), (2, first, 0, (1,)), (1, rest, 1, (0,)), (3, rest, 1, (1,))], [w_lo, w3], "gate_y2")
    f_m, f_p = mpp(fu, YP), mpp(fd, YM)
    (wz1,) = move([wz], [wshape], [(0, None, 0, None)], [wf_m, wf_p, fu], "gate_x2")
    wz_m, wz_p = sp(wz1, XP), sp(wz1, XM)
    (w3,) = hold([w3], [wz1])
    o_w = sp(w3, CORE)
    st = stats([p0, pz, p_m, p_p, pz_m, pz_p], [wz1])
    wz_lo, wz_hi, wz2 = move(
        [wz_m, wz_p, wz1], [(3, HB, DB), (3, HB, DB), wshape],
        [(0, lo, 0, None), (1, hi, 1, None), (2, None, 2, None)],
        [f_m, f_p, o_w, st], "gate_x3")
    wzf_m, wzf_p = sp(wz_lo, XP), sp(wz_hi, XM)
    wf_m, wf_p = hold([wf_m, wf_p], [wz_lo])
    o_fm, o_fp = sp(wf_m, CORE), sp(wf_p, CORE)
    o_z, o_zm, o_zp = (sp(v, CORE) for v in (wz2, wz_m, wz_p))
    def source(dy, dz):
        m = mx(dy, dz)
        dx = (m % 4 - x) % 4
        return jnp.where(dx == 3, 1, jnp.where(dx == 1, 2, jnp.where(dx == 2, 3, 0))) + jnp.where(m // 4 == zh, 0, 4)

    entries = [mx(0, 0), mx(0, 1), mx(-1, 0), mx(1, 0), mx(-1, 1), mx(1, 1), mx(2, 0), mx(2, 1), core,
               mw(0, 0), mw(-1, 0), mw(1, 0), mw(2, 0), mw(0, 1), mw(-1, 1), mw(1, 1), mw(2, 1), core]
    calls = []
    for yb, xb in (([(1, 1), (-1, 1), (2, 1)], []), ([], [(1, 1), (-1, 1)]),
                   ([(2, 0), (1, 0), (-1, 0), (0, 1)], []), ([], [(2, 1), (1, 0), (-1, 0), (0, 1)]),
                   ([(0, 0)], [(0, 0), (2, 0)])):
        calls.append((len(entries), yb, xb))
        entries += [core] + [source(*b) for b in yb] + [mw(*b) for b in xb]
    table = ivec(*entries)
    n_own, n_oth, st = normalize(table, st, [p0, pz, p_m, p_p, pz_m, pz_p, f_m, f_p], wz_lo)
    mean, rstd = st[:, 0:1], st[:, 1:2]
    wzf_m, wzf_p, n_oth = hold([wzf_m, wzf_p, n_oth], [o_z])
    o_zfm, o_zfp = sp(wzf_m, CORE), sp(wzf_p, CORE)
    (n_oth,) = hold([n_oth], [o_zfm, o_zfp, o_zm, o_zp, o_fm, o_fp])
    n_other = sp(n_oth, CORE)
    ws = [w1, w_m, w_p, wf_m, wf_p, o_w, o_fm, o_fp,
          wz2, wz_m, wz_p, wzf_m, wzf_p, o_z, o_zm, o_zp, o_zfm, o_zfp]
    heads_out, dqkv, mom = attend(table, counts.reshape(4), n_own, n_oth, ws, grad_out)

    d_other = sp(dqkv, CORE)

    def blocks(call, deps, **kw):
        base, yb, xb = calls[call]
        return grads(table, base, len(yb), len(xb), dqkv, d_other if xb else dqkv, ws, n_own,
                     n_other if xb else n_own, deps, **kw)

    yu, yd, y2 = blocks(0, [mom], tail=True)
    ya = [mpp(yu, YP), mpp(yd, YM), mpp(y2, Y2)]
    xu, xd = blocks(1, [yu])
    xa = [sp(xu, XP), sp(xd, XM)]
    y2o, y1u, y1d, y0p = blocks(2, [xu])
    x2, x1u, x1d, x0p = blocks(3, [y0p])
    xa.append(sp(x2, X2))
    y_out = sum_rows(y0p, mom, ya, [x0p])
    yz = mpp(y_out, ZLO)
    yb1, yb2 = mpp(y1u, YP), mpp(y1d, YM)
    y0, x0, x2o = blocks(4, [y_out])
    x_out = sum_blocks([x0p, *xa], [y0])
    x1u, x1d = hold([x1u, x1d], [y0])
    xb1, xb2 = sp(x1u, XP), sp(x1d, XM)
    (y2o,) = hold([y2o], [yz, yb1, yb2, x_out])
    (x_out,) = hold([x_out], [y2o])
    yb3, xz = mpp(y2o, Y2), sp(x_out, ZHI)
    (x2o,) = hold([x2o], [xb1, xb2, x_out])
    xb3 = sp(x2o, X2)

    f = lambda v: v.astype(F32)
    mom = jnp.sum((f(y_out[ROWS:ROWS + 6]) + f(yz[ROWS:ROWS + 6])).reshape(2, 3, 2 * DB), axis=1)[:, :ROWS] / D
    gn = f(y0) + f(yb1) + f(yb2) + f(yb3) + f(yz[:ROWS])
    xhat = (f(patches) - mean) * rstd
    gg = jnp.sum(gn * xhat, axis=0)
    for perm in (CORE, ZHI):
        gg = gg + sp(gg, perm)
    gg = (gg + sp(gg, X2)) + (sp(gg, XP) + sp(gg, XM))
    grad_p = ((gn * gain[None, :] - mom[0][:, None] - xhat * mom[1][:, None]) * rstd).astype(BF)
    gw = jnp.transpose(f(x0) + f(xb1) + f(xb2) + f(xb3) + f(xz), (1, 0, 2))
    return heads_out, grad_p, gg, gw


def solution(mesh):
    placed = (P("seq", "mp"), P("mp"), P("seq", None, "mp"), P("seq", None), P("seq", "mp"))
    return jax.shard_map(
        local,
        mesh=mesh,
        in_specs=placed,
        out_specs=(P("seq", "mp"), P("seq", "mp"), P("mp"), P("seq", None, "mp")),
        check_vma=False,
    )
```

```python
import functools

import jax
import jax.numpy as jnp
from jax import lax
from jax.experimental import pallas as pl
from jax.experimental.pallas import tpu as pltpu
from jax.sharding import PartitionSpec as P

HD = 128
NH = 3
ROWS = 576
HALF = ROWS // 2
EXT = ROWS + 16
DB = 384
HB = DB // 2
D = 6144
CW = 3 * DB
EPS = 1e-06
BF = jnp.bfloat16
F32 = jnp.float32
HBM = pl.BlockSpec(memory_space=pltpu.HBM)
VMEM = pl.BlockSpec(memory_space=pltpu.VMEM)
SMEM = pl.BlockSpec(memory_space=pltpu.SMEM)


def seq_perm(f):
    out = []
    for i in range(16):
        zh, x, c = f(i // 8, (i // 2) % 4, i % 2)
        out.append((i, (zh * 4 + x % 4) * 2 + c))
    return out


def mp_perm(f):
    out = []
    for i in range(8):
        y, zl = f(i // 2, i % 2)
        out.append((i, (y % 4) * 2 + zl))
    return out


CORE = seq_perm(lambda zh, x, c: (zh, x, 1 - c))
ZHI = seq_perm(lambda zh, x, c: (1 - zh, x, c))
XP = seq_perm(lambda zh, x, c: (zh, x + 1, c))
XM = seq_perm(lambda zh, x, c: (zh, x - 1, c))
X2 = seq_perm(lambda zh, x, c: (zh, x + 2, c))
ZLO = mp_perm(lambda y, zl: (y, 1 - zl))
YP = mp_perm(lambda y, zl: (y + 1, zl))
YM = mp_perm(lambda y, zl: (y - 1, zl))
Y2 = mp_perm(lambda y, zl: (y + 2, zl))


def sp(v, perm):
    return lax.ppermute(v, "seq", perm)


def mpp(v, perm):
    return lax.ppermute(v, "mp", perm)


def nt(a, b):
    return lax.dot_general(a, b, (((1,), (1,)), ((), ())), preferred_element_type=F32)


def tn(a, b):
    return lax.dot_general(a, b, (((0,), (0,)), ((), ())), preferred_element_type=F32)


def nn(a, b):
    return lax.dot_general(a, b, (((1,), (0,)), ((), ())), preferred_element_type=F32)


def sds(shape, dtype=BF):
    return jax.ShapeDtypeStruct(shape, dtype)


def params(mib=63):
    return pltpu.CompilerParams(vmem_limit_bytes=mib << 20)


def cost(flops, nbytes, exps=0):
    return pl.CostEstimate(flops=int(flops), bytes_accessed=int(nbytes), transcendentals=exps)


def sliced(shape, index):
    if not index:
        return shape
    out = []
    for n, i in zip(shape, index):
        if not isinstance(i, int):
            out.append(n if isinstance(i, slice) else i.size)
    return tuple(out) + tuple(shape[len(index):])


def move(inputs, outs, plan, deps, name):
    def kernel(*refs):
        ins = refs[:len(inputs)]
        dst = refs[len(inputs) + len(deps):][:len(outs)]
        *bufs, sem = refs[len(inputs) + len(deps) + len(outs):]
        get = [pltpu.make_async_copy(ins[i].at[si] if si else ins[i], bufs[k], sem.at[k, 0])
               for k, (i, si, o, so) in enumerate(plan)]
        put = [pltpu.make_async_copy(bufs[k], dst[o].at[so] if so else dst[o], sem.at[k, 1])
               for k, (i, si, o, so) in enumerate(plan)]
        for c in get:
            c.start()
        for g, p in zip(get, put):
            g.wait()
            p.start()
        for p in put:
            p.wait()

    return pl.pallas_call(
        kernel,
        in_specs=[HBM] * (len(inputs) + len(deps)),
        out_specs=[HBM] * len(outs),
        out_shape=[sds(s) for s in outs],
        scratch_shapes=[pltpu.VMEM(sliced(inputs[i].shape, si), BF) for i, si, o, so in plan]
        + [pltpu.SemaphoreType.DMA((len(plan), 2))],
        compiler_params=params(),
        cost_estimate=cost(0, 4 << 20),
        name=name,
    )(*inputs, *deps)


def hold(values, deps):
    def kernel(*refs):
        pass

    n = len(values)
    return pl.pallas_call(
        kernel,
        in_specs=[HBM] * (n + len(deps)),
        out_specs=[HBM] * n,
        out_shape=[sds(v.shape, v.dtype) for v in values],
        input_output_aliases={k: k for k in range(n)},
        compiler_params=params(),
        cost_estimate=cost(0, 1 << 10),
        name="hold",
    )(*values, *deps)


def extend_kernel(p, gain, out):
    out[pl.ds(0, ROWS), :] = p[...]
    g = gain[...].reshape(1, 2 * DB)
    hi = g.astype(BF).astype(F32)
    mid = (g - hi).astype(BF).astype(F32)
    row = lax.broadcasted_iota(jnp.int32, (16, 2 * DB), 0)
    tail = jnp.where(row == 0, hi, jnp.where(row == 1, mid, jnp.where(row == 2, g - hi - mid, 0.0)))
    out[pl.ds(ROWS, 16), :] = tail.astype(BF)


def extend(patches, gain):
    return pl.pallas_call(
        extend_kernel,
        out_shape=sds((EXT, 2 * DB)),
        compiler_params=params(),
        cost_estimate=cost(0, 2 << 20),
        name="extend",
    )(patches, gain)


def merge(n, mean, m2, chunk):
    v = chunk.astype(F32)
    cm = jnp.sum(v, axis=1, keepdims=True) * (1.0 / 768)
    dv = v - cm
    c2 = jnp.sum(dv * dv, axis=1, keepdims=True)
    if n == 0:
        return cm, c2
    delta = cm - mean
    return mean + delta * (1.0 / (n + 1)), m2 + c2 + delta * delta * (768.0 * n / (n + 1))


def two_lanes(a, b):
    lane = lax.broadcasted_iota(jnp.int32, (ROWS, 128), 1)
    return jnp.where(lane == 0, a, jnp.where(lane == 1, b, 0.0))


def stats_kernel(*refs, nraw, ndeps):
    raws = refs[:nraw]
    out, buf, sem = refs[nraw + ndeps:]
    copies = [pltpu.make_async_copy(r, buf.at[j], sem.at[j]) for j, r in enumerate(raws)]
    for c in copies:
        c.start()
    mean = m2 = None
    for j, c in enumerate(copies):
        c.wait()
        mean, m2 = merge(j, mean, m2, buf[j, pl.ds(0, ROWS), :])
    out[...] = two_lanes(mean, m2)


def stats(raws, deps):
    n = len(raws)
    return pl.pallas_call(
        functools.partial(stats_kernel, nraw=n, ndeps=len(deps)),
        in_specs=[HBM] * (n + len(deps)),
        out_specs=VMEM,
        out_shape=sds((ROWS, 128), F32),
        scratch_shapes=[pltpu.VMEM((n, EXT, 2 * DB), BF), pltpu.SemaphoreType.DMA((n,))],
        compiler_params=params(),
        cost_estimate=cost(0, 4 << 20),
        name="row_stats",
    )(*raws, *deps)


def norm_kernel(idx, st, r0, r1, r2, r3, r4, r5, fm, fp, _, n_own, n_oth, st_out, raw, nrm, sr, so):
    core = idx[8]
    copies = []
    for j in range(2):
        copies.append(pltpu.make_async_copy(fm.at[j], raw.at[6 + j, pl.ds(0, HALF)], sr.at[j]))
        copies.append(pltpu.make_async_copy(fp.at[j], raw.at[6 + j, pl.ds(HALF, EXT - HALF)], sr.at[2 + j]))
    for j, r in enumerate((r0, r1, r2, r3, r4, r5)):
        copies.append(pltpu.make_async_copy(r, raw.at[j], sr.at[4 + j]))
    for c in copies:
        c.start()
    for c in copies[:4]:
        c.wait()
    mean, m2 = st[:, 0:1], st[:, 1:2]
    for j in range(2):
        mean, m2 = merge(6 + j, mean, m2, raw[6 + j, pl.ds(0, ROWS), :])
    rstd = lax.rsqrt(m2 * (1.0 / D) + EPS)
    st_out[...] = two_lanes(mean, rstd)
    out = []
    own = pl.ds(pl.multiple_of(core * DB, 128), DB)
    oth = pl.ds(pl.multiple_of((1 - core) * DB, 128), DB)
    for j in (6, 7, 0, 1, 2, 3, 4, 5):
        if j < 6:
            copies[4 + j].wait()
        tail = raw[j, pl.ds(ROWS, 16), :]
        t = tail.astype(F32)
        g = t[0:1] + t[1:2] + t[2:3]
        nrm[j, pl.ds(0, ROWS), :] = ((raw[j, pl.ds(0, ROWS), :].astype(F32) - mean) * rstd * g).astype(BF)
        nrm[j, pl.ds(ROWS, 16), :] = tail
        mine = [pltpu.make_async_copy(nrm.at[j, :, own], n_own.at[idx[j]], so.at[j, 0]),
                pltpu.make_async_copy(nrm.at[j, :, oth], n_oth.at[idx[j]], so.at[j, 1])]
        for c in mine:
            c.start()
        out += mine
    for c in out:
        c.wait()


def normalize(index, st, raws, after):
    return pl.pallas_call(
        norm_kernel,
        in_specs=[SMEM, VMEM] + [HBM] * (len(raws) + 1),
        out_specs=[HBM, HBM, VMEM],
        out_shape=[sds((8, EXT, DB)), sds((8, EXT, DB)), sds((ROWS, 128), F32)],
        scratch_shapes=[
            pltpu.VMEM((8, EXT, 2 * DB), BF),
            pltpu.VMEM((8, EXT, 2 * DB), BF),
            pltpu.SemaphoreType.DMA((10,)),
            pltpu.SemaphoreType.DMA((8, 2)),
        ],
        compiler_params=params(),
        cost_estimate=cost(0, 8 << 20),
        name="normalize",
    )(index, st, *raws, after)


NW = 18


def w_sources(refs):
    own, packed, far, pair, other = refs[:5], refs[5], refs[6:8], refs[8:13], refs[13:18]
    out = [((own[k],), (packed.at[k],)) if k < 3 else (own[3:5], far) for k in range(4)]
    return out + [((pair[k],), (other[k],)) if k < 3 else (pair[3:5], other[3:5]) for k in range(4)]


def w_copies(parts, buf, half, sem):
    out = []
    rows = DB // len(parts)
    for h, part in enumerate(parts):
        at = pl.ds(pl.multiple_of(half * DB + h * rows, 64), rows)
        out += [pltpu.make_async_copy(part.at[j], buf.at[at, pl.ds(j * DB, DB)], sem.at[h, j]) for j in range(3)]
    return out


def to_rows(m1, m2):
    row = lax.broadcasted_iota(jnp.int32, (16, m1.shape[1]), 0)
    out = jnp.zeros((16, m1.shape[1]), F32)
    for k, m in enumerate((m1, m2)):
        hi = m.astype(BF).astype(F32)
        mid = (m - hi).astype(BF).astype(F32)
        for j, part in enumerate((hi, mid, m - hi - mid)):
            out = jnp.where(row == 3 * k + j, part, out)
    return out.astype(BF)


def split(v):
    hi = v.astype(BF)
    return hi, (v - hi.astype(F32)).astype(BF)


def attn_kernel(idx, counts, n_own, n_oth, *refs):
    w_refs, refs = refs[:NW], refs[NW:]
    g_ref, out_ref, dqkv_ref, mom_ref, qkv, nv, wv, mom_s, sn, sw = refs
    h = pl.program_id(0)

    @pl.when(h == 0)
    def _():
        core = idx[17]
        copies = []
        for k, (mine, other) in enumerate(w_sources(w_refs)):
            m = idx[9 + k]
            at = (k % 2) * 2 * DB
            lanes = lambda c: pl.ds(pl.multiple_of(at + c * DB, 128), DB)
            copies.append([pltpu.make_async_copy(n_own.at[m], nv.at[k // 2, :, lanes(core)], sn.at[k, 0]),
                           pltpu.make_async_copy(n_oth.at[m], nv.at[k // 2, :, lanes(1 - core)], sn.at[k, 1])]
                          + w_copies(mine, wv.at[k // 2, pl.ds(at, 2 * DB)], core, sw.at[k, 0])
                          + w_copies(other, wv.at[k // 2, pl.ds(at, 2 * DB)], 1 - core, sw.at[k, 1]))
            for c in copies[-1]:
                c.start()
        mom_s[...] = jnp.zeros_like(mom_s)
        for k in range(4):
            for c in copies[2 * k] + copies[2 * k + 1]:
                c.wait()
            t = nn(nv[k], wv[k])
            if k == 0:
                qkv[...] = t
            else:
                qkv[...] += t

    col = lambda j: pl.ds(pl.multiple_of((j * NH + h) * HD, 128), HD)
    q_ref, k_ref, v_ref = (qkv.at[:, col(j)] for j in range(3))
    e0 = counts[0]
    e1 = e0 + counts[1]
    e2 = e1 + counts[2]
    rid = lax.broadcasted_iota(jnp.int32, (ROWS, 1), 0)
    cid = lax.broadcasted_iota(jnp.int32, (1, ROWS), 1)
    img = lambda p: (p >= e0).astype(jnp.int32) + (p >= e1).astype(jnp.int32) + (p >= e2).astype(jnp.int32)
    same = img(rid) == img(cid)
    scale = HD ** (-0.5)
    q = q_ref[:ROWS, :] * scale
    k = k_ref[:ROWS, :]
    v = v_ref[:ROWS, :]
    qh, ql = split(q)
    kh, kl = split(k)
    vb = v.astype(BF)
    g = g_ref[...]
    s = nt(jnp.concatenate([qh, qh, ql], 1), jnp.concatenate([kh, kl, kh], 1))
    s = jnp.where(same, s, -1e30)
    p = jnp.exp(s - jnp.max(s, axis=1, keepdims=True))
    p = p * (1.0 / jnp.sum(p, axis=1, keepdims=True))
    pb = p.astype(BF)
    out_ref[...] = nn(pb, vb).astype(BF)
    dp = nt(g, vb)
    dv = tn(pb, g)
    ds = p * (dp - jnp.sum(dp * p, axis=1, keepdims=True))
    dsb = ds.astype(BF)
    dq = (nn(dsb, kh) * scale).astype(BF)
    dk = tn(dsb, qh).astype(BF)
    dv = dv.astype(BF)
    dqkv_ref[0] = dq
    dqkv_ref[1] = dk
    dqkv_ref[2] = dv
    m1 = jnp.zeros((ROWS, 1), F32)
    m2 = jnp.zeros((ROWS, 1), F32)
    for d, r in ((dq, q_ref), (dk, k_ref), (dv, v_ref)):
        df = d.astype(F32)
        u = r[ROWS:ROWS + 1, :] + r[ROWS + 1:ROWS + 2, :] + r[ROWS + 2:ROWS + 3, :]
        m1 = m1 + jnp.sum(df * u, axis=1, keepdims=True)
        m2 = m2 + jnp.sum(df * r[:ROWS, :], axis=1, keepdims=True)
    mom_s[pl.ds(0, ROWS), :] += two_lanes(m1, m2)

    @pl.when(h == NH - 1)
    def _():
        t = jnp.transpose(mom_s[...])
        mom_ref[...] = jnp.zeros_like(mom_ref)
        mom_ref[:, pl.ds(0, 640)] = to_rows(t[0:1, :], t[1:2, :])


def attend(index, counts, n_own, n_oth, ws, grad_out):
    return pl.pallas_call(
        attn_kernel,
        grid=(NH,),
        in_specs=[SMEM, SMEM] + [HBM] * (2 + NW) + [pl.BlockSpec((ROWS, HD), lambda h: (0, h))],
        out_specs=[
            pl.BlockSpec((ROWS, HD), lambda h: (0, h)),
            pl.BlockSpec((3, ROWS, HD), lambda h: (0, 0, h)),
            pl.BlockSpec((16, 2 * DB), lambda h: (0, 0)),
        ],
        out_shape=[sds((ROWS, DB)), sds((3, ROWS, DB)), sds((16, 2 * DB))],
        scratch_shapes=[
            pltpu.VMEM((EXT, CW), F32),
            pltpu.VMEM((4, EXT, 4 * DB), BF),
            pltpu.VMEM((4, 4 * DB, CW), BF),
            pltpu.VMEM((640, 128), F32),
            pltpu.SemaphoreType.DMA((8, 2)),
            pltpu.SemaphoreType.DMA((8, 2, 2, 3)),
        ],
        compiler_params=params(),
        cost_estimate=cost(2 * EXT * D * CW, 28 << 20, NH * ROWS * ROWS),
        name="attention",
    )(index, counts, n_own, n_oth, *ws, grad_out)


def grads_kernel(idx, d1, d2, *refs, base, ny, nx, ndeps, ysplit, xsplit, tail):
    w_refs, (n1, n2), extra, refs = refs[:NW], refs[NW:NW + 2], refs[NW + 1 + ndeps], refs[NW + 2 + ndeps:]
    outs = list(refs[:-8])
    wv, nv, dcat, oy, ox, sd, si, so = refs[-8:]
    core = idx[base]
    dc = [pltpu.make_async_copy(d1.at[j], dcat.at[pl.ds(0, ROWS), pl.ds(j * DB, DB)], sd.at[0, j]) for j in range(3)]
    if nx:
        dc += [pltpu.make_async_copy(d2.at[j], dcat.at[pl.ds(ROWS, ROWS), pl.ds(j * DB, DB)], sd.at[1, j])
               for j in range(3)]
    for c in dc[:3]:
        c.start()
    sources = w_sources(w_refs)
    for i in range(ny):
        a = idx[base + 1 + i]
        for k, (mine, other) in enumerate(sources):
            @pl.when(a == k)
            def _():
                for c in w_copies(mine, wv.at[i], core, si.at[i, 0]) + w_copies(other, wv.at[i], 1 - core, si.at[i, 1]):
                    c.start()
    for c in dc[3:]:
        c.start()
    ncs = []
    for i in range(nx):
        m = idx[base + 1 + ny + i]
        ncs.append([pltpu.make_async_copy(n1.at[m, pl.ds(0, ROWS)], nv.at[i, pl.ds(0, ROWS)], si.at[ny + i, 0, 0, 0]),
                    pltpu.make_async_copy(n2.at[m, pl.ds(0, ROWS)], nv.at[i, pl.ds(ROWS, ROWS)], si.at[ny + i, 1, 0, 0])])
        for c in ncs[-1]:
            c.start()
    ends = []
    if tail:
        ends = [pltpu.make_async_copy(extra, oy.at[i, pl.ds(ROWS, 16)], so.at[i, 1]) for i in range(ny)]
        for c in ends:
            c.start()
    pending = []

    def put(src, dst, sem):
        c = pltpu.make_async_copy(src, dst, sem)
        c.start()
        pending.append(c)

    for c in dc[:3]:
        c.wait()
    for i in range(ny):
        a = idx[base + 1 + i]
        for e in range(2):
            halves = jnp.logical_or(a == 7, a == 3)

            @pl.when(halves)
            def _():
                for c in w_copies(sources[7][e], wv.at[i], e, si.at[i, e]):
                    c.wait()

            @pl.when(jnp.logical_not(halves))
            def _():
                for c in w_copies(sources[0][e], wv.at[i], e, si.at[i, e]):
                    c.wait()
        oy[i, pl.ds(0, ROWS), :] = nt(dcat[pl.ds(0, ROWS), :], wv[i]).astype(BF)
        if tail:
            ends[i].wait()
        if i in ysplit:
            put(oy.at[i, pl.ds(0, HALF)], outs.pop(0), so.at[i, 0])
            put(oy.at[i, pl.ds(HALF, HALF)], outs.pop(0), so.at[i, 1])
        else:
            put(oy.at[i], outs.pop(0), so.at[i, 0])
    for c in dc[3:]:
        c.wait()
    for i in range(nx):
        for c in ncs[i]:
            c.wait()
        t = tn(nv[i], dcat[...]).astype(BF)
        for j in range(3):
            ox[i, j] = t[:, j * DB:(j + 1) * DB]
        if i in xsplit:
            put(ox.at[i, :, pl.ds(0, HB)], outs.pop(0), so.at[ny + i, 0])
            put(ox.at[i, :, pl.ds(HB, HB)], outs.pop(0), so.at[ny + i, 1])
        else:
            put(ox.at[i], outs.pop(0), so.at[ny + i, 0])
    for c in pending:
        c.wait()


def grads(table, base, ny, nx, dqkv, d_other, ws, normed, other, deps, ysplit=(), xsplit=(), tail=False):
    shapes, yrows = [], EXT if tail else ROWS
    for i in range(ny):
        shapes += [(HALF, 2 * DB)] * 2 if i in ysplit else [(yrows, 2 * DB)]
    for i in range(nx):
        shapes += [(3, HB, DB)] * 2 if i in xsplit else [(3, DB, DB)]
    deps = list(deps)
    return pl.pallas_call(
        functools.partial(grads_kernel, base=base, ny=ny, nx=nx, ndeps=len(deps), ysplit=ysplit, xsplit=xsplit,
                          tail=tail),
        in_specs=[SMEM] + [HBM] * (4 + NW + len(deps)),
        out_specs=[HBM] * len(shapes),
        out_shape=[sds(s) for s in shapes],
        scratch_shapes=[
            pltpu.VMEM((max(ny, 1), 2 * DB, CW), BF),
            pltpu.VMEM((max(nx, 1), 2 * ROWS, DB), BF),
            pltpu.VMEM((2 * ROWS, CW), BF),
            pltpu.VMEM((max(ny, 1), yrows, 2 * DB), BF),
            pltpu.VMEM((max(nx, 1), 3, DB, DB), BF),
            pltpu.SemaphoreType.DMA((2, 3)),
            pltpu.SemaphoreType.DMA((ny + nx, 2, 2, 3)),
            pltpu.SemaphoreType.DMA((ny + nx, 2)),
        ],
        compiler_params=params(),
        cost_estimate=cost(0, 1 << 12),
        name="grads",
    )(table, dqkv, d_other, *ws, normed, other, *deps)


def sum_rows_kernel(mine, own, *refs):
    out = refs[-1]
    total = mine[...].astype(F32)
    rows = own[...].astype(F32)
    for r in refs[:3]:
        total = total + r[pl.ds(0, ROWS), :].astype(F32)
        rows = rows + r[pl.ds(ROWS, 16), :].astype(F32)
    out[pl.ds(0, ROWS), :] = total.astype(BF)
    m1 = rows[0:1] + rows[1:2] + rows[2:3]
    m2 = rows[3:4] + rows[4:5] + rows[5:6]
    out[pl.ds(ROWS, 16), :] = to_rows(m1, m2)


def sum_rows(mine, own, arrived, deps):
    whole = lambda v: pl.BlockSpec(v.shape, lambda i: (0,) * v.ndim)
    return pl.pallas_call(
        sum_rows_kernel,
        grid=(1,),
        in_specs=[whole(v) for v in (mine, own, *arrived)] + [HBM] * len(deps),
        out_specs=whole(arrived[0]),
        out_shape=sds(arrived[0].shape),
        compiler_params=params(),
        cost_estimate=cost(0, 1 << 12),
        name="sum_rows",
    )(mine, own, *arrived, *deps)


def sum_kernel(*refs, n):
    total = refs[0][...].astype(F32)
    for r in refs[1:n]:
        total = total + r[...].astype(F32)
    refs[-1][...] = total.astype(BF)


def early_kernel(a, b, c, d, out):
    out[...] = (a[...].astype(F32) + b[...].astype(F32)) + (c[...].astype(F32) + d[...].astype(F32))


def early_sum(vs):
    spec = pl.BlockSpec((ROWS // 3, 2 * DB), lambda i: (i, 0))
    return pl.pallas_call(
        early_kernel,
        grid=(3,),
        in_specs=[spec] * 4,
        out_specs=spec,
        out_shape=sds((ROWS, 2 * DB), F32),
        compiler_params=params(),
        cost_estimate=cost(0, 1 << 12),
        name="early_sum",
    )(*vs)


def sum_blocks(vs, deps):
    n = len(vs)
    spec = pl.BlockSpec((1, DB, DB), lambda i: (i, 0, 0))
    return pl.pallas_call(
        functools.partial(sum_kernel, n=n),
        grid=(3,),
        in_specs=[spec] * n + [HBM] * len(deps),
        out_specs=spec,
        out_shape=sds(vs[0].shape),
        compiler_params=params(),
        cost_estimate=cost(0, 1 << 12),
        name="sum_blocks",
    )(*vs, *deps)


def ivec(*v):
    return jnp.stack([jnp.asarray(e, jnp.int32) for e in v])


def local(patches, gain, w_qkv, counts, grad_out):
    si, mi = lax.axis_index("seq"), lax.axis_index("mp")
    core, x, zh = si % 2, (si // 2) % 4, si // 8
    y, zl = mi // 2, mi % 2
    mw = lambda dx, dz: jnp.where(dz == 0, zh, 1 - zh) * 4 + (x + dx) % 4
    mx = lambda dy, dz: ((y + dy) % 4) * 2 + jnp.where(dz == 0, zl, 1 - zl)
    rows, wshape = (EXT, 2 * DB), (3, DB, DB)
    lo, hi = (slice(None), pl.ds(0, HB)), (slice(None), pl.ds(HB, HB))
    first, rest = (pl.ds(0, HALF),), (pl.ds(HALF, EXT - HALF),)

    p0 = extend(patches, gain)
    w = jnp.transpose(w_qkv, (1, 0, 2))
    p_m, p_p, pz = mpp(p0, YP), mpp(p0, YM), mpp(p0, ZLO)
    w_m, w_p = sp(w, XP), sp(w, XM)
    pz1, w1 = move([pz, w], [rows, wshape], [(0, None, 0, None), (1, None, 1, None)], [p_m, p_p], "gate_y1")
    pz_m, pz_p = mpp(pz1, YP), mpp(pz1, YM)
    wz = sp(w1, ZHI)
    w_lo, w_hi = move([w_m, w_p], [(3, HB, DB)] * 2, [(0, lo, 0, None), (1, hi, 1, None)], [pz1], "gate_x1")
    wf_m, wf_p = sp(w_lo, XP), sp(w_hi, XM)
    (w3,) = move([w1, w_m, w_p], [(3,) + wshape], [(k, None, 0, (k,)) for k in range(3)], [w_lo], "pack")
    fu, fd = move(
        [p_m, p_p, pz_m, pz_p], [(2, HALF, 2 * DB), (2, EXT - HALF, 2 * DB)],
        [(0, first, 0, (0,)), (2, first, 0, (1,)), (1, rest, 1, (0,)), (3, rest, 1, (1,))], [w_lo, w3], "gate_y2")
    f_m, f_p = mpp(fu, YP), mpp(fd, YM)
    (wz1,) = move([wz], [wshape], [(0, None, 0, None)], [wf_m, wf_p, fu], "gate_x2")
    wz_m, wz_p = sp(wz1, XP), sp(wz1, XM)
    (w3,) = hold([w3], [wz1])
    o_w = sp(w3, CORE)
    st = stats([p0, pz, p_m, p_p, pz_m, pz_p], [wz1])
    wz_lo, wz_hi, wz2 = move(
        [wz_m, wz_p, wz1], [(3, HB, DB), (3, HB, DB), wshape],
        [(0, lo, 0, None), (1, hi, 1, None), (2, None, 2, None)],
        [f_m, f_p, o_w, st], "gate_x3")
    wzf_m, wzf_p = sp(wz_lo, XP), sp(wz_hi, XM)
    wf_m, wf_p = hold([wf_m, wf_p], [wz_lo])
    o_fm, o_fp = sp(wf_m, CORE), sp(wf_p, CORE)
    o_z, o_zm, o_zp = (sp(v, CORE) for v in (wz2, wz_m, wz_p))
    def source(dy, dz):
        m = mx(dy, dz)
        dx = (m % 4 - x) % 4
        return jnp.where(dx == 3, 1, jnp.where(dx == 1, 2, jnp.where(dx == 2, 3, 0))) + jnp.where(m // 4 == zh, 0, 4)

    entries = [mx(0, 0), mx(0, 1), mx(-1, 0), mx(1, 0), mx(-1, 1), mx(1, 1), mx(2, 0), mx(2, 1), core,
               mw(0, 0), mw(-1, 0), mw(1, 0), mw(2, 0), mw(0, 1), mw(-1, 1), mw(1, 1), mw(2, 1), core]
    calls = []
    for yb, xb in (([(1, 1), (-1, 1), (2, 1)], []), ([], [(1, 1), (-1, 1)]),
                   ([(2, 0), (1, 0), (-1, 0), (0, 1)], []), ([], [(2, 1), (1, 0), (-1, 0), (0, 1)]),
                   ([(0, 0)], [(0, 0), (2, 0)])):
        calls.append((len(entries), yb, xb))
        entries += [core] + [source(*b) for b in yb] + [mw(*b) for b in xb]
    table = ivec(*entries)
    n_own, n_oth, st = normalize(table, st, [p0, pz, p_m, p_p, pz_m, pz_p, f_m, f_p], wz_lo)
    mean, rstd = st[:, 0:1], st[:, 1:2]
    wzf_m, wzf_p, n_oth = hold([wzf_m, wzf_p, n_oth], [o_z])
    o_zfm, o_zfp = sp(wzf_m, CORE), sp(wzf_p, CORE)
    (n_oth,) = hold([n_oth], [o_zfm, o_zfp, o_zm, o_zp, o_fm, o_fp])
    n_other = sp(n_oth, CORE)
    ws = [w1, w_m, w_p, wf_m, wf_p, o_w, o_fm, o_fp,
          wz2, wz_m, wz_p, wzf_m, wzf_p, o_z, o_zm, o_zp, o_zfm, o_zfp]
    heads_out, dqkv, mom = attend(table, counts.reshape(4), n_own, n_oth, ws, grad_out)

    d_other = sp(dqkv, CORE)

    def blocks(call, deps, **kw):
        base, yb, xb = calls[call]
        return grads(table, base, len(yb), len(xb), dqkv, d_other if xb else dqkv, ws, n_own,
                     n_other if xb else n_own, deps, **kw)

    yu, yd, y2 = blocks(0, [mom], tail=True)
    ya = [mpp(yu, YP), mpp(yd, YM), mpp(y2, Y2)]
    xu, xd = blocks(1, [yu])
    xa = [sp(xu, XP), sp(xd, XM)]
    y2o, y1u, y1d, y0p = blocks(2, [xu])
    x2, x1u, x1d, x0p = blocks(3, [y0p])
    xa.append(sp(x2, X2))
    y_out = sum_rows(y0p, mom, ya, [x0p])
    yz = mpp(y_out, ZLO)
    yb1, yb2 = mpp(y1u, YP), mpp(y1d, YM)
    y0, x0, x2o = blocks(4, [y_out])
    x_out = sum_blocks([x0p, *xa], [y0])
    x1u, x1d = hold([x1u, x1d], [y0])
    xb1, xb2 = sp(x1u, XP), sp(x1d, XM)
    early = early_sum([y0, yb1, yb2, yz])
    (y2o,) = hold([y2o], [yz, yb1, yb2, x_out])
    (x_out,) = hold([x_out], [y2o])
    yb3, xz = mpp(y2o, Y2), sp(x_out, ZHI)
    (x2o,) = hold([x2o], [xb1, xb2, x_out])
    xb3 = sp(x2o, X2)

    f = lambda v: v.astype(F32)
    mom = jnp.sum((f(y_out[ROWS:ROWS + 6]) + f(yz[ROWS:ROWS + 6])).reshape(2, 3, 2 * DB), axis=1)[:, :ROWS] / D
    gn = early + f(yb3)
    xhat = (f(patches) - mean) * rstd
    gg = jnp.sum(gn * xhat, axis=0)
    for perm in (CORE, ZHI):
        gg = gg + sp(gg, perm)
    gg = (gg + sp(gg, X2)) + (sp(gg, XP) + sp(gg, XM))
    grad_p = ((gn * gain[None, :] - mom[0][:, None] - xhat * mom[1][:, None]) * rstd).astype(BF)
    gw = jnp.transpose(f(x0) + f(xb1) + f(xb2) + f(xb3) + f(xz), (1, 0, 2))
    return heads_out, grad_p, gg, gw


def solution(mesh):
    placed = (P("seq", "mp"), P("mp"), P("seq", None, "mp"), P("seq", None), P("seq", "mp"))
    return jax.shard_map(
        local,
        mesh=mesh,
        in_specs=placed,
        out_specs=(P("seq", "mp"), P("seq", "mp"), P("mp"), P("seq", None, "mp")),
        check_vma=False,
    )
```
